32 devices in a mesh: rows: 8 (over z, core), wide: 4 (over y, x).
Axes of the slice: x: 2, y: 2, z: 4, core: 2. Of those that a mesh axis runs over, the one named last changes fastest.
Arguments:
- block_input: bfloat16 [8, 3328, 1152], P('rows', 'wide'), may hold values from -6 to 6
- long_skip: bfloat16 [8, 3328, 1152], P('rows', 'wide'), may hold values from -6 to 6
- segment_ids: int32 [8, 3328], P('rows'), may hold values from 0 to 12, as said below
- item_lengths: int32 [8, 12], P('rows'), may hold values from 0 to 1026, as said below
- skip_weight: bfloat16 [2304, 1152], P('wide'), may hold values from -0.125 to 0.125
- first_gain: bfloat16 [1152], P('wide'), may hold values from 0.25 to 1.75
- first_shift: bfloat16 [1152], P('wide'), may hold values from -1.75 to 1.75
- qkv_weight: bfloat16 [1152, 3456], P('wide'), may hold values from -0.25 to 0.25
- out_weight: bfloat16 [1152, 1152], P('wide'), may hold values from -2 to 2
- second_gain: bfloat16 [1152], P('wide'), may hold values from 0.25 to 1.75
- second_shift: bfloat16 [1152], P('wide'), may hold values from -1.75 to 1.75
- up_weight: bfloat16 [1152, 4608], P('wide'), may hold values from -0.1875 to 0.1875
- down_weight: bfloat16 [4608, 1152], P('wide'), may hold values from -0.09375 to 0.09375
- output_grad: bfloat16 [8, 3328, 1152], P('rows', 'wide'), may hold values from -6 to 6
Outputs:
- layer_output: float32 [8, 3328, 1152], P('rows', 'wide')
- input_grad: float32 [8, 3328, 1152], P('rows', 'wide')
- skip_grad: float32 [8, 3328, 1152], P('rows', 'wide')
- skip_weight_grad: float32 [2304, 1152], P('wide')
- first_gain_grad: float32 [1152], P('wide')
- first_shift_grad: float32 [1152], P('wide')
- qkv_weight_grad: float32 [1152, 3456], P('wide')
- out_weight_grad: float32 [1152, 1152], P('wide')
- second_gain_grad: float32 [1152], P('wide')
- second_shift_grad: float32 [1152], P('wide')
- up_weight_grad: float32 [1152, 4608], P('wide')
- down_weight_grad: float32 [4608, 1152], P('wide')
The draws below stay inside these ranges and needn't reach their ends.
Inputs may be any that keep to these rules, and one draw needn't show every extreme that they name: `item_lengths`: each row lists the lengths of its items, each 258 or 1026, in the order in which they stand in the row, followed by zeros; the lengths of a row sum to less than 3328, and some row holds 3328 // 1026 long items. `segment_ids`: positions of a row carry the number of their item (0 for the first, counting the entries of item_lengths in order); the positions after the last item carry 12.
All inputs are finite; a program needn't handle non-finite values.
Results may differ from the reference program's by a relative error of at most 0.02.
Values may be sent and summed in bfloat16 or wider, within the bound.
A program may use at most 320 MiB of HBM per device.

```python
import jax
import jax.numpy as jnp
from jax import lax

D = 1152
HEADS = 16
HEAD = 72
FF = 4608
ROW_LEN = 3328
SHORT = 258
LONG = 1026
QBLOCKS = 4
NITEM = 12
ROWS = 8


def packing(key):
    base_key = jax.random.fold_in(key, 7)
    row_index = jnp.arange(ROWS, dtype=jnp.int32)
    most_long = ROW_LEN // LONG
    long_count = jax.random.randint(jax.random.fold_in(base_key, 1), (ROWS,), 0, most_long + 1)
    long_count = jnp.where(row_index == 0, most_long, long_count).astype(jnp.int32)
    short_count = (ROW_LEN - long_count * LONG) // SHORT
    item_count = long_count + short_count
    slot_index = jnp.arange(NITEM, dtype=jnp.int32)
    rank_scores = jax.random.randint(jax.random.fold_in(base_key, 2), (ROWS, NITEM), 0, 1 << 20) * NITEM + slot_index[None, :]
    used_slot = slot_index[None, :] < item_count[:, None]
    rank_scores = jnp.where(used_slot, rank_scores, (1 << 20) * NITEM + NITEM)
    ordering = jnp.argsort(rank_scores, axis=1)
    rank_of = jnp.argsort(ordering, axis=1)
    long_flag = rank_of < long_count[:, None]
    item_sizes = jnp.where(used_slot, jnp.where(long_flag, LONG, SHORT), 0)
    return item_sizes.astype(jnp.int32)


def draw_item_lengths(key, part):
    return packing(key)


def draw_segment_ids(key, part):
    item_sizes = packing(key)
    item_ends = jnp.cumsum(item_sizes, axis=1)
    positions = jnp.arange(ROW_LEN, dtype=jnp.int32)
    passed = positions[None, :, None] >= item_ends[:, None, :]
    return jnp.sum(passed.astype(jnp.int32), axis=2).astype(jnp.int32)


def block_scale(key, extent, pieces, least, high):
    def one(axis_at, parts):
        draws = jax.random.uniform(jax.random.fold_in(jax.random.fold_in(key, 6), axis_at), (parts,), jnp.float32, least / len(pieces), high / len(pieces))
        return jnp.repeat(jnp.exp(draws), extent[axis_at] // parts).reshape((-1,) + (1,) * (len(extent) - axis_at - 1))

    gain = one(*pieces[0])
    for cut in pieces[1:]:
        gain = gain * one(*cut)
    return gain


def centred(stream_key, shape, width, reach, pieces=(), kind=jnp.bfloat16):
    values = jax.random.normal(stream_key, shape, jnp.float32) * width
    if len(pieces) > 0:
        values = block_scale(stream_key, shape, pieces, -0.22, 0.18) * values
    return jnp.clip(values, min=-reach, max=reach).astype(kind)


def setup_inputs(seed: int = 0) -> dict:
    arg_keys = jax.random.split(jax.random.key(seed), 15)
    block_input = centred(arg_keys[0], (ROWS, ROW_LEN, D), 1.0, 6.0, ((0, 8), (1, 4)))
    long_skip = centred(arg_keys[1], (ROWS, ROW_LEN, D), 1.0, 6.0, ((0, 8), (1, 4)))
    segment_ids = draw_segment_ids(jax.random.fold_in(arg_keys[14], 71), 0)
    item_lengths = draw_item_lengths(jax.random.fold_in(arg_keys[14], 71), 0)
    skip_weight = centred(arg_keys[4], (2 * D, D), (2 * D) ** -0.5, 0.125, ((0, 4),))
    first_gain = jnp.clip(1.0 + 0.15 * jax.random.normal(arg_keys[5], (D,), jnp.float32), 0.25, 1.75).astype(jnp.bfloat16)
    first_shift = centred(arg_keys[6], (D,), 0.3, 1.75, ((0, 4),))
    qkv_weight = centred(arg_keys[7], (D, 3 * D), (D // 2) ** -0.5, 0.25, ((0, 4),))
    out_weight = centred(arg_keys[8], (D, D), (max(D // 128, 8)) ** -0.5, 2.0, ((0, 4),))
    second_gain = jnp.clip(1.0 + 0.15 * jax.random.normal(arg_keys[9], (D,), jnp.float32), 0.25, 1.75).astype(jnp.bfloat16)
    second_shift = centred(arg_keys[10], (D,), 0.3, 1.75, ((0, 4),))
    up_weight = centred(arg_keys[11], (D, FF), D ** -0.5, 0.1875, ((0, 4),))
    down_weight = centred(arg_keys[12], (FF, D), FF ** -0.5, 0.09375, ((0, 4),))
    output_grad = centred(arg_keys[13], (ROWS, ROW_LEN, D), 1.0, 6.0, ((0, 8), (1, 4)))
    return dict(block_input=block_input, long_skip=long_skip, segment_ids=segment_ids, item_lengths=item_lengths, skip_weight=skip_weight, first_gain=first_gain, first_shift=first_shift, qkv_weight=qkv_weight, out_weight=out_weight, second_gain=second_gain, second_shift=second_shift, up_weight=up_weight, down_weight=down_weight, output_grad=output_grad)


@jax.custom_vjp
def low(v):
    return lax.optimization_barrier(v.astype(jnp.bfloat16)).astype(jnp.float32)

@jax.custom_vjp
def low_back(v):
    return v

def low_keep(v):
    return (low(v), None)

def low_pass(kept, grad):
    return (grad,)

def back_keep(v):
    return (v, None)

def back_low(kept, grad):
    return (low(grad),)
low.defvjp(low_keep, low_pass)
low_back.defvjp(back_keep, back_low)
highest = lax.Precision.HIGHEST

def matmul(left_arr, right_arr):
    return jnp.dot(left_arr, right_arr, precision=highest)

def layer_norm(values, gain_row, shift_row):
    centre = values - lax.optimization_barrier(jnp.mean(values, axis=-1, keepdims=True))
    spread = lax.optimization_barrier(jnp.mean(centre * centre, axis=-1, keepdims=True))
    return centre * lax.rsqrt(spread + 1e-05) * gain_row + shift_row

def attend_row(query_rows, key_rows, value_rows, seg_row, valid_row):
    factor = HEAD ** (-0.5)
    block_len = ROW_LEN // QBLOCKS

    def one_block(packed):
        query_blk, seg_blk, valid_blk = packed
        scores = jnp.einsum('qhd,khd->hqk', query_blk, key_rows, precision=highest) * factor
        scores = low_back(scores)
        allowed = (seg_blk[:, None] == seg_row[None, :]) & (valid_blk[:, None] == valid_row[None, :])
        masked = jnp.where(allowed[None], scores, -1e+30)
        largest = lax.optimization_barrier(jnp.max(masked, axis=-1, keepdims=True))
        exponent = jnp.exp(masked - largest)
        softmax_out = low(exponent / lax.optimization_barrier(jnp.sum(exponent, axis=-1, keepdims=True)))
        mixed_out = jnp.einsum('hqk,khd->qhd', softmax_out, value_rows, precision=highest)
        return mixed_out * valid_blk[:, None, None].astype(mixed_out.dtype)
    outputs = lax.map(jax.checkpoint(one_block), (query_rows.reshape(QBLOCKS, block_len, HEADS, HEAD), seg_row.reshape(QBLOCKS, block_len), valid_row.reshape(QBLOCKS, block_len)))
    return outputs.reshape(ROW_LEN, HEADS * HEAD)

def row_layer(weights, packed):
    skip_weight, first_gain, first_shift, qkv_weight, out_weight, second_gain, second_shift, up_weight, down_weight = weights
    block_row, skip_row, seg_row, valid_row = packed
    joined = jnp.concatenate([block_row, skip_row], axis=-1)
    hidden = low_back(matmul(joined, skip_weight))
    first_normed = low(layer_norm(hidden, first_gain, first_shift))
    qkv_all = low_back(low(matmul(first_normed, qkv_weight))).reshape(ROW_LEN, 3, HEADS, HEAD)
    attended = attend_row(qkv_all[:, 0], qkv_all[:, 1], qkv_all[:, 2], seg_row, valid_row)
    attended = low_back(low(attended))
    mid_state = hidden + low_back(matmul(attended, out_weight))
    second_normed = low(layer_norm(mid_state, second_gain, second_shift))
    upper_proj = low_back(matmul(second_normed, up_weight))
    active = low(jax.nn.gelu(upper_proj, approximate=False))
    return mid_state + matmul(active, down_weight)

def reference(block_input, long_skip, segment_ids, item_lengths, skip_weight, first_gain, first_shift, qkv_weight, out_weight, second_gain, second_shift, up_weight, down_weight, output_grad):
    row_totals = lax.optimization_barrier(jnp.sum(item_lengths, axis=1))
    valid_mask = jnp.arange(ROW_LEN, dtype=jnp.int32)[None, :] < row_totals[:, None]
    weights = tuple((weight_arr.astype(jnp.float32) for weight_arr in (skip_weight, first_gain, first_shift, qkv_weight, out_weight, second_gain, second_shift, up_weight, down_weight)))

    def forward(block_f, skip_f, weight_set):

        def per_row(packed):
            return row_layer(weight_set, packed)
        return lax.map(jax.checkpoint(per_row), (block_f, skip_f, segment_ids, valid_mask))
    output, pullback = jax.vjp(forward, block_input.astype(jnp.float32), long_skip.astype(jnp.float32), weights)
    input_grad, skip_grad, weight_grads = pullback(output_grad.astype(jnp.float32))
    return (output, input_grad, skip_grad, weight_grads[0], weight_grads[1], weight_grads[2], weight_grads[3], weight_grads[4], weight_grads[5], weight_grads[6], weight_grads[7], weight_grads[8])
```

```python
import functools
import jax, jax.numpy as jnp
from jax import lax
from jax.experimental import pallas as pl
from jax.experimental.pallas import tpu as pltpu
HEAD=72; SHORT=258; LONG=1026; NITEM=12
LOG2E=1.4426950408889634
SCALE=HEAD**-0.5
QT=384

def kwin(n): return (n + 29 + 31)//32*32
def qwin(n): return (n + 15 + QT-1)//QT*QT

def nt(a,b): return lax.dot_general(a,b,(((1,),(1,)),((),())),preferred_element_type=jnp.float32)
def nn(a,b): return lax.dot_general(a,b,(((1,),(0,)),((),())),preferred_element_type=jnp.float32)
def tn(a,b): return lax.dot_general(a,b,(((0,),(0,)),((),())),preferred_element_type=jnp.float32)

def windows(start, size, row_len):
    k0 = pl.multiple_of(jnp.minimum(start//16*16, row_len-kwin(size)),16)
    q0 = pl.multiple_of(jnp.minimum(start//16*16, row_len-qwin(size)),16)
    return k0,q0

def split_heads(src_ref, dst_ref, count, chunk=416):
    rows=src_ref.shape[0]
    @pl.loop(0, rows//chunk)
    def _(i):
        r=pl.ds(pl.multiple_of(i*chunk,16),chunk)
        block=src_ref[r,:]
        for j in range(count):
            dst_ref[j,r,:]=block[:,j*HEAD:(j+1)*HEAD]

def join_heads(src_ref, dst_ref, count, chunk=416):
    rows=dst_ref.shape[0]
    @pl.loop(0, rows//chunk)
    def _(i):
        r=pl.ds(pl.multiple_of(i*chunk,16),chunk)
        dst_ref[r,:]=jnp.concatenate([src_ref[j,r,:] for j in range(count)],axis=1)

def zero(ref, chunk=416):
    rows=ref.shape[1]
    @pl.loop(0, rows//chunk)
    def _(i):
        r=pl.ds(pl.multiple_of(i*chunk,16),chunk)
        for j in range(ref.shape[0]):
            ref[j,r,:]=jnp.zeros((chunk,ref.shape[2]),ref.dtype)

def for_items(len_ref, one):
    def step(i, start):
        size=len_ref[0,i]
        @pl.when(size==LONG)
        def _(): one(i,start,LONG)
        @pl.when(size==SHORT)
        def _(): one(i,start,SHORT)
        return start+size
    lax.fori_loop(0,len_ref.shape[1],step,jnp.int32(0))

def mask_edges(values, start, k0, size, fill):
    n=values.shape[0]; body=size//32*32
    off=start-k0
    top=lax.broadcasted_iota(jnp.int32,(32,values.shape[1]),0)
    low=jnp.where(top>=off,values[:32],fill)
    high=jnp.where(top+body<off+size,values[body:],fill)
    return jnp.concatenate([low,values[32:body],high],axis=0)

def attend_kernel(heads, len_ref, qkv_ref, out_ref, lse_ref, split_ref, acc_ref):
    row_len=qkv_ref.shape[0]
    split_heads(qkv_ref, split_ref, 3*heads)
    zero(acc_ref)
    lse_ref[...]=jnp.zeros_like(lse_ref)
    def one(item,start,size):
        k0,q0=windows(start,size,row_len)
        kr=pl.ds(k0,kwin(size))
        @pl.loop(0,qwin(size)//QT)
        def _(t):
            qr=pl.ds(pl.multiple_of(q0+t*QT,16),QT)
            col=q0+t*QT+lax.broadcasted_iota(jnp.int32,(1,QT),1)
            live=(col>=start)&(col<start+size)
            for h in range(heads):
                s=nt(split_ref[heads+h,kr,:],split_ref[h,qr,:])
                s=mask_edges(s,start,k0,size,-1e30)
                m=jnp.max(s,axis=0,keepdims=True)
                p=jnp.exp2((s-m)*(SCALE*LOG2E))
                l=jnp.sum(p,axis=0,keepdims=True)
                o=tn(split_ref[2*heads+h,kr,:],p.astype(jnp.bfloat16))
                o=jnp.where(live,o/l,0.0)
                acc_ref[h,qr,:]+=o.T.astype(jnp.bfloat16)
                lse_ref[item,pl.ds(t*heads+h,1),:]=m*(SCALE*LOG2E)+jnp.log2(l)
    for_items(len_ref,one)
    join_heads(acc_ref,out_ref,heads)

def attend_back_kernel(heads, len_ref, qkv_ref, grad_ref, lse_ref, out_ref, split_ref, gsplit_ref, acc_ref, dk_ref, dv_ref):
    row_len=qkv_ref.shape[0]
    split_heads(qkv_ref, split_ref, 3*heads)
    split_heads(grad_ref, gsplit_ref, heads)
    zero(acc_ref)
    def one(item,start,size):
        k0,q0=windows(start,size,row_len)
        kw=kwin(size)
        kr=pl.ds(k0,kw)
        for h in range(heads):
            dk_ref[h,:kw,:]=jnp.zeros((kw,HEAD),jnp.float32)
            dv_ref[h,:kw,:]=jnp.zeros((kw,HEAD),jnp.float32)
        @pl.loop(0,qwin(size)//QT)
        def _(t):
            qr=pl.ds(pl.multiple_of(q0+t*QT,16),QT)
            col=q0+t*QT+lax.broadcasted_iota(jnp.int32,(1,QT),1)
            live=(col>=start)&(col<start+size)
            for h in range(heads):
                k=split_ref[heads+h,kr,:]; q=split_ref[h,qr,:]; g=gsplit_ref[h,qr,:]
                lse=jnp.where(live,lse_ref[item,pl.ds(t*heads+h,1),:],1e30)
                s=nt(k,q)
                p=jnp.exp2(s*(SCALE*LOG2E)-lse)
                p=mask_edges(p,start,k0,size,0.0)
                dv_ref[h,:kw,:]+=nn(p.astype(jnp.bfloat16),g)
                dp=nt(split_ref[2*heads+h,kr,:],g)
                delta=jnp.sum(p*dp,axis=0,keepdims=True)
                ds=(p*(dp-delta)).astype(jnp.bfloat16)
                dk_ref[h,:kw,:]+=nn(ds,q)
                dq=tn(k,ds)*SCALE
                acc_ref[h,qr,:]+=dq.T.astype(jnp.bfloat16)
        for h in range(heads):
            acc_ref[heads+h,kr,:]+=(dk_ref[h,:kw,:]*SCALE).astype(jnp.bfloat16)
            acc_ref[2*heads+h,kr,:]+=dv_ref[h,:kw,:].astype(jnp.bfloat16)
    for_items(len_ref,one)
    join_heads(acc_ref,out_ref,3*heads)

VM=pl.BlockSpec(memory_space=pltpu.VMEM); SM=pl.BlockSpec(memory_space=pltpu.SMEM)
def attend(lens,qkv,heads):
    n=qkv.shape[0]
    nt_=heads*(qwin(LONG)//QT)
    return pl.pallas_call(functools.partial(attend_kernel,heads),
      out_shape=(jax.ShapeDtypeStruct((n,heads*HEAD),jnp.bfloat16),jax.ShapeDtypeStruct((NITEM,nt_,QT),jnp.float32)),
      in_specs=[SM,VM],out_specs=(VM,VM),
      scratch_shapes=[pltpu.VMEM((3*heads,n,HEAD),jnp.bfloat16),pltpu.VMEM((heads,n,HEAD),jnp.bfloat16)],
      compiler_params=pltpu.CompilerParams(vmem_limit_bytes=56*2**20))(lens,qkv)
def attend_back(lens,qkv,grad,lse,heads):
    n=qkv.shape[0]
    return pl.pallas_call(functools.partial(attend_back_kernel,heads),
      out_shape=jax.ShapeDtypeStruct((n,3*heads*HEAD),jnp.bfloat16),
      in_specs=[SM,VM,VM,VM],out_specs=VM,
      scratch_shapes=[pltpu.VMEM((3*heads,n,HEAD),jnp.bfloat16),pltpu.VMEM((heads,n,HEAD),jnp.bfloat16),pltpu.VMEM((3*heads,n,HEAD),jnp.bfloat16),
        pltpu.VMEM((heads,kwin(LONG),HEAD),jnp.float32),pltpu.VMEM((heads,kwin(LONG),HEAD),jnp.float32)],
      compiler_params=pltpu.CompilerParams(vmem_limit_bytes=60*2**20))(lens,qkv,grad,lse)


F32=jnp.float32; BF=jnp.bfloat16
ANY=pl.BlockSpec(memory_space=pl.ANY)

def gelu_parts(u):
    z=jnp.exp2(u*u*(-0.5*1.4426950408889634))
    t=1.0/(1.0+(0.3275911*0.7071067811865476)*jnp.abs(u))
    poly=((((1.061405429*t-1.453152027)*t+1.421413741)*t-0.284496736)*t+0.254829592)*t
    tail=0.5*poly*z
    cdf=jnp.where(u>=0,1.0-tail,tail)
    return u*cdf, cdf+u*(z*0.3989422804014327)

def mlp_kernel(tile, hidden_ref, att_ref, outw_ref, gain_ref, shift_ref, g_ref, upo_ref, uph_ref, dno_ref, dnh_ref,
               lay_ref, gmid_ref, gatt_ref, gow_ref, small_ref, gupo_ref, guph_ref, gdno_ref, gdnh_ref,
               att_s, n2_s, xhat_s, rstd_s, act_s, gu_s, upb, dnb, gub, gdb, in_sem, out_sem):
    parts,tokens,cols=att_ref.shape
    d=hidden_ref.shape[1]
    tc=tokens//2 if tokens>416 else tokens
    nch=tokens//tc
    half=upo_ref.shape[1]; steps=half//tile
    cc=d//3; fc=256

    def fetch(j,act):
        slot=lax.rem(j,2)
        for first,(us,ds) in ((True,(uph_ref,dnh_ref)),(False,(upo_ref,dno_ref))):
            cond=(j<steps) if first else (j>=steps)
            @pl.when(cond)
            def _():
                k=j if first else j-steps
                off=pl.multiple_of(k*tile,tile)
                act(pltpu.make_async_copy(us.at[:,pl.ds(off,tile)],upb.at[slot],in_sem.at[slot,0]))
                act(pltpu.make_async_copy(ds.at[pl.ds(off,tile),:],dnb.at[slot],in_sem.at[slot,1]))
    def flush(j,act):
        slot=lax.rem(j,2)
        for first,(us,ds) in ((True,(guph_ref,gdnh_ref)),(False,(gupo_ref,gdno_ref))):
            cond=(j<steps) if first else (j>=steps)
            @pl.when(cond)
            def _():
                k=j if first else j-steps
                off=pl.multiple_of(k*tile,tile)
                act(pltpu.make_async_copy(gub.at[slot],us.at[:,pl.ds(off,tile)],out_sem.at[slot,0]))
                act(pltpu.make_async_copy(gdb.at[slot],ds.at[pl.ds(off,tile),:],out_sem.at[slot,1]))
    start=lambda c: c.start()
    wait=lambda c: c.wait()
    fetch(jnp.int32(0),start)
    gain=gain_ref[...]; shift=shift_ref[...]
    sub=tc//2
    @pl.loop(0,2*nch)
    def _(i):
        r=pl.ds(pl.multiple_of(i*sub,16),sub)
        joined=jnp.concatenate([att_ref[p,r,:] for p in range(parts)],axis=1)
        att_s[r,:]=joined
        mid=hidden_ref[r,:]+nn(joined,outw_ref[...])
        lay_ref[r,:]=mid
        cen=mid-jnp.mean(mid,axis=1,keepdims=True)
        inv=lax.rsqrt(jnp.mean(cen*cen,axis=1,keepdims=True)+1e-5)
        xhat=cen*inv
        xhat_s[r,:]=xhat
        rstd_s[r,:]=jnp.broadcast_to(inv,(sub,128))
        n2_s[r,:]=(xhat*gain+shift).astype(BF)
        gmid_ref[r,:]=jnp.zeros((sub,d),F32)
    @pl.loop(0,2*steps)
    def _(j):
        slot=lax.rem(j,2)
        @pl.when(j+1<2*steps)
        def _(): fetch(j+1,start)
        fetch(j,wait)
        @pl.when(j>=2)
        def _(): flush(j-2,wait)
        @pl.loop(0,nch)
        def _(i):
            r=pl.ds(pl.multiple_of(i*tc,16),tc)
            for k in range(tile//fc):
                f=pl.ds(k*fc,fc)
                u=nn(n2_s[r,:],upb[slot,:,f])
                a,dg=gelu_parts(u)
                act_s[r,f]=a.astype(BF)
                ga=nt(g_ref[r,:],dnb[slot,f,:])
                gu_s[r,f]=(ga*dg).astype(BF)
        @pl.loop(0,nch)
        def _(i):
            r=pl.ds(pl.multiple_of(i*tc,16),tc)
            for k in range(3):
                cr=pl.ds(k*cc,cc)
                lay_ref[r,cr]+=nn(act_s[r,:],dnb[slot,:,cr])
                gmid_ref[r,cr]+=nt(gu_s[r,:],upb[slot,cr,:])
        for k in range(tile//fc):
            f=pl.ds(k*fc,fc)
            gdb[slot,f,:]=tn(act_s[:,f],g_ref[...]).astype(BF)
        for k in range(3):
            cr=pl.ds(k*cc,cc)
            gub[slot,cr,:]=tn(n2_s[:,cr],gu_s[...]).astype(BF)
        flush(j,start)
    small_ref[...]=jnp.zeros_like(small_ref)
    @pl.loop(0,2*nch)
    def _(i):
        r=pl.ds(pl.multiple_of(i*sub,16),sub)
        gs=gmid_ref[r,:]; xhat=xhat_s[r,:]
        small_ref[0:1,:]+=jnp.sum(gs*xhat,axis=0,keepdims=True)
        small_ref[1:2,:]+=jnp.sum(gs,axis=0,keepdims=True)
        e=gs*gain
        back=e-jnp.mean(e,axis=1,keepdims=True)-xhat*jnp.mean(e*xhat,axis=1,keepdims=True)
        gm=g_ref[r,:].astype(F32)+back*rstd_s[r,0:1]
        gmid_ref[r,:]=gm
        low=gm.astype(BF)
        n2_s[r,:]=low
        ga=nt(low,outw_ref[...]).astype(BF)
        for p in range(parts):
            gatt_ref[p,r,:]=ga[:,p*cols:(p+1)*cols]
    for k in range(3):
        cr=pl.ds(k*cc,cc)
        gow_ref[cr,:]=tn(att_s[:,cr],n2_s[...]).astype(BF)
    flush(jnp.int32(2*steps-2),wait)
    flush(jnp.int32(2*steps-1),wait)

def mlp(hidden,att,outw,gain,shift,g,upo,uph,dno,dnh):
    tokens,d=hidden.shape; half=upo.shape[1]; tile=half//3
    S=jax.ShapeDtypeStruct
    flops=2*tokens*d*(half*2*6+d*3)
    return pl.pallas_call(functools.partial(mlp_kernel,tile),
        out_shape=(S((tokens,d),F32),S((tokens,d),F32),S(att.shape,BF),S((d,d),BF),S((8,d),F32),
                   S(upo.shape,BF),S(upo.shape,BF),S(dno.shape,BF),S(dno.shape,BF)),
        in_specs=[VM]*6+[ANY]*4,
        out_specs=(VM,)*5+(ANY,)*4,
        scratch_shapes=[pltpu.VMEM((tokens,d),BF),pltpu.VMEM((tokens,d),BF),pltpu.VMEM((tokens,d),F32),pltpu.VMEM((tokens,128),F32),
            pltpu.VMEM((tokens,tile),BF),pltpu.VMEM((tokens,tile),BF),
            pltpu.VMEM((2,d,tile),BF),pltpu.VMEM((2,tile,d),BF),pltpu.VMEM((2,d,tile),BF),pltpu.VMEM((2,tile,d),BF),
            pltpu.SemaphoreType.DMA((2,2)),pltpu.SemaphoreType.DMA((2,2))],
        compiler_params=pltpu.CompilerParams(vmem_limit_bytes=62*2**20),
        cost_estimate=pl.CostEstimate(flops=flops,bytes_accessed=60*2**20,transcendentals=tokens*half*2))(
        hidden,att,outw,gain,shift,g,upo,uph,dno,dnh)


from jax.sharding import Mesh, PartitionSpec as P
WIDE=("y","x"); ROWS=("z","core")
SWAP=[(0,1),(1,0)]

def swap_cores(values):
    return lax.ppermute(values,"core",SWAP)

def pick(values, index, axis):
    return lax.dynamic_index_in_dim(values,index,axis,keepdims=False)

def place_halves(mine, other, core, axis):
    first=jnp.where(core==0,mine,other); second=jnp.where(core==0,other,mine)
    return jnp.stack([first,second],axis=axis)

def dot(a,b): return jnp.dot(a,b,preferred_element_type=F32)

def norm(values):
    cen=values-jnp.mean(values,axis=1,keepdims=True)
    inv=lax.rsqrt(jnp.mean(cen*cen,axis=1,keepdims=True)+1e-5)
    return cen*inv,inv

def on_device(nw, block_input, long_skip, segment_ids, item_lengths, skip_weight, first_gain, first_shift, qkv_weight,
              out_weight, second_gain, second_shift, up_weight, down_weight, output_grad):
    core=lax.axis_index("core")
    _,tokens,d=block_input.shape
    heads=qkv_weight.shape[1]//(3*HEAD*nw); hd=heads*HEAD
    ff=up_weight.shape[1]; fb=ff//(2*nw)
    gather=lambda v: lax.all_gather(v,WIDE,axis=0,tiled=True)
    vec=gather(jnp.stack([first_gain,first_shift,second_gain,second_shift],axis=1)).T.astype(F32)
    gain1,shift1,gain2,shift2=[vec[i:i+1] for i in range(4)]
    w_skip=gather(skip_weight)
    joined=jnp.concatenate([block_input[0],long_skip[0]],axis=1)
    w_heads=qkv_weight.reshape(d//nw,3,nw,hd).transpose(2,0,1,3)
    w_heads=lax.all_to_all(w_heads,WIDE,0,0).reshape(d,3*hd)
    hidden=dot(joined,w_skip)
    xhat1,inv1=norm(hidden)
    normed_all=gather((xhat1*gain1+shift1).astype(BF))
    qkv=dot(normed_all,w_heads).astype(BF)
    w_out=gather(out_weight)
    up_mine=gather(pick(up_weight.reshape(d//nw,nw,2,fb),core,2).reshape(d//nw,nw*fb))
    down_mine=gather(pick(down_weight.reshape(2,fb,d),core,0))
    up_other,down_other=swap_cores(up_mine),swap_cores(down_mine)
    att,lse=attend(item_lengths,qkv,heads)
    att=lax.all_to_all(att.reshape(nw,tokens,hd),WIDE,0,0)
    lay,gmid,gatt,gow,small,gupo,guph,gdno,gdnh=mlp(hidden,att,w_out,gain2,shift2,output_grad[0],up_mine,up_other,down_mine,down_other)
    grad_heads=lax.all_to_all(gatt,WIDE,0,0).reshape(nw*tokens,hd)

    def reduce_mine(mine,other):
        both=(mine.astype(F32)+swap_cores(other).astype(F32)).astype(BF)
        share=lax.psum_scatter(both,WIDE,scatter_dimension=0,tiled=True)
        return lax.psum(share,"z")
    def both_cores(mine,axis):
        return place_halves(mine,swap_cores(mine),core,axis).astype(F32)
    up_share=both_cores(reduce_mine(gupo,guph).reshape(d//nw,nw,fb),2).reshape(d//nw,ff)
    down_share=both_cores(reduce_mine(gdno,gdnh),0).reshape(ff//nw,d)
    def by_rows(grad):
        rows=grad.shape[0]//nw
        cut=grad.reshape(nw,2,rows//2,grad.shape[1])
        mine=reduce_mine(pick(cut,core,1).reshape(-1,grad.shape[1]),pick(cut,1-core,1).reshape(-1,grad.shape[1]))
        return both_cores(mine,0).reshape(rows,-1)
    out_share=by_rows(gow)
    grad_qkv=attend_back(item_lengths,qkv,grad_heads,lse,heads)
    part_first=nt(grad_qkv,w_heads).astype(BF)
    grad_first=lax.psum_scatter(part_first,WIDE,scatter_dimension=0,tiled=True).astype(F32)
    gqkv=tn(normed_all,grad_qkv).astype(BF).reshape(nw,2,d//nw//2,3*hd)
    gqkv=(pick(gqkv,core,1).astype(F32)+swap_cores(pick(gqkv,1-core,1)).astype(F32)).astype(BF)
    gqkv=lax.all_to_all(lax.psum(gqkv,"z"),WIDE,0,0).reshape(nw,-1,3,hd).transpose(1,2,0,3)
    qkv_share=both_cores(gqkv,0).reshape(d//nw,-1)
    e1=grad_first*gain1
    back=inv1*(e1-jnp.mean(e1,axis=1,keepdims=True)-xhat1*jnp.mean(e1*xhat1,axis=1,keepdims=True))
    grad_hidden=(gmid+back).astype(BF)
    skip_share=by_rows(tn(joined,grad_hidden).astype(BF))
    grad_joined=nt(grad_hidden,w_skip)
    smalls=jnp.stack([jnp.sum(grad_first*xhat1,axis=0),jnp.sum(grad_first,axis=0),small[0],small[1]],axis=1)
    smalls=lax.psum(lax.psum_scatter(smalls.astype(BF),WIDE,scatter_dimension=0,tiled=True),ROWS).astype(F32)
    return (lay[None],grad_joined[:,:d][None],grad_joined[:,d:][None],skip_share,smalls[:,0],smalls[:,1],qkv_share,out_share,
            smalls[:,2],smalls[:,3],up_share,down_share)

def solution(mesh):
    rows,wide=mesh.devices.shape
    side=2 if wide==4 else int(wide**0.5)
    grid=Mesh(mesh.devices.reshape(rows//2,2,wide//side,side),("z","core","y","x"))
    tok=P(ROWS,WIDE,None); row=P(ROWS,None); mat=P(WIDE,None); vec=P(WIDE)
    return jax.shard_map(functools.partial(on_device,wide),mesh=grid,
        in_specs=(tok,tok,row,row,mat,vec,vec,mat,mat,vec,vec,mat,mat,tok),
        out_specs=(tok,tok,tok,mat,vec,vec,mat,mat,vec,vec,mat,mat),check_vma=False)
```

```python
import functools
import jax, jax.numpy as jnp
from jax import lax
from jax.experimental import pallas as pl
from jax.experimental.pallas import tpu as pltpu
HEAD=72; SHORT=258; LONG=1026; NITEM=12
LOG2E=1.4426950408889634
SCALE=HEAD**-0.5
QT=384

def kwin(n): return (n + 29 + 31)//32*32
def qwin(n): return (n + 15 + QT-1)//QT*QT

def nt(a,b): return lax.dot_general(a,b,(((1,),(1,)),((),())),preferred_element_type=jnp.float32)
def nn(a,b): return lax.dot_general(a,b,(((1,),(0,)),((),())),preferred_element_type=jnp.float32)
def tn(a,b): return lax.dot_general(a,b,(((0,),(0,)),((),())),preferred_element_type=jnp.float32)

def windows(start, size, row_len):
    k0 = pl.multiple_of(jnp.minimum(start//16*16, row_len-kwin(size)),16)
    q0 = pl.multiple_of(jnp.minimum(start//16*16, row_len-qwin(size)),16)
    return k0,q0

def split_heads(src_ref, dst_ref, count, chunk=416):
    rows=src_ref.shape[0]
    @pl.loop(0, rows//chunk)
    def _(i):
        r=pl.ds(pl.multiple_of(i*chunk,16),chunk)
        block=src_ref[r,:]
        for j in range(count):
            dst_ref[j,r,:]=block[:,j*HEAD:(j+1)*HEAD]

def join_heads(src_ref, dst_ref, count, chunk=416):
    rows=dst_ref.shape[0]
    @pl.loop(0, rows//chunk)
    def _(i):
        r=pl.ds(pl.multiple_of(i*chunk,16),chunk)
        dst_ref[r,:]=jnp.concatenate([src_ref[j,r,:] for j in range(count)],axis=1)

def zero(ref, chunk=416):
    rows=ref.shape[1]
    @pl.loop(0, rows//chunk)
    def _(i):
        r=pl.ds(pl.multiple_of(i*chunk,16),chunk)
        for j in range(ref.shape[0]):
            ref[j,r,:]=jnp.zeros((chunk,ref.shape[2]),ref.dtype)

def for_items(len_ref, one):
    def step(i, start):
        size=len_ref[0,i]
        @pl.when(size==LONG)
        def _(): one(i,start,LONG)
        @pl.when(size==SHORT)
        def _(): one(i,start,SHORT)
        return start+size
    lax.fori_loop(0,len_ref.shape[1],step,jnp.int32(0))

def mask_edges(values, start, k0, size, fill):
    n=values.shape[0]; body=size//32*32
    off=start-k0
    top=lax.broadcasted_iota(jnp.int32,(32,values.shape[1]),0)
    low=jnp.where(top>=off,values[:32],fill)
    high=jnp.where(top+body<off+size,values[body:],fill)
    return jnp.concatenate([low,values[32:body],high],axis=0)

def attend_kernel(heads, len_ref, qkv_ref, out_ref, lse_ref, split_ref, acc_ref):
    row_len=qkv_ref.shape[0]
    split_heads(qkv_ref, split_ref, 3*heads)
    zero(acc_ref)
    lse_ref[...]=jnp.zeros_like(lse_ref)
    def one(item,start,size):
        k0,q0=windows(start,size,row_len)
        kr=pl.ds(k0,kwin(size))
        @pl.loop(0,qwin(size)//QT)
        def _(t):
            qr=pl.ds(pl.multiple_of(q0+t*QT,16),QT)
            col=q0+t*QT+lax.broadcasted_iota(jnp.int32,(1,QT),1)
            live=(col>=start)&(col<start+size)
            for h in range(heads):
                s=nt(split_ref[heads+h,kr,:],split_ref[h,qr,:])
                s=mask_edges(s,start,k0,size,-1e30)
                m=jnp.max(s,axis=0,keepdims=True)
                p=jnp.exp2((s-m)*(SCALE*LOG2E))
                l=jnp.sum(p,axis=0,keepdims=True)
                o=tn(split_ref[2*heads+h,kr,:],p.astype(jnp.bfloat16))
                o=jnp.where(live,o/l,0.0)
                acc_ref[h,qr,:]+=o.T.astype(jnp.bfloat16)
                lse_ref[item,pl.ds(t*heads+h,1),:]=m*(SCALE*LOG2E)+jnp.log2(l)
    for_items(len_ref,one)
    join_heads(acc_ref,out_ref,heads)

def attend_back_kernel(heads, len_ref, qkv_ref, grad_ref, lse_ref, out_ref, split_ref, gsplit_ref, acc_ref, dk_ref, dv_ref):
    row_len=qkv_ref.shape[0]
    split_heads(qkv_ref, split_ref, 3*heads)
    split_heads(grad_ref, gsplit_ref, heads)
    zero(acc_ref)
    def one(item,start,size):
        k0,q0=windows(start,size,row_len)
        kw=kwin(size)
        kr=pl.ds(k0,kw)
        for h in range(heads):
            dk_ref[h,:kw,:]=jnp.zeros((kw,HEAD),jnp.float32)
            dv_ref[h,:kw,:]=jnp.zeros((kw,HEAD),jnp.float32)
        @pl.loop(0,qwin(size)//QT)
        def _(t):
            qr=pl.ds(pl.multiple_of(q0+t*QT,16),QT)
            col=q0+t*QT+lax.broadcasted_iota(jnp.int32,(1,QT),1)
            live=(col>=start)&(col<start+size)
            for h in range(heads):
                k=split_ref[heads+h,kr,:]; q=split_ref[h,qr,:]; g=gsplit_ref[h,qr,:]
                lse=jnp.where(live,lse_ref[item,pl.ds(t*heads+h,1),:],1e30)
                s=nt(k,q)
                p=jnp.exp2(s*(SCALE*LOG2E)-lse)
                p=mask_edges(p,start,k0,size,0.0)
                dv_ref[h,:kw,:]+=nn(p.astype(jnp.bfloat16),g)
                dp=nt(split_ref[2*heads+h,kr,:],g)
                delta=jnp.sum(p*dp,axis=0,keepdims=True)
                ds=(p*(dp-delta)).astype(jnp.bfloat16)
                dk_ref[h,:kw,:]+=nn(ds,q)
                dq=tn(k,ds)*SCALE
                acc_ref[h,qr,:]+=dq.T.astype(jnp.bfloat16)
        for h in range(heads):
            acc_ref[heads+h,kr,:]+=(dk_ref[h,:kw,:]*SCALE).astype(jnp.bfloat16)
            acc_ref[2*heads+h,kr,:]+=dv_ref[h,:kw,:].astype(jnp.bfloat16)
    for_items(len_ref,one)
    join_heads(acc_ref,out_ref,3*heads)

VM=pl.BlockSpec(memory_space=pltpu.VMEM); SM=pl.BlockSpec(memory_space=pltpu.SMEM)
def attend(lens,qkv,heads):
    n=qkv.shape[0]
    nt_=heads*(qwin(LONG)//QT)
    return pl.pallas_call(functools.partial(attend_kernel,heads),
      out_shape=(jax.ShapeDtypeStruct((n,heads*HEAD),jnp.bfloat16),jax.ShapeDtypeStruct((NITEM,nt_,QT),jnp.float32)),
      in_specs=[SM,VM],out_specs=(VM,VM),
      scratch_shapes=[pltpu.VMEM((3*heads,n,HEAD),jnp.bfloat16),pltpu.VMEM((heads,n,HEAD),jnp.bfloat16)],
      compiler_params=pltpu.CompilerParams(vmem_limit_bytes=56*2**20),
      cost_estimate=pl.CostEstimate(flops=heads*n*n*HEAD*4,bytes_accessed=12*2**20,transcendentals=heads*n*n//3))(lens,qkv)
def attend_back(lens,qkv,grad,lse,heads):
    n=qkv.shape[0]
    return pl.pallas_call(functools.partial(attend_back_kernel,heads),
      out_shape=jax.ShapeDtypeStruct((n,3*heads*HEAD),jnp.bfloat16),
      in_specs=[SM,VM,VM,VM],out_specs=VM,
      scratch_shapes=[pltpu.VMEM((3*heads,n,HEAD),jnp.bfloat16),pltpu.VMEM((heads,n,HEAD),jnp.bfloat16),pltpu.VMEM((3*heads,n,HEAD),jnp.bfloat16),
        pltpu.VMEM((heads,kwin(LONG),HEAD),jnp.float32),pltpu.VMEM((heads,kwin(LONG),HEAD),jnp.float32)],
      compiler_params=pltpu.CompilerParams(vmem_limit_bytes=60*2**20),
      cost_estimate=pl.CostEstimate(flops=heads*n*n*HEAD*10,bytes_accessed=20*2**20,transcendentals=heads*n*n//3))(lens,qkv,grad,lse)


F32=jnp.float32; BF=jnp.bfloat16
ANY=pl.BlockSpec(memory_space=pl.ANY)

def gelu_parts(u):
    z=jnp.exp2(u*u*(-0.5*1.4426950408889634))
    t=1.0/(1.0+(0.3275911*0.7071067811865476)*jnp.abs(u))
    poly=((((1.061405429*t-1.453152027)*t+1.421413741)*t-0.284496736)*t+0.254829592)*t
    tail=0.5*poly*z
    cdf=jnp.where(u>=0,1.0-tail,tail)
    return u*cdf, cdf+u*(z*0.3989422804014327)

def mlp_kernel(tile, hidden_ref, att_ref, outw_ref, gain_ref, shift_ref, g_ref, upo_ref, uph_ref, dno_ref, dnh_ref,
               lay_ref, gmid_ref, gatt_ref, gow_ref, small_ref, gupo_ref, guph_ref, gdno_ref, gdnh_ref,
               att_s, n2_s, xhat_s, rstd_s, act_s, gu_s, upb, dnb, gub, gdb, in_sem, out_sem):
    parts,tokens,cols=att_ref.shape
    d=hidden_ref.shape[1]
    tc=tokens//2 if tokens>416 else tokens
    nch=tokens//tc
    half=upo_ref.shape[1]; steps=half//tile
    cc=d//3; fc=256

    def fetch(j,act):
        slot=lax.rem(j,2)
        for first,(us,ds) in ((True,(uph_ref,dnh_ref)),(False,(upo_ref,dno_ref))):
            cond=(j<steps) if first else (j>=steps)
            @pl.when(cond)
            def _():
                k=j if first else j-steps
                off=pl.multiple_of(k*tile,tile)
                act(pltpu.make_async_copy(us.at[:,pl.ds(off,tile)],upb.at[slot],in_sem.at[slot,0]))
                act(pltpu.make_async_copy(ds.at[pl.ds(off,tile),:],dnb.at[slot],in_sem.at[slot,1]))
    def flush(j,act):
        slot=lax.rem(j,2)
        for first,(us,ds) in ((True,(guph_ref,gdnh_ref)),(False,(gupo_ref,gdno_ref))):
            cond=(j<steps) if first else (j>=steps)
            @pl.when(cond)
            def _():
                k=j if first else j-steps
                off=pl.multiple_of(k*tile,tile)
                act(pltpu.make_async_copy(gub.at[slot],us.at[:,pl.ds(off,tile)],out_sem.at[slot,0]))
                act(pltpu.make_async_copy(gdb.at[slot],ds.at[pl.ds(off,tile),:],out_sem.at[slot,1]))
    start=lambda c: c.start()
    wait=lambda c: c.wait()
    fetch(jnp.int32(0),start)
    gain=gain_ref[...]; shift=shift_ref[...]
    sub=tc//2
    @pl.loop(0,2*nch)
    def _(i):
        r=pl.ds(pl.multiple_of(i*sub,16),sub)
        joined=jnp.concatenate([att_ref[p,r,:] for p in range(parts)],axis=1)
        att_s[r,:]=joined
        mid=hidden_ref[r,:]+nn(joined,outw_ref[...])
        lay_ref[r,:]=mid
        cen=mid-jnp.mean(mid,axis=1,keepdims=True)
        inv=lax.rsqrt(jnp.mean(cen*cen,axis=1,keepdims=True)+1e-5)
        xhat=cen*inv
        xhat_s[r,:]=xhat
        rstd_s[r,:]=jnp.broadcast_to(inv,(sub,128))
        n2_s[r,:]=(xhat*gain+shift).astype(BF)
        gmid_ref[r,:]=jnp.zeros((sub,d),F32)
    @pl.loop(0,2*steps)
    def _(j):
        slot=lax.rem(j,2)
        @pl.when(j+1<2*steps)
        def _(): fetch(j+1,start)
        fetch(j,wait)
        @pl.when(j>=2)
        def _(): flush(j-2,wait)
        @pl.loop(0,nch)
        def _(i):
            r=pl.ds(pl.multiple_of(i*tc,16),tc)
            for k in range(tile//fc):
                f=pl.ds(k*fc,fc)
                u=nn(n2_s[r,:],upb[slot,:,f])
                a,dg=gelu_parts(u)
                act_s[r,f]=a.astype(BF)
                ga=nt(g_ref[r,:],dnb[slot,f,:])
                gu_s[r,f]=(ga*dg).astype(BF)
        @pl.loop(0,nch)
        def _(i):
            r=pl.ds(pl.multiple_of(i*tc,16),tc)
            for k in range(3):
                cr=pl.ds(k*cc,cc)
                lay_ref[r,cr]+=nn(act_s[r,:],dnb[slot,:,cr])
                gmid_ref[r,cr]+=nt(gu_s[r,:],upb[slot,cr,:])
        for k in range(tile//fc):
            f=pl.ds(k*fc,fc)
            gdb[slot,f,:]=tn(act_s[:,f],g_ref[...]).astype(BF)
        for k in range(3):
            cr=pl.ds(k*cc,cc)
            gub[slot,cr,:]=tn(n2_s[:,cr],gu_s[...]).astype(BF)
        flush(j,start)
    small_ref[...]=jnp.zeros_like(small_ref)
    @pl.loop(0,2*nch)
    def _(i):
        r=pl.ds(pl.multiple_of(i*sub,16),sub)
        gs=gmid_ref[r,:]; xhat=xhat_s[r,:]
        small_ref[0:1,:]+=jnp.sum(gs*xhat,axis=0,keepdims=True)
        small_ref[1:2,:]+=jnp.sum(gs,axis=0,keepdims=True)
        e=gs*gain
        back=e-jnp.mean(e,axis=1,keepdims=True)-xhat*jnp.mean(e*xhat,axis=1,keepdims=True)
        gm=g_ref[r,:].astype(F32)+back*rstd_s[r,0:1]
        gmid_ref[r,:]=gm
        low=gm.astype(BF)
        n2_s[r,:]=low
        ga=nt(low,outw_ref[...]).astype(BF)
        for p in range(parts):
            gatt_ref[p,r,:]=ga[:,p*cols:(p+1)*cols]
    for k in range(3):
        cr=pl.ds(k*cc,cc)
        gow_ref[cr,:]=tn(att_s[:,cr],n2_s[...]).astype(BF)
    flush(jnp.int32(2*steps-2),wait)
    flush(jnp.int32(2*steps-1),wait)

def mlp(hidden,att,outw,gain,shift,g,upo,uph,dno,dnh):
    tokens,d=hidden.shape; half=upo.shape[1]; tile=half//3
    S=jax.ShapeDtypeStruct
    flops=2*tokens*d*(half*2*6+d*3)
    return pl.pallas_call(functools.partial(mlp_kernel,tile),
        out_shape=(S((tokens,d),F32),S((tokens,d),F32),S(att.shape,BF),S((d,d),BF),S((8,d),F32),
                   S(upo.shape,BF),S(upo.shape,BF),S(dno.shape,BF),S(dno.shape,BF)),
        in_specs=[VM]*6+[ANY]*4,
        out_specs=(VM,)*5+(ANY,)*4,
        scratch_shapes=[pltpu.VMEM((tokens,d),BF),pltpu.VMEM((tokens,d),BF),pltpu.VMEM((tokens,d),F32),pltpu.VMEM((tokens,128),F32),
            pltpu.VMEM((tokens,tile),BF),pltpu.VMEM((tokens,tile),BF),
            pltpu.VMEM((2,d,tile),BF),pltpu.VMEM((2,tile,d),BF),pltpu.VMEM((2,d,tile),BF),pltpu.VMEM((2,tile,d),BF),
            pltpu.SemaphoreType.DMA((2,2)),pltpu.SemaphoreType.DMA((2,2))],
        compiler_params=pltpu.CompilerParams(vmem_limit_bytes=62*2**20),
        cost_estimate=pl.CostEstimate(flops=flops,bytes_accessed=60*2**20,transcendentals=tokens*half*2))(
        hidden,att,outw,gain,shift,g,upo,uph,dno,dnh)


MESH=pl.DeviceIdType.MESH

def place():
    x,y,c=lax.axis_index("x"),lax.axis_index("y"),lax.axis_index("core")
    return x,y,c,2*y+x,2*y+1-x,2-2*y+x,3-2*y-x

class Links:
    def __init__(self,send,recv):
        self.send,self.recv,self.sent=send,recv,[]
        x,y,c=lax.axis_index("x"),lax.axis_index("y"),lax.axis_index("core")
        self.to={"X":{"x":1-x},"Y":{"y":1-y},"D":{"x":1-x,"y":1-y},"C":{"core":1-c}}
    def meet(self,who):
        barrier=pltpu.get_barrier_semaphore()
        for t in who:
            pl.semaphore_signal(barrier,inc=1,device_id=self.to[t],device_id_type=MESH)
        pl.semaphore_wait(barrier,len(who))
    def start(self,k,t,src,dst):
        copy=pltpu.make_async_remote_copy(src_ref=src,dst_ref=dst,send_sem=self.send.at[k],recv_sem=self.recv.at[k],
                                          device_id=self.to[t],device_id_type=MESH)
        copy.start()
        self.sent.append(copy)
    def got(self,k,t,dst):
        pltpu.make_async_remote_copy(src_ref=dst,dst_ref=dst,send_sem=self.send.at[k],recv_sem=self.recv.at[k],
                                     device_id=self.to[t],device_id_type=MESH).wait_recv()
    def finish(self):
        for copy in self.sent: copy.wait_send()

def first_kernel(block_ref,long_ref,skip_ref,qkvw_ref,vec_ref,
                 hidden_out,normed_out,qkv_out,heads_out,wskip_out,vec_out,
                 ws,ns,hs,piece,hid,qs,vs,send,recv,local):
    x,y,c,w,wx,wy,wd=place()
    tokens,d=block_ref.shape
    sr=skip_ref.shape[0]; half=sr//2; part=half//2
    kr=qkvw_ref.shape[0]; kh=kr//2; hd=qkvw_ref.shape[1]//12
    tc=tokens//4
    mul=pl.multiple_of
    net=Links(send,recv)
    net.meet("XYDC")
    def srows(b,core,p): return pl.ds(mul(b*sr+core*half+p*part,16),part)
    def mine(p): return pl.ds(mul(c*half+p*part,16),part)
    net.start(0,"X",skip_ref.at[mine(0)],ws.at[srows(w,c,0)])
    net.start(2,"Y",skip_ref.at[mine(1)],ws.at[srows(w,c,1)])
    net.start(1,"X",skip_ref.at[mine(1)],ws.at[srows(w,c,1)])
    net.start(3,"Y",skip_ref.at[mine(0)],ws.at[srows(w,c,0)])
    own=pltpu.make_async_copy(skip_ref,ws.at[pl.ds(mul(w*sr,16),sr)],local.at[0])
    own.start()
    for k,t in ((30,"X"),(31,"Y"),(32,"D")): net.start(k,t,vec_ref,vs.at[w])
    vs[w]=vec_ref[...]
    for p in range(4):
        piece[p]=jnp.concatenate([qkvw_ref[:,(s*4+p)*hd:(s*4+p+1)*hd] for s in range(3)],axis=1)
    own_heads=pltpu.make_async_copy(piece.at[w],hs.at[pl.ds(mul(w*kr,16),kr)],local.at[1])
    own_heads.start()
    def pass_on(k,t,b,p,onward):
        r=srows(b,c,p)
        net.got(k,t,ws.at[r])
        for k2,t2 in onward: net.start(k2,t2,ws.at[r],ws.at[r])
    pass_on(0,"X",wx,0,((4,"Y"),(6,"C")))
    pass_on(2,"Y",wy,1,((5,"X"),(7,"C")))
    pass_on(1,"X",wx,1,((8,"C"),))
    pass_on(3,"Y",wy,0,((9,"C"),))
    def hrows(b,core): return pl.ds(mul(b*kr+core*kh,16),kh)
    cut=pl.ds(mul(c*kh,16),kh)
    net.start(12,"X",piece.at[wx,cut],hs.at[hrows(w,c)])
    net.start(13,"Y",piece.at[wy,cut],hs.at[hrows(w,c)])
    net.start(14,"D",piece.at[wd,cut],hs.at[hrows(w,c)])
    own.wait()
    net.got(6,"C",ws.at[srows(wx,1-c,0)])
    net.got(8,"C",ws.at[srows(wx,1-c,1)])
    near=pl.ds(mul(y*d,16),d); far=pl.ds(mul((1-y)*d,16),d)
    def tok(i): return pl.ds(mul(i*tc,16),tc)
    @pl.loop(0,4)
    def _(i):
        lhs=jnp.where(y==0,block_ref[tok(i),:],long_ref[tok(i),:])
        hid[tok(i),:]=nn(lhs,ws[near,:])
    pass_on(4,"Y",wd,0,((10,"C"),))
    pass_on(5,"X",wd,1,((11,"C"),))
    net.got(7,"C",ws.at[srows(wy,1-c,1)])
    net.got(9,"C",ws.at[srows(wy,1-c,0)])
    net.got(10,"C",ws.at[srows(wd,1-c,0)])
    net.got(11,"C",ws.at[srows(wd,1-c,1)])
    for k,t,b in ((30,"X",wx),(31,"Y",wy),(32,"D",wd)): net.got(k,t,vs.at[b])
    gain=jnp.concatenate([vs[p,0:1,:] for p in range(4)],axis=1)
    shift=jnp.concatenate([vs[p,1:2,:] for p in range(4)],axis=1)
    def nrows(b,i): return pl.ds(mul(b*tokens+i*tc,16),tc)
    def spread(i,t):
        net.start((18 if t=="X" else 22)+i,t,ns.at[nrows(w,i)],ns.at[nrows(w,i)])
    for i in range(4):
        r=tok(i)
        lhs=jnp.where(y==0,long_ref[r,:],block_ref[r,:])
        h=hid[r,:]+nn(lhs,ws[far,:])
        hid[r,:]=h
        cen=h-jnp.mean(h,axis=1,keepdims=True)
        inv=lax.rsqrt(jnp.mean(cen*cen,axis=1,keepdims=True)+1e-5)
        ns[nrows(w,i),:]=(cen*inv*gain+shift).astype(BF)
        spread(i,"XYXY"[i])
    for i,t in ((1,"X"),(0,"Y"),(3,"X"),(2,"Y")): spread(i,t)
    outs=[]
    def put(k,src,dst):
        copy=pltpu.make_async_copy(src,dst,local.at[k]); copy.start(); outs.append(copy)
    put(2,ws,wskip_out); put(3,hid,hidden_out); put(7,vs,vec_out)
    for j,(t,b) in enumerate((("X",wx),("Y",wy),("D",wd))):
        net.got(12+j,t,hs.at[hrows(b,c)])
        net.start(15+j,"C",hs.at[hrows(b,c)],hs.at[hrows(b,c)])
    for j,b in enumerate((wx,wy,wd)):
        net.got(15+j,"C",hs.at[hrows(b,1-c)])
    own_heads.wait()
    put(4,hs,heads_out)
    def project(b,i): qs[nrows(b,i),:]=nn(ns[nrows(b,i),:],hs[...]).astype(BF)
    @pl.loop(0,4)
    def _(i): project(w,i)
    for i,t,b,k,k2,t2 in ((0,"X",wx,18,26,"Y"),(1,"Y",wy,22,27,"X"),(2,"X",wx,18,28,"Y"),(3,"Y",wy,22,29,"X")):
        net.got(k+i,t,ns.at[nrows(b,i)])
        net.start(k2,t2,ns.at[nrows(b,i)],ns.at[nrows(b,i)])
    @pl.loop(0,2)
    def _(i): project(wx,2*i)
    @pl.loop(0,2)
    def _(i): project(wy,2*i+1)
    for i in (1,3):
        net.got(18+i,"X",ns.at[nrows(wx,i)])
        project(wx,i)
        net.got(22+i-1,"Y",ns.at[nrows(wy,i-1)])
        project(wy,i-1)
    for i,t,k in ((0,"Y",26),(1,"X",27),(2,"Y",28),(3,"X",29)):
        net.got(k,t,ns.at[nrows(wd,i)])
        project(wd,i)
    put(5,ns,normed_out); put(6,qs,qkv_out)
    for copy in outs: copy.wait()
    net.finish()

def first(block,long,skipw,qkvw,vecs):
    tokens,d=block.shape; S=jax.ShapeDtypeStruct; hd3=qkvw.shape[1]//4
    V=pltpu.VMEM
    return pl.pallas_call(first_kernel,
        out_shape=(S((tokens,d),F32),S((4*tokens,d),BF),S((4*tokens,hd3),BF),S((d,hd3),BF),S((2*d,d),BF),S((4,)+vecs.shape,F32)),
        in_specs=[VM]*5,out_specs=(ANY,)*6,
        scratch_shapes=[V((2*d,d),BF),V((4*tokens,d),BF),V((d,hd3),BF),V((4,d//4,hd3),BF),V((tokens,d),F32),V((4*tokens,hd3),BF),V((4,)+vecs.shape,F32),
            pltpu.SemaphoreType.DMA((33,)),pltpu.SemaphoreType.DMA((33,)),pltpu.SemaphoreType.DMA((8,))],
        compiler_params=pltpu.CompilerParams(vmem_limit_bytes=56*2**20,collective_id=0,has_side_effects=True),
        cost_estimate=pl.CostEstimate(flops=2*tokens*d*d*5,bytes_accessed=40*2**20,transcendentals=0))(
        block,long,skipw,qkvw,vecs)

def last_kernel(gq_ref,heads_ref,normed_ref,hidden_ref,gmid_ref,gain_ref,block_ref,long_ref,wskip_ref,
                gin_ref,gsk_ref,small_ref,gqkv_out,gskip_out,
                big,part,rx,ry,dx,dy,gw,gwr,gsr,send,recv,local):
    x,y,c,w,wx,wy,wd=place()
    tokens,d=block_ref.shape
    tc=tokens//4; kr=d//4; kh=kr//2; sr=d//2; sh=sr//2
    mul=pl.multiple_of
    net=Links(send,recv)
    load=pltpu.make_async_copy(normed_ref,big,local.at[0])
    load.start()
    net.meet("XYC")
    def tok(i): return pl.ds(i*tc,tc)
    def partial(b,i):
        return nt(gq_ref[pl.ds(mul(b*tokens+i*tc,16),tc),:],heads_ref[...])
    for i,t,dst,k in ((0,"X",dx,0),(2,"Y",dy,2),(1,"X",dx,1),(3,"Y",dy,3)):
        part[2,tok(i),:]=partial(wd,i).astype(BF)
        net.start(k,t,part.at[2,tok(i)],dst.at[tok(i%2)])
    for i,t,b,dst,k in ((0,"X",wx,rx,4),(2,"Y",wy,ry,10),(1,"X",wx,rx,5),(3,"Y",wy,ry,11)):
        s=0 if t=="X" else 1
        part[s,tok(i),:]=partial(b,i).astype(BF)
        net.start(k,t,part.at[s,tok(i)],dst.at[tok(i)])
    for i,t,b,dst,k,src,k2,t2 in ((2,"X",wx,rx,6,dy,2,"Y"),(0,"Y",wy,ry,8,dx,0,"X"),(3,"X",wx,rx,7,dy,3,"Y"),(1,"Y",wy,ry,9,dx,1,"X")):
        s=0 if t=="X" else 1
        mine=partial(b,i)
        net.got(k2,t2,src.at[tok(i%2)])
        part[s,tok(i),:]=(mine+src[tok(i%2),:].astype(F32)).astype(BF)
        net.start(k,t,part.at[s,tok(i)],dst.at[tok(i)])
    @pl.loop(0,4)
    def _(i):
        r=pl.ds(mul(i*tc,16),tc)
        gin_ref[r,:]=nt(gq_ref[pl.ds(mul(w*tokens+i*tc,16),tc),:],heads_ref[...])
    load.wait()
    cc=d//3
    for k in range(3):
        cr=pl.ds(k*cc,cc)
        gw[cr,:]=tn(big[:,cr],gq_ref[...]).astype(BF)
    def rows(b,core): return pl.ds(mul(b*kr+core*kh,16),kh)
    for b in range(4):
        net.start(12+b,"C",gw.at[rows(b,1-c)],gwr.at[pl.ds(b*kh,kh)])
    outs=[]
    for b in range(4):
        r=pl.ds(b*kh,kh)
        net.got(12+b,"C",gwr.at[r])
        gwr[r,:]=(gwr[r,:].astype(F32)+gw[rows(b,c),:].astype(F32)).astype(BF)
    copy=pltpu.make_async_copy(gwr,gqkv_out,local.at[1]); copy.start(); outs.append(copy)
    small_ref[...]=jnp.zeros_like(small_ref)
    gain=gain_ref[...]
    for i in (0,2,1,3):
        r=tok(i)
        net.got(4+i,"X",rx.at[r])
        net.got(8+i,"Y",ry.at[r])
        gf=gin_ref[r,:]+rx[r,:].astype(F32)+ry[r,:].astype(F32)
        h=hidden_ref[r,:]
        cen=h-jnp.mean(h,axis=1,keepdims=True)
        inv=lax.rsqrt(jnp.mean(cen*cen,axis=1,keepdims=True)+1e-5)
        xhat=cen*inv
        small_ref[0:1,:]+=jnp.sum(gf*xhat,axis=0,keepdims=True)
        small_ref[1:2,:]+=jnp.sum(gf,axis=0,keepdims=True)
        e=gf*gain
        back=e-jnp.mean(e,axis=1,keepdims=True)-xhat*jnp.mean(e*xhat,axis=1,keepdims=True)
        gh=(gmid_ref[r,:]+back*inv).astype(BF)
        big[pl.ds(2*d+i*tc,tc),:]=gh
        gin_ref[r,:]=nt(gh,wskip_ref[:d,:])
        gsk_ref[r,:]=nt(gh,wskip_ref[d:,:])
    for k in range(6):
        src=block_ref if k<3 else long_ref
        big[pl.ds(k*cc,cc),:]=tn(src[:,(k%3)*cc:(k%3+1)*cc],big[2*d:2*d+tokens,:]).astype(BF)
    def srows(b,core): return pl.ds(mul(b*sr+core*sh,16),sh)
    for b in range(4):
        net.start(16+b,"C",big.at[srows(b,1-c)],gsr.at[pl.ds(b*sh,sh)])
    for b in range(4):
        r=pl.ds(b*sh,sh)
        net.got(16+b,"C",gsr.at[r])
        gsr[r,:]=(gsr[r,:].astype(F32)+big[srows(b,c),:].astype(F32)).astype(BF)
    copy=pltpu.make_async_copy(gsr,gskip_out,local.at[2]); copy.start(); outs.append(copy)
    for copy in outs: copy.wait()
    net.finish()

def last(gq,heads,normed,hidden,gmid,gain,block,long,wskip):
    tokens,d=block.shape; S=jax.ShapeDtypeStruct; hd3=gq.shape[1]
    V=pltpu.VMEM
    return pl.pallas_call(last_kernel,
        out_shape=(S((tokens,d),F32),S((tokens,d),F32),S((8,d),F32),S((d//2,hd3),BF),S((d,d),BF)),
        in_specs=[VM,VM,ANY]+[VM]*6,out_specs=(VM,VM,VM,ANY,ANY),
        scratch_shapes=[V((4*tokens,d),BF),V((3,tokens,d),BF),V((tokens,d),BF),V((tokens,d),BF),V((tokens//2,d),BF),V((tokens//2,d),BF),
            V((d,hd3),BF),V((d//2,hd3),BF),V((d,d),BF),
            pltpu.SemaphoreType.DMA((20,)),pltpu.SemaphoreType.DMA((20,)),pltpu.SemaphoreType.DMA((3,))],
        compiler_params=pltpu.CompilerParams(vmem_limit_bytes=63*2**20,collective_id=1,has_side_effects=True),
        cost_estimate=pl.CostEstimate(flops=2*tokens*d*d*10,bytes_accessed=60*2**20,transcendentals=0))(
        gq,heads,normed,hidden,gmid,gain,block,long,wskip)

from jax.sharding import Mesh, PartitionSpec as P
WIDE=("y","x"); ROWS=("z","core")
SWAP=[(0,1),(1,0)]

def swap_cores(values):
    return lax.ppermute(values,"core",SWAP)

def pick(values, index, axis):
    return lax.dynamic_index_in_dim(values,index,axis,keepdims=False)

def place_halves(mine, other, core, axis):
    first=jnp.where(core==0,mine,other); second=jnp.where(core==0,other,mine)
    return jnp.stack([first,second],axis=axis)

def dot(a,b): return jnp.dot(a,b,preferred_element_type=F32)

def norm(values):
    cen=values-jnp.mean(values,axis=1,keepdims=True)
    inv=lax.rsqrt(jnp.mean(cen*cen,axis=1,keepdims=True)+1e-5)
    return cen*inv,inv

def on_device(nw, block_input, long_skip, segment_ids, item_lengths, skip_weight, first_gain, first_shift, qkv_weight,
              out_weight, second_gain, second_shift, up_weight, down_weight, output_grad):
    core=lax.axis_index("core")
    _,tokens,d=block_input.shape
    heads=qkv_weight.shape[1]//(3*HEAD*nw); hd=heads*HEAD
    ff=up_weight.shape[1]; fb=ff//(2*nw)
    gather=lambda v: lax.all_gather(v,WIDE,axis=0,tiled=True)
    near=nw==4
    vecs=jnp.stack([first_gain,first_shift,second_gain,second_shift]+[first_gain]*4).astype(F32)
    if near:
        hidden,normed_all,qkv,w_heads,w_skip,vecs=first(block_input[0],long_skip[0],skip_weight,qkv_weight,vecs)
        vec=vecs.transpose(1,0,2).reshape(8,d)
        gain1,shift1,gain2,shift2=[vec[i:i+1] for i in range(4)]
        qkv,up_weight,down_weight,out_weight=lax.optimization_barrier((qkv,up_weight,down_weight,out_weight))
    else:
        vec=gather(vecs.astype(BF).T).T.astype(F32)
        gain1,shift1,gain2,shift2=[vec[i:i+1] for i in range(4)]
        w_skip=gather(skip_weight)
        joined=jnp.concatenate([block_input[0],long_skip[0]],axis=1)
        w_heads=qkv_weight.reshape(d//nw,3,nw,hd).transpose(2,0,1,3)
        w_heads=lax.all_to_all(w_heads,WIDE,0,0).reshape(d,3*hd)
        hidden=dot(joined,w_skip)
        xhat1,inv1=norm(hidden)
        normed_all=gather((xhat1*gain1+shift1).astype(BF))
        qkv=dot(normed_all,w_heads).astype(BF)
    w_out=gather(out_weight)
    up_mine=gather(pick(up_weight.reshape(d//nw,nw,2,fb),core,2).reshape(d//nw,nw*fb))
    down_mine=gather(pick(down_weight.reshape(2,fb,d),core,0))
    att,lse=attend(item_lengths,qkv,heads)
    att,up_mine,down_mine=lax.optimization_barrier((att,up_mine,down_mine))
    up_other,down_other=swap_cores(up_mine),swap_cores(down_mine)
    att=lax.all_to_all(att.reshape(nw,tokens,hd),WIDE,0,0)
    lay,gmid,gatt,gow,small,gupo,guph,gdno,gdnh=mlp(hidden,att,w_out,gain2,shift2,output_grad[0],up_mine,up_other,down_mine,down_other)
    grad_heads=lax.all_to_all(gatt,WIDE,0,0).reshape(nw*tokens,hd)

    def scatter(mine,other):
        both=(mine.astype(F32)+swap_cores(other).astype(F32)).astype(BF)
        return lax.psum_scatter(both,WIDE,scatter_dimension=0,tiled=True)
    def both_cores(mine,axis):
        return place_halves(mine,swap_cores(mine),core,axis).astype(F32)
    def by_rows(grad):
        cut=grad.reshape(nw,2,-1,grad.shape[1])
        return scatter(pick(cut,core,1).reshape(-1,grad.shape[1]),pick(cut,1-core,1).reshape(-1,grad.shape[1]))
    early=scatter(gupo,guph),scatter(gdno,gdnh),by_rows(gow)
    grad_qkv=attend_back(item_lengths,qkv,grad_heads,lse,heads)
    grad_qkv,early=lax.optimization_barrier((grad_qkv,early))
    early=lax.psum(early,"z")
    if near:
        gin,gsk,small1,gqkv,gskip=last(grad_qkv,w_heads,normed_all,hidden,gmid,gain1,block_input[0],long_skip[0],w_skip)
        gqkv=gqkv.reshape(nw,-1,3*hd)
        gskip=lax.psum_scatter(gskip,WIDE,scatter_dimension=0,tiled=True)
    else:
        part_first=nt(grad_qkv,w_heads).astype(BF)
        grad_first=lax.psum_scatter(part_first,WIDE,scatter_dimension=0,tiled=True).astype(F32)
        gqkv=tn(normed_all,grad_qkv).astype(BF).reshape(nw,2,d//nw//2,3*hd)
        gqkv=(pick(gqkv,core,1).astype(F32)+swap_cores(pick(gqkv,1-core,1)).astype(F32)).astype(BF)
        e1=grad_first*gain1
        across=inv1*(e1-jnp.mean(e1,axis=1,keepdims=True)-xhat1*jnp.mean(e1*xhat1,axis=1,keepdims=True))
        grad_hidden=(gmid+across).astype(BF)
        gskip=by_rows(tn(joined,grad_hidden).astype(BF))
        grad_joined=nt(grad_hidden,w_skip)
        gin,gsk=grad_joined[:,:d],grad_joined[:,d:]
        small1=jnp.stack([jnp.sum(grad_first*xhat1,axis=0),jnp.sum(grad_first,axis=0)])
    gqkv,gskip,early=lax.optimization_barrier((gqkv,gskip,early))
    gqkv,gskip=lax.psum((gqkv,gskip),"z")
    up_share=both_cores(early[0].reshape(d//nw,nw,fb),2).reshape(d//nw,ff)
    down_share=both_cores(early[1],0).reshape(ff//nw,d)
    out_share=both_cores(early[2],0).reshape(d//nw,d)
    skip_share=both_cores(gskip,0).reshape(2*d//nw,d)
    gqkv=lax.all_to_all(gqkv,WIDE,0,0).reshape(nw,-1,3,hd).transpose(1,2,0,3)
    qkv_share=both_cores(gqkv,0).reshape(d//nw,-1)
    smalls=jnp.stack([small1[0],small1[1],small[0],small[1]],axis=1)
    smalls=lax.psum(lax.psum_scatter(smalls.astype(BF),WIDE,scatter_dimension=0,tiled=True),ROWS).astype(F32)
    return (lay[None],gin[None],gsk[None],skip_share,smalls[:,0],smalls[:,1],qkv_share,out_share,
            smalls[:,2],smalls[:,3],up_share,down_share)

def solution(mesh):
    rows,wide=mesh.devices.shape
    side=2 if wide==4 else int(wide**0.5)
    grid=Mesh(mesh.devices.reshape(rows//2,2,wide//side,side),("z","core","y","x"))
    tok=P(ROWS,WIDE,None); row=P(ROWS,None); mat=P(WIDE,None); vec=P(WIDE)
    return jax.shard_map(functools.partial(on_device,wide),mesh=grid,
        in_specs=(tok,tok,row,row,mat,vec,vec,mat,mat,vec,vec,mat,mat,tok),
        out_specs=(tok,tok,tok,mat,vec,vec,mat,mat,vec,vec,mat,mat),check_vma=False)
```

```python
import functools
import jax, jax.numpy as jnp
from jax import lax
from jax.experimental import pallas as pl
from jax.experimental.pallas import tpu as pltpu
HEAD=72; SHORT=258; LONG=1026; NITEM=12
LOG2E=1.4426950408889634
SCALE=HEAD**-0.5
QT=384

def kwin(n): return (n + 29 + 31)//32*32
def qwin(n): return (n + 15 + QT-1)//QT*QT

def nt(a,b): return lax.dot_general(a,b,(((1,),(1,)),((),())),preferred_element_type=jnp.float32)
def nn(a,b): return lax.dot_general(a,b,(((1,),(0,)),((),())),preferred_element_type=jnp.float32)
def tn(a,b): return lax.dot_general(a,b,(((0,),(0,)),((),())),preferred_element_type=jnp.float32)

def windows(start, size, row_len):
    k0 = pl.multiple_of(jnp.minimum(start//16*16, row_len-kwin(size)),16)
    q0 = pl.multiple_of(jnp.minimum(start//16*16, row_len-qwin(size)),16)
    return k0,q0

def split_heads(src_ref, dst_ref, count, chunk=416):
    rows=src_ref.shape[0]
    @pl.loop(0, rows//chunk)
    def _(i):
        r=pl.ds(pl.multiple_of(i*chunk,16),chunk)
        block=src_ref[r,:]
        for j in range(count):
            dst_ref[j,r,:]=block[:,j*HEAD:(j+1)*HEAD]

def join_heads(src_ref, dst_ref, count, chunk=416):
    rows=dst_ref.shape[0]
    @pl.loop(0, rows//chunk)
    def _(i):
        r=pl.ds(pl.multiple_of(i*chunk,16),chunk)
        dst_ref[r,:]=jnp.concatenate([src_ref[j,r,:] for j in range(count)],axis=1)

def zero(ref, chunk=416):
    rows=ref.shape[1]
    @pl.loop(0, rows//chunk)
    def _(i):
        r=pl.ds(pl.multiple_of(i*chunk,16),chunk)
        for j in range(ref.shape[0]):
            ref[j,r,:]=jnp.zeros((chunk,ref.shape[2]),ref.dtype)

def for_items(len_ref, one):
    def step(i, start):
        size=len_ref[0,i]
        @pl.when(size==LONG)
        def _(): one(i,start,LONG)
        @pl.when(size==SHORT)
        def _(): one(i,start,SHORT)
        return start+size
    lax.fori_loop(0,len_ref.shape[1],step,jnp.int32(0))

def mask_edges(values, start, k0, size, fill):
    n=values.shape[0]; body=size//32*32
    off=start-k0
    top=lax.broadcasted_iota(jnp.int32,(32,values.shape[1]),0)
    low=jnp.where(top>=off,values[:32],fill)
    high=jnp.where(top+body<off+size,values[body:],fill)
    return jnp.concatenate([low,values[32:body],high],axis=0)

def attend_kernel(heads, len_ref, qkv_ref, out_ref, lse_ref, split_ref, acc_ref):
    row_len=qkv_ref.shape[0]
    split_heads(qkv_ref, split_ref, 3*heads)
    zero(acc_ref)
    lse_ref[...]=jnp.zeros_like(lse_ref)
    def one(item,start,size):
        k0,q0=windows(start,size,row_len)
        kr=pl.ds(k0,kwin(size))
        @pl.loop(0,qwin(size)//QT)
        def _(t):
            qr=pl.ds(pl.multiple_of(q0+t*QT,16),QT)
            col=q0+t*QT+lax.broadcasted_iota(jnp.int32,(1,QT),1)
            live=(col>=start)&(col<start+size)
            for h in range(heads):
                s=nt(split_ref[heads+h,kr,:],split_ref[h,qr,:])
                s=mask_edges(s,start,k0,size,-1e30)
                m=jnp.max(s,axis=0,keepdims=True)
                p=jnp.exp2((s-m)*(SCALE*LOG2E))
                l=jnp.sum(p,axis=0,keepdims=True)
                o=tn(split_ref[2*heads+h,kr,:],p.astype(jnp.bfloat16))
                o=jnp.where(live,o/l,0.0)
                acc_ref[h,qr,:]+=o.T.astype(jnp.bfloat16)
                lse_ref[item,pl.ds(t*heads+h,1),:]=m*(SCALE*LOG2E)+jnp.log2(l)
    for_items(len_ref,one)
    join_heads(acc_ref,out_ref,heads)

def attend_back_kernel(heads, len_ref, qkv_ref, grad_ref, lse_ref, out_ref, split_ref, gsplit_ref, acc_ref, dk_ref, dv_ref):
    row_len=qkv_ref.shape[0]
    split_heads(qkv_ref, split_ref, 3*heads)
    split_heads(grad_ref, gsplit_ref, heads)
    zero(acc_ref)
    def one(item,start,size):
        k0,q0=windows(start,size,row_len)
        kw=kwin(size)
        kr=pl.ds(k0,kw)
        for h in range(heads):
            dk_ref[h,:kw,:]=jnp.zeros((kw,HEAD),jnp.float32)
            dv_ref[h,:kw,:]=jnp.zeros((kw,HEAD),jnp.float32)
        @pl.loop(0,qwin(size)//QT)
        def _(t):
            qr=pl.ds(pl.multiple_of(q0+t*QT,16),QT)
            col=q0+t*QT+lax.broadcasted_iota(jnp.int32,(1,QT),1)
            live=(col>=start)&(col<start+size)
            for h in range(heads):
                k=split_ref[heads+h,kr,:]; q=split_ref[h,qr,:]; g=gsplit_ref[h,qr,:]
                lse=jnp.where(live,lse_ref[item,pl.ds(t*heads+h,1),:],1e30)
                s=nt(k,q)
                p=jnp.exp2(s*(SCALE*LOG2E)-lse)
                p=mask_edges(p,start,k0,size,0.0)
                dv_ref[h,:kw,:]+=nn(p.astype(jnp.bfloat16),g)
                dp=nt(split_ref[2*heads+h,kr,:],g)
                delta=jnp.sum(p*dp,axis=0,keepdims=True)
                ds=(p*(dp-delta)).astype(jnp.bfloat16)
                dk_ref[h,:kw,:]+=nn(ds,q)
                dq=tn(k,ds)*SCALE
                acc_ref[h,qr,:]+=dq.T.astype(jnp.bfloat16)
        for h in range(heads):
            acc_ref[heads+h,kr,:]+=(dk_ref[h,:kw,:]*SCALE).astype(jnp.bfloat16)
            acc_ref[2*heads+h,kr,:]+=dv_ref[h,:kw,:].astype(jnp.bfloat16)
    for_items(len_ref,one)
    join_heads(acc_ref,out_ref,3*heads)

VM=pl.BlockSpec(memory_space=pltpu.VMEM); SM=pl.BlockSpec(memory_space=pltpu.SMEM)
def attend(lens,qkv,heads):
    n=qkv.shape[0]
    nt_=heads*(qwin(LONG)//QT)
    return pl.pallas_call(functools.partial(attend_kernel,heads),
      out_shape=(jax.ShapeDtypeStruct((n,heads*HEAD),jnp.bfloat16),jax.ShapeDtypeStruct((NITEM,nt_,QT),jnp.float32)),
      in_specs=[SM,VM],out_specs=(VM,VM),
      scratch_shapes=[pltpu.VMEM((3*heads,n,HEAD),jnp.bfloat16),pltpu.VMEM((heads,n,HEAD),jnp.bfloat16)],
      compiler_params=pltpu.CompilerParams(vmem_limit_bytes=56*2**20),
      cost_estimate=pl.CostEstimate(flops=heads*n*n*HEAD*4,bytes_accessed=12*2**20,transcendentals=heads*n*n//3))(lens,qkv)
def attend_back(lens,qkv,grad,lse,heads):
    n=qkv.shape[0]
    return pl.pallas_call(functools.partial(attend_back_kernel,heads),
      out_shape=jax.ShapeDtypeStruct((n,3*heads*HEAD),jnp.bfloat16),
      in_specs=[SM,VM,VM,VM],out_specs=VM,
      scratch_shapes=[pltpu.VMEM((3*heads,n,HEAD),jnp.bfloat16),pltpu.VMEM((heads,n,HEAD),jnp.bfloat16),pltpu.VMEM((3*heads,n,HEAD),jnp.bfloat16),
        pltpu.VMEM((heads,kwin(LONG),HEAD),jnp.float32),pltpu.VMEM((heads,kwin(LONG),HEAD),jnp.float32)],
      compiler_params=pltpu.CompilerParams(vmem_limit_bytes=60*2**20),
      cost_estimate=pl.CostEstimate(flops=heads*n*n*HEAD*10,bytes_accessed=20*2**20,transcendentals=heads*n*n//3))(lens,qkv,grad,lse)


F32=jnp.float32; BF=jnp.bfloat16
ANY=pl.BlockSpec(memory_space=pl.ANY)

def gelu_parts(u):
    z=jnp.exp2(u*u*(-0.5*1.4426950408889634))
    t=1.0/(1.0+(0.3275911*0.7071067811865476)*jnp.abs(u))
    poly=((((1.061405429*t-1.453152027)*t+1.421413741)*t-0.284496736)*t+0.254829592)*t
    tail=0.5*poly*z
    cdf=jnp.where(u>=0,1.0-tail,tail)
    return u*cdf, cdf+u*(z*0.3989422804014327)

def mlp_kernel(tile, hidden_ref, att_ref, outw_ref, gain_ref, shift_ref, g_ref, upo_ref, uph_ref, dno_ref, dnh_ref,
               lay_ref, gmid_ref, gatt_ref, gow_ref, small_ref, gupo_ref, guph_ref, gdno_ref, gdnh_ref,
               att_s, n2_s, xhat_s, rstd_s, act_s, gu_s, upb, dnb, gub, gdb, in_sem, out_sem):
    parts,tokens,cols=att_ref.shape
    d=hidden_ref.shape[1]
    tc=tokens//2 if tokens>416 else tokens
    nch=tokens//tc
    half=upo_ref.shape[1]; steps=half//tile
    cc=d//3; fc=256

    def fetch(j,act):
        slot=lax.rem(j,2)
        for first,(us,ds) in ((True,(uph_ref,dnh_ref)),(False,(upo_ref,dno_ref))):
            cond=(j<steps) if first else (j>=steps)
            @pl.when(cond)
            def _():
                k=j if first else j-steps
                off=pl.multiple_of(k*tile,tile)
                act(pltpu.make_async_copy(us.at[:,pl.ds(off,tile)],upb.at[slot],in_sem.at[slot,0]))
                act(pltpu.make_async_copy(ds.at[pl.ds(off,tile),:],dnb.at[slot],in_sem.at[slot,1]))
    def flush(j,act):
        slot=lax.rem(j,2)
        for first,(us,ds) in ((True,(guph_ref,gdnh_ref)),(False,(gupo_ref,gdno_ref))):
            cond=(j<steps) if first else (j>=steps)
            @pl.when(cond)
            def _():
                k=j if first else j-steps
                off=pl.multiple_of(k*tile,tile)
                act(pltpu.make_async_copy(gub.at[slot],us.at[:,pl.ds(off,tile)],out_sem.at[slot,0]))
                act(pltpu.make_async_copy(gdb.at[slot],ds.at[pl.ds(off,tile),:],out_sem.at[slot,1]))
    start=lambda c: c.start()
    wait=lambda c: c.wait()
    fetch(jnp.int32(0),start)
    gain=gain_ref[...]; shift=shift_ref[...]
    sub=tc//2
    @pl.loop(0,2*nch)
    def _(i):
        r=pl.ds(pl.multiple_of(i*sub,16),sub)
        joined=jnp.concatenate([att_ref[p,r,:] for p in range(parts)],axis=1)
        att_s[r,:]=joined
        mid=hidden_ref[r,:]+nn(joined,outw_ref[...])
        lay_ref[r,:]=mid
        cen=mid-jnp.mean(mid,axis=1,keepdims=True)
        inv=lax.rsqrt(jnp.mean(cen*cen,axis=1,keepdims=True)+1e-5)
        xhat=cen*inv
        xhat_s[r,:]=xhat
        rstd_s[r,:]=jnp.broadcast_to(inv,(sub,128))
        n2_s[r,:]=(xhat*gain+shift).astype(BF)
        gmid_ref[r,:]=jnp.zeros((sub,d),F32)
    @pl.loop(0,2*steps)
    def _(j):
        slot=lax.rem(j,2)
        @pl.when(j+1<2*steps)
        def _(): fetch(j+1,start)
        fetch(j,wait)
        @pl.when(j>=2)
        def _(): flush(j-2,wait)
        @pl.loop(0,nch)
        def _(i):
            r=pl.ds(pl.multiple_of(i*tc,16),tc)
            for k in range(tile//fc):
                f=pl.ds(k*fc,fc)
                u=nn(n2_s[r,:],upb[slot,:,f])
                a,dg=gelu_parts(u)
                act_s[r,f]=a.astype(BF)
                ga=nt(g_ref[r,:],dnb[slot,f,:])
                gu_s[r,f]=(ga*dg).astype(BF)
        @pl.loop(0,nch)
        def _(i):
            r=pl.ds(pl.multiple_of(i*tc,16),tc)
            for k in range(3):
                cr=pl.ds(k*cc,cc)
                lay_ref[r,cr]+=nn(act_s[r,:],dnb[slot,:,cr])
                gmid_ref[r,cr]+=nt(gu_s[r,:],upb[slot,cr,:])
        for k in range(tile//fc):
            f=pl.ds(k*fc,fc)
            gdb[slot,f,:]=tn(act_s[:,f],g_ref[...]).astype(BF)
        for k in range(3):
            cr=pl.ds(k*cc,cc)
            gub[slot,cr,:]=tn(n2_s[:,cr],gu_s[...]).astype(BF)
        flush(j,start)
    small_ref[...]=jnp.zeros_like(small_ref)
    @pl.loop(0,2*nch)
    def _(i):
        r=pl.ds(pl.multiple_of(i*sub,16),sub)
        gs=gmid_ref[r,:]; xhat=xhat_s[r,:]
        small_ref[0:1,:]+=jnp.sum(gs*xhat,axis=0,keepdims=True)
        small_ref[1:2,:]+=jnp.sum(gs,axis=0,keepdims=True)
        e=gs*gain
        back=e-jnp.mean(e,axis=1,keepdims=True)-xhat*jnp.mean(e*xhat,axis=1,keepdims=True)
        gm=g_ref[r,:].astype(F32)+back*rstd_s[r,0:1]
        gmid_ref[r,:]=gm
        low=gm.astype(BF)
        n2_s[r,:]=low
        ga=nt(low,outw_ref[...]).astype(BF)
        for p in range(parts):
            gatt_ref[p,r,:]=ga[:,p*cols:(p+1)*cols]
    for k in range(3):
        cr=pl.ds(k*cc,cc)
        gow_ref[cr,:]=tn(att_s[:,cr],n2_s[...]).astype(BF)
    flush(jnp.int32(2*steps-2),wait)
    flush(jnp.int32(2*steps-1),wait)

def mlp(hidden,att,outw,gain,shift,g,upo,uph,dno,dnh):
    tokens,d=hidden.shape; half=upo.shape[1]; tile=half//3
    S=jax.ShapeDtypeStruct
    flops=2*tokens*d*(half*2*6+d*3)
    return pl.pallas_call(functools.partial(mlp_kernel,tile),
        out_shape=(S((tokens,d),F32),S((tokens,d),F32),S(att.shape,BF),S((d,d),BF),S((8,d),F32),
                   S(upo.shape,BF),S(upo.shape,BF),S(dno.shape,BF),S(dno.shape,BF)),
        in_specs=[VM]*6+[ANY]*4,
        out_specs=(VM,)*5+(ANY,)*4,
        scratch_shapes=[pltpu.VMEM((tokens,d),BF),pltpu.VMEM((tokens,d),BF),pltpu.VMEM((tokens,d),F32),pltpu.VMEM((tokens,128),F32),
            pltpu.VMEM((tokens,tile),BF),pltpu.VMEM((tokens,tile),BF),
            pltpu.VMEM((2,d,tile),BF),pltpu.VMEM((2,tile,d),BF),pltpu.VMEM((2,d,tile),BF),pltpu.VMEM((2,tile,d),BF),
            pltpu.SemaphoreType.DMA((2,2)),pltpu.SemaphoreType.DMA((2,2))],
        compiler_params=pltpu.CompilerParams(vmem_limit_bytes=62*2**20),
        cost_estimate=pl.CostEstimate(flops=flops,bytes_accessed=60*2**20,transcendentals=tokens*half*2))(
        hidden,att,outw,gain,shift,g,upo,uph,dno,dnh)


MESH=pl.DeviceIdType.MESH

def place():
    x,y,c=lax.axis_index("x"),lax.axis_index("y"),lax.axis_index("core")
    return x,y,c,2*y+x,2*y+1-x,2-2*y+x,3-2*y-x

class Links:
    def __init__(self,send,recv):
        self.send,self.recv,self.sent=send,recv,[]
        x,y,c=lax.axis_index("x"),lax.axis_index("y"),lax.axis_index("core")
        self.to={"X":{"x":1-x},"Y":{"y":1-y},"D":{"x":1-x,"y":1-y},"C":{"core":1-c}}
    def meet(self,who):
        barrier=pltpu.get_barrier_semaphore()
        for t in who:
            pl.semaphore_signal(barrier,inc=1,device_id=self.to[t],device_id_type=MESH)
        pl.semaphore_wait(barrier,len(who))
    def start(self,k,t,src,dst):
        copy=pltpu.make_async_remote_copy(src_ref=src,dst_ref=dst,send_sem=self.send.at[k],recv_sem=self.recv.at[k],
                                          device_id=self.to[t],device_id_type=MESH)
        copy.start()
        self.sent.append(copy)
    def got(self,k,t,dst):
        pltpu.make_async_remote_copy(src_ref=dst,dst_ref=dst,send_sem=self.send.at[k],recv_sem=self.recv.at[k],
                                     device_id=self.to[t],device_id_type=MESH).wait_recv()
    def finish(self):
        for copy in self.sent: copy.wait_send()

def first_kernel(block_ref,long_ref,skip_ref,qkvw_ref,vec_ref,
                 hidden_out,normed_out,qkv_out,heads_out,wskip_out,vec_out,
                 ws,ns,hs,piece,hid,qs,vs,send,recv,local):
    x,y,c,w,wx,wy,wd=place()
    tokens,d=block_ref.shape
    sr=skip_ref.shape[0]; half=sr//2; part=half//2
    kr=qkvw_ref.shape[0]; kh=kr//2; hd=qkvw_ref.shape[1]//12
    tc=tokens//4
    mul=pl.multiple_of
    net=Links(send,recv)
    net.meet("XYDC")
    def srows(b,core,p): return pl.ds(mul(b*sr+core*half+p*part,16),part)
    def mine(p): return pl.ds(mul(c*half+p*part,16),part)
    net.start(0,"X",skip_ref.at[mine(0)],ws.at[srows(w,c,0)])
    net.start(2,"Y",skip_ref.at[mine(1)],ws.at[srows(w,c,1)])
    net.start(1,"X",skip_ref.at[mine(1)],ws.at[srows(w,c,1)])
    net.start(3,"Y",skip_ref.at[mine(0)],ws.at[srows(w,c,0)])
    own=pltpu.make_async_copy(skip_ref,ws.at[pl.ds(mul(w*sr,16),sr)],local.at[0])
    own.start()
    for k,t in ((30,"X"),(31,"Y"),(32,"D")): net.start(k,t,vec_ref,vs.at[w])
    vs[w]=vec_ref[...]
    for p in range(4):
        piece[p]=jnp.concatenate([qkvw_ref[:,(s*4+p)*hd:(s*4+p+1)*hd] for s in range(3)],axis=1)
    own_heads=pltpu.make_async_copy(piece.at[w],hs.at[pl.ds(mul(w*kr,16),kr)],local.at[1])
    own_heads.start()
    def pass_on(k,t,b,p,onward):
        r=srows(b,c,p)
        net.got(k,t,ws.at[r])
        for k2,t2 in onward: net.start(k2,t2,ws.at[r],ws.at[r])
    pass_on(0,"X",wx,0,((4,"Y"),(6,"C")))
    pass_on(2,"Y",wy,1,((5,"X"),(7,"C")))
    pass_on(1,"X",wx,1,((8,"C"),))
    pass_on(3,"Y",wy,0,((9,"C"),))
    def hrows(b,core): return pl.ds(mul(b*kr+core*kh,16),kh)
    cut=pl.ds(mul(c*kh,16),kh)
    net.start(12,"X",piece.at[wx,cut],hs.at[hrows(w,c)])
    net.start(13,"Y",piece.at[wy,cut],hs.at[hrows(w,c)])
    net.start(14,"D",piece.at[wd,cut],hs.at[hrows(w,c)])
    own.wait()
    net.got(6,"C",ws.at[srows(wx,1-c,0)])
    net.got(8,"C",ws.at[srows(wx,1-c,1)])
    near=pl.ds(mul(y*d,16),d); far=pl.ds(mul((1-y)*d,16),d)
    def tok(i): return pl.ds(mul(i*tc,16),tc)
    @pl.loop(0,4)
    def _(i):
        lhs=jnp.where(y==0,block_ref[tok(i),:],long_ref[tok(i),:])
        hid[tok(i),:]=nn(lhs,ws[near,:])
    pass_on(4,"Y",wd,0,((10,"C"),))
    pass_on(5,"X",wd,1,((11,"C"),))
    net.got(7,"C",ws.at[srows(wy,1-c,1)])
    net.got(9,"C",ws.at[srows(wy,1-c,0)])
    net.got(10,"C",ws.at[srows(wd,1-c,0)])
    net.got(11,"C",ws.at[srows(wd,1-c,1)])
    for k,t,b in ((30,"X",wx),(31,"Y",wy),(32,"D",wd)): net.got(k,t,vs.at[b])
    gain=jnp.concatenate([vs[p,0:1,:] for p in range(4)],axis=1)
    shift=jnp.concatenate([vs[p,1:2,:] for p in range(4)],axis=1)
    def nrows(b,i): return pl.ds(mul(b*tokens+i*tc,16),tc)
    def spread(i,t):
        net.start((18 if t=="X" else 22)+i,t,ns.at[nrows(w,i)],ns.at[nrows(w,i)])
    for i in range(4):
        r=tok(i)
        lhs=jnp.where(y==0,long_ref[r,:],block_ref[r,:])
        h=hid[r,:]+nn(lhs,ws[far,:])
        hid[r,:]=h
        cen=h-jnp.mean(h,axis=1,keepdims=True)
        inv=lax.rsqrt(jnp.mean(cen*cen,axis=1,keepdims=True)+1e-5)
        ns[nrows(w,i),:]=(cen*inv*gain+shift).astype(BF)
        spread(i,"XYXY"[i])
    for i,t in ((1,"X"),(0,"Y"),(3,"X"),(2,"Y")): spread(i,t)
    outs=[]
    def put(k,src,dst):
        copy=pltpu.make_async_copy(src,dst,local.at[k]); copy.start(); outs.append(copy)
    put(2,ws,wskip_out); put(3,hid,hidden_out); put(7,vs,vec_out)
    for j,(t,b) in enumerate((("X",wx),("Y",wy),("D",wd))):
        net.got(12+j,t,hs.at[hrows(b,c)])
        net.start(15+j,"C",hs.at[hrows(b,c)],hs.at[hrows(b,c)])
    for j,b in enumerate((wx,wy,wd)):
        net.got(15+j,"C",hs.at[hrows(b,1-c)])
    own_heads.wait()
    put(4,hs,heads_out)
    def project(b,i): qs[nrows(b,i),:]=nn(ns[nrows(b,i),:],hs[...]).astype(BF)
    @pl.loop(0,4)
    def _(i): project(w,i)
    for i,t,b,k,k2,t2 in ((0,"X",wx,18,26,"Y"),(1,"Y",wy,22,27,"X"),(2,"X",wx,18,28,"Y"),(3,"Y",wy,22,29,"X")):
        net.got(k+i,t,ns.at[nrows(b,i)])
        net.start(k2,t2,ns.at[nrows(b,i)],ns.at[nrows(b,i)])
    @pl.loop(0,2)
    def _(i): project(wx,2*i)
    @pl.loop(0,2)
    def _(i): project(wy,2*i+1)
    for i in (1,3):
        net.got(18+i,"X",ns.at[nrows(wx,i)])
        project(wx,i)
        net.got(22+i-1,"Y",ns.at[nrows(wy,i-1)])
        project(wy,i-1)
    for i,t,k in ((0,"Y",26),(1,"X",27),(2,"Y",28),(3,"X",29)):
        net.got(k,t,ns.at[nrows(wd,i)])
        project(wd,i)
    put(5,ns,normed_out); put(6,qs,qkv_out)
    for copy in outs: copy.wait()
    net.finish()

def first(block,long,skipw,qkvw,vecs):
    tokens,d=block.shape; S=jax.ShapeDtypeStruct; hd3=qkvw.shape[1]//4
    V=pltpu.VMEM
    return pl.pallas_call(first_kernel,
        out_shape=(S((tokens,d),F32),S((4*tokens,d),BF),S((4*tokens,hd3),BF),S((d,hd3),BF),S((2*d,d),BF),S((4,)+vecs.shape,F32)),
        in_specs=[VM]*5,out_specs=(ANY,)*6,
        scratch_shapes=[V((2*d,d),BF),V((4*tokens,d),BF),V((d,hd3),BF),V((4,d//4,hd3),BF),V((tokens,d),F32),V((4*tokens,hd3),BF),V((4,)+vecs.shape,F32),
            pltpu.SemaphoreType.DMA((33,)),pltpu.SemaphoreType.DMA((33,)),pltpu.SemaphoreType.DMA((8,))],
        compiler_params=pltpu.CompilerParams(vmem_limit_bytes=56*2**20,collective_id=0,has_side_effects=True),
        cost_estimate=pl.CostEstimate(flops=2*tokens*d*d*5,bytes_accessed=40*2**20,transcendentals=0))(
        block,long,skipw,qkvw,vecs)

class Chain:
    def __init__(self,net,k,own,up_in,down_in,up_out,down_out):
        self.net,self.k,self.own=net,k,own
        self.up_in,self.down_in,self.up_out,self.down_out=up_in,down_in,up_out,down_out
        self.z,self.n=lax.axis_index("z"),lax.axis_size("z")
    def copy(self,up,src):
        k=self.k+(0 if up else 1)
        return pltpu.make_async_remote_copy(src_ref=src,dst_ref=self.up_in if up else self.down_in,
            send_sem=self.net.send.at[k],recv_sem=self.net.recv.at[k],
            device_id={"z":self.z+1 if up else self.z-1},device_id_type=MESH)
    def hop(self,h):
        for up in (True,False):
            here=self.z==(h if up else self.n-1-h)
            inn,out=(self.up_in,self.up_out) if up else (self.down_in,self.down_out)
            @pl.when(here)
            def _():
                if h==0:
                    self.copy(up,self.own).start()
                else:
                    self.copy(up,inn).wait_recv()
                    out[...]=(self.own[...].astype(F32)+inn[...].astype(F32)).astype(out.dtype)
                    self.copy(up,out).start()
    def total(self):
        first,final=self.z==0,self.z==self.n-1
        @pl.when(first)
        def _():
            self.copy(False,self.down_in).wait_recv()
            self.copy(True,self.own).wait_send()
            self.own[...]=(self.own[...].astype(F32)+self.down_in[...].astype(F32)).astype(self.own.dtype)
        @pl.when(final)
        def _():
            self.copy(True,self.up_in).wait_recv()
            self.copy(False,self.own).wait_send()
            self.own[...]=(self.own[...].astype(F32)+self.up_in[...].astype(F32)).astype(self.own.dtype)
        @pl.when(jnp.logical_not(first|final))
        def _():
            self.copy(True,self.up_out).wait_send()
            self.copy(False,self.down_out).wait_send()
            self.own[...]=(self.own[...].astype(F32)+self.up_in[...].astype(F32)+self.down_in[...].astype(F32)).astype(self.own.dtype)

def meet_all(net,who):
    z,n=lax.axis_index("z"),lax.axis_size("z")
    barrier=pltpu.get_barrier_semaphore()
    for t in who:
        pl.semaphore_signal(barrier,inc=1,device_id=net.to[t],device_id_type=MESH)
    @pl.when(z>0)
    def _(): pl.semaphore_signal(barrier,inc=1,device_id={"z":z-1},device_id_type=MESH)
    @pl.when(z<n-1)
    def _(): pl.semaphore_signal(barrier,inc=1,device_id={"z":z+1},device_id_type=MESH)
    ends=(z==0)|(z==n-1)
    @pl.when(ends)
    def _(): pl.semaphore_wait(barrier,len(who)+1)
    @pl.when(jnp.logical_not(ends))
    def _(): pl.semaphore_wait(barrier,len(who)+2)

SEG=3
def last_kernel(gq_ref,heads_ref,normed_ref,hidden_ref,gmid_ref,gain_ref,block_ref,long_ref,wskip_ref,small_ref,
                gin_out,gsk_out,small_out,gqkv_out,gskip_out,
                big,part,rx,ry,dx,dy,gw,gwr,gsr,qz,fq,sdx,sdy,srx,sry,own,sz,fs,sm,sin,smz,send,recv,local):
    x,y,c,w,wx,wy,wd=place()
    tokens,d=block_ref.shape
    tc=tokens//4; kr=d//4; kh=kr//2; sr=d//2; sh=sr//2; sq=sh//2
    mul=pl.multiple_of
    net=Links(send,recv)
    load=pltpu.make_async_copy(normed_ref,big,local.at[0])
    load.start()
    meet_all(net,"XYDC")
    def tok(i): return pl.ds(i*tc,tc)
    def pr(s,i): return pl.ds(s*tokens+i*tc,tc)
    def partial(b,i):
        return nt(gq_ref[pl.ds(mul(b*tokens+i*tc,16),tc),:],heads_ref[...])
    for i,t,dst,k in ((0,"X",dx,0),(2,"Y",dy,2),(1,"X",dx,1),(3,"Y",dy,3)):
        part[pr(2,i),:]=partial(wd,i).astype(BF)
        net.start(k,t,part.at[pr(2,i)],dst.at[tok(i%2)])
    for i,t,b,dst,k in ((0,"X",wx,rx,4),(2,"Y",wy,ry,10),(1,"X",wx,rx,5),(3,"Y",wy,ry,11)):
        s=0 if t=="X" else 1
        part[pr(s,i),:]=partial(b,i).astype(BF)
        net.start(k,t,part.at[pr(s,i)],dst.at[tok(i)])
    @pl.loop(0,4)
    def _(i):
        r=pl.ds(mul(i*tc,16),tc)
        part[pl.ds(mul(3*tokens+i*tc,16),tc),:]=nt(gq_ref[pl.ds(mul(w*tokens+i*tc,16),tc),:],heads_ref[...]).astype(BF)
    load.wait()
    cc=d//3
    def weight_grad(k):
        cr=pl.ds(k*cc,cc)
        gw[cr,:]=tn(big[:,cr],gq_ref[...]).astype(BF)
    def relay(i,t,b,dst,k,src,k2,t2):
        s=0 if t=="X" else 1
        mine=partial(b,i)
        net.got(k2,t2,src.at[tok(i%2)])
        part[pr(s,i),:]=(mine+src[tok(i%2),:].astype(F32)).astype(BF)
        net.start(k,t,part.at[pr(s,i)],dst.at[tok(i)])
    weight_grad(0)
    relay(2,"X",wx,rx,6,dy,2,"Y")
    relay(0,"Y",wy,ry,8,dx,0,"X")
    weight_grad(1)
    weight_grad(2)
    def rows(b,core): return pl.ds(mul(b*kr+core*kh,16),kh)
    for b in range(4):
        net.start(12+b,"C",gw.at[rows(b,1-c)],gwr.at[pl.ds(b*kh,kh)])
    relay(3,"X",wx,rx,7,dy,3,"Y")
    relay(1,"Y",wy,ry,9,dx,1,"X")
    for b in range(4):
        r=pl.ds(b*kh,kh)
        net.got(12+b,"C",gwr.at[r])
        gwr[r,:]=(gwr[r,:].astype(F32)+gw[rows(b,c),:].astype(F32)).astype(BF)
    halves=[pl.ds(i*2*kh,2*kh) for i in range(2)]
    chains=[Chain(net,40+2*i,gwr.at[r],*[qz.at[j,r] for j in range(4)]) for i,r in enumerate(halves)]
    for chain in chains: chain.hop(0)
    gain=gain_ref[...]
    sm[...]=jnp.zeros_like(sm)
    for h in range(1,lax.axis_size("z")-2):
        for chain in chains: chain.hop(h)
    for i in (0,2,1,3):
        r=tok(i)
        net.got(4+i,"X",rx.at[r])
        net.got(8+i,"Y",ry.at[r])
        gf=part[pr(3,i),:].astype(F32)+rx[r,:].astype(F32)+ry[r,:].astype(F32)
        h=hidden_ref[r,:]
        cen=h-jnp.mean(h,axis=1,keepdims=True)
        inv=lax.rsqrt(jnp.mean(cen*cen,axis=1,keepdims=True)+1e-5)
        xhat=cen*inv
        sm[0:1,:]+=jnp.sum(gf*xhat,axis=0,keepdims=True)
        sm[1:2,:]+=jnp.sum(gf,axis=0,keepdims=True)
        e=gf*gain
        back=e-jnp.mean(e,axis=1,keepdims=True)-xhat*jnp.mean(e*xhat,axis=1,keepdims=True)
        big[pl.ds(2*d+i*tc,tc),:]=(gmid_ref[r,:]+back*inv).astype(BF)
    sm[2:4,:]=small_ref[0:2,:]
    for k in range(6):
        src=block_ref if k<3 else long_ref
        big[pl.ds(k*cc,cc),:]=tn(src[:,(k%3)*cc:(k%3+1)*cc],big[2*d:2*d+tokens,:]).astype(BF)
    def srows(b,core): return pl.ds(mul(b*sr+core*sh,16),sh)
    for b in range(4):
        net.start(16+b,"C",big.at[srows(b,1-c)],gsr.at[pl.ds(b*sh,sh)])
    net.start(20,"C",sm,sin.at[0])
    for copy in net.sent[:16]: copy.wait_send()
    net.sent=net.sent[16:]
    wload=pltpu.make_async_copy(wskip_ref,part.at[pl.ds(0,2*d)],local.at[1])
    wload.start()
    for chain in chains: chain.hop(lax.axis_size("z")-2)
    for b in range(4):
        r=pl.ds(b*sh,sh)
        net.got(16+b,"C",gsr.at[r])
        gsr[r,:]=(gsr[r,:].astype(F32)+big[srows(b,c),:].astype(F32)).astype(BF)
    def quarter(b,i): return pl.ds(mul(b*sh+i*sq,16),sq)
    top,low=pl.ds(0,sq),pl.ds(sq,sq)
    net.start(21,"X",gsr.at[quarter(wd,0)],sdx)
    net.start(22,"Y",gsr.at[quarter(wd,1)],sdy)
    net.start(23,"X",gsr.at[quarter(wx,0)],srx.at[top])
    net.start(24,"Y",gsr.at[quarter(wy,1)],sry.at[low])
    net.got(20,"C",sin.at[0])
    smz[6]=sm[...]+sin[0]
    net.start(27,"X",smz.at[6],sin.at[1])
    for chain in chains: chain.total()
    def qrows(b): return pl.ds(mul(b*kh,16),kh)
    for j,(t,b) in enumerate((("X",wx),("Y",wy),("D",wd))):
        net.start(29+j,t,gwr.at[qrows(b)],fq.at[w,c])
    fq[w,c]=gwr[qrows(w),:]
    wload.wait()
    @pl.loop(0,4)
    def _(i):
        r=pl.ds(mul(i*tc,16),tc)
        gh=big[pl.ds(mul(2*d+i*tc,16),tc),:]
        rx[r,:]=nt(gh,part[:d,:]).astype(BF)
        ry[r,:]=nt(gh,part[d:2*d,:]).astype(BF)
    outs=[]
    def put(k,src,dst):
        copy=pltpu.make_async_copy(src,dst,local.at[k]); copy.start(); outs.append(copy)
    put(2,rx,gin_out); put(3,ry,gsk_out)
    net.got(21,"X",sdx)
    gsr[quarter(wy,0),:]=(gsr[quarter(wy,0),:].astype(F32)+sdx[...].astype(F32)).astype(BF)
    net.start(25,"Y",gsr.at[quarter(wy,0)],sry.at[top])
    net.got(22,"Y",sdy)
    gsr[quarter(wx,1),:]=(gsr[quarter(wx,1),:].astype(F32)+sdy[...].astype(F32)).astype(BF)
    net.start(26,"X",gsr.at[quarter(wx,1)],srx.at[low])
    net.got(27,"X",sin.at[1])
    smz[0]=smz[6]+sin[1]
    net.start(28,"Y",smz.at[0],sin.at[2])
    for j,(t,b) in enumerate((("X",wx),("Y",wy),("D",wd))):
        net.got(29+j,t,fq.at[b,c])
    for b in range(4):
        net.start(32+b,"C",fq.at[b,c],fq.at[b,c])
    net.got(28,"Y",sin.at[2])
    smz[1]=smz[0]+sin[2]
    net.got(23,"X",srx.at[top]); net.got(25,"Y",sry.at[top])
    net.got(24,"Y",sry.at[low]); net.got(26,"X",srx.at[low])
    own[...]=(gsr[pl.ds(mul(w*sh,16),sh),:].astype(F32)+srx[...].astype(F32)+sry[...].astype(F32)).astype(BF)
    seg=sh//SEG
    chains=[Chain(net,44,smz.at[1],smz.at[2],smz.at[3],smz.at[4],smz.at[5])]
    for i in range(SEG):
        r=pl.ds(i*seg,seg)
        chains.append(Chain(net,46+2*i,own.at[r],*[sz.at[j,r] for j in range(4)]))
    for h in range(lax.axis_size("z")-1):
        for chain in chains: chain.hop(h)
    for chain in chains: chain.total()
    net.start(36,"C",own,fs)
    for b in range(4): net.got(32+b,"C",fq.at[b,1-c])
    put(4,fq,gqkv_out); put(5,smz.at[1],small_out); put(6,own,gskip_out.at[c])
    net.got(36,"C",fs)
    put(7,fs,gskip_out.at[1-c])
    for copy in outs: copy.wait()
    net.finish()

def last(gq,heads,normed,hidden,gmid,gain,block,long,wskip,small):
    tokens,d=block.shape; S=jax.ShapeDtypeStruct; hd3=gq.shape[1]
    V=pltpu.VMEM
    return pl.pallas_call(last_kernel,
        out_shape=(S((tokens,d),BF),S((tokens,d),BF),S((8,d),F32),S((4,2,d//8,hd3),BF),S((2,d//4,d),BF)),
        in_specs=[VM,VM,ANY]+[VM]*5+[ANY,VM],out_specs=(ANY,)*5,
        scratch_shapes=[V((4*tokens,d),BF),V((4*tokens,d),BF),V((tokens,d),BF),V((tokens,d),BF),V((tokens//2,d),BF),V((tokens//2,d),BF),
            V((d,hd3),BF),V((d//2,hd3),BF),V((d,d),BF),V((4,d//2,hd3),BF),V((4,2,d//8,hd3),BF),
            V((d//8,d),BF),V((d//8,d),BF),V((d//4,d),BF),V((d//4,d),BF),V((d//4,d),BF),V((4,d//4,d),BF),V((d//4,d),BF),
            V((8,d),F32),V((3,8,d),F32),V((7,8,d),F32),
            pltpu.SemaphoreType.DMA((52,)),pltpu.SemaphoreType.DMA((52,)),pltpu.SemaphoreType.DMA((8,))],
        compiler_params=pltpu.CompilerParams(vmem_limit_bytes=63*2**20,collective_id=1,has_side_effects=True),
        cost_estimate=pl.CostEstimate(flops=2*tokens*d*d*10,bytes_accessed=60*2**20,transcendentals=0))(
        gq,heads,normed,hidden,gmid,gain,block,long,wskip,small)

def assemble_kernel(gin_ref,gsk_ref,skip_ref,gq_ref,um_ref,uo_ref,dm_ref,do_ref,om_ref,oo_ref,
                    gin_out,gsk_out,skip_out,qkv_out,up_out,down_out,out_out,
                    s0,s1,s2,s3,s4,s5,s6,local):
    first=lax.axis_index("core")==0
    copies=[]
    def put(src,dst):
        copy=pltpu.make_async_copy(src,dst,local.at[len(copies)]); copy.start(); copies.append(copy)
    def chunks(n,body,size=144):
        @pl.loop(0,n//size)
        def _(i): body(pl.ds(pl.multiple_of(i*size,16),size))
    def wide(dst,src):
        def body(r): dst[r,:]=src[r,:].astype(F32)
        chunks(dst.shape[0],body,208 if dst.shape[0]%208==0 else 144)
    wide(s0,gin_ref); put(s0,gin_out)
    wide(s1,gsk_ref); put(s1,gsk_out)
    def pair(dst,mine,other):
        h=mine.shape[0]
        a=mine.shape[0]
        def body(r):
            m,o=mine[r,:].astype(F32),other[r,:].astype(F32)
            dst[0,r,:]=jnp.where(first,m,o)
            dst[1,r,:]=jnp.where(first,o,m)
        chunks(h,body)
    pair(s5,dm_ref,do_ref); put(s5,down_out)
    pair(s6,om_ref,oo_ref); put(s6,out_out)
    fb=um_ref.shape[1]//4
    def up(r):
        m,o=um_ref[r,:].astype(F32),uo_ref[r,:].astype(F32)
        a,b=jnp.where(first,m,o),jnp.where(first,o,m)
        s4[r,:]=jnp.concatenate([v[:,p*fb:(p+1)*fb] for p in range(4) for v in (a,b)],axis=1)
    chunks(s4.shape[0],up,48); put(s4,up_out)
    def skip(r): s2[r,:]=skip_ref[r,:].astype(F32)
    chunks(s2.shape[0],skip); put(s2,skip_out)
    hd=gq_ref.shape[3]//3; kh=gq_ref.shape[2]
    for core in range(2):
        for i in range(kh//48):
            r=pl.ds(i*48,48)
            s3[pl.ds(core*kh+i*48,48),:]=jnp.concatenate([gq_ref[p,core,r,s*hd:(s+1)*hd].astype(F32) for s in range(3) for p in range(4)],axis=1)
    put(s3,qkv_out)
    for copy in copies: copy.wait()

def assemble(gin,gsk,skip,gq,um,uo,dm,do,om,oo):
    S=lambda *s: jax.ShapeDtypeStruct(s,F32)
    tokens,d=gin.shape
    shapes=(S(tokens,d),S(tokens,d),S(*skip.shape),S(d//4,3*d),S(d//4,2*um.shape[1]),S(2,*dm.shape),S(2,*om.shape))
    return pl.pallas_call(assemble_kernel,out_shape=shapes,in_specs=[VM]*10,out_specs=(ANY,)*7,
        scratch_shapes=[pltpu.VMEM(s.shape,F32) for s in shapes]+[pltpu.SemaphoreType.DMA((7,))],
        compiler_params=pltpu.CompilerParams(vmem_limit_bytes=60*2**20),
        cost_estimate=pl.CostEstimate(flops=0,bytes_accessed=40*2**20,transcendentals=0))(
        gin,gsk,skip,gq,um,uo,dm,do,om,oo)

from jax.sharding import Mesh, PartitionSpec as P
WIDE=("y","x"); ROWS=("z","core")
SWAP=[(0,1),(1,0)]

def swap_cores(values):
    return lax.ppermute(values,"core",SWAP)

def pick(values, index, axis):
    return lax.dynamic_index_in_dim(values,index,axis,keepdims=False)

def place_halves(mine, other, core, axis):
    first=jnp.where(core==0,mine,other); second=jnp.where(core==0,other,mine)
    return jnp.stack([first,second],axis=axis)

def dot(a,b): return jnp.dot(a,b,preferred_element_type=F32)

def norm(values):
    cen=values-jnp.mean(values,axis=1,keepdims=True)
    inv=lax.rsqrt(jnp.mean(cen*cen,axis=1,keepdims=True)+1e-5)
    return cen*inv,inv

def on_device(nw, block_input, long_skip, segment_ids, item_lengths, skip_weight, first_gain, first_shift, qkv_weight,
              out_weight, second_gain, second_shift, up_weight, down_weight, output_grad):
    core=lax.axis_index("core")
    _,tokens,d=block_input.shape
    heads=qkv_weight.shape[1]//(3*HEAD*nw); hd=heads*HEAD
    ff=up_weight.shape[1]; fb=ff//(2*nw)
    gather=lambda v: lax.all_gather(v,WIDE,axis=0,tiled=True)
    near=nw==4
    vecs=jnp.stack([first_gain,first_shift,second_gain,second_shift]+[first_gain]*4).astype(F32)
    if near:
        hidden,normed_all,qkv,w_heads,w_skip,vecs=first(block_input[0],long_skip[0],skip_weight,qkv_weight,vecs)
        vec=vecs.transpose(1,0,2).reshape(8,d)
        gain1,shift1,gain2,shift2=[vec[i:i+1] for i in range(4)]
        qkv,up_weight,down_weight,out_weight=lax.optimization_barrier((qkv,up_weight,down_weight,out_weight))
    else:
        vec=gather(vecs.astype(BF).T).T.astype(F32)
        gain1,shift1,gain2,shift2=[vec[i:i+1] for i in range(4)]
        w_skip=gather(skip_weight)
        joined=jnp.concatenate([block_input[0],long_skip[0]],axis=1)
        w_heads=qkv_weight.reshape(d//nw,3,nw,hd).transpose(2,0,1,3)
        w_heads=lax.all_to_all(w_heads,WIDE,0,0).reshape(d,3*hd)
        hidden=dot(joined,w_skip)
        xhat1,inv1=norm(hidden)
        normed_all=gather((xhat1*gain1+shift1).astype(BF))
        qkv=dot(normed_all,w_heads).astype(BF)
    w_out=gather(out_weight)
    up_mine=gather(pick(up_weight.reshape(d//nw,nw,2,fb),core,2).reshape(d//nw,nw*fb))
    down_mine=gather(pick(down_weight.reshape(2,fb,d),core,0))
    att,lse=attend(item_lengths,qkv,heads)
    att,up_mine,down_mine=lax.optimization_barrier((att,up_mine,down_mine))
    up_other,down_other=swap_cores(up_mine),swap_cores(down_mine)
    att=lax.all_to_all(att.reshape(nw,tokens,hd),WIDE,0,0)
    lay,gmid,gatt,gow,small,gupo,guph,gdno,gdnh=mlp(hidden,att,w_out,gain2,shift2,output_grad[0],up_mine,up_other,down_mine,down_other)
    grad_heads=lax.all_to_all(gatt,WIDE,0,0).reshape(nw*tokens,hd)

    def scatter(mine,other):
        both=(mine.astype(F32)+swap_cores(other).astype(F32)).astype(BF)
        return lax.psum_scatter(both,WIDE,scatter_dimension=0,tiled=True)
    def both_cores(mine,axis):
        return place_halves(mine,swap_cores(mine),core,axis).astype(F32)
    def by_rows(grad):
        cut=grad.reshape(nw,2,-1,grad.shape[1])
        return scatter(pick(cut,core,1).reshape(-1,grad.shape[1]),pick(cut,1-core,1).reshape(-1,grad.shape[1]))
    early=scatter(gupo,guph),scatter(gdno,gdnh),by_rows(gow)
    grad_qkv=attend_back(item_lengths,qkv,grad_heads,lse,heads)
    grad_qkv,early=lax.optimization_barrier((grad_qkv,early))
    early=lax.psum(early,"z")
    if near:
        gin,gsk,smalls,gqkv,gskip=last(grad_qkv,w_heads,normed_all,hidden,gmid,gain1,block_input[0],long_skip[0],w_skip,small)
        gskip,early=lax.optimization_barrier((gskip,early))
        others=swap_cores(early)
        gin,gsk,skip_share,qkv_share,up_share,down_share,out_share=assemble(gin,gsk,gskip.reshape(-1,d),gqkv,
            early[0],others[0],early[1],others[1],early[2],others[2])
        down_share,out_share=down_share.reshape(-1,d),out_share.reshape(-1,d)
        smalls=lax.dynamic_slice_in_dim(smalls[:4],(2*lax.axis_index("y")+lax.axis_index("x"))*(d//nw),d//nw,axis=1).T
    else:
        part_first=nt(grad_qkv,w_heads).astype(BF)
        grad_first=lax.psum_scatter(part_first,WIDE,scatter_dimension=0,tiled=True).astype(F32)
        gqkv=tn(normed_all,grad_qkv).astype(BF).reshape(nw,2,d//nw//2,3*hd)
        gqkv=(pick(gqkv,core,1).astype(F32)+swap_cores(pick(gqkv,1-core,1)).astype(F32)).astype(BF)
        e1=grad_first*gain1
        across=inv1*(e1-jnp.mean(e1,axis=1,keepdims=True)-xhat1*jnp.mean(e1*xhat1,axis=1,keepdims=True))
        grad_hidden=(gmid+across).astype(BF)
        gskip=by_rows(tn(joined,grad_hidden).astype(BF))
        grad_joined=nt(grad_hidden,w_skip)
        gin,gsk=grad_joined[:,:d],grad_joined[:,d:]
        small1=jnp.stack([jnp.sum(grad_first*xhat1,axis=0),jnp.sum(grad_first,axis=0)])
        gqkv,gskip,early=lax.optimization_barrier((gqkv,gskip,early))
        gqkv,gskip=lax.psum((gqkv,gskip),"z")
        up_share=both_cores(early[0].reshape(d//nw,nw,fb),2).reshape(d//nw,ff)
        down_share=both_cores(early[1],0).reshape(ff//nw,d)
        out_share=both_cores(early[2],0).reshape(d//nw,d)
        skip_share=both_cores(gskip,0).reshape(2*d//nw,d)
        gqkv=lax.all_to_all(gqkv,WIDE,0,0).reshape(nw,-1,3,hd).transpose(1,2,0,3)
        qkv_share=both_cores(gqkv,0).reshape(d//nw,-1)
        smalls=jnp.stack([small1[0],small1[1],small[0],small[1]],axis=1)
        smalls=lax.psum(lax.psum_scatter(smalls.astype(BF),WIDE,scatter_dimension=0,tiled=True),ROWS).astype(F32)
    return (lay[None],gin[None],gsk[None],skip_share,smalls[:,0],smalls[:,1],qkv_share,out_share,
            smalls[:,2],smalls[:,3],up_share,down_share)

def solution(mesh):
    rows,wide=mesh.devices.shape
    side=2 if wide==4 else int(wide**0.5)
    grid=Mesh(mesh.devices.reshape(rows//2,2,wide//side,side),("z","core","y","x"))
    tok=P(ROWS,WIDE,None); row=P(ROWS,None); mat=P(WIDE,None); vec=P(WIDE)
    return jax.shard_map(functools.partial(on_device,wide),mesh=grid,
        in_specs=(tok,tok,row,row,mat,vec,vec,mat,mat,vec,vec,mat,mat,tok),
        out_specs=(tok,tok,tok,mat,vec,vec,mat,mat,vec,vec,mat,mat),check_vma=False)
```

```python
import functools
import jax, jax.numpy as jnp
from jax import lax
from jax.experimental import pallas as pl
from jax.experimental.pallas import tpu as pltpu
HEAD=72; SHORT=258; LONG=1026; NITEM=12
LOG2E=1.4426950408889634
SCALE=HEAD**-0.5
QT=384

def kwin(n): return (n + 29 + 31)//32*32
def qwin(n): return (n + 15 + QT-1)//QT*QT

def nt(a,b): return lax.dot_general(a,b,(((1,),(1,)),((),())),preferred_element_type=jnp.float32)
def nn(a,b): return lax.dot_general(a,b,(((1,),(0,)),((),())),preferred_element_type=jnp.float32)
def tn(a,b): return lax.dot_general(a,b,(((0,),(0,)),((),())),preferred_element_type=jnp.float32)

def windows(start, size, row_len):
    k0 = pl.multiple_of(jnp.minimum(start//16*16, row_len-kwin(size)),16)
    q0 = pl.multiple_of(jnp.minimum(start//16*16, row_len-qwin(size)),16)
    return k0,q0

def split_heads(src_ref, dst_ref, count, chunk=416):
    rows=src_ref.shape[0]
    @pl.loop(0, rows//chunk)
    def _(i):
        r=pl.ds(pl.multiple_of(i*chunk,16),chunk)
        block=src_ref[r,:]
        for j in range(count):
            dst_ref[j,r,:]=block[:,j*HEAD:(j+1)*HEAD]

def join_heads(src_ref, dst_ref, count, chunk=416):
    rows=dst_ref.shape[0]
    @pl.loop(0, rows//chunk)
    def _(i):
        r=pl.ds(pl.multiple_of(i*chunk,16),chunk)
        dst_ref[r,:]=jnp.concatenate([src_ref[j,r,:] for j in range(count)],axis=1)

def zero(ref, chunk=416):
    rows=ref.shape[1]
    @pl.loop(0, rows//chunk)
    def _(i):
        r=pl.ds(pl.multiple_of(i*chunk,16),chunk)
        for j in range(ref.shape[0]):
            ref[j,r,:]=jnp.zeros((chunk,ref.shape[2]),ref.dtype)

def for_items(len_ref, one):
    def step(i, start):
        size=len_ref[0,i]
        @pl.when(size==LONG)
        def _(): one(i,start,LONG)
        @pl.when(size==SHORT)
        def _(): one(i,start,SHORT)
        return start+size
    lax.fori_loop(0,len_ref.shape[1],step,jnp.int32(0))

def mask_edges(values, start, k0, size, fill):
    n=values.shape[0]; body=size//32*32
    off=start-k0
    top=lax.broadcasted_iota(jnp.int32,(32,values.shape[1]),0)
    low=jnp.where(top>=off,values[:32],fill)
    high=jnp.where(top+body<off+size,values[body:],fill)
    return jnp.concatenate([low,values[32:body],high],axis=0)

def attend_kernel(heads, len_ref, qkv_ref, out_ref, lse_ref, split_ref, acc_ref):
    row_len=qkv_ref.shape[0]
    split_heads(qkv_ref, split_ref, 3*heads)
    zero(acc_ref)
    lse_ref[...]=jnp.zeros_like(lse_ref)
    def one(item,start,size):
        k0,q0=windows(start,size,row_len)
        kr=pl.ds(k0,kwin(size))
        @pl.loop(0,qwin(size)//QT)
        def _(t):
            qr=pl.ds(pl.multiple_of(q0+t*QT,16),QT)
            col=q0+t*QT+lax.broadcasted_iota(jnp.int32,(1,QT),1)
            live=(col>=start)&(col<start+size)
            for h in range(heads):
                s=nt(split_ref[heads+h,kr,:],split_ref[h,qr,:])
                s=mask_edges(s,start,k0,size,-1e30)
                m=jnp.max(s,axis=0,keepdims=True)
                p=jnp.exp2((s-m)*(SCALE*LOG2E))
                l=jnp.sum(p,axis=0,keepdims=True)
                o=tn(split_ref[2*heads+h,kr,:],p.astype(jnp.bfloat16))
                o=jnp.where(live,o/l,0.0)
                acc_ref[h,qr,:]+=o.T.astype(jnp.bfloat16)
                lse_ref[item,pl.ds(t*heads+h,1),:]=m*(SCALE*LOG2E)+jnp.log2(l)
    for_items(len_ref,one)
    join_heads(acc_ref,out_ref,heads)

def attend_back_kernel(heads, len_ref, qkv_ref, grad_ref, lse_ref, out_ref, split_ref, gsplit_ref, acc_ref, dk_ref, dv_ref):
    row_len=qkv_ref.shape[0]
    split_heads(qkv_ref, split_ref, 3*heads)
    split_heads(grad_ref, gsplit_ref, heads)
    zero(acc_ref)
    def one(item,start,size):
        k0,q0=windows(start,size,row_len)
        kw=kwin(size)
        kr=pl.ds(k0,kw)
        for h in range(heads):
            dk_ref[h,:kw,:]=jnp.zeros((kw,HEAD),jnp.float32)
            dv_ref[h,:kw,:]=jnp.zeros((kw,HEAD),jnp.float32)
        @pl.loop(0,qwin(size)//QT)
        def _(t):
            qr=pl.ds(pl.multiple_of(q0+t*QT,16),QT)
            col=q0+t*QT+lax.broadcasted_iota(jnp.int32,(1,QT),1)
            live=(col>=start)&(col<start+size)
            for h in range(heads):
                k=split_ref[heads+h,kr,:]; q=split_ref[h,qr,:]; g=gsplit_ref[h,qr,:]
                lse=jnp.where(live,lse_ref[item,pl.ds(t*heads+h,1),:],1e30)
                s=nt(k,q)
                p=jnp.exp2(s*(SCALE*LOG2E)-lse)
                p=mask_edges(p,start,k0,size,0.0)
                dv_ref[h,:kw,:]+=nn(p.astype(jnp.bfloat16),g)
                dp=nt(split_ref[2*heads+h,kr,:],g)
                delta=jnp.sum(p*dp,axis=0,keepdims=True)
                ds=(p*(dp-delta)).astype(jnp.bfloat16)
                dk_ref[h,:kw,:]+=nn(ds,q)
                dq=tn(k,ds)*SCALE
                acc_ref[h,qr,:]+=dq.T.astype(jnp.bfloat16)
        for h in range(heads):
            acc_ref[heads+h,kr,:]+=(dk_ref[h,:kw,:]*SCALE).astype(jnp.bfloat16)
            acc_ref[2*heads+h,kr,:]+=dv_ref[h,:kw,:].astype(jnp.bfloat16)
    for_items(len_ref,one)
    join_heads(acc_ref,out_ref,3*heads)

VM=pl.BlockSpec(memory_space=pltpu.VMEM); SM=pl.BlockSpec(memory_space=pltpu.SMEM)
def attend(lens,qkv,heads):
    n=qkv.shape[0]
    nt_=heads*(qwin(LONG)//QT)
    return pl.pallas_call(functools.partial(attend_kernel,heads),
      out_shape=(jax.ShapeDtypeStruct((n,heads*HEAD),jnp.bfloat16),jax.ShapeDtypeStruct((NITEM,nt_,QT),jnp.float32)),
      in_specs=[SM,VM],out_specs=(VM,VM),
      scratch_shapes=[pltpu.VMEM((3*heads,n,HEAD),jnp.bfloat16),pltpu.VMEM((heads,n,HEAD),jnp.bfloat16)],
      compiler_params=pltpu.CompilerParams(vmem_limit_bytes=56*2**20),
      cost_estimate=pl.CostEstimate(flops=heads*n*n*HEAD*4,bytes_accessed=12*2**20,transcendentals=heads*n*n//3))(lens,qkv)
def attend_back(lens,qkv,grad,lse,heads):
    n=qkv.shape[0]
    return pl.pallas_call(functools.partial(attend_back_kernel,heads),
      out_shape=jax.ShapeDtypeStruct((n,3*heads*HEAD),jnp.bfloat16),
      in_specs=[SM,VM,VM,VM],out_specs=VM,
      scratch_shapes=[pltpu.VMEM((3*heads,n,HEAD),jnp.bfloat16),pltpu.VMEM((heads,n,HEAD),jnp.bfloat16),pltpu.VMEM((3*heads,n,HEAD),jnp.bfloat16),
        pltpu.VMEM((heads,kwin(LONG),HEAD),jnp.float32),pltpu.VMEM((heads,kwin(LONG),HEAD),jnp.float32)],
      compiler_params=pltpu.CompilerParams(vmem_limit_bytes=60*2**20),
      cost_estimate=pl.CostEstimate(flops=heads*n*n*HEAD*10,bytes_accessed=20*2**20,transcendentals=heads*n*n//3))(lens,qkv,grad,lse)


F32=jnp.float32; BF=jnp.bfloat16
ANY=pl.BlockSpec(memory_space=pl.ANY)

def gelu_parts(u):
    z=jnp.exp2(u*u*(-0.5*1.4426950408889634))
    t=1.0/(1.0+(0.3275911*0.7071067811865476)*jnp.abs(u))
    poly=((((1.061405429*t-1.453152027)*t+1.421413741)*t-0.284496736)*t+0.254829592)*t
    tail=0.5*poly*z
    cdf=jnp.where(u>=0,1.0-tail,tail)
    return u*cdf, cdf+u*(z*0.3989422804014327)

def mlp_kernel(tile, hidden_ref, att_ref, outw_ref, gain_ref, shift_ref, g_ref, upo_ref, uph_ref, dno_ref, dnh_ref,
               lay_ref, gmid_ref, gatt_ref, gow_ref, small_ref, gupo_ref, guph_ref, gdno_ref, gdnh_ref,
               att_s, n2_s, xhat_s, rstd_s, act_s, gu_s, upb, dnb, gub, gdb, in_sem, out_sem):
    parts,tokens,cols=att_ref.shape
    d=hidden_ref.shape[1]
    tc=tokens//2 if tokens>416 else tokens
    nch=tokens//tc
    half=upo_ref.shape[1]; steps=half//tile
    cc=d//3; fc=256

    def fetch(j,act):
        slot=lax.rem(j,2)
        for first,(us,ds) in ((True,(uph_ref,dnh_ref)),(False,(upo_ref,dno_ref))):
            cond=(j<steps) if first else (j>=steps)
            @pl.when(cond)
            def _():
                k=j if first else j-steps
                off=pl.multiple_of(k*tile,tile)
                act(pltpu.make_async_copy(us.at[:,pl.ds(off,tile)],upb.at[slot],in_sem.at[slot,0]))
                act(pltpu.make_async_copy(ds.at[pl.ds(off,tile),:],dnb.at[slot],in_sem.at[slot,1]))
    def flush(j,act):
        slot=lax.rem(j,2)
        for first,(us,ds) in ((True,(guph_ref,gdnh_ref)),(False,(gupo_ref,gdno_ref))):
            cond=(j<steps) if first else (j>=steps)
            @pl.when(cond)
            def _():
                k=j if first else j-steps
                off=pl.multiple_of(k*tile,tile)
                act(pltpu.make_async_copy(gub.at[slot],us.at[:,pl.ds(off,tile)],out_sem.at[slot,0]))
                act(pltpu.make_async_copy(gdb.at[slot],ds.at[pl.ds(off,tile),:],out_sem.at[slot,1]))
    start=lambda c: c.start()
    wait=lambda c: c.wait()
    fetch(jnp.int32(0),start)
    gain=gain_ref[...]; shift=shift_ref[...]
    sub=tc//2
    @pl.loop(0,2*nch)
    def _(i):
        r=pl.ds(pl.multiple_of(i*sub,16),sub)
        joined=jnp.concatenate([att_ref[p,r,:] for p in range(parts)],axis=1)
        att_s[r,:]=joined
        mid=hidden_ref[r,:]+nn(joined,outw_ref[...])
        lay_ref[r,:]=mid
        cen=mid-jnp.mean(mid,axis=1,keepdims=True)
        inv=lax.rsqrt(jnp.mean(cen*cen,axis=1,keepdims=True)+1e-5)
        xhat=cen*inv
        xhat_s[r,:]=xhat
        rstd_s[r,:]=jnp.broadcast_to(inv,(sub,128))
        n2_s[r,:]=(xhat*gain+shift).astype(BF)
        gmid_ref[r,:]=jnp.zeros((sub,d),F32)
    @pl.loop(0,2*steps)
    def _(j):
        slot=lax.rem(j,2)
        @pl.when(j+1<2*steps)
        def _(): fetch(j+1,start)
        fetch(j,wait)
        @pl.when(j>=2)
        def _(): flush(j-2,wait)
        @pl.loop(0,nch)
        def _(i):
            r=pl.ds(pl.multiple_of(i*tc,16),tc)
            for k in range(tile//fc):
                f=pl.ds(k*fc,fc)
                u=nn(n2_s[r,:],upb[slot,:,f])
                a,dg=gelu_parts(u)
                act_s[r,f]=a.astype(BF)
                ga=nt(g_ref[r,:],dnb[slot,f,:])
                gu_s[r,f]=(ga*dg).astype(BF)
        @pl.loop(0,nch)
        def _(i):
            r=pl.ds(pl.multiple_of(i*tc,16),tc)
            for k in range(3):
                cr=pl.ds(k*cc,cc)
                lay_ref[r,cr]+=nn(act_s[r,:],dnb[slot,:,cr])
                gmid_ref[r,cr]+=nt(gu_s[r,:],upb[slot,cr,:])
        for k in range(tile//fc):
            f=pl.ds(k*fc,fc)
            gdb[slot,f,:]=tn(act_s[:,f],g_ref[...]).astype(BF)
        for k in range(3):
            cr=pl.ds(k*cc,cc)
            gub[slot,cr,:]=tn(n2_s[:,cr],gu_s[...]).astype(BF)
        flush(j,start)
    small_ref[...]=jnp.zeros_like(small_ref)
    @pl.loop(0,2*nch)
    def _(i):
        r=pl.ds(pl.multiple_of(i*sub,16),sub)
        gs=gmid_ref[r,:]; xhat=xhat_s[r,:]
        small_ref[0:1,:]+=jnp.sum(gs*xhat,axis=0,keepdims=True)
        small_ref[1:2,:]+=jnp.sum(gs,axis=0,keepdims=True)
        e=gs*gain
        back=e-jnp.mean(e,axis=1,keepdims=True)-xhat*jnp.mean(e*xhat,axis=1,keepdims=True)
        gm=g_ref[r,:].astype(F32)+back*rstd_s[r,0:1]
        gmid_ref[r,:]=gm
        low=gm.astype(BF)
        n2_s[r,:]=low
        ga=nt(low,outw_ref[...]).astype(BF)
        for p in range(parts):
            gatt_ref[p,r,:]=ga[:,p*cols:(p+1)*cols]
    for k in range(3):
        cr=pl.ds(k*cc,cc)
        gow_ref[cr,:]=tn(att_s[:,cr],n2_s[...]).astype(BF)
    flush(jnp.int32(2*steps-2),wait)
    flush(jnp.int32(2*steps-1),wait)

def mlp(hidden,att,outw,gain,shift,g,upo,uph,dno,dnh):
    tokens,d=hidden.shape; half=upo.shape[1]; tile=half//3
    S=jax.ShapeDtypeStruct
    flops=2*tokens*d*(half*2*6+d*3)
    return pl.pallas_call(functools.partial(mlp_kernel,tile),
        out_shape=(S((tokens,d),F32),S((tokens,d),F32),S(att.shape,BF),S((d,d),BF),S((8,d),F32),
                   S(upo.shape,BF),S(upo.shape,BF),S(dno.shape,BF),S(dno.shape,BF)),
        in_specs=[VM]*6+[ANY]*4,
        out_specs=(VM,)*5+(ANY,)*4,
        scratch_shapes=[pltpu.VMEM((tokens,d),BF),pltpu.VMEM((tokens,d),BF),pltpu.VMEM((tokens,d),F32),pltpu.VMEM((tokens,128),F32),
            pltpu.VMEM((tokens,tile),BF),pltpu.VMEM((tokens,tile),BF),
            pltpu.VMEM((2,d,tile),BF),pltpu.VMEM((2,tile,d),BF),pltpu.VMEM((2,d,tile),BF),pltpu.VMEM((2,tile,d),BF),
            pltpu.SemaphoreType.DMA((2,2)),pltpu.SemaphoreType.DMA((2,2))],
        compiler_params=pltpu.CompilerParams(vmem_limit_bytes=62*2**20),
        cost_estimate=pl.CostEstimate(flops=flops,bytes_accessed=60*2**20,transcendentals=tokens*half*2))(
        hidden,att,outw,gain,shift,g,upo,uph,dno,dnh)


MESH=pl.DeviceIdType.MESH

def place():
    x,y,c=lax.axis_index("x"),lax.axis_index("y"),lax.axis_index("core")
    return x,y,c,2*y+x,2*y+1-x,2-2*y+x,3-2*y-x

class Links:
    def __init__(self,send,recv):
        self.send,self.recv,self.sent=send,recv,[]
        x,y,c=lax.axis_index("x"),lax.axis_index("y"),lax.axis_index("core")
        self.to={"X":{"x":1-x},"Y":{"y":1-y},"D":{"x":1-x,"y":1-y},"C":{"core":1-c}}
    def meet(self,who):
        barrier=pltpu.get_barrier_semaphore()
        for t in who:
            pl.semaphore_signal(barrier,inc=1,device_id=self.to[t],device_id_type=MESH)
        pl.semaphore_wait(barrier,len(who))
    def start(self,k,t,src,dst):
        copy=pltpu.make_async_remote_copy(src_ref=src,dst_ref=dst,send_sem=self.send.at[k],recv_sem=self.recv.at[k],
                                          device_id=self.to[t],device_id_type=MESH)
        copy.start()
        self.sent.append(copy)
    def got(self,k,t,dst):
        pltpu.make_async_remote_copy(src_ref=dst,dst_ref=dst,send_sem=self.send.at[k],recv_sem=self.recv.at[k],
                                     device_id=self.to[t],device_id_type=MESH).wait_recv()
    def finish(self):
        for copy in self.sent: copy.wait_send()

def first_kernel(block_ref,long_ref,skip_ref,qkvw_ref,vec_ref,
                 hidden_out,normed_out,qkv_out,heads_out,wskip_out,vec_out,
                 ws,ns,hs,piece,hid,qs,vs,send,recv,local):
    x,y,c,w,wx,wy,wd=place()
    tokens,d=block_ref.shape
    sr=skip_ref.shape[0]; half=sr//2; part=half//2
    kr=qkvw_ref.shape[0]; kh=kr//2; hd=qkvw_ref.shape[1]//12
    tc=tokens//4
    mul=pl.multiple_of
    net=Links(send,recv)
    net.meet("XYDC")
    def srows(b,core,p): return pl.ds(mul(b*sr+core*half+p*part,16),part)
    def mine(p): return pl.ds(mul(c*half+p*part,16),part)
    net.start(0,"X",skip_ref.at[mine(0)],ws.at[srows(w,c,0)])
    net.start(2,"Y",skip_ref.at[mine(1)],ws.at[srows(w,c,1)])
    net.start(1,"X",skip_ref.at[mine(1)],ws.at[srows(w,c,1)])
    net.start(3,"Y",skip_ref.at[mine(0)],ws.at[srows(w,c,0)])
    own=pltpu.make_async_copy(skip_ref,ws.at[pl.ds(mul(w*sr,16),sr)],local.at[0])
    own.start()
    for k,t in ((30,"X"),(31,"Y"),(32,"D")): net.start(k,t,vec_ref,vs.at[w])
    vs[w]=vec_ref[...]
    for p in range(4):
        piece[p]=jnp.concatenate([qkvw_ref[:,(s*4+p)*hd:(s*4+p+1)*hd] for s in range(3)],axis=1)
    own_heads=pltpu.make_async_copy(piece.at[w],hs.at[pl.ds(mul(w*kr,16),kr)],local.at[1])
    own_heads.start()
    def pass_on(k,t,b,p,onward):
        r=srows(b,c,p)
        net.got(k,t,ws.at[r])
        for k2,t2 in onward: net.start(k2,t2,ws.at[r],ws.at[r])
    pass_on(0,"X",wx,0,((4,"Y"),(6,"C")))
    pass_on(2,"Y",wy,1,((5,"X"),(7,"C")))
    pass_on(1,"X",wx,1,((8,"C"),))
    pass_on(3,"Y",wy,0,((9,"C"),))
    def hrows(b,core): return pl.ds(mul(b*kr+core*kh,16),kh)
    cut=pl.ds(mul(c*kh,16),kh)
    net.start(12,"X",piece.at[wx,cut],hs.at[hrows(w,c)])
    net.start(13,"Y",piece.at[wy,cut],hs.at[hrows(w,c)])
    net.start(14,"D",piece.at[wd,cut],hs.at[hrows(w,c)])
    own.wait()
    net.got(6,"C",ws.at[srows(wx,1-c,0)])
    net.got(8,"C",ws.at[srows(wx,1-c,1)])
    near=pl.ds(mul(y*d,16),d); far=pl.ds(mul((1-y)*d,16),d)
    def tok(i): return pl.ds(mul(i*tc,16),tc)
    @pl.loop(0,4)
    def _(i):
        lhs=jnp.where(y==0,block_ref[tok(i),:],long_ref[tok(i),:])
        hid[tok(i),:]=nn(lhs,ws[near,:])
    pass_on(4,"Y",wd,0,((10,"C"),))
    pass_on(5,"X",wd,1,((11,"C"),))
    net.got(7,"C",ws.at[srows(wy,1-c,1)])
    net.got(9,"C",ws.at[srows(wy,1-c,0)])
    net.got(10,"C",ws.at[srows(wd,1-c,0)])
    net.got(11,"C",ws.at[srows(wd,1-c,1)])
    for k,t,b in ((30,"X",wx),(31,"Y",wy),(32,"D",wd)): net.got(k,t,vs.at[b])
    gain=jnp.concatenate([vs[p,0:1,:] for p in range(4)],axis=1)
    shift=jnp.concatenate([vs[p,1:2,:] for p in range(4)],axis=1)
    def nrows(b,i): return pl.ds(mul(b*tokens+i*tc,16),tc)
    def spread(i,t):
        net.start((18 if t=="X" else 22)+i,t,ns.at[nrows(w,i)],ns.at[nrows(w,i)])
    for i in range(4):
        r=tok(i)
        lhs=jnp.where(y==0,long_ref[r,:],block_ref[r,:])
        h=hid[r,:]+nn(lhs,ws[far,:])
        hid[r,:]=h
        cen=h-jnp.mean(h,axis=1,keepdims=True)
        inv=lax.rsqrt(jnp.mean(cen*cen,axis=1,keepdims=True)+1e-5)
        ns[nrows(w,i),:]=(cen*inv*gain+shift).astype(BF)
        spread(i,"XYXY"[i])
    for i,t in ((1,"X"),(0,"Y"),(3,"X"),(2,"Y")): spread(i,t)
    outs=[]
    def put(k,src,dst):
        copy=pltpu.make_async_copy(src,dst,local.at[k]); copy.start(); outs.append(copy)
    put(2,ws,wskip_out); put(3,hid,hidden_out); put(7,vs,vec_out)
    for j,(t,b) in enumerate((("X",wx),("Y",wy),("D",wd))):
        net.got(12+j,t,hs.at[hrows(b,c)])
        net.start(15+j,"C",hs.at[hrows(b,c)],hs.at[hrows(b,c)])
    for j,b in enumerate((wx,wy,wd)):
        net.got(15+j,"C",hs.at[hrows(b,1-c)])
    own_heads.wait()
    put(4,hs,heads_out)
    def project(b,i): qs[nrows(b,i),:]=nn(ns[nrows(b,i),:],hs[...]).astype(BF)
    @pl.loop(0,4)
    def _(i): project(w,i)
    for i,t,b,k,k2,t2 in ((0,"X",wx,18,26,"Y"),(1,"Y",wy,22,27,"X"),(2,"X",wx,18,28,"Y"),(3,"Y",wy,22,29,"X")):
        net.got(k+i,t,ns.at[nrows(b,i)])
        net.start(k2,t2,ns.at[nrows(b,i)],ns.at[nrows(b,i)])
    @pl.loop(0,2)
    def _(i): project(wx,2*i)
    @pl.loop(0,2)
    def _(i): project(wy,2*i+1)
    for i in (1,3):
        net.got(18+i,"X",ns.at[nrows(wx,i)])
        project(wx,i)
        net.got(22+i-1,"Y",ns.at[nrows(wy,i-1)])
        project(wy,i-1)
    for i,t,k in ((0,"Y",26),(1,"X",27),(2,"Y",28),(3,"X",29)):
        net.got(k,t,ns.at[nrows(wd,i)])
        project(wd,i)
    put(5,ns,normed_out); put(6,qs,qkv_out)
    for copy in outs: copy.wait()
    net.finish()

def first(block,long,skipw,qkvw,vecs):
    tokens,d=block.shape; S=jax.ShapeDtypeStruct; hd3=qkvw.shape[1]//4
    V=pltpu.VMEM
    return pl.pallas_call(first_kernel,
        out_shape=(S((tokens,d),F32),S((4*tokens,d),BF),S((4*tokens,hd3),BF),S((d,hd3),BF),S((2*d,d),BF),S((4,)+vecs.shape,F32)),
        in_specs=[VM]*5,out_specs=(ANY,)*6,
        scratch_shapes=[V((2*d,d),BF),V((4*tokens,d),BF),V((d,hd3),BF),V((4,d//4,hd3),BF),V((tokens,d),F32),V((4*tokens,hd3),BF),V((4,)+vecs.shape,F32),
            pltpu.SemaphoreType.DMA((33,)),pltpu.SemaphoreType.DMA((33,)),pltpu.SemaphoreType.DMA((8,))],
        compiler_params=pltpu.CompilerParams(vmem_limit_bytes=56*2**20,collective_id=0,has_side_effects=True),
        cost_estimate=pl.CostEstimate(flops=2*tokens*d*d*5,bytes_accessed=40*2**20,transcendentals=0))(
        block,long,skipw,qkvw,vecs)

class Chain:
    def __init__(self,net,k,own,up_in,down_in,up_out,down_out):
        self.net,self.k,self.own=net,k,own
        self.up_in,self.down_in,self.up_out,self.down_out=up_in,down_in,up_out,down_out
        self.z,self.n=lax.axis_index("z"),lax.axis_size("z")
    def copy(self,up,src):
        k=self.k+(0 if up else 1)
        return pltpu.make_async_remote_copy(src_ref=src,dst_ref=self.up_in if up else self.down_in,
            send_sem=self.net.send.at[k],recv_sem=self.net.recv.at[k],
            device_id={"z":self.z+1 if up else self.z-1},device_id_type=MESH)
    def hop(self,h):
        for up in (True,False):
            here=self.z==(h if up else self.n-1-h)
            inn,out=(self.up_in,self.up_out) if up else (self.down_in,self.down_out)
            @pl.when(here)
            def _():
                if h==0:
                    self.copy(up,self.own).start()
                else:
                    self.copy(up,inn).wait_recv()
                    out[...]=(self.own[...].astype(F32)+inn[...].astype(F32)).astype(out.dtype)
                    self.copy(up,out).start()
    def total(self):
        first,final=self.z==0,self.z==self.n-1
        @pl.when(first)
        def _():
            self.copy(False,self.down_in).wait_recv()
            self.copy(True,self.own).wait_send()
            self.own[...]=(self.own[...].astype(F32)+self.down_in[...].astype(F32)).astype(self.own.dtype)
        @pl.when(final)
        def _():
            self.copy(True,self.up_in).wait_recv()
            self.copy(False,self.own).wait_send()
            self.own[...]=(self.own[...].astype(F32)+self.up_in[...].astype(F32)).astype(self.own.dtype)
        @pl.when(jnp.logical_not(first|final))
        def _():
            self.copy(True,self.up_out).wait_send()
            self.copy(False,self.down_out).wait_send()
            self.own[...]=(self.own[...].astype(F32)+self.up_in[...].astype(F32)+self.down_in[...].astype(F32)).astype(self.own.dtype)

def meet_all(net,who):
    z,n=lax.axis_index("z"),lax.axis_size("z")
    barrier=pltpu.get_barrier_semaphore()
    for t in who:
        pl.semaphore_signal(barrier,inc=1,device_id=net.to[t],device_id_type=MESH)
    @pl.when(z>0)
    def _(): pl.semaphore_signal(barrier,inc=1,device_id={"z":z-1},device_id_type=MESH)
    @pl.when(z<n-1)
    def _(): pl.semaphore_signal(barrier,inc=1,device_id={"z":z+1},device_id_type=MESH)
    ends=(z==0)|(z==n-1)
    @pl.when(ends)
    def _(): pl.semaphore_wait(barrier,len(who)+1)
    @pl.when(jnp.logical_not(ends))
    def _(): pl.semaphore_wait(barrier,len(who)+2)

SEG=3
def last_kernel(gq_ref,heads_ref,normed_ref,hidden_ref,gmid_ref,gain_ref,block_ref,long_ref,wskip_ref,small_ref,
                gin_out,gsk_out,small_out,gqkv_out,gskip_out,
                big,part,rx,ry,dx,dy,gw,gwr,gsr,qz,fq,sdx,sdy,srx,sry,own,sz,fs,sm,sin,smz,send,recv,local):
    x,y,c,w,wx,wy,wd=place()
    tokens,d=block_ref.shape
    tc=tokens//4; kr=d//4; kh=kr//2; sr=d//2; sh=sr//2; sq=sh//2
    mul=pl.multiple_of
    net=Links(send,recv)
    load=pltpu.make_async_copy(normed_ref,big,local.at[0])
    load.start()
    meet_all(net,"XYDC")
    def tok(i): return pl.ds(i*tc,tc)
    def pr(s,i): return pl.ds(s*tokens+i*tc,tc)
    def partial(b,i):
        return nt(gq_ref[pl.ds(mul(b*tokens+i*tc,16),tc),:],heads_ref[...])
    for i,t,dst,k in ((0,"X",dx,0),(2,"Y",dy,2),(1,"X",dx,1),(3,"Y",dy,3)):
        part[pr(2,i),:]=partial(wd,i).astype(BF)
        net.start(k,t,part.at[pr(2,i)],dst.at[tok(i%2)])
    for i,t,b,dst,k in ((0,"X",wx,rx,4),(2,"Y",wy,ry,10),(1,"X",wx,rx,5),(3,"Y",wy,ry,11)):
        s=0 if t=="X" else 1
        part[pr(s,i),:]=partial(b,i).astype(BF)
        net.start(k,t,part.at[pr(s,i)],dst.at[tok(i)])
    @pl.loop(0,4)
    def _(i):
        r=pl.ds(mul(i*tc,16),tc)
        part[pl.ds(mul(3*tokens+i*tc,16),tc),:]=nt(gq_ref[pl.ds(mul(w*tokens+i*tc,16),tc),:],heads_ref[...]).astype(BF)
    load.wait()
    cc=d//3
    def weight_grad(k):
        cr=pl.ds(k*cc,cc)
        gw[cr,:]=tn(big[:,cr],gq_ref[...]).astype(BF)
    def relay(i,t,b,dst,k,src,k2,t2):
        s=0 if t=="X" else 1
        mine=partial(b,i)
        net.got(k2,t2,src.at[tok(i%2)])
        part[pr(s,i),:]=(mine+src[tok(i%2),:].astype(F32)).astype(BF)
        net.start(k,t,part.at[pr(s,i)],dst.at[tok(i)])
    weight_grad(0)
    relay(2,"X",wx,rx,6,dy,2,"Y")
    relay(0,"Y",wy,ry,8,dx,0,"X")
    weight_grad(1)
    weight_grad(2)
    def rows(b,core): return pl.ds(mul(b*kr+core*kh,16),kh)
    for b in range(4):
        net.start(12+b,"C",gw.at[rows(b,1-c)],gwr.at[pl.ds(b*kh,kh)])
    relay(3,"X",wx,rx,7,dy,3,"Y")
    relay(1,"Y",wy,ry,9,dx,1,"X")
    for b in range(4):
        r=pl.ds(b*kh,kh)
        net.got(12+b,"C",gwr.at[r])
        gwr[r,:]=(gwr[r,:].astype(F32)+gw[rows(b,c),:].astype(F32)).astype(BF)
    halves=[pl.ds(i*2*kh,2*kh) for i in range(2)]
    chains=[Chain(net,40+2*i,gwr.at[r],*[qz.at[j,r] for j in range(4)]) for i,r in enumerate(halves)]
    for chain in chains: chain.hop(0)
    gain=gain_ref[...]
    sm[...]=jnp.zeros_like(sm)
    for h in range(1,lax.axis_size("z")-2):
        for chain in chains: chain.hop(h)
    for i in (0,2,1,3):
        r=tok(i)
        net.got(4+i,"X",rx.at[r])
        net.got(8+i,"Y",ry.at[r])
        gf=part[pr(3,i),:].astype(F32)+rx[r,:].astype(F32)+ry[r,:].astype(F32)
        h=hidden_ref[r,:]
        cen=h-jnp.mean(h,axis=1,keepdims=True)
        inv=lax.rsqrt(jnp.mean(cen*cen,axis=1,keepdims=True)+1e-5)
        xhat=cen*inv
        sm[0:1,:]+=jnp.sum(gf*xhat,axis=0,keepdims=True)
        sm[1:2,:]+=jnp.sum(gf,axis=0,keepdims=True)
        e=gf*gain
        back=e-jnp.mean(e,axis=1,keepdims=True)-xhat*jnp.mean(e*xhat,axis=1,keepdims=True)
        big[pl.ds(2*d+i*tc,tc),:]=(gmid_ref[r,:]+back*inv).astype(BF)
    sm[2:4,:]=small_ref[0:2,:]
    for k in range(6):
        src=block_ref if k<3 else long_ref
        big[pl.ds(k*cc,cc),:]=tn(src[:,(k%3)*cc:(k%3+1)*cc],big[2*d:2*d+tokens,:]).astype(BF)
    def srows(b,core): return pl.ds(mul(b*sr+core*sh,16),sh)
    for b in range(4):
        net.start(16+b,"C",big.at[srows(b,1-c)],gsr.at[pl.ds(b*sh,sh)])
    net.start(20,"C",sm,sin.at[0])
    for copy in net.sent[:16]: copy.wait_send()
    net.sent=net.sent[16:]
    wload=pltpu.make_async_copy(wskip_ref,part.at[pl.ds(0,2*d)],local.at[1])
    wload.start()
    for chain in chains: chain.hop(lax.axis_size("z")-2)
    for b in range(4):
        r=pl.ds(b*sh,sh)
        net.got(16+b,"C",gsr.at[r])
        gsr[r,:]=(gsr[r,:].astype(F32)+big[srows(b,c),:].astype(F32)).astype(BF)
    def quarter(b,i): return pl.ds(mul(b*sh+i*sq,16),sq)
    top,low=pl.ds(0,sq),pl.ds(sq,sq)
    net.start(21,"X",gsr.at[quarter(wd,0)],sdx)
    net.start(22,"Y",gsr.at[quarter(wd,1)],sdy)
    net.start(23,"X",gsr.at[quarter(wx,0)],srx.at[top])
    net.start(24,"Y",gsr.at[quarter(wy,1)],sry.at[low])
    net.got(20,"C",sin.at[0])
    smz[6]=sm[...]+sin[0]
    net.start(27,"X",smz.at[6],sin.at[1])
    for chain in chains: chain.total()
    def qrows(b): return pl.ds(mul(b*kh,16),kh)
    for j,(t,b) in enumerate((("X",wx),("Y",wy),("D",wd))):
        net.start(29+j,t,gwr.at[qrows(b)],fq.at[w,c])
    fq[w,c]=gwr[qrows(w),:]
    wload.wait()
    @pl.loop(0,4)
    def _(i):
        r=pl.ds(mul(i*tc,16),tc)
        gh=big[pl.ds(mul(2*d+i*tc,16),tc),:]
        rx[r,:]=nt(gh,part[:d,:]).astype(BF)
        ry[r,:]=nt(gh,part[d:2*d,:]).astype(BF)
    outs=[]
    def put(k,src,dst):
        copy=pltpu.make_async_copy(src,dst,local.at[k]); copy.start(); outs.append(copy)
    put(2,rx,gin_out); put(3,ry,gsk_out)
    net.got(21,"X",sdx)
    gsr[quarter(wy,0),:]=(gsr[quarter(wy,0),:].astype(F32)+sdx[...].astype(F32)).astype(BF)
    net.start(25,"Y",gsr.at[quarter(wy,0)],sry.at[top])
    net.got(22,"Y",sdy)
    gsr[quarter(wx,1),:]=(gsr[quarter(wx,1),:].astype(F32)+sdy[...].astype(F32)).astype(BF)
    net.start(26,"X",gsr.at[quarter(wx,1)],srx.at[low])
    net.got(27,"X",sin.at[1])
    smz[0]=smz[6]+sin[1]
    net.start(28,"Y",smz.at[0],sin.at[2])
    for j,(t,b) in enumerate((("X",wx),("Y",wy),("D",wd))):
        net.got(29+j,t,fq.at[b,c])
    for b in range(4):
        net.start(32+b,"C",fq.at[b,c],fq.at[b,c])
    net.got(28,"Y",sin.at[2])
    smz[1]=smz[0]+sin[2]
    net.got(23,"X",srx.at[top]); net.got(25,"Y",sry.at[top])
    net.got(24,"Y",sry.at[low]); net.got(26,"X",srx.at[low])
    own[...]=(gsr[pl.ds(mul(w*sh,16),sh),:].astype(F32)+srx[...].astype(F32)+sry[...].astype(F32)).astype(BF)
    seg=sh//SEG
    chains=[Chain(net,44,smz.at[1],smz.at[2],smz.at[3],smz.at[4],smz.at[5])]
    for i in range(SEG):
        r=pl.ds(i*seg,seg)
        chains.append(Chain(net,46+2*i,own.at[r],*[sz.at[j,r] for j in range(4)]))
    for h in range(lax.axis_size("z")-1):
        for chain in chains: chain.hop(h)
    for chain in chains: chain.total()
    net.start(36,"C",own,fs)
    for b in range(4): net.got(32+b,"C",fq.at[b,1-c])
    put(4,fq,gqkv_out); put(5,smz.at[1],small_out); put(6,own,gskip_out.at[c])
    net.got(36,"C",fs)
    put(7,fs,gskip_out.at[1-c])
    for copy in outs: copy.wait()
    net.finish()

def last(gq,heads,normed,hidden,gmid,gain,block,long,wskip,small):
    tokens,d=block.shape; S=jax.ShapeDtypeStruct; hd3=gq.shape[1]
    V=pltpu.VMEM
    return pl.pallas_call(last_kernel,
        out_shape=(S((tokens,d),BF),S((tokens,d),BF),S((8,d),F32),S((4,2,d//8,hd3),BF),S((2,d//4,d),BF)),
        in_specs=[VM,VM,ANY]+[VM]*5+[ANY,VM],out_specs=(ANY,)*5,
        scratch_shapes=[V((4*tokens,d),BF),V((4*tokens,d),BF),V((tokens,d),BF),V((tokens,d),BF),V((tokens//2,d),BF),V((tokens//2,d),BF),
            V((d,hd3),BF),V((d//2,hd3),BF),V((d,d),BF),V((4,d//2,hd3),BF),V((4,2,d//8,hd3),BF),
            V((d//8,d),BF),V((d//8,d),BF),V((d//4,d),BF),V((d//4,d),BF),V((d//4,d),BF),V((4,d//4,d),BF),V((d//4,d),BF),
            V((8,d),F32),V((3,8,d),F32),V((7,8,d),F32),
            pltpu.SemaphoreType.DMA((52,)),pltpu.SemaphoreType.DMA((52,)),pltpu.SemaphoreType.DMA((8,))],
        compiler_params=pltpu.CompilerParams(vmem_limit_bytes=63*2**20,collective_id=1,has_side_effects=True),
        cost_estimate=pl.CostEstimate(flops=2*tokens*d*d*10,bytes_accessed=60*2**20,transcendentals=0))(
        gq,heads,normed,hidden,gmid,gain,block,long,wskip,small)

SPLIT=((0,640),(640,512))
def middle_kernel(hidden_ref,att_ref,g_ref,gain_ref,shift_ref,outw_ref,outx_ref,outy_ref,upw_ref,upx_ref,upy_ref,dnw_ref,
                  lay_out,gmid_ref,gh_out,gow_out,small_ref,gup_out,gdn_out,uland,dland,
                  att_in,att_s,outw_s,n2_s,xhat_s,rstd_s,lay_s,act_s,gu_s,upb,dnb,gub,gdb,land_u,land_d,
                  send,recv,csend,crecv,fetch_sem,flush_sem,local):
    x,y,c,w,wx,wy,wd=place()
    tokens,d=hidden_ref.shape
    cols=att_ref.shape[1]
    kr=d//4; kh=kr//2; dh=d//2; dq=dh//2
    tc=tokens//4; th=tokens//2
    mul=pl.multiple_of
    net=Links(send,recv)
    left=[]
    def start(k,t,src,dst,view):
        pltpu.make_async_remote_copy(src_ref=src,dst_ref=dst,send_sem=send.at[k],recv_sem=recv.at[k],
                                     device_id=net.to[t],device_id_type=MESH).start()
        left.append((k,t,view))
    def blk(b): return pl.ds(mul(b*d,128),d)
    def urow(b,core): return pl.ds(mul(b*kr+core*kh,16),kh)
    def drow(b,core,p): return pl.ds(mul(b*d+core*dh+p*dq,16),dq)
    def trow(b): return pl.ds(mul(b*tokens,16),tokens)
    uview=uland.at[pl.ds(0,kh),pl.ds(0,d)]
    dview=dland.at[pl.ds(0,dq)]
    net.meet("XYDC")
    for j,(t,b) in enumerate((("X",wx),("Y",wy),("D",wd))):
        start(j,t,att_ref.at[trow(b)],att_in.at[w],att_in.at[0])
    own_att=pltpu.make_async_copy(att_ref.at[trow(w)],att_in.at[w],local.at[0])
    own_att.start()
    cut=kh//32*16+16
    def orow(b,core,lo,n): return pl.ds(mul(b*kr+core*kh+lo,16),n)
    start(3,"Y",outx_ref.at[pl.ds(0,cut)],outw_s.at[orow(wx,c,0,cut)],outw_s.at[pl.ds(0,cut)])
    start(4,"X",outy_ref.at[pl.ds(cut,kh-cut)],outw_s.at[orow(wy,c,cut,kh-cut)],outw_s.at[pl.ds(0,kh-cut)])
    start(5,"C",outx_ref,outw_s.at[urow(wx,c)],outw_s.at[pl.ds(0,kh)])
    start(6,"C",outy_ref,outw_s.at[urow(wy,c)],outw_s.at[pl.ds(0,kh)])
    start(7,"Y",upx_ref.at[:,blk(wy)],uland.at[urow(wx,c),blk(wy)],uview)
    start(8,"X",upy_ref.at[:,blk(w)],uland.at[urow(wy,c),blk(w)],uview)
    order=(w,wx,wy,wd)
    def up_core(i):
        start(11+2*i,"C",upx_ref.at[:,blk(order[i])],uland.at[urow(wx,c),blk(order[i])],uview)
        start(12+2*i,"C",upy_ref.at[:,blk(order[i])],uland.at[urow(wy,c),blk(order[i])],uview)
    up_core(0)
    outw_s[pl.ds(mul(w*kr,16),kr),:]=outw_ref[...]
    outw_s[urow(wx,c),:]=outx_ref[...]
    outw_s[urow(wy,c),:]=outy_ref[...]

    diag_id=(7,8,10,9)
    def diag_from(i): return "Y" if i in (0,3) else "X"
    def up_relay(i):
        view=uland.at[urow(wd,c),blk(order[i])]
        net.got(diag_id[i],diag_from(i),view)
        start(19+i,"C",view,view,uview)
    def up_sources(i):
        b=order[i]
        net.got(11+2*i,"C",uland.at[urow(wx,1-c),blk(b)])
        net.got(12+2*i,"C",uland.at[urow(wy,1-c),blk(b)])
        net.got(19+i,"C",uland.at[urow(wd,1-c),blk(b)])
        return [(upw_ref.at[:,blk(b)],pl.ds(mul(w*kr,16),kr)),(upx_ref.at[:,blk(b)],urow(wx,c)),(upy_ref.at[:,blk(b)],urow(wy,c)),
                (uland.at[urow(wx,1-c),blk(b)],urow(wx,1-c)),(uland.at[urow(wy,1-c),blk(b)],urow(wy,1-c)),
                (uland.at[pl.ds(mul(wd*kr,16),kr),blk(b)],pl.ds(mul(wd*kr,16),kr))]
    def fetch(i):
        slot=i%2
        for j,(src,rows) in enumerate(up_sources(i)):
            pltpu.make_async_copy(src,upb.at[slot,rows],fetch_sem.at[slot,j]).start()
        src=dnw_ref if i==0 else dland.at[pl.ds(mul(order[i]*d,16),d)]
        pltpu.make_async_copy(src,dnb.at[slot],fetch_sem.at[slot,6]).start()
    def fetched(slot):
        for j,n in enumerate((kr,kh,kh,kh,kh,kr)):
            view=upb.at[slot,pl.ds(0,n)]
            pltpu.make_async_copy(view,view,fetch_sem.at[slot,j]).wait()
        pltpu.make_async_copy(dnb.at[slot],dnb.at[slot],fetch_sem.at[slot,6]).wait()
    def down_relay(k,t,b,p,onward):
        r=drow(b,c,p)
        net.got(k,t,dland.at[r])
        for k2,t2 in onward: start(k2,t2,dland.at[r],dland.at[r],dview)
    def down_core(k,b,p): net.got(k,"C",dland.at[drow(b,1-c,p)])

    for j,(t,b) in enumerate((("X",wx),("Y",wy),("D",wd))):
        net.got(j,t,att_in.at[b])
    start(9,"Y",upx_ref.at[:,blk(wx)],uland.at[urow(wx,c),blk(wx)],uview)
    start(10,"X",upy_ref.at[:,blk(wd)],uland.at[urow(wy,c),blk(wd)],uview)
    def dmine(p): return dnw_ref.at[pl.ds(mul(c*dh+p*dq,16),dq)]
    start(23,"X",dmine(0),dland.at[drow(w,c,0)],dview)
    start(25,"Y",dmine(1),dland.at[drow(w,c,1)],dview)
    start(24,"X",dmine(1),dland.at[drow(w,c,1)],dview)
    start(26,"Y",dmine(0),dland.at[drow(w,c,0)],dview)
    net.got(3,"Y",outw_s.at[orow(wd,c,0,cut)])
    net.got(4,"X",outw_s.at[orow(wd,c,cut,kh-cut)])
    start(35,"C",outw_s.at[urow(wd,c)],outw_s.at[urow(wd,c)],outw_s.at[pl.ds(0,kh)])
    up_relay(0)
    for i in (1,2,3): up_core(i)
    net.got(5,"C",outw_s.at[urow(wx,1-c)]); net.got(6,"C",outw_s.at[urow(wy,1-c)])
    net.got(35,"C",outw_s.at[urow(wd,1-c)])
    own_att.wait()
    fetch(0)
    gain=gain_ref[...]; shift=shift_ref[...]
    @pl.loop(0,4)
    def _(i):
        r=pl.ds(mul(i*tc,16),tc)
        joined=jnp.concatenate([att_in[p,r,:] for p in range(4)],axis=1)
        att_s[r,:]=joined
        mid=hidden_ref[r,:]+nn(joined,outw_s[...])
        lay_s[r,:]=mid
        cen=mid-jnp.mean(mid,axis=1,keepdims=True)
        inv=lax.rsqrt(jnp.mean(cen*cen,axis=1,keepdims=True)+1e-5)
        xhat=cen*inv
        xhat_s[r,:]=xhat
        rstd_s[r,:]=jnp.broadcast_to(inv,(tc,128))
        n2_s[r,:]=(xhat*gain+shift).astype(BF)
        gmid_ref[r,:]=jnp.zeros((tc,d),F32)

    def pieces(slot):
        out=[(gub,pl.ds(mul(p*kr+(1-c)*kh,16),kh),land_u.at[slot,pl.ds(p*kh,kh)]) for p in range(4)]
        return out+[(gdb,pl.ds(mul((1-c)*dh,16),dh),land_d.at[slot])]
    def exchange(slot,act):
        for j,(ref,r,dst) in enumerate(pieces(slot)):
            act(pltpu.make_async_remote_copy(src_ref=ref.at[r],dst_ref=dst,send_sem=csend.at[slot,j],recv_sem=crecv.at[slot,j],
                                             device_id=net.to["C"],device_id_type=MESH))
    def flush(b,act):
        for p in range(4):
            act(pltpu.make_async_copy(gub.at[pl.ds(mul(p*kr+c*kh,16),kh)],gup_out.at[pl.ds(p*kh,kh),blk(b)],flush_sem.at[p]))
        act(pltpu.make_async_copy(gdb.at[pl.ds(mul(c*dh,16),dh)],gdn_out.at[pl.ds(mul(b*dh,16),dh)],flush_sem.at[4]))
    go=lambda copy: copy.start()
    def finalize(i):
        slot=lax.rem(i,2)
        exchange(slot,lambda copy: copy.wait())
        for p in range(4):
            r=pl.ds(mul(p*kr+c*kh,16),kh)
            gub[r,:]=(gub[r,:].astype(F32)+land_u[slot,pl.ds(p*kh,kh),:].astype(F32)).astype(BF)
        for p in range(2):
            r=pl.ds(mul(c*dh+p*dq,16),dq)
            gdb[r,:]=(gdb[r,:].astype(F32)+land_d[slot,pl.ds(p*dq,dq),:].astype(F32)).astype(BF)
    def block_of(i):
        return 2*lax.rem(y+i//2,2)+lax.rem(x+lax.rem(i,2),2)

    @pl.loop(0,4)
    def _(i):
        slot=lax.rem(i,2)
        fetched(slot)
        @pl.loop(0,2)
        def _(t):
            r=pl.ds(mul(t*th,16),th)
            for lo,n in SPLIT:
                f=pl.ds(lo,n)
                u=nn(n2_s[r,:],upb[slot,:,f])
                a,dg=gelu_parts(u)
                act_s[r,f]=a.astype(BF)
                gu_s[r,f]=(nt(g_ref[r,:],dnb[slot,f,:])*dg).astype(BF)
        @pl.when(i>=1)
        def _():
            finalize(i-1)
            flush(block_of(i-1),go)
        @pl.when(i==0)
        def _():
            for j in (1,2,3): up_relay(j)
        @pl.loop(0,2)
        def _(t):
            r=pl.ds(mul(t*th,16),th)
            for lo,n in SPLIT:
                f=pl.ds(lo,n)
                lay_s[r,f]+=nn(act_s[r,:],dnb[slot,:,f])
                gmid_ref[r,f]+=nt(gu_s[r,:],upb[slot,f,:])
        @pl.when(i==0)
        def _():
            down_relay(23,"X",wx,0,((27,"Y"),(29,"C")))
            down_relay(25,"Y",wy,1,((28,"X"),(30,"C")))
            down_relay(24,"X",wx,1,((31,"C"),))
            down_core(29,wx,0); down_core(31,wx,1)
            fetch(1)
        @pl.when(i==1)
        def _():
            down_relay(26,"Y",wy,0,((32,"C"),))
            down_core(30,wy,1); down_core(32,wy,0)
            down_relay(27,"Y",wd,0,((33,"C"),))
            down_relay(28,"X",wd,1,((34,"C"),))
            fetch(2)
        @pl.when(i==2)
        def _():
            down_core(33,wd,0); down_core(34,wd,1)
            fetch(3)
        @pl.when(i>=1)
        def _(): flush(block_of(i-1),lambda copy: copy.wait())
        for lo,n in SPLIT:
            f=pl.ds(lo,n)
            gdb[f,:]=tn(act_s[:,f],g_ref[...]).astype(BF)
            gub[f,:]=tn(n2_s[:,f],gu_s[...]).astype(BF)
        exchange(slot,go)
    act_s[...]=lay_s[...].astype(BF)
    lay_copy=pltpu.make_async_copy(act_s,lay_out,local.at[1])
    lay_copy.start()
    small_ref[...]=jnp.zeros_like(small_ref)
    for i in range(4):
        r=pl.ds(i*tc,tc)
        gs=gmid_ref[r,:]; xhat=xhat_s[r,:]
        small_ref[0:1,:]+=jnp.sum(gs*xhat,axis=0,keepdims=True)
        small_ref[1:2,:]+=jnp.sum(gs,axis=0,keepdims=True)
        e=gs*gain
        back=e-jnp.mean(e,axis=1,keepdims=True)-xhat*jnp.mean(e*xhat,axis=1,keepdims=True)
        gm=g_ref[r,:].astype(F32)+back*rstd_s[r,0:1]
        gmid_ref[r,:]=gm
        low=gm.astype(BF)
        n2_s[r,:]=low
        ga=nt(low,outw_s[...]).astype(BF)
        for p in range(4): att_in[p,r,:]=ga[:,p*cols:(p+1)*cols]
        for j,(t,b) in enumerate((("X",wx),("Y",wy),("D",wd))):
            start(36+3*i+j,t,att_in.at[b,r],gh_out.at[w,r],gh_out.at[0,pl.ds(0,tc)])
    own_grad=pltpu.make_async_copy(att_in.at[w],gh_out.at[w],local.at[2])
    own_grad.start()
    finalize(3)
    flush(wd,go)
    flush(wd,lambda copy: copy.wait())
    for lo,n in SPLIT:
        f=pl.ds(lo,n)
        gub[f,:]=tn(att_s[:,f],n2_s[...]).astype(BF)
    for p in range(4):
        start(48+p,"C",gub.at[pl.ds(mul(p*kr+(1-c)*kh,16),kh)],land_u.at[0,pl.ds(p*kh,kh)],land_u.at[0,pl.ds(0,kh)])
    for p in range(4):
        net.got(48+p,"C",land_u.at[0,pl.ds(p*kh,kh)])
        r=pl.ds(mul(p*kr+c*kh,16),kh)
        land_u[1,pl.ds(p*kh,kh),:]=(gub[r,:].astype(F32)+land_u[0,pl.ds(p*kh,kh),:].astype(F32)).astype(BF)
    out_copy=pltpu.make_async_copy(land_u.at[1],gow_out,local.at[3])
    out_copy.start()
    for i in range(4):
        for j,(t,b) in enumerate((("X",wx),("Y",wy),("D",wd))):
            net.got(36+3*i+j,t,gh_out.at[b,pl.ds(i*tc,tc)])
    for copy in (lay_copy,own_grad,out_copy): copy.wait()
    for k,t,view in left:
        pltpu.make_async_remote_copy(src_ref=view,dst_ref=view,send_sem=send.at[k],recv_sem=recv.at[k],
                                     device_id=net.to[t],device_id_type=MESH).wait_send()

def middle(hidden,att,g,gain,shift,outw,outx,outy,upw,upx,upy,dnw):
    tokens,d=hidden.shape; cols=att.shape[1]; ff=upw.shape[1]
    S=jax.ShapeDtypeStruct; V=pltpu.VMEM; D=pltpu.SemaphoreType.DMA
    return pl.pallas_call(middle_kernel,
        out_shape=(S((tokens,d),BF),S((tokens,d),F32),S((4,tokens,cols),BF),S((d//2,d),BF),S((8,d),F32),S((d//2,ff),BF),S((ff//2,d),BF),
                   S((d,ff),BF),S((ff,d),BF)),
        in_specs=[VM,ANY]+[VM]*6+[ANY]*4,out_specs=(ANY,VM,ANY,ANY,VM)+(ANY,)*4,
        scratch_shapes=[V((4,tokens,cols),BF),V((tokens,d),BF),V((d,d),BF),V((tokens,d),BF),V((tokens,d),F32),V((tokens,128),F32),
            V((tokens,d),F32),V((tokens,d),BF),V((tokens,d),BF),V((2,d,d),BF),V((2,d,d),BF),V((d,d),BF),V((d,d),BF),
            V((2,d//2,d),BF),V((2,d//2,d),BF),D((52,)),D((52,)),D((2,5)),D((2,5)),D((2,7)),D((5,)),D((4,))],
        compiler_params=pltpu.CompilerParams(vmem_limit_bytes=63*2**20,collective_id=2,has_side_effects=True),
        cost_estimate=pl.CostEstimate(flops=2*tokens*d*(ff*6+d*3),bytes_accessed=60*2**20,transcendentals=tokens*ff*2))(
        hidden,att,g,gain,shift,outw,outx,outy,upw,upx,upy,dnw)

def assemble_kernel(lay_ref,gin_ref,gsk_ref,skip_ref,gq_ref,um_ref,uo_ref,dm_ref,do_ref,om_ref,oo_ref,
                    lay_out,gin_out,gsk_out,skip_out,qkv_out,up_out,down_out,out_out,
                    s0,s1,s2,s3,s4,s5,s6,s7,local):
    first=lax.axis_index("core")==0
    copies=[]
    def put(src,dst):
        copy=pltpu.make_async_copy(src,dst,local.at[len(copies)]); copy.start(); copies.append(copy)
    def chunks(n,body,size=144):
        @pl.loop(0,n//size)
        def _(i): body(pl.ds(pl.multiple_of(i*size,16),size))
    def wide(dst,src):
        def body(r): dst[r,:]=src[r,:].astype(F32)
        chunks(dst.shape[0],body,208 if dst.shape[0]%208==0 else 144)
    wide(s7,lay_ref); put(s7,lay_out)
    wide(s0,gin_ref); put(s0,gin_out)
    wide(s1,gsk_ref); put(s1,gsk_out)
    def pair(dst,mine,other,size=144):
        h=mine.shape[0]
        def body(r):
            m,o=mine[r,:].astype(F32),other[r,:].astype(F32)
            dst[0,r,:]=jnp.where(first,m,o)
            dst[1,r,:]=jnp.where(first,o,m)
        chunks(h,body,size)
    pair(s5,dm_ref,do_ref); put(s5,down_out)
    pair(s6,om_ref,oo_ref); put(s6,out_out)
    pair(s4,um_ref,uo_ref,48); put(s4,up_out)
    def skip(r): s2[r,:]=skip_ref[r,:].astype(F32)
    chunks(s2.shape[0],skip); put(s2,skip_out)
    hd=gq_ref.shape[3]//3; kh=gq_ref.shape[2]
    for core in range(2):
        for i in range(kh//48):
            r=pl.ds(i*48,48)
            s3[pl.ds(core*kh+i*48,48),:]=jnp.concatenate([gq_ref[p,core,r,s*hd:(s+1)*hd].astype(F32) for s in range(3) for p in range(4)],axis=1)
    put(s3,qkv_out)
    for copy in copies: copy.wait()

def assemble(lay,gin,gsk,skip,gq,um,uo,dm,do,om,oo):
    S=lambda *s: jax.ShapeDtypeStruct(s,F32)
    tokens,d=gin.shape
    shapes=(S(tokens,d),S(tokens,d),S(*skip.shape),S(d//4,3*d),S(2,*um.shape),S(2,*dm.shape),S(2,*om.shape))
    return pl.pallas_call(assemble_kernel,out_shape=(shapes[0],)+shapes,in_specs=[VM]*11,out_specs=(ANY,)*8,
        scratch_shapes=[pltpu.VMEM(s.shape,F32) for s in shapes+shapes[:1]]+[pltpu.SemaphoreType.DMA((8,))],
        compiler_params=pltpu.CompilerParams(vmem_limit_bytes=60*2**20),
        cost_estimate=pl.CostEstimate(flops=0,bytes_accessed=40*2**20,transcendentals=0))(
        lay,gin,gsk,skip,gq,um,uo,dm,do,om,oo)

from jax.sharding import Mesh, PartitionSpec as P
WIDE=("y","x"); ROWS=("z","core")
SWAP=[(0,1),(1,0)]

def swap_cores(values):
    return lax.ppermute(values,"core",SWAP)

def pick(values, index, axis):
    return lax.dynamic_index_in_dim(values,index,axis,keepdims=False)

def place_halves(mine, other, core, axis):
    first=jnp.where(core==0,mine,other); second=jnp.where(core==0,other,mine)
    return jnp.stack([first,second],axis=axis)

def dot(a,b): return jnp.dot(a,b,preferred_element_type=F32)

def norm(values):
    cen=values-jnp.mean(values,axis=1,keepdims=True)
    inv=lax.rsqrt(jnp.mean(cen*cen,axis=1,keepdims=True)+1e-5)
    return cen*inv,inv

def on_device(nw, block_input, long_skip, segment_ids, item_lengths, skip_weight, first_gain, first_shift, qkv_weight,
              out_weight, second_gain, second_shift, up_weight, down_weight, output_grad):
    core=lax.axis_index("core")
    _,tokens,d=block_input.shape
    heads=qkv_weight.shape[1]//(3*HEAD*nw); hd=heads*HEAD
    ff=up_weight.shape[1]; fb=ff//(2*nw)
    gather=lambda v: lax.all_gather(v,WIDE,axis=0,tiled=True)
    near=nw==4
    vecs=jnp.stack([first_gain,first_shift,second_gain,second_shift]+[first_gain]*4).astype(F32)
    if near:
        hidden,normed_all,qkv,w_heads,w_skip,vecs=first(block_input[0],long_skip[0],skip_weight,qkv_weight,vecs)
        vec=vecs.transpose(1,0,2).reshape(8,d)
        gain1,shift1,gain2,shift2=[vec[i:i+1] for i in range(4)]
        half=lambda v: lax.dynamic_slice_in_dim(v,core*(v.shape[0]//2),v.shape[0]//2)
        qkv,up_half,out_half=lax.optimization_barrier((qkv,half(up_weight),half(out_weight)))
        up_x,out_x=lax.ppermute((up_half,out_half),"x",SWAP)
        up_y,out_y=lax.ppermute((up_half,out_half),"y",SWAP)
    else:
        vec=gather(vecs.astype(BF).T).T.astype(F32)
        gain1,shift1,gain2,shift2=[vec[i:i+1] for i in range(4)]
        w_skip=gather(skip_weight)
        joined=jnp.concatenate([block_input[0],long_skip[0]],axis=1)
        w_heads=qkv_weight.reshape(d//nw,3,nw,hd).transpose(2,0,1,3)
        w_heads=lax.all_to_all(w_heads,WIDE,0,0).reshape(d,3*hd)
        hidden=dot(joined,w_skip)
        xhat1,inv1=norm(hidden)
        normed_all=gather((xhat1*gain1+shift1).astype(BF))
        qkv=dot(normed_all,w_heads).astype(BF)
    att,lse=attend(item_lengths,qkv,heads)
    if near:
        lay,gmid,gatt,gow,small,gup,gdn,_,_=middle(hidden,att,output_grad[0],gain2,shift2,out_weight,out_x,out_y,
            up_weight,up_x,up_y,down_weight)
    else:
        w_out=gather(out_weight)
        up_mine=gather(pick(up_weight.reshape(d//nw,nw,2,fb),core,2).reshape(d//nw,nw*fb))
        down_mine=gather(pick(down_weight.reshape(2,fb,d),core,0))
        up_other,down_other=swap_cores(up_mine),swap_cores(down_mine)
        att=lax.all_to_all(att.reshape(nw,tokens,hd),WIDE,0,0)
        lay,gmid,gatt,gow,small,gupo,guph,gdno,gdnh=mlp(hidden,att,w_out,gain2,shift2,output_grad[0],up_mine,up_other,down_mine,down_other)
        gatt=lax.all_to_all(gatt,WIDE,0,0)
    grad_heads=gatt.reshape(nw*tokens,hd)

    def scatter(mine,other):
        both=(mine.astype(F32)+swap_cores(other).astype(F32)).astype(BF)
        return lax.psum_scatter(both,WIDE,scatter_dimension=0,tiled=True)
    def both_cores(mine,axis):
        return place_halves(mine,swap_cores(mine),core,axis).astype(F32)
    def by_rows(grad):
        cut=grad.reshape(nw,2,-1,grad.shape[1])
        return scatter(pick(cut,core,1).reshape(-1,grad.shape[1]),pick(cut,1-core,1).reshape(-1,grad.shape[1]))
    if near:
        early=tuple(lax.psum_scatter(v,WIDE,scatter_dimension=0,tiled=True) for v in (gup,gdn,gow))
    else:
        early=scatter(gupo,guph),scatter(gdno,gdnh),by_rows(gow)
    grad_qkv=attend_back(item_lengths,qkv,grad_heads,lse,heads)
    grad_qkv,early=lax.optimization_barrier((grad_qkv,early))
    early=lax.psum(early,"z")
    if near:
        gin,gsk,smalls,gqkv,gskip=last(grad_qkv,w_heads,normed_all,hidden,gmid,gain1,block_input[0],long_skip[0],w_skip,small)
        gskip,early=lax.optimization_barrier((gskip,early))
        others=swap_cores(early)
        lay,gin,gsk,skip_share,qkv_share,up_share,down_share,out_share=assemble(lay,gin,gsk,gskip.reshape(-1,d),gqkv,
            early[0],others[0],early[1],others[1],early[2],others[2])
        up_share,down_share,out_share=up_share.reshape(-1,ff),down_share.reshape(-1,d),out_share.reshape(-1,d)
        smalls=lax.dynamic_slice_in_dim(smalls[:4],(2*lax.axis_index("y")+lax.axis_index("x"))*(d//nw),d//nw,axis=1).T
    else:
        part_first=nt(grad_qkv,w_heads).astype(BF)
        grad_first=lax.psum_scatter(part_first,WIDE,scatter_dimension=0,tiled=True).astype(F32)
        gqkv=tn(normed_all,grad_qkv).astype(BF).reshape(nw,2,d//nw//2,3*hd)
        gqkv=(pick(gqkv,core,1).astype(F32)+swap_cores(pick(gqkv,1-core,1)).astype(F32)).astype(BF)
        e1=grad_first*gain1
        across=inv1*(e1-jnp.mean(e1,axis=1,keepdims=True)-xhat1*jnp.mean(e1*xhat1,axis=1,keepdims=True))
        grad_hidden=(gmid+across).astype(BF)
        gskip=by_rows(tn(joined,grad_hidden).astype(BF))
        grad_joined=nt(grad_hidden,w_skip)
        gin,gsk=grad_joined[:,:d],grad_joined[:,d:]
        small1=jnp.stack([jnp.sum(grad_first*xhat1,axis=0),jnp.sum(grad_first,axis=0)])
        gqkv,gskip,early=lax.optimization_barrier((gqkv,gskip,early))
        gqkv,gskip=lax.psum((gqkv,gskip),"z")
        up_share=both_cores(early[0].reshape(d//nw,nw,fb),2).reshape(d//nw,ff)
        down_share=both_cores(early[1],0).reshape(ff//nw,d)
        out_share=both_cores(early[2],0).reshape(d//nw,d)
        skip_share=both_cores(gskip,0).reshape(2*d//nw,d)
        gqkv=lax.all_to_all(gqkv,WIDE,0,0).reshape(nw,-1,3,hd).transpose(1,2,0,3)
        qkv_share=both_cores(gqkv,0).reshape(d//nw,-1)
        smalls=jnp.stack([small1[0],small1[1],small[0],small[1]],axis=1)
        smalls=lax.psum(lax.psum_scatter(smalls.astype(BF),WIDE,scatter_dimension=0,tiled=True),ROWS).astype(F32)
    return (lay[None],gin[None],gsk[None],skip_share,smalls[:,0],smalls[:,1],qkv_share,out_share,
            smalls[:,2],smalls[:,3],up_share,down_share)

def solution(mesh):
    rows,wide=mesh.devices.shape
    side=2 if wide==4 else int(wide**0.5)
    grid=Mesh(mesh.devices.reshape(rows//2,2,wide//side,side),("z","core","y","x"))
    tok=P(ROWS,WIDE,None); row=P(ROWS,None); mat=P(WIDE,None); vec=P(WIDE)
    return jax.shard_map(functools.partial(on_device,wide),mesh=grid,
        in_specs=(tok,tok,row,row,mat,vec,vec,mat,mat,vec,vec,mat,mat,tok),
        out_specs=(tok,tok,tok,mat,vec,vec,mat,mat,vec,vec,mat,mat),check_vma=False)
```

```python
import functools
import jax, jax.numpy as jnp
from jax import lax
from jax.experimental import pallas as pl
from jax.experimental.pallas import tpu as pltpu
HEAD=72; SHORT=258; LONG=1026; NITEM=12
LOG2E=1.4426950408889634
SCALE=HEAD**-0.5
QT=384

def kwin(n): return (n + 29 + 31)//32*32
def qwin(n): return (n + 15 + QT-1)//QT*QT

def nt(a,b): return lax.dot_general(a,b,(((1,),(1,)),((),())),preferred_element_type=jnp.float32)
def nn(a,b): return lax.dot_general(a,b,(((1,),(0,)),((),())),preferred_element_type=jnp.float32)
def tn(a,b): return lax.dot_general(a,b,(((0,),(0,)),((),())),preferred_element_type=jnp.float32)

def windows(start, size, row_len):
    k0 = pl.multiple_of(jnp.minimum(start//16*16, row_len-kwin(size)),16)
    q0 = pl.multiple_of(jnp.minimum(start//16*16, row_len-qwin(size)),16)
    return k0,q0

def split_heads(src_ref, dst_ref, count, chunk=416):
    rows=src_ref.shape[0]
    @pl.loop(0, rows//chunk)
    def _(i):
        r=pl.ds(pl.multiple_of(i*chunk,16),chunk)
        block=src_ref[r,:]
        for j in range(count):
            dst_ref[j,r,:]=block[:,j*HEAD:(j+1)*HEAD]

def join_heads(src_ref, dst_ref, count, chunk=416):
    rows=dst_ref.shape[0]
    @pl.loop(0, rows//chunk)
    def _(i):
        r=pl.ds(pl.multiple_of(i*chunk,16),chunk)
        dst_ref[r,:]=jnp.concatenate([src_ref[j,r,:] for j in range(count)],axis=1)

def zero(ref, chunk=416):
    rows=ref.shape[1]
    @pl.loop(0, rows//chunk)
    def _(i):
        r=pl.ds(pl.multiple_of(i*chunk,16),chunk)
        for j in range(ref.shape[0]):
            ref[j,r,:]=jnp.zeros((chunk,ref.shape[2]),ref.dtype)

def for_items(len_ref, one):
    def step(i, start):
        size=len_ref[0,i]
        @pl.when(size==LONG)
        def _(): one(i,start,LONG)
        @pl.when(size==SHORT)
        def _(): one(i,start,SHORT)
        return start+size
    lax.fori_loop(0,len_ref.shape[1],step,jnp.int32(0))

def mask_edges(values, start, k0, size, fill):
    n=values.shape[0]; body=size//32*32
    off=start-k0
    top=lax.broadcasted_iota(jnp.int32,(32,values.shape[1]),0)
    low=jnp.where(top>=off,values[:32],fill)
    high=jnp.where(top+body<off+size,values[body:],fill)
    return jnp.concatenate([low,values[32:body],high],axis=0)

def attend_kernel(heads, len_ref, qkv_ref, out_ref, lse_ref, split_ref, acc_ref):
    row_len=qkv_ref.shape[0]
    split_heads(qkv_ref, split_ref, 3*heads)
    zero(acc_ref)
    lse_ref[...]=jnp.zeros_like(lse_ref)
    def one(item,start,size):
        k0,q0=windows(start,size,row_len)
        kr=pl.ds(k0,kwin(size))
        @pl.loop(0,qwin(size)//QT)
        def _(t):
            qr=pl.ds(pl.multiple_of(q0+t*QT,16),QT)
            col=q0+t*QT+lax.broadcasted_iota(jnp.int32,(1,QT),1)
            live=(col>=start)&(col<start+size)
            for h in range(heads):
                s=nt(split_ref[heads+h,kr,:],split_ref[h,qr,:])
                s=mask_edges(s,start,k0,size,-1e30)
                m=jnp.max(s,axis=0,keepdims=True)
                p=jnp.exp2((s-m)*(SCALE*LOG2E))
                l=jnp.sum(p,axis=0,keepdims=True)
                o=tn(split_ref[2*heads+h,kr,:],p.astype(jnp.bfloat16))
                o=jnp.where(live,o/l,0.0)
                acc_ref[h,qr,:]+=o.T.astype(jnp.bfloat16)
                lse_ref[item,pl.ds(t*heads+h,1),:]=m*(SCALE*LOG2E)+jnp.log2(l)
    for_items(len_ref,one)
    join_heads(acc_ref,out_ref,heads)

def attend_back_kernel(heads, len_ref, qkv_ref, grad_ref, lse_ref, out_ref, split_ref, gsplit_ref, acc_ref, dk_ref, dv_ref):
    row_len=qkv_ref.shape[0]
    split_heads(qkv_ref, split_ref, 3*heads)
    split_heads(grad_ref, gsplit_ref, heads)
    zero(acc_ref)
    def one(item,start,size):
        k0,q0=windows(start,size,row_len)
        kw=kwin(size)
        kr=pl.ds(k0,kw)
        for h in range(heads):
            dk_ref[h,:kw,:]=jnp.zeros((kw,HEAD),jnp.float32)
            dv_ref[h,:kw,:]=jnp.zeros((kw,HEAD),jnp.float32)
        @pl.loop(0,qwin(size)//QT)
        def _(t):
            qr=pl.ds(pl.multiple_of(q0+t*QT,16),QT)
            col=q0+t*QT+lax.broadcasted_iota(jnp.int32,(1,QT),1)
            live=(col>=start)&(col<start+size)
            for h in range(heads):
                k=split_ref[heads+h,kr,:]; q=split_ref[h,qr,:]; g=gsplit_ref[h,qr,:]
                lse=jnp.where(live,lse_ref[item,pl.ds(t*heads+h,1),:],1e30)
                s=nt(k,q)
                p=jnp.exp2(s*(SCALE*LOG2E)-lse)
                p=mask_edges(p,start,k0,size,0.0)
                dv_ref[h,:kw,:]+=nn(p.astype(jnp.bfloat16),g)
                dp=nt(split_ref[2*heads+h,kr,:],g)
                delta=jnp.sum(p*dp,axis=0,keepdims=True)
                ds=(p*(dp-delta)).astype(jnp.bfloat16)
                dk_ref[h,:kw,:]+=nn(ds,q)
                dq=tn(k,ds)*SCALE
                acc_ref[h,qr,:]+=dq.T.astype(jnp.bfloat16)
        for h in range(heads):
            acc_ref[heads+h,kr,:]+=(dk_ref[h,:kw,:]*SCALE).astype(jnp.bfloat16)
            acc_ref[2*heads+h,kr,:]+=dv_ref[h,:kw,:].astype(jnp.bfloat16)
    for_items(len_ref,one)
    join_heads(acc_ref,out_ref,3*heads)

VM=pl.BlockSpec(memory_space=pltpu.VMEM); SM=pl.BlockSpec(memory_space=pltpu.SMEM)
def attend(lens,qkv,heads):
    n=qkv.shape[0]
    nt_=heads*(qwin(LONG)//QT)
    return pl.pallas_call(functools.partial(attend_kernel,heads),
      out_shape=(jax.ShapeDtypeStruct((n,heads*HEAD),jnp.bfloat16),jax.ShapeDtypeStruct((NITEM,nt_,QT),jnp.float32)),
      in_specs=[SM,VM],out_specs=(VM,VM),
      scratch_shapes=[pltpu.VMEM((3*heads,n,HEAD),jnp.bfloat16),pltpu.VMEM((heads,n,HEAD),jnp.bfloat16)],
      compiler_params=pltpu.CompilerParams(vmem_limit_bytes=56*2**20),
      cost_estimate=pl.CostEstimate(flops=heads*n*n*HEAD*4,bytes_accessed=12*2**20,transcendentals=heads*n*n//3))(lens,qkv)
def attend_back(lens,qkv,grad,lse,heads):
    n=qkv.shape[0]
    return pl.pallas_call(functools.partial(attend_back_kernel,heads),
      out_shape=jax.ShapeDtypeStruct((n,3*heads*HEAD),jnp.bfloat16),
      in_specs=[SM,VM,VM,VM],out_specs=VM,
      scratch_shapes=[pltpu.VMEM((3*heads,n,HEAD),jnp.bfloat16),pltpu.VMEM((heads,n,HEAD),jnp.bfloat16),pltpu.VMEM((3*heads,n,HEAD),jnp.bfloat16),
        pltpu.VMEM((heads,kwin(LONG),HEAD),jnp.float32),pltpu.VMEM((heads,kwin(LONG),HEAD),jnp.float32)],
      compiler_params=pltpu.CompilerParams(vmem_limit_bytes=60*2**20),
      cost_estimate=pl.CostEstimate(flops=heads*n*n*HEAD*10,bytes_accessed=20*2**20,transcendentals=heads*n*n//3))(lens,qkv,grad,lse)


F32=jnp.float32; BF=jnp.bfloat16
ANY=pl.BlockSpec(memory_space=pl.ANY)

def gelu_parts(u):
    z=jnp.exp2(u*u*(-0.5*1.4426950408889634))
    t=1.0/(1.0+(0.3275911*0.7071067811865476)*jnp.abs(u))
    poly=((((1.061405429*t-1.453152027)*t+1.421413741)*t-0.284496736)*t+0.254829592)*t
    tail=0.5*poly*z
    cdf=jnp.where(u>=0,1.0-tail,tail)
    return u*cdf, cdf+u*(z*0.3989422804014327)

def mlp_kernel(tile, hidden_ref, att_ref, outw_ref, gain_ref, shift_ref, g_ref, upo_ref, uph_ref, dno_ref, dnh_ref,
               lay_ref, gmid_ref, gatt_ref, gow_ref, small_ref, gupo_ref, guph_ref, gdno_ref, gdnh_ref,
               att_s, n2_s, xhat_s, rstd_s, act_s, gu_s, upb, dnb, gub, gdb, in_sem, out_sem):
    parts,tokens,cols=att_ref.shape
    d=hidden_ref.shape[1]
    tc=tokens//2 if tokens>416 else tokens
    nch=tokens//tc
    half=upo_ref.shape[1]; steps=half//tile
    cc=d//3; fc=256

    def fetch(j,act):
        slot=lax.rem(j,2)
        for first,(us,ds) in ((True,(uph_ref,dnh_ref)),(False,(upo_ref,dno_ref))):
            cond=(j<steps) if first else (j>=steps)
            @pl.when(cond)
            def _():
                k=j if first else j-steps
                off=pl.multiple_of(k*tile,tile)
                act(pltpu.make_async_copy(us.at[:,pl.ds(off,tile)],upb.at[slot],in_sem.at[slot,0]))
                act(pltpu.make_async_copy(ds.at[pl.ds(off,tile),:],dnb.at[slot],in_sem.at[slot,1]))
    def flush(j,act):
        slot=lax.rem(j,2)
        for first,(us,ds) in ((True,(guph_ref,gdnh_ref)),(False,(gupo_ref,gdno_ref))):
            cond=(j<steps) if first else (j>=steps)
            @pl.when(cond)
            def _():
                k=j if first else j-steps
                off=pl.multiple_of(k*tile,tile)
                act(pltpu.make_async_copy(gub.at[slot],us.at[:,pl.ds(off,tile)],out_sem.at[slot,0]))
                act(pltpu.make_async_copy(gdb.at[slot],ds.at[pl.ds(off,tile),:],out_sem.at[slot,1]))
    start=lambda c: c.start()
    wait=lambda c: c.wait()
    fetch(jnp.int32(0),start)
    gain=gain_ref[...]; shift=shift_ref[...]
    sub=tc//2
    @pl.loop(0,2*nch)
    def _(i):
        r=pl.ds(pl.multiple_of(i*sub,16),sub)
        joined=jnp.concatenate([att_ref[p,r,:] for p in range(parts)],axis=1)
        att_s[r,:]=joined
        mid=hidden_ref[r,:]+nn(joined,outw_ref[...])
        lay_ref[r,:]=mid
        cen=mid-jnp.mean(mid,axis=1,keepdims=True)
        inv=lax.rsqrt(jnp.mean(cen*cen,axis=1,keepdims=True)+1e-5)
        xhat=cen*inv
        xhat_s[r,:]=xhat
        rstd_s[r,:]=jnp.broadcast_to(inv,(sub,128))
        n2_s[r,:]=(xhat*gain+shift).astype(BF)
        gmid_ref[r,:]=jnp.zeros((sub,d),F32)
    @pl.loop(0,2*steps)
    def _(j):
        slot=lax.rem(j,2)
        @pl.when(j+1<2*steps)
        def _(): fetch(j+1,start)
        fetch(j,wait)
        @pl.when(j>=2)
        def _(): flush(j-2,wait)
        @pl.loop(0,nch)
        def _(i):
            r=pl.ds(pl.multiple_of(i*tc,16),tc)
            for k in range(tile//fc):
                f=pl.ds(k*fc,fc)
                u=nn(n2_s[r,:],upb[slot,:,f])
                a,dg=gelu_parts(u)
                act_s[r,f]=a.astype(BF)
                ga=nt(g_ref[r,:],dnb[slot,f,:])
                gu_s[r,f]=(ga*dg).astype(BF)
        @pl.loop(0,nch)
        def _(i):
            r=pl.ds(pl.multiple_of(i*tc,16),tc)
            for k in range(3):
                cr=pl.ds(k*cc,cc)
                lay_ref[r,cr]+=nn(act_s[r,:],dnb[slot,:,cr])
                gmid_ref[r,cr]+=nt(gu_s[r,:],upb[slot,cr,:])
        for k in range(tile//fc):
            f=pl.ds(k*fc,fc)
            gdb[slot,f,:]=tn(act_s[:,f],g_ref[...]).astype(BF)
        for k in range(3):
            cr=pl.ds(k*cc,cc)
            gub[slot,cr,:]=tn(n2_s[:,cr],gu_s[...]).astype(BF)
        flush(j,start)
    small_ref[...]=jnp.zeros_like(small_ref)
    @pl.loop(0,2*nch)
    def _(i):
        r=pl.ds(pl.multiple_of(i*sub,16),sub)
        gs=gmid_ref[r,:]; xhat=xhat_s[r,:]
        small_ref[0:1,:]+=jnp.sum(gs*xhat,axis=0,keepdims=True)
        small_ref[1:2,:]+=jnp.sum(gs,axis=0,keepdims=True)
        e=gs*gain
        back=e-jnp.mean(e,axis=1,keepdims=True)-xhat*jnp.mean(e*xhat,axis=1,keepdims=True)
        gm=g_ref[r,:].astype(F32)+back*rstd_s[r,0:1]
        gmid_ref[r,:]=gm
        low=gm.astype(BF)
        n2_s[r,:]=low
        ga=nt(low,outw_ref[...]).astype(BF)
        for p in range(parts):
            gatt_ref[p,r,:]=ga[:,p*cols:(p+1)*cols]
    for k in range(3):
        cr=pl.ds(k*cc,cc)
        gow_ref[cr,:]=tn(att_s[:,cr],n2_s[...]).astype(BF)
    flush(jnp.int32(2*steps-2),wait)
    flush(jnp.int32(2*steps-1),wait)

def mlp(hidden,att,outw,gain,shift,g,upo,uph,dno,dnh):
    tokens,d=hidden.shape; half=upo.shape[1]; tile=half//3
    S=jax.ShapeDtypeStruct
    flops=2*tokens*d*(half*2*6+d*3)
    return pl.pallas_call(functools.partial(mlp_kernel,tile),
        out_shape=(S((tokens,d),F32),S((tokens,d),F32),S(att.shape,BF),S((d,d),BF),S((8,d),F32),
                   S(upo.shape,BF),S(upo.shape,BF),S(dno.shape,BF),S(dno.shape,BF)),
        in_specs=[VM]*6+[ANY]*4,
        out_specs=(VM,)*5+(ANY,)*4,
        scratch_shapes=[pltpu.VMEM((tokens,d),BF),pltpu.VMEM((tokens,d),BF),pltpu.VMEM((tokens,d),F32),pltpu.VMEM((tokens,128),F32),
            pltpu.VMEM((tokens,tile),BF),pltpu.VMEM((tokens,tile),BF),
            pltpu.VMEM((2,d,tile),BF),pltpu.VMEM((2,tile,d),BF),pltpu.VMEM((2,d,tile),BF),pltpu.VMEM((2,tile,d),BF),
            pltpu.SemaphoreType.DMA((2,2)),pltpu.SemaphoreType.DMA((2,2))],
        compiler_params=pltpu.CompilerParams(vmem_limit_bytes=62*2**20),
        cost_estimate=pl.CostEstimate(flops=flops,bytes_accessed=60*2**20,transcendentals=tokens*half*2))(
        hidden,att,outw,gain,shift,g,upo,uph,dno,dnh)


MESH=pl.DeviceIdType.MESH

def place():
    x,y,c=lax.axis_index("x"),lax.axis_index("y"),lax.axis_index("core")
    return x,y,c,2*y+x,2*y+1-x,2-2*y+x,3-2*y-x

class Links:
    def __init__(self,send,recv):
        self.send,self.recv,self.sent=send,recv,[]
        x,y,c=lax.axis_index("x"),lax.axis_index("y"),lax.axis_index("core")
        self.to={"X":{"x":1-x},"Y":{"y":1-y},"D":{"x":1-x,"y":1-y},"C":{"core":1-c}}
    def meet(self,who):
        barrier=pltpu.get_barrier_semaphore()
        for t in who:
            pl.semaphore_signal(barrier,inc=1,device_id=self.to[t],device_id_type=MESH)
        pl.semaphore_wait(barrier,len(who))
    def start(self,k,t,src,dst):
        copy=pltpu.make_async_remote_copy(src_ref=src,dst_ref=dst,send_sem=self.send.at[k],recv_sem=self.recv.at[k],
                                          device_id=self.to[t],device_id_type=MESH)
        copy.start()
        self.sent.append(copy)
    def got(self,k,t,dst):
        pltpu.make_async_remote_copy(src_ref=dst,dst_ref=dst,send_sem=self.send.at[k],recv_sem=self.recv.at[k],
                                     device_id=self.to[t],device_id_type=MESH).wait_recv()
    def finish(self):
        for copy in self.sent: copy.wait_send()

def first_kernel(block_ref,long_ref,skip_ref,qkvw_ref,vec_ref,
                 hidden_out,normed_out,qkv_out,heads_out,wskip_out,vec_out,
                 ws,ns,hs,piece,hid,qs,vs,send,recv,local):
    x,y,c,w,wx,wy,wd=place()
    tokens,d=block_ref.shape
    sr=skip_ref.shape[0]; half=sr//2; part=half//2
    kr=qkvw_ref.shape[0]; kh=kr//2; hd=qkvw_ref.shape[1]//12
    tc=tokens//4
    mul=pl.multiple_of
    net=Links(send,recv)
    net.meet("XYDC")
    def srows(b,core,p): return pl.ds(mul(b*sr+core*half+p*part,16),part)
    def mine(p): return pl.ds(mul(c*half+p*part,16),part)
    net.start(0,"X",skip_ref.at[mine(0)],ws.at[srows(w,c,0)])
    net.start(2,"Y",skip_ref.at[mine(1)],ws.at[srows(w,c,1)])
    net.start(1,"X",skip_ref.at[mine(1)],ws.at[srows(w,c,1)])
    net.start(3,"Y",skip_ref.at[mine(0)],ws.at[srows(w,c,0)])
    own=pltpu.make_async_copy(skip_ref,ws.at[pl.ds(mul(w*sr,16),sr)],local.at[0])
    own.start()
    for k,t in ((30,"X"),(31,"Y"),(32,"D")): net.start(k,t,vec_ref,vs.at[w])
    vs[w]=vec_ref[...]
    for p in range(4):
        piece[p]=jnp.concatenate([qkvw_ref[:,(s*4+p)*hd:(s*4+p+1)*hd] for s in range(3)],axis=1)
    own_heads=pltpu.make_async_copy(piece.at[w],hs.at[pl.ds(mul(w*kr,16),kr)],local.at[1])
    own_heads.start()
    def pass_on(k,t,b,p,onward):
        r=srows(b,c,p)
        net.got(k,t,ws.at[r])
        for k2,t2 in onward: net.start(k2,t2,ws.at[r],ws.at[r])
    pass_on(0,"X",wx,0,((4,"Y"),(6,"C")))
    pass_on(2,"Y",wy,1,((5,"X"),(7,"C")))
    pass_on(1,"X",wx,1,((8,"C"),))
    pass_on(3,"Y",wy,0,((9,"C"),))
    def hrows(b,core): return pl.ds(mul(b*kr+core*kh,16),kh)
    cut=pl.ds(mul(c*kh,16),kh)
    net.start(12,"X",piece.at[wx,cut],hs.at[hrows(w,c)])
    net.start(13,"Y",piece.at[wy,cut],hs.at[hrows(w,c)])
    net.start(14,"D",piece.at[wd,cut],hs.at[hrows(w,c)])
    own.wait()
    net.got(6,"C",ws.at[srows(wx,1-c,0)])
    net.got(8,"C",ws.at[srows(wx,1-c,1)])
    near=pl.ds(mul(y*d,16),d); far=pl.ds(mul((1-y)*d,16),d)
    def tok(i): return pl.ds(mul(i*tc,16),tc)
    @pl.loop(0,4)
    def _(i):
        lhs=jnp.where(y==0,block_ref[tok(i),:],long_ref[tok(i),:])
        hid[tok(i),:]=nn(lhs,ws[near,:])
    pass_on(4,"Y",wd,0,((10,"C"),))
    pass_on(5,"X",wd,1,((11,"C"),))
    net.got(7,"C",ws.at[srows(wy,1-c,1)])
    net.got(9,"C",ws.at[srows(wy,1-c,0)])
    net.got(10,"C",ws.at[srows(wd,1-c,0)])
    net.got(11,"C",ws.at[srows(wd,1-c,1)])
    for k,t,b in ((30,"X",wx),(31,"Y",wy),(32,"D",wd)): net.got(k,t,vs.at[b])
    gain=jnp.concatenate([vs[p,0:1,:] for p in range(4)],axis=1)
    shift=jnp.concatenate([vs[p,1:2,:] for p in range(4)],axis=1)
    def nrows(b,i): return pl.ds(mul(b*tokens+i*tc,16),tc)
    def spread(i,t):
        net.start((18 if t=="X" else 22)+i,t,ns.at[nrows(w,i)],ns.at[nrows(w,i)])
    for i in range(4):
        r=tok(i)
        lhs=jnp.where(y==0,long_ref[r,:],block_ref[r,:])
        h=hid[r,:]+nn(lhs,ws[far,:])
        hid[r,:]=h
        cen=h-jnp.mean(h,axis=1,keepdims=True)
        inv=lax.rsqrt(jnp.mean(cen*cen,axis=1,keepdims=True)+1e-5)
        ns[nrows(w,i),:]=(cen*inv*gain+shift).astype(BF)
        spread(i,"XYXY"[i])
    for i,t in ((1,"X"),(0,"Y"),(3,"X"),(2,"Y")): spread(i,t)
    outs=[]
    def put(k,src,dst):
        copy=pltpu.make_async_copy(src,dst,local.at[k]); copy.start(); outs.append(copy)
    put(2,ws,wskip_out); put(3,hid,hidden_out); put(7,vs,vec_out)
    for j,(t,b) in enumerate((("X",wx),("Y",wy),("D",wd))):
        net.got(12+j,t,hs.at[hrows(b,c)])
        net.start(15+j,"C",hs.at[hrows(b,c)],hs.at[hrows(b,c)])
    for j,b in enumerate((wx,wy,wd)):
        net.got(15+j,"C",hs.at[hrows(b,1-c)])
    own_heads.wait()
    put(4,hs,heads_out)
    def project(b,i): qs[nrows(b,i),:]=nn(ns[nrows(b,i),:],hs[...]).astype(BF)
    @pl.loop(0,4)
    def _(i): project(w,i)
    for i,t,b,k,k2,t2 in ((0,"X",wx,18,26,"Y"),(1,"Y",wy,22,27,"X"),(2,"X",wx,18,28,"Y"),(3,"Y",wy,22,29,"X")):
        net.got(k+i,t,ns.at[nrows(b,i)])
        net.start(k2,t2,ns.at[nrows(b,i)],ns.at[nrows(b,i)])
    @pl.loop(0,2)
    def _(i): project(wx,2*i)
    @pl.loop(0,2)
    def _(i): project(wy,2*i+1)
    for i in (1,3):
        net.got(18+i,"X",ns.at[nrows(wx,i)])
        project(wx,i)
        net.got(22+i-1,"Y",ns.at[nrows(wy,i-1)])
        project(wy,i-1)
    for i,t,k in ((0,"Y",26),(1,"X",27),(2,"Y",28),(3,"X",29)):
        net.got(k,t,ns.at[nrows(wd,i)])
        project(wd,i)
    put(5,ns,normed_out); put(6,qs,qkv_out)
    for copy in outs: copy.wait()
    net.finish()

def first(block,long,skipw,qkvw,vecs):
    tokens,d=block.shape; S=jax.ShapeDtypeStruct; hd3=qkvw.shape[1]//4
    V=pltpu.VMEM
    return pl.pallas_call(first_kernel,
        out_shape=(S((tokens,d),F32),S((4*tokens,d),BF),S((4*tokens,hd3),BF),S((d,hd3),BF),S((2*d,d),BF),S((4,)+vecs.shape,F32)),
        in_specs=[VM]*5,out_specs=(ANY,)*6,
        scratch_shapes=[V((2*d,d),BF),V((4*tokens,d),BF),V((d,hd3),BF),V((4,d//4,hd3),BF),V((tokens,d),F32),V((4*tokens,hd3),BF),V((4,)+vecs.shape,F32),
            pltpu.SemaphoreType.DMA((33,)),pltpu.SemaphoreType.DMA((33,)),pltpu.SemaphoreType.DMA((8,))],
        compiler_params=pltpu.CompilerParams(vmem_limit_bytes=56*2**20,collective_id=0,has_side_effects=True),
        cost_estimate=pl.CostEstimate(flops=2*tokens*d*d*5,bytes_accessed=40*2**20,transcendentals=0))(
        block,long,skipw,qkvw,vecs)

class Chain:
    def __init__(self,net,k,own,up_in,down_in,up_out,down_out):
        self.net,self.k,self.own=net,k,own
        self.up_in,self.down_in,self.up_out,self.down_out=up_in,down_in,up_out,down_out
        self.z,self.n=lax.axis_index("z"),lax.axis_size("z")
    def copy(self,up,src):
        k=self.k+(0 if up else 1)
        return pltpu.make_async_remote_copy(src_ref=src,dst_ref=self.up_in if up else self.down_in,
            send_sem=self.net.send.at[k],recv_sem=self.net.recv.at[k],
            device_id={"z":self.z+1 if up else self.z-1},device_id_type=MESH)
    def hop(self,h):
        for up in (True,False):
            here=self.z==(h if up else self.n-1-h)
            inn,out=(self.up_in,self.up_out) if up else (self.down_in,self.down_out)
            @pl.when(here)
            def _():
                if h==0:
                    self.copy(up,self.own).start()
                else:
                    self.copy(up,inn).wait_recv()
                    out[...]=(self.own[...].astype(F32)+inn[...].astype(F32)).astype(out.dtype)
                    self.copy(up,out).start()
    def total(self):
        first,final=self.z==0,self.z==self.n-1
        @pl.when(first)
        def _():
            self.copy(False,self.down_in).wait_recv()
            self.copy(True,self.own).wait_send()
            self.own[...]=(self.own[...].astype(F32)+self.down_in[...].astype(F32)).astype(self.own.dtype)
        @pl.when(final)
        def _():
            self.copy(True,self.up_in).wait_recv()
            self.copy(False,self.own).wait_send()
            self.own[...]=(self.own[...].astype(F32)+self.up_in[...].astype(F32)).astype(self.own.dtype)
        @pl.when(jnp.logical_not(first|final))
        def _():
            self.copy(True,self.up_out).wait_send()
            self.copy(False,self.down_out).wait_send()
            self.own[...]=(self.own[...].astype(F32)+self.up_in[...].astype(F32)+self.down_in[...].astype(F32)).astype(self.own.dtype)

def meet_all(net,who):
    z,n=lax.axis_index("z"),lax.axis_size("z")
    barrier=pltpu.get_barrier_semaphore()
    for t in who:
        pl.semaphore_signal(barrier,inc=1,device_id=net.to[t],device_id_type=MESH)
    @pl.when(z>0)
    def _(): pl.semaphore_signal(barrier,inc=1,device_id={"z":z-1},device_id_type=MESH)
    @pl.when(z<n-1)
    def _(): pl.semaphore_signal(barrier,inc=1,device_id={"z":z+1},device_id_type=MESH)
    ends=(z==0)|(z==n-1)
    @pl.when(ends)
    def _(): pl.semaphore_wait(barrier,len(who)+1)
    @pl.when(jnp.logical_not(ends))
    def _(): pl.semaphore_wait(barrier,len(who)+2)

SEG=3
def last_kernel(gq_ref,heads_ref,normed_ref,hidden_ref,gmid_ref,gain_ref,block_ref,long_ref,wskip_ref,small_ref,
                gin_out,gsk_out,small_out,gqkv_out,gskip_out,
                big,part,rx,ry,dx,dy,gw,gwr,gsr,qz,fq,sdx,sdy,srx,sry,own,sz,fs,sm,sin,smz,send,recv,local):
    x,y,c,w,wx,wy,wd=place()
    tokens,d=block_ref.shape
    tc=tokens//4; kr=d//4; kh=kr//2; sr=d//2; sh=sr//2; sq=sh//2
    mul=pl.multiple_of
    net=Links(send,recv)
    load=pltpu.make_async_copy(normed_ref,big,local.at[0])
    load.start()
    meet_all(net,"XYDC")
    def tok(i): return pl.ds(i*tc,tc)
    def pr(s,i): return pl.ds(s*tokens+i*tc,tc)
    def partial(b,i):
        return nt(gq_ref[pl.ds(mul(b*tokens+i*tc,16),tc),:],heads_ref[...])
    for i,t,dst,k in ((0,"X",dx,0),(2,"Y",dy,2),(1,"X",dx,1),(3,"Y",dy,3)):
        part[pr(2,i),:]=partial(wd,i).astype(BF)
        net.start(k,t,part.at[pr(2,i)],dst.at[tok(i%2)])
    for i,t,b,dst,k in ((0,"X",wx,rx,4),(2,"Y",wy,ry,10),(1,"X",wx,rx,5),(3,"Y",wy,ry,11)):
        s=0 if t=="X" else 1
        part[pr(s,i),:]=partial(b,i).astype(BF)
        net.start(k,t,part.at[pr(s,i)],dst.at[tok(i)])
    @pl.loop(0,4)
    def _(i):
        r=pl.ds(mul(i*tc,16),tc)
        part[pl.ds(mul(3*tokens+i*tc,16),tc),:]=nt(gq_ref[pl.ds(mul(w*tokens+i*tc,16),tc),:],heads_ref[...]).astype(BF)
    load.wait()
    cc=d//3
    def weight_grad(k):
        cr=pl.ds(k*cc,cc)
        gw[cr,:]=tn(big[:,cr],gq_ref[...]).astype(BF)
    def relay(i,t,b,dst,k,src,k2,t2):
        s=0 if t=="X" else 1
        mine=partial(b,i)
        net.got(k2,t2,src.at[tok(i%2)])
        part[pr(s,i),:]=(mine+src[tok(i%2),:].astype(F32)).astype(BF)
        net.start(k,t,part.at[pr(s,i)],dst.at[tok(i)])
    weight_grad(0)
    relay(2,"X",wx,rx,6,dy,2,"Y")
    relay(0,"Y",wy,ry,8,dx,0,"X")
    weight_grad(1)
    weight_grad(2)
    def rows(b,core): return pl.ds(mul(b*kr+core*kh,16),kh)
    for b in range(4):
        net.start(12+b,"C",gw.at[rows(b,1-c)],gwr.at[pl.ds(b*kh,kh)])
    relay(3,"X",wx,rx,7,dy,3,"Y")
    relay(1,"Y",wy,ry,9,dx,1,"X")
    for b in range(4):
        r=pl.ds(b*kh,kh)
        net.got(12+b,"C",gwr.at[r])
        gwr[r,:]=(gwr[r,:].astype(F32)+gw[rows(b,c),:].astype(F32)).astype(BF)
    halves=[pl.ds(i*2*kh,2*kh) for i in range(2)]
    chains=[Chain(net,40+2*i,gwr.at[r],*[qz.at[j,r] for j in range(4)]) for i,r in enumerate(halves)]
    for chain in chains: chain.hop(0)
    gain=gain_ref[...]
    sm[...]=jnp.zeros_like(sm)
    for h in range(1,lax.axis_size("z")-2):
        for chain in chains: chain.hop(h)
    for i in (0,2,1,3):
        r=tok(i)
        net.got(4+i,"X",rx.at[r])
        net.got(8+i,"Y",ry.at[r])
        gf=part[pr(3,i),:].astype(F32)+rx[r,:].astype(F32)+ry[r,:].astype(F32)
        h=hidden_ref[r,:]
        cen=h-jnp.mean(h,axis=1,keepdims=True)
        inv=lax.rsqrt(jnp.mean(cen*cen,axis=1,keepdims=True)+1e-5)
        xhat=cen*inv
        sm[0:1,:]+=jnp.sum(gf*xhat,axis=0,keepdims=True)
        sm[1:2,:]+=jnp.sum(gf,axis=0,keepdims=True)
        e=gf*gain
        back=e-jnp.mean(e,axis=1,keepdims=True)-xhat*jnp.mean(e*xhat,axis=1,keepdims=True)
        big[pl.ds(2*d+i*tc,tc),:]=(gmid_ref[r,:]+back*inv).astype(BF)
    sm[2:4,:]=small_ref[0:2,:]
    for k in range(6):
        src=block_ref if k<3 else long_ref
        big[pl.ds(k*cc,cc),:]=tn(src[:,(k%3)*cc:(k%3+1)*cc],big[2*d:2*d+tokens,:]).astype(BF)
    def srows(b,core): return pl.ds(mul(b*sr+core*sh,16),sh)
    for b in range(4):
        net.start(16+b,"C",big.at[srows(b,1-c)],gsr.at[pl.ds(b*sh,sh)])
    net.start(20,"C",sm,sin.at[0])
    for copy in net.sent[:16]: copy.wait_send()
    net.sent=net.sent[16:]
    wload=pltpu.make_async_copy(wskip_ref,part.at[pl.ds(0,2*d)],local.at[1])
    wload.start()
    for chain in chains: chain.hop(lax.axis_size("z")-2)
    for b in range(4):
        r=pl.ds(b*sh,sh)
        net.got(16+b,"C",gsr.at[r])
        gsr[r,:]=(gsr[r,:].astype(F32)+big[srows(b,c),:].astype(F32)).astype(BF)
    def quarter(b,i): return pl.ds(mul(b*sh+i*sq,16),sq)
    top,low=pl.ds(0,sq),pl.ds(sq,sq)
    net.start(21,"X",gsr.at[quarter(wd,0)],sdx)
    net.start(22,"Y",gsr.at[quarter(wd,1)],sdy)
    net.start(23,"X",gsr.at[quarter(wx,0)],srx.at[top])
    net.start(24,"Y",gsr.at[quarter(wy,1)],sry.at[low])
    net.got(20,"C",sin.at[0])
    smz[6]=sm[...]+sin[0]
    net.start(27,"X",smz.at[6],sin.at[1])
    for chain in chains: chain.total()
    def qrows(b): return pl.ds(mul(b*kh,16),kh)
    for j,(t,b) in enumerate((("X",wx),("Y",wy),("D",wd))):
        net.start(29+j,t,gwr.at[qrows(b)],fq.at[w,c])
    fq[w,c]=gwr[qrows(w),:]
    wload.wait()
    @pl.loop(0,4)
    def _(i):
        r=pl.ds(mul(i*tc,16),tc)
        gh=big[pl.ds(mul(2*d+i*tc,16),tc),:]
        rx[r,:]=nt(gh,part[:d,:]).astype(BF)
        ry[r,:]=nt(gh,part[d:2*d,:]).astype(BF)
    outs=[]
    def put(k,src,dst):
        copy=pltpu.make_async_copy(src,dst,local.at[k]); copy.start(); outs.append(copy)
    put(2,rx,gin_out); put(3,ry,gsk_out)
    net.got(21,"X",sdx)
    gsr[quarter(wy,0),:]=(gsr[quarter(wy,0),:].astype(F32)+sdx[...].astype(F32)).astype(BF)
    net.start(25,"Y",gsr.at[quarter(wy,0)],sry.at[top])
    net.got(22,"Y",sdy)
    gsr[quarter(wx,1),:]=(gsr[quarter(wx,1),:].astype(F32)+sdy[...].astype(F32)).astype(BF)
    net.start(26,"X",gsr.at[quarter(wx,1)],srx.at[low])
    net.got(27,"X",sin.at[1])
    smz[0]=smz[6]+sin[1]
    net.start(28,"Y",smz.at[0],sin.at[2])
    for j,(t,b) in enumerate((("X",wx),("Y",wy),("D",wd))):
        net.got(29+j,t,fq.at[b,c])
    for b in range(4):
        net.start(32+b,"C",fq.at[b,c],fq.at[b,c])
    net.got(28,"Y",sin.at[2])
    smz[1]=smz[0]+sin[2]
    net.got(23,"X",srx.at[top]); net.got(25,"Y",sry.at[top])
    net.got(24,"Y",sry.at[low]); net.got(26,"X",srx.at[low])
    own[...]=(gsr[pl.ds(mul(w*sh,16),sh),:].astype(F32)+srx[...].astype(F32)+sry[...].astype(F32)).astype(BF)
    seg=sh//SEG
    chains=[Chain(net,44,smz.at[1],smz.at[2],smz.at[3],smz.at[4],smz.at[5])]
    for i in range(SEG):
        r=pl.ds(i*seg,seg)
        chains.append(Chain(net,46+2*i,own.at[r],*[sz.at[j,r] for j in range(4)]))
    for h in range(lax.axis_size("z")-1):
        for chain in chains: chain.hop(h)
    for chain in chains: chain.total()
    net.start(36,"C",own,fs)
    for b in range(4): net.got(32+b,"C",fq.at[b,1-c])
    put(4,fq,gqkv_out); put(5,smz.at[1],small_out); put(6,own,gskip_out.at[c])
    net.got(36,"C",fs)
    put(7,fs,gskip_out.at[1-c])
    for copy in outs: copy.wait()
    net.finish()

def last(gq,heads,normed,hidden,gmid,gain,block,long,wskip,small):
    tokens,d=block.shape; S=jax.ShapeDtypeStruct; hd3=gq.shape[1]
    V=pltpu.VMEM
    return pl.pallas_call(last_kernel,
        out_shape=(S((tokens,d),BF),S((tokens,d),BF),S((8,d),F32),S((4,2,d//8,hd3),BF),S((2,d//4,d),BF)),
        in_specs=[VM,VM,ANY]+[VM]*5+[ANY,VM],out_specs=(ANY,)*5,
        scratch_shapes=[V((4*tokens,d),BF),V((4*tokens,d),BF),V((tokens,d),BF),V((tokens,d),BF),V((tokens//2,d),BF),V((tokens//2,d),BF),
            V((d,hd3),BF),V((d//2,hd3),BF),V((d,d),BF),V((4,d//2,hd3),BF),V((4,2,d//8,hd3),BF),
            V((d//8,d),BF),V((d//8,d),BF),V((d//4,d),BF),V((d//4,d),BF),V((d//4,d),BF),V((4,d//4,d),BF),V((d//4,d),BF),
            V((8,d),F32),V((3,8,d),F32),V((7,8,d),F32),
            pltpu.SemaphoreType.DMA((52,)),pltpu.SemaphoreType.DMA((52,)),pltpu.SemaphoreType.DMA((8,))],
        compiler_params=pltpu.CompilerParams(vmem_limit_bytes=63*2**20,collective_id=1,has_side_effects=True),
        cost_estimate=pl.CostEstimate(flops=2*tokens*d*d*10,bytes_accessed=60*2**20,transcendentals=0))(
        gq,heads,normed,hidden,gmid,gain,block,long,wskip,small)

SPLIT=((0,640),(640,512))
def middle_kernel(hidden_ref,att_ref,g_ref,gain_ref,shift_ref,outw_ref,outx_ref,outy_ref,upw_ref,upx_ref,upy_ref,dnw_ref,
                  lay_out,gmid_ref,gh_out,gow_out,small_ref,gup_out,gdn_out,sxu_out,sxd_out,syu_out,syd_out,uland,dland,ux_out,uy_out,dx_out,dy_out,
                  att_in,att_s,outw_s,n2_s,xhat_s,rstd_s,lay_s,act_s,gu_s,upb,dnb,gub,gdb,land_u,land_d,low_s,
                  send,recv,csend,crecv,fetch_sem,flush_sem,local,usem,urecv,bring_sem):
    x,y,c,w,wx,wy,wd=place()
    tokens,d=hidden_ref.shape
    cols=att_ref.shape[1]
    kr=d//4; kh=kr//2; dh=d//2; dq=dh//2
    tc=tokens//4; th=tokens//2
    mul=pl.multiple_of
    net=Links(send,recv)
    left=[]
    def start(k,t,src,dst,view):
        pltpu.make_async_remote_copy(src_ref=src,dst_ref=dst,send_sem=send.at[k],recv_sem=recv.at[k],
                                     device_id=net.to[t],device_id_type=MESH).start()
        left.append((k,t,view))
    def blk(b): return pl.ds(mul(b*d,128),d)
    def urow(b,core): return pl.ds(mul(b*kr+core*kh,16),kh)
    def drow(b,core,p): return pl.ds(mul(b*d+core*dh+p*dq,16),dq)
    def trow(b): return pl.ds(mul(b*tokens,16),tokens)
    uview=uland.at[pl.ds(0,kh),pl.ds(0,d)]
    dview=dland.at[pl.ds(0,dq)]
    net.meet("XYDC")
    for j,(t,b) in enumerate((("X",wx),("Y",wy),("D",wd))):
        start(j,t,att_ref.at[trow(b)],att_in.at[w],att_in.at[0])
    own_att=pltpu.make_async_copy(att_ref.at[trow(w)],att_in.at[w],local.at[0])
    own_att.start()
    cut=kh//32*16+16
    def orow(b,core,lo,n): return pl.ds(mul(b*kr+core*kh+lo,16),n)
    start(3,"Y",outx_ref.at[pl.ds(0,cut)],outw_s.at[orow(wx,c,0,cut)],outw_s.at[pl.ds(0,cut)])
    start(4,"X",outy_ref.at[pl.ds(cut,kh-cut)],outw_s.at[orow(wy,c,cut,kh-cut)],outw_s.at[pl.ds(0,kh-cut)])
    start(5,"C",outx_ref,outw_s.at[urow(wx,c)],outw_s.at[pl.ds(0,kh)])
    start(6,"C",outy_ref,outw_s.at[urow(wy,c)],outw_s.at[pl.ds(0,kh)])
    start(7,"Y",upx_ref.at[:,blk(wy)],uland.at[urow(wx,c),blk(wy)],uview)
    start(8,"X",upy_ref.at[:,blk(w)],uland.at[urow(wy,c),blk(w)],uview)
    order=(w,wx,wd,wy)
    def up_core(i):
        start(11+2*i,"C",upx_ref.at[:,blk(order[i])],uland.at[urow(wx,c),blk(order[i])],uview)
        start(12+2*i,"C",upy_ref.at[:,blk(order[i])],uland.at[urow(wy,c),blk(order[i])],uview)
    up_core(0)
    outw_s[pl.ds(mul(w*kr,16),kr),:]=outw_ref[...]
    outw_s[urow(wx,c),:]=outx_ref[...]
    outw_s[urow(wy,c),:]=outy_ref[...]

    diag_id=(7,8,9,10)
    def diag_from(i): return "YX"[i%2]
    def up_relay(i):
        view=uland.at[urow(wd,c),blk(order[i])]
        net.got(diag_id[i],diag_from(i),view)
        start(19+i,"C",view,view,uview)
    def up_sources(i):
        b=order[i]
        net.got(11+2*i,"C",uland.at[urow(wx,1-c),blk(b)])
        net.got(12+2*i,"C",uland.at[urow(wy,1-c),blk(b)])
        net.got(19+i,"C",uland.at[urow(wd,1-c),blk(b)])
        return [(upw_ref.at[:,blk(b)],pl.ds(mul(w*kr,16),kr)),(upx_ref.at[:,blk(b)],urow(wx,c)),(upy_ref.at[:,blk(b)],urow(wy,c)),
                (uland.at[urow(wx,1-c),blk(b)],urow(wx,1-c)),(uland.at[urow(wy,1-c),blk(b)],urow(wy,1-c)),
                (uland.at[pl.ds(mul(wd*kr,16),kr),blk(b)],pl.ds(mul(wd*kr,16),kr))]
    def fetch(i):
        slot=i%2
        for j,(src,rows) in enumerate(up_sources(i)):
            pltpu.make_async_copy(src,upb.at[slot,rows],fetch_sem.at[slot,j]).start()
        src=dnw_ref if i==0 else dland.at[pl.ds(mul(order[i]*d,16),d)]
        pltpu.make_async_copy(src,dnb.at[slot],fetch_sem.at[slot,6]).start()
    def fetched(slot):
        for j,n in enumerate((kr,kh,kh,kh,kh,kr)):
            view=upb.at[slot,pl.ds(0,n)]
            pltpu.make_async_copy(view,view,fetch_sem.at[slot,j]).wait()
        pltpu.make_async_copy(dnb.at[slot],dnb.at[slot],fetch_sem.at[slot,6]).wait()
    def down_relay(k,t,b,p,onward):
        r=drow(b,c,p)
        net.got(k,t,dland.at[r])
        for k2,t2 in onward: start(k2,t2,dland.at[r],dland.at[r],dview)
    def down_core(k,b,p): net.got(k,"C",dland.at[drow(b,1-c,p)])

    for j,(t,b) in enumerate((("X",wx),("Y",wy),("D",wd))):
        net.got(j,t,att_in.at[b])
    start(9,"Y",upx_ref.at[:,blk(wx)],uland.at[urow(wx,c),blk(wx)],uview)
    start(10,"X",upy_ref.at[:,blk(wd)],uland.at[urow(wy,c),blk(wd)],uview)
    def dmine(p): return dnw_ref.at[pl.ds(mul(c*dh+p*dq,16),dq)]
    start(23,"X",dmine(0),dland.at[drow(w,c,0)],dview)
    start(25,"Y",dmine(1),dland.at[drow(w,c,1)],dview)
    start(24,"X",dmine(1),dland.at[drow(w,c,1)],dview)
    start(26,"Y",dmine(0),dland.at[drow(w,c,0)],dview)
    net.got(3,"Y",outw_s.at[orow(wd,c,0,cut)])
    net.got(4,"X",outw_s.at[orow(wd,c,cut,kh-cut)])
    start(35,"C",outw_s.at[urow(wd,c)],outw_s.at[urow(wd,c)],outw_s.at[pl.ds(0,kh)])
    up_relay(0)
    for i in (1,2,3): up_core(i)
    net.got(5,"C",outw_s.at[urow(wx,1-c)]); net.got(6,"C",outw_s.at[urow(wy,1-c)])
    net.got(35,"C",outw_s.at[urow(wd,1-c)])
    own_att.wait()
    fetch(0)
    gain=gain_ref[...]; shift=shift_ref[...]
    @pl.loop(0,4)
    def _(i):
        r=pl.ds(mul(i*tc,16),tc)
        joined=jnp.concatenate([att_in[p,r,:] for p in range(4)],axis=1)
        att_s[r,:]=joined
        mid=hidden_ref[r,:]+nn(joined,outw_s[...])
        lay_s[r,:]=mid
        cen=mid-jnp.mean(mid,axis=1,keepdims=True)
        inv=lax.rsqrt(jnp.mean(cen*cen,axis=1,keepdims=True)+1e-5)
        xhat=cen*inv
        xhat_s[r,:]=xhat
        rstd_s[r,:]=jnp.broadcast_to(inv,(tc,128))
        n2_s[r,:]=(xhat*gain+shift).astype(BF)
        gmid_ref[r,:]=jnp.zeros((tc,d),F32)

    def pieces(slot):
        out=[(gub,pl.ds(mul(p*kr+(1-c)*kh,16),kh),land_u.at[slot,pl.ds(p*kh,kh)]) for p in range(4)]
        return out+[(gdb,pl.ds(mul((1-c)*dh,16),dh),land_d.at[slot])]
    def exchange(slot,act):
        for j,(ref,r,dst) in enumerate(pieces(slot)):
            act(pltpu.make_async_remote_copy(src_ref=ref.at[r],dst_ref=dst,send_sem=csend.at[slot,j],recv_sem=crecv.at[slot,j],
                                             device_id=net.to["C"],device_id_type=MESH))
    def flush(b,act):
        for p in range(4):
            act(pltpu.make_async_copy(gub.at[pl.ds(mul(p*kr+c*kh,16),kh)],gup_out.at[pl.ds(p*kh,kh),blk(b)],flush_sem.at[p]))
        act(pltpu.make_async_copy(gdb.at[pl.ds(mul(c*dh,16),dh)],gdn_out.at[pl.ds(mul(b*dh,16),dh)],flush_sem.at[4]))
    go=lambda copy: copy.start()
    done=lambda copy: copy.wait()
    def finalize(i):
        slot=lax.rem(i,2)
        exchange(slot,lambda copy: copy.wait())
        for p in range(4):
            r=pl.ds(mul(p*kr+c*kh,16),kh)
            gub[r,:]=(gub[r,:].astype(F32)+land_u[slot,pl.ds(p*kh,kh),:].astype(F32)).astype(BF)
        for p in range(2):
            r=pl.ds(mul(c*dh+p*dq,16),dq)
            gdb[r,:]=(gdb[r,:].astype(F32)+land_d[slot,pl.ds(p*dq,dq),:].astype(F32)).astype(BF)
    def block_of(i):
        return 2*lax.rem(y+i//2,2)+lax.rem(x+(i+1)//2,2)

    usend=[pl.ds(0,cut),pl.ds(cut,kh-cut)]
    def ahead(i,b,act):
        for j,(t,dst) in enumerate((("X",ux_out),("Y",uy_out))):
            n=usend[j]
            src=gup_out.at[pl.ds(mul(wd*kh+n.start,16),n.size),blk(b)]
            act(pltpu.make_async_remote_copy(src_ref=src,dst_ref=dst.at[:,blk(b)],send_sem=usem.at[i,j],recv_sem=urecv.at[i,j],
                                             device_id=net.to[t],device_id_type=MESH))
    def ahead_down(act):
        for j,(t,dst) in enumerate((("X",dx_out),("Y",dy_out))):
            act(pltpu.make_async_remote_copy(src_ref=gdn_out.at[pl.ds(mul(wd*dh+j*dq,16),dq)],dst_ref=dst,
                                             send_sem=usem.at[4,j],recv_sem=urecv.at[4,j],device_id=net.to[t],device_id_type=MESH))
    def weight_grads():
        for lo,n in SPLIT:
            f=pl.ds(lo,n)
            gdb[f,:]=tn(act_s[:,f],g_ref[...]).astype(BF)
            gub[f,:]=tn(n2_s[:,f],gu_s[...]).astype(BF)
    @pl.loop(0,4)
    def _(i):
        slot=lax.rem(i,2)
        fetched(slot)
        @pl.loop(0,2)
        def _(t):
            r=pl.ds(mul(t*th,16),th)
            for lo,n in SPLIT:
                f=pl.ds(lo,n)
                u=nn(n2_s[r,:],upb[slot,:,f])
                a,dg=gelu_parts(u)
                act_s[r,f]=a.astype(BF)
                gu_s[r,f]=(nt(g_ref[r,:],dnb[slot,f,:])*dg).astype(BF)
        @pl.when(i>=1)
        def _():
            finalize(i-1)
            flush(block_of(i-1),go)
        @pl.when(i==0)
        def _():
            for j in (1,2,3): up_relay(j)
        @pl.loop(0,2)
        def _(t):
            r=pl.ds(mul(t*th,16),th)
            for lo,n in SPLIT:
                f=pl.ds(lo,n)
                lay_s[r,f]+=nn(act_s[r,:],dnb[slot,:,f])
                gmid_ref[r,f]+=nt(gu_s[r,:],upb[slot,f,:])
        @pl.when(i==0)
        def _():
            down_relay(23,"X",wx,0,((27,"Y"),(29,"C")))
            down_relay(25,"Y",wy,1,((28,"X"),(30,"C")))
            down_relay(24,"X",wx,1,((31,"C"),))
            down_core(29,wx,0); down_core(31,wx,1)
            fetch(1)
        @pl.when(i==1)
        def _():
            down_relay(27,"Y",wd,0,((33,"C"),))
            down_relay(28,"X",wd,1,((34,"C"),))
            down_relay(26,"Y",wy,0,((32,"C"),))
            down_core(33,wd,0); down_core(34,wd,1)
            fetch(2)
        @pl.when(i==2)
        def _():
            down_core(30,wy,1); down_core(32,wy,0)
            fetch(3)
        @pl.when(i>=1)
        def _():
            flush(block_of(i-1),done)
            ahead(i-1,block_of(i-1),go)
        @pl.when(i==3)
        def _(): ahead_down(go)
        @pl.when(i<3)
        def _():
            weight_grads()
            exchange(slot,go)
    small_ref[...]=jnp.zeros_like(small_ref)
    for i in range(4):
        r=pl.ds(i*tc,tc)
        gs=gmid_ref[r,:]; xhat=xhat_s[r,:]
        small_ref[0:1,:]+=jnp.sum(gs*xhat,axis=0,keepdims=True)
        small_ref[1:2,:]+=jnp.sum(gs,axis=0,keepdims=True)
        e=gs*gain
        back=e-jnp.mean(e,axis=1,keepdims=True)-xhat*jnp.mean(e*xhat,axis=1,keepdims=True)
        gm=g_ref[r,:].astype(F32)+back*rstd_s[r,0:1]
        gmid_ref[r,:]=gm
        low=gm.astype(BF)
        low_s[r,:]=low
        ga=nt(low,outw_s[...]).astype(BF)
        for p in range(4): att_in[p,r,:]=ga[:,p*cols:(p+1)*cols]
        for j,(t,b) in enumerate((("X",wx),("Y",wy),("D",wd))):
            start(36+3*i+j,t,att_in.at[b,r],gh_out.at[w,r],gh_out.at[0,pl.ds(0,tc)])
    own_grad=pltpu.make_async_copy(att_in.at[w],gh_out.at[w],local.at[2])
    own_grad.start()
    weight_grads()
    exchange(1,go)
    act_s[...]=lay_s[...].astype(BF)
    lay_copy=pltpu.make_async_copy(act_s,lay_out,local.at[1])
    lay_copy.start()
    finalize(3)
    flush(wy,go)
    flush(wy,done)
    ahead(3,wy,go)
    for lo,n in SPLIT:
        f=pl.ds(lo,n)
        gub[f,:]=tn(att_s[:,f],low_s[...]).astype(BF)
    for p in range(4):
        start(48+p,"C",gub.at[pl.ds(mul(p*kr+(1-c)*kh,16),kh)],land_u.at[0,pl.ds(p*kh,kh)],land_u.at[0,pl.ds(0,kh)])
    def bring(k,src,dst):
        copy=pltpu.make_async_copy(src,dst,bring_sem.at[k]); copy.start(); return copy
    def spot(j,b): return pl.ds((4*j+b)*kh,kh)
    copies=[]
    for j,b2 in enumerate((wx,wy)):
        for b in range(4):
            copies.append(bring(4*j+b,gup_out.at[pl.ds(mul(b2*kh,16),kh),pl.ds(b*d,d)],upb.at[0,spot(j,b)]))
        copies.append(bring(16+j,gdn_out.at[pl.ds(mul(b2*dh,16),dh)],dnb.at[0,pl.ds(j*dh,dh)]))
    for i in range(4): ahead(i,order[i],done)
    ahead_down(done)
    for j,(src,n) in enumerate(((uy_out,usend[1]),(ux_out,usend[0]))):
        for b in range(4):
            copies.append(bring(8+4*j+b,src.at[:,pl.ds(b*d,d)],upb.at[1,pl.ds((4*j+b)*kh,n.size)]))
    copies.append(bring(18,dy_out,dnb.at[1,pl.ds(0,dq)]))
    copies.append(bring(19,dx_out,dnb.at[1,pl.ds(dq,dq)]))
    for copy in copies: copy.wait()
    copies=[]
    for j,(uo,do) in enumerate(((sxu_out,sxd_out),(syu_out,syd_out))):
        n=usend[1-j]
        for b in range(4):
            lo=(4*j+b)*kh
            r=pl.ds(lo+n.start,n.size)
            upb[0,r,:]=(upb[0,r,:].astype(F32)+upb[1,pl.ds(lo,n.size),:].astype(F32)).astype(BF)
            copies.append(bring(4*j+b,upb.at[0,spot(j,b)],uo.at[:,pl.ds(b*d,d)]))
        r=pl.ds(j*dh+(1-j)*dq,dq)
        dnb[0,r,:]=(dnb[0,r,:].astype(F32)+dnb[1,pl.ds(j*dq,dq),:].astype(F32)).astype(BF)
        copies.append(bring(16+j,dnb.at[0,pl.ds(j*dh,dh)],do.at[pl.ds(0,dh)]))
    for p in range(4):
        net.got(48+p,"C",land_u.at[0,pl.ds(p*kh,kh)])
        r=pl.ds(mul(p*kr+c*kh,16),kh)
        land_u[1,pl.ds(p*kh,kh),:]=(gub[r,:].astype(F32)+land_u[0,pl.ds(p*kh,kh),:].astype(F32)).astype(BF)
    for k,(b,dst) in enumerate(((w,gow_out.at[0]),(wd,gow_out.at[1]),(wx,sxd_out.at[pl.ds(dh,kh)]),(wy,syd_out.at[pl.ds(dh,kh)]))):
        copies.append(bring(8+k,land_u.at[1,pl.ds(mul(b*kh,16),kh)],dst))
    for i in range(4):
        for j,(t,b) in enumerate((("X",wx),("Y",wy),("D",wd))):
            net.got(36+3*i+j,t,gh_out.at[b,pl.ds(i*tc,tc)])
    for copy in [lay_copy,own_grad]+copies: copy.wait()
    for k,t,view in left:
        pltpu.make_async_remote_copy(src_ref=view,dst_ref=view,send_sem=send.at[k],recv_sem=recv.at[k],
                                     device_id=net.to[t],device_id_type=MESH).wait_send()

def middle(hidden,att,g,gain,shift,outw,outx,outy,upw,upx,upy,dnw):
    tokens,d=hidden.shape; cols=att.shape[1]; ff=upw.shape[1]
    S=jax.ShapeDtypeStruct; V=pltpu.VMEM; D=pltpu.SemaphoreType.DMA
    kh=d//8; cut=kh//32*16+16
    return pl.pallas_call(middle_kernel,
        out_shape=(S((tokens,d),BF),S((tokens,d),F32),S((4,tokens,cols),BF),S((2,kh,d),BF),S((8,d),F32),S((d//2,ff),BF),S((ff//2,d),BF),
                   S((kh,ff),BF),S((ff//8+kh,d),BF),S((kh,ff),BF),S((ff//8+kh,d),BF),
                   S((d,ff),BF),S((ff,d),BF),S((cut,ff),BF),S((kh-cut,ff),BF),S((ff//16,d),BF),S((ff//16,d),BF)),
        in_specs=[VM,ANY]+[VM]*6+[ANY]*4,out_specs=(ANY,VM,ANY,ANY,VM)+(ANY,)*12,
        scratch_shapes=[V((4,tokens,cols),BF),V((tokens,d),BF),V((d,d),BF),V((tokens,d),BF),V((tokens,d),F32),V((tokens,128),F32),
            V((tokens,d),F32),V((tokens,d),BF),V((tokens,d),BF),V((2,d,d),BF),V((2,d,d),BF),V((d,d),BF),V((d,d),BF),
            V((2,d//2,d),BF),V((2,d//2,d),BF),V((tokens,d),BF),D((52,)),D((52,)),D((2,5)),D((2,5)),D((2,7)),D((5,)),D((4,)),
            D((5,2)),D((5,2)),D((20,))],
        compiler_params=pltpu.CompilerParams(vmem_limit_bytes=63*2**20,collective_id=2,has_side_effects=True),
        cost_estimate=pl.CostEstimate(flops=2*tokens*d*(ff*6+d*3),bytes_accessed=60*2**20,transcendentals=tokens*ff*2))(
        hidden,att,g,gain,shift,outw,outx,outy,upw,upx,upy,dnw)

def assemble_kernel(lay_ref,gin_ref,gsk_ref,skip_ref,gq_ref,um_ref,uo_ref,dm_ref,do_ref,om_ref,oo_ref,
                    lay_out,gin_out,gsk_out,skip_out,qkv_out,up_out,down_out,out_out,
                    s0,s1,s2,s3,s4,s5,s6,s7,local):
    first=lax.axis_index("core")==0
    copies=[]
    def put(src,dst):
        copy=pltpu.make_async_copy(src,dst,local.at[len(copies)]); copy.start(); copies.append(copy)
    def chunks(n,body,size=144):
        @pl.loop(0,n//size)
        def _(i): body(pl.ds(pl.multiple_of(i*size,16),size))
    def wide(dst,src):
        def body(r): dst[r,:]=src[r,:].astype(F32)
        chunks(dst.shape[0],body,208 if dst.shape[0]%208==0 else 144)
    wide(s7,lay_ref); put(s7,lay_out)
    wide(s0,gin_ref); put(s0,gin_out)
    wide(s1,gsk_ref); put(s1,gsk_out)
    def pair(dst,mine,other,size=144):
        h=mine.shape[0]
        def body(r):
            m,o=mine[r,:].astype(F32),other[r,:].astype(F32)
            dst[0,r,:]=jnp.where(first,m,o)
            dst[1,r,:]=jnp.where(first,o,m)
        chunks(h,body,size)
    pair(s5,dm_ref,do_ref); put(s5,down_out)
    pair(s6,om_ref,oo_ref); put(s6,out_out)
    pair(s4,um_ref,uo_ref,48); put(s4,up_out)
    def skip(r): s2[r,:]=skip_ref[r,:].astype(F32)
    chunks(s2.shape[0],skip); put(s2,skip_out)
    hd=gq_ref.shape[3]//3; kh=gq_ref.shape[2]
    for core in range(2):
        for i in range(kh//48):
            r=pl.ds(i*48,48)
            s3[pl.ds(core*kh+i*48,48),:]=jnp.concatenate([gq_ref[p,core,r,s*hd:(s+1)*hd].astype(F32) for s in range(3) for p in range(4)],axis=1)
    put(s3,qkv_out)
    for copy in copies: copy.wait()

def assemble(lay,gin,gsk,skip,gq,um,uo,dm,do,om,oo):
    S=lambda *s: jax.ShapeDtypeStruct(s,F32)
    tokens,d=gin.shape
    shapes=(S(tokens,d),S(tokens,d),S(*skip.shape),S(d//4,3*d),S(2,*um.shape),S(2,*dm.shape),S(2,*om.shape))
    return pl.pallas_call(assemble_kernel,out_shape=(shapes[0],)+shapes,in_specs=[VM]*11,out_specs=(ANY,)*8,
        scratch_shapes=[pltpu.VMEM(s.shape,F32) for s in shapes+shapes[:1]]+[pltpu.SemaphoreType.DMA((8,))],
        compiler_params=pltpu.CompilerParams(vmem_limit_bytes=60*2**20),
        cost_estimate=pl.CostEstimate(flops=0,bytes_accessed=40*2**20,transcendentals=0))(
        lay,gin,gsk,skip,gq,um,uo,dm,do,om,oo)

from jax.sharding import Mesh, PartitionSpec as P
WIDE=("y","x"); ROWS=("z","core")
SWAP=[(0,1),(1,0)]

def swap_cores(values):
    return lax.ppermute(values,"core",SWAP)

def pick(values, index, axis):
    return lax.dynamic_index_in_dim(values,index,axis,keepdims=False)

def place_halves(mine, other, core, axis):
    first=jnp.where(core==0,mine,other); second=jnp.where(core==0,other,mine)
    return jnp.stack([first,second],axis=axis)

def dot(a,b): return jnp.dot(a,b,preferred_element_type=F32)

def norm(values):
    cen=values-jnp.mean(values,axis=1,keepdims=True)
    inv=lax.rsqrt(jnp.mean(cen*cen,axis=1,keepdims=True)+1e-5)
    return cen*inv,inv

def on_device(nw, block_input, long_skip, segment_ids, item_lengths, skip_weight, first_gain, first_shift, qkv_weight,
              out_weight, second_gain, second_shift, up_weight, down_weight, output_grad):
    core=lax.axis_index("core")
    _,tokens,d=block_input.shape
    heads=qkv_weight.shape[1]//(3*HEAD*nw); hd=heads*HEAD
    ff=up_weight.shape[1]; fb=ff//(2*nw)
    gather=lambda v: lax.all_gather(v,WIDE,axis=0,tiled=True)
    near=nw==4
    vecs=jnp.stack([first_gain,first_shift,second_gain,second_shift]+[first_gain]*4).astype(F32)
    if near:
        hidden,normed_all,qkv,w_heads,w_skip,vecs=first(block_input[0],long_skip[0],skip_weight,qkv_weight,vecs)
        vec=vecs.transpose(1,0,2).reshape(8,d)
        gain1,shift1,gain2,shift2=[vec[i:i+1] for i in range(4)]
        half=lambda v: lax.dynamic_slice_in_dim(v,core*(v.shape[0]//2),v.shape[0]//2)
        qkv,up_half,out_half=lax.optimization_barrier((qkv,half(up_weight),half(out_weight)))
        up_x,out_x=lax.ppermute((up_half,out_half),"x",SWAP)
        up_y,out_y=lax.ppermute((up_half,out_half),"y",SWAP)
    else:
        vec=gather(vecs.astype(BF).T).T.astype(F32)
        gain1,shift1,gain2,shift2=[vec[i:i+1] for i in range(4)]
        w_skip=gather(skip_weight)
        joined=jnp.concatenate([block_input[0],long_skip[0]],axis=1)
        w_heads=qkv_weight.reshape(d//nw,3,nw,hd).transpose(2,0,1,3)
        w_heads=lax.all_to_all(w_heads,WIDE,0,0).reshape(d,3*hd)
        hidden=dot(joined,w_skip)
        xhat1,inv1=norm(hidden)
        normed_all=gather((xhat1*gain1+shift1).astype(BF))
        qkv=dot(normed_all,w_heads).astype(BF)
    att,lse=attend(item_lengths,qkv,heads)
    if near:
        lay,gmid,gatt,gow,small,gup,gdn,sxu,sxd,syu,syd=middle(hidden,att,output_grad[0],gain2,shift2,out_weight,out_x,out_y,
            up_weight,up_x,up_y,down_weight)[:11]
    else:
        w_out=gather(out_weight)
        up_mine=gather(pick(up_weight.reshape(d//nw,nw,2,fb),core,2).reshape(d//nw,nw*fb))
        down_mine=gather(pick(down_weight.reshape(2,fb,d),core,0))
        up_other,down_other=swap_cores(up_mine),swap_cores(down_mine)
        att=lax.all_to_all(att.reshape(nw,tokens,hd),WIDE,0,0)
        lay,gmid,gatt,gow,small,gupo,guph,gdno,gdnh=mlp(hidden,att,w_out,gain2,shift2,output_grad[0],up_mine,up_other,down_mine,down_other)
        gatt=lax.all_to_all(gatt,WIDE,0,0)
    grad_heads=gatt.reshape(nw*tokens,hd)

    def scatter(mine,other):
        both=(mine.astype(F32)+swap_cores(other).astype(F32)).astype(BF)
        return lax.psum_scatter(both,WIDE,scatter_dimension=0,tiled=True)
    def both_cores(mine,axis):
        return place_halves(mine,swap_cores(mine),core,axis).astype(F32)
    def by_rows(grad):
        cut=grad.reshape(nw,2,-1,grad.shape[1])
        return scatter(pick(cut,core,1).reshape(-1,grad.shape[1]),pick(cut,1-core,1).reshape(-1,grad.shape[1]))
    if near:
        wide=2*lax.axis_index("y")+lax.axis_index("x")
        part=lambda v: lax.dynamic_index_in_dim(v.reshape(4,-1,v.shape[1]),wide,0,False)
        from_x=lax.ppermute((sxu,sxd),"x",SWAP)
        from_y=lax.ppermute((syu,syd),"y",SWAP)
        from_d=lax.ppermute(gow[1],WIDE,[(i,3-i) for i in range(4)])
    else:
        early=scatter(gupo,guph),scatter(gdno,gdnh),by_rows(gow)
    grad_qkv=attend_back(item_lengths,qkv,grad_heads,lse,heads)
    if near:
        grad_qkv,from_x,from_y,from_d=lax.optimization_barrier((grad_qkv,from_x,from_y,from_d))
        up_sum=part(gup).astype(F32)+from_x[0].astype(F32)+from_y[0].astype(F32)
        rows=gdn.shape[0]//4
        pair=from_x[1].astype(F32)+from_y[1].astype(F32)
        down_sum=part(gdn).astype(F32)+pair[:rows]
        out_sum=gow[0].astype(F32)+pair[rows:]+from_d.astype(F32)
        early=up_sum.astype(BF),down_sum.astype(BF),out_sum.astype(BF)
    grad_qkv,early=lax.optimization_barrier((grad_qkv,early))
    early=lax.psum(early,"z")
    if near:
        gin,gsk,smalls,gqkv,gskip=last(grad_qkv,w_heads,normed_all,hidden,gmid,gain1,block_input[0],long_skip[0],w_skip,small)
        gskip,early=lax.optimization_barrier((gskip,early))
        others=swap_cores(early)
        lay,gin,gsk,skip_share,qkv_share,up_share,down_share,out_share=assemble(lay,gin,gsk,gskip.reshape(-1,d),gqkv,
            early[0],others[0],early[1],others[1],early[2],others[2])
        up_share,down_share,out_share=up_share.reshape(-1,ff),down_share.reshape(-1,d),out_share.reshape(-1,d)
        smalls=lax.dynamic_slice_in_dim(smalls[:4],(2*lax.axis_index("y")+lax.axis_index("x"))*(d//nw),d//nw,axis=1).T
    else:
        part_first=nt(grad_qkv,w_heads).astype(BF)
        grad_first=lax.psum_scatter(part_first,WIDE,scatter_dimension=0,tiled=True).astype(F32)
        gqkv=tn(normed_all,grad_qkv).astype(BF).reshape(nw,2,d//nw//2,3*hd)
        gqkv=(pick(gqkv,core,1).astype(F32)+swap_cores(pick(gqkv,1-core,1)).astype(F32)).astype(BF)
        e1=grad_first*gain1
        across=inv1*(e1-jnp.mean(e1,axis=1,keepdims=True)-xhat1*jnp.mean(e1*xhat1,axis=1,keepdims=True))
        grad_hidden=(gmid+across).astype(BF)
        gskip=by_rows(tn(joined,grad_hidden).astype(BF))
        grad_joined=nt(grad_hidden,w_skip)
        gin,gsk=grad_joined[:,:d],grad_joined[:,d:]
        small1=jnp.stack([jnp.sum(grad_first*xhat1,axis=0),jnp.sum(grad_first,axis=0)])
        gqkv,gskip,early=lax.optimization_barrier((gqkv,gskip,early))
        gqkv,gskip=lax.psum((gqkv,gskip),"z")
        up_share=both_cores(early[0].reshape(d//nw,nw,fb),2).reshape(d//nw,ff)
        down_share=both_cores(early[1],0).reshape(ff//nw,d)
        out_share=both_cores(early[2],0).reshape(d//nw,d)
        skip_share=both_cores(gskip,0).reshape(2*d//nw,d)
        gqkv=lax.all_to_all(gqkv,WIDE,0,0).reshape(nw,-1,3,hd).transpose(1,2,0,3)
        qkv_share=both_cores(gqkv,0).reshape(d//nw,-1)
        smalls=jnp.stack([small1[0],small1[1],small[0],small[1]],axis=1)
        smalls=lax.psum(lax.psum_scatter(smalls.astype(BF),WIDE,scatter_dimension=0,tiled=True),ROWS).astype(F32)
    return (lay[None],gin[None],gsk[None],skip_share,smalls[:,0],smalls[:,1],qkv_share,out_share,
            smalls[:,2],smalls[:,3],up_share,down_share)

def solution(mesh):
    rows,wide=mesh.devices.shape
    side=2 if wide==4 else int(wide**0.5)
    grid=Mesh(mesh.devices.reshape(rows//2,2,wide//side,side),("z","core","y","x"))
    tok=P(ROWS,WIDE,None); row=P(ROWS,None); mat=P(WIDE,None); vec=P(WIDE)
    return jax.shard_map(functools.partial(on_device,wide),mesh=grid,
        in_specs=(tok,tok,row,row,mat,vec,vec,mat,mat,vec,vec,mat,mat,tok),
        out_specs=(tok,tok,tok,mat,vec,vec,mat,mat,vec,vec,mat,mat),check_vma=False)
```

```python
import functools
import jax, jax.numpy as jnp
from jax import lax
from jax.experimental import pallas as pl
from jax.experimental.pallas import tpu as pltpu
HEAD=72; SHORT=258; LONG=1026; NITEM=12
LOG2E=1.4426950408889634
SCALE=HEAD**-0.5
QT=384

def kwin(n): return (n + 29 + 31)//32*32
def qwin(n): return (n + 15 + QT-1)//QT*QT

def nt(a,b): return lax.dot_general(a,b,(((1,),(1,)),((),())),preferred_element_type=jnp.float32)
def nn(a,b): return lax.dot_general(a,b,(((1,),(0,)),((),())),preferred_element_type=jnp.float32)
def tn(a,b): return lax.dot_general(a,b,(((0,),(0,)),((),())),preferred_element_type=jnp.float32)

def windows(start, size, row_len):
    k0 = pl.multiple_of(jnp.minimum(start//16*16, row_len-kwin(size)),16)
    q0 = pl.multiple_of(jnp.minimum(start//16*16, row_len-qwin(size)),16)
    return k0,q0

def split_heads(src_ref, dst_ref, count, chunk=416):
    rows=src_ref.shape[0]
    @pl.loop(0, rows//chunk)
    def _(i):
        r=pl.ds(pl.multiple_of(i*chunk,16),chunk)
        block=src_ref[r,:]
        for j in range(count):
            dst_ref[j,r,:]=block[:,j*HEAD:(j+1)*HEAD]

def join_heads(src_ref, dst_ref, count, chunk=416):
    rows=dst_ref.shape[0]
    @pl.loop(0, rows//chunk)
    def _(i):
        r=pl.ds(pl.multiple_of(i*chunk,16),chunk)
        dst_ref[r,:]=jnp.concatenate([src_ref[j,r,:] for j in range(count)],axis=1)

def zero(ref, chunk=416):
    rows=ref.shape[1]
    @pl.loop(0, rows//chunk)
    def _(i):
        r=pl.ds(pl.multiple_of(i*chunk,16),chunk)
        for j in range(ref.shape[0]):
            ref[j,r,:]=jnp.zeros((chunk,ref.shape[2]),ref.dtype)

def for_items(len_ref, one):
    def step(i, start):
        size=len_ref[0,i]
        @pl.when(size==LONG)
        def _(): one(i,start,LONG)
        @pl.when(size==SHORT)
        def _(): one(i,start,SHORT)
        return start+size
    lax.fori_loop(0,len_ref.shape[1],step,jnp.int32(0))

def mask_edges(values, start, k0, size, fill):
    n=values.shape[0]; body=size//32*32
    off=start-k0
    top=lax.broadcasted_iota(jnp.int32,(32,values.shape[1]),0)
    low=jnp.where(top>=off,values[:32],fill)
    high=jnp.where(top+body<off+size,values[body:],fill)
    return jnp.concatenate([low,values[32:body],high],axis=0)

def attend_kernel(heads, len_ref, qkv_ref, out_ref, lse_ref, split_ref, acc_ref):
    row_len=qkv_ref.shape[0]
    split_heads(qkv_ref, split_ref, 3*heads)
    zero(acc_ref)
    lse_ref[...]=jnp.zeros_like(lse_ref)
    def one(item,start,size):
        k0,q0=windows(start,size,row_len)
        kr=pl.ds(k0,kwin(size))
        @pl.loop(0,qwin(size)//QT)
        def _(t):
            qr=pl.ds(pl.multiple_of(q0+t*QT,16),QT)
            col=q0+t*QT+lax.broadcasted_iota(jnp.int32,(1,QT),1)
            live=(col>=start)&(col<start+size)
            for h in range(heads):
                s=nt(split_ref[heads+h,kr,:],split_ref[h,qr,:])
                s=mask_edges(s,start,k0,size,-1e30)
                m=jnp.max(s,axis=0,keepdims=True)
                p=jnp.exp2((s-m)*(SCALE*LOG2E))
                l=jnp.sum(p,axis=0,keepdims=True)
                o=tn(split_ref[2*heads+h,kr,:],p.astype(jnp.bfloat16))
                o=jnp.where(live,o/l,0.0)
                acc_ref[h,qr,:]+=o.T.astype(jnp.bfloat16)
                lse_ref[item,pl.ds(t*heads+h,1),:]=m*(SCALE*LOG2E)+jnp.log2(l)
    for_items(len_ref,one)
    join_heads(acc_ref,out_ref,heads)

def attend_back_kernel(heads, len_ref, qkv_ref, grad_ref, lse_ref, out_ref, split_ref, gsplit_ref, acc_ref, dk_ref, dv_ref):
    row_len=qkv_ref.shape[0]
    split_heads(qkv_ref, split_ref, 3*heads)
    split_heads(grad_ref, gsplit_ref, heads)
    zero(acc_ref)
    def one(item,start,size):
        k0,q0=windows(start,size,row_len)
        kw=kwin(size)
        kr=pl.ds(k0,kw)
        for h in range(heads):
            dk_ref[h,:kw,:]=jnp.zeros((kw,HEAD),jnp.float32)
            dv_ref[h,:kw,:]=jnp.zeros((kw,HEAD),jnp.float32)
        @pl.loop(0,qwin(size)//QT)
        def _(t):
            qr=pl.ds(pl.multiple_of(q0+t*QT,16),QT)
            col=q0+t*QT+lax.broadcasted_iota(jnp.int32,(1,QT),1)
            live=(col>=start)&(col<start+size)
            for h in range(heads):
                k=split_ref[heads+h,kr,:]; q=split_ref[h,qr,:]; g=gsplit_ref[h,qr,:]
                lse=jnp.where(live,lse_ref[item,pl.ds(t*heads+h,1),:],1e30)
                s=nt(k,q)
                p=jnp.exp2(s*(SCALE*LOG2E)-lse)
                p=mask_edges(p,start,k0,size,0.0)
                dv_ref[h,:kw,:]+=nn(p.astype(jnp.bfloat16),g)
                dp=nt(split_ref[2*heads+h,kr,:],g)
                delta=jnp.sum(p*dp,axis=0,keepdims=True)
                ds=(p*(dp-delta)).astype(jnp.bfloat16)
                dk_ref[h,:kw,:]+=nn(ds,q)
                dq=tn(k,ds)*SCALE
                acc_ref[h,qr,:]+=dq.T.astype(jnp.bfloat16)
        for h in range(heads):
            acc_ref[heads+h,kr,:]+=(dk_ref[h,:kw,:]*SCALE).astype(jnp.bfloat16)
            acc_ref[2*heads+h,kr,:]+=dv_ref[h,:kw,:].astype(jnp.bfloat16)
    for_items(len_ref,one)
    join_heads(acc_ref,out_ref,3*heads)

VM=pl.BlockSpec(memory_space=pltpu.VMEM); SM=pl.BlockSpec(memory_space=pltpu.SMEM)
def attend(lens,qkv,heads):
    n=qkv.shape[0]
    nt_=heads*(qwin(LONG)//QT)
    return pl.pallas_call(functools.partial(attend_kernel,heads),
      out_shape=(jax.ShapeDtypeStruct((n,heads*HEAD),jnp.bfloat16),jax.ShapeDtypeStruct((NITEM,nt_,QT),jnp.float32)),
      in_specs=[SM,VM],out_specs=(VM,VM),
      scratch_shapes=[pltpu.VMEM((3*heads,n,HEAD),jnp.bfloat16),pltpu.VMEM((heads,n,HEAD),jnp.bfloat16)],
      compiler_params=pltpu.CompilerParams(vmem_limit_bytes=56*2**20),
      cost_estimate=pl.CostEstimate(flops=heads*n*n*HEAD*4,bytes_accessed=12*2**20,transcendentals=heads*n*n//3))(lens,qkv)
def attend_back(lens,qkv,grad,lse,heads):
    n=qkv.shape[0]
    return pl.pallas_call(functools.partial(attend_back_kernel,heads),
      out_shape=jax.ShapeDtypeStruct((n,3*heads*HEAD),jnp.bfloat16),
      in_specs=[SM,VM,VM,VM],out_specs=VM,
      scratch_shapes=[pltpu.VMEM((3*heads,n,HEAD),jnp.bfloat16),pltpu.VMEM((heads,n,HEAD),jnp.bfloat16),pltpu.VMEM((3*heads,n,HEAD),jnp.bfloat16),
        pltpu.VMEM((heads,kwin(LONG),HEAD),jnp.float32),pltpu.VMEM((heads,kwin(LONG),HEAD),jnp.float32)],
      compiler_params=pltpu.CompilerParams(vmem_limit_bytes=60*2**20),
      cost_estimate=pl.CostEstimate(flops=heads*n*n*HEAD*10,bytes_accessed=20*2**20,transcendentals=heads*n*n//3))(lens,qkv,grad,lse)


F32=jnp.float32; BF=jnp.bfloat16
ANY=pl.BlockSpec(memory_space=pl.ANY)

def gelu_parts(u):
    z=jnp.exp2(u*u*(-0.5*1.4426950408889634))
    t=1.0/(1.0+(0.3275911*0.7071067811865476)*jnp.abs(u))
    poly=((((1.061405429*t-1.453152027)*t+1.421413741)*t-0.284496736)*t+0.254829592)*t
    tail=0.5*poly*z
    cdf=jnp.where(u>=0,1.0-tail,tail)
    return u*cdf, cdf+u*(z*0.3989422804014327)

def mlp_kernel(tile, hidden_ref, att_ref, outw_ref, gain_ref, shift_ref, g_ref, upo_ref, uph_ref, dno_ref, dnh_ref,
               lay_ref, gmid_ref, gatt_ref, gow_ref, small_ref, gupo_ref, guph_ref, gdno_ref, gdnh_ref,
               att_s, n2_s, xhat_s, rstd_s, act_s, gu_s, upb, dnb, gub, gdb, in_sem, out_sem):
    parts,tokens,cols=att_ref.shape
    d=hidden_ref.shape[1]
    tc=tokens//2 if tokens>416 else tokens
    nch=tokens//tc
    half=upo_ref.shape[1]; steps=half//tile
    cc=d//3; fc=256

    def fetch(j,act):
        slot=lax.rem(j,2)
        for first,(us,ds) in ((True,(uph_ref,dnh_ref)),(False,(upo_ref,dno_ref))):
            cond=(j<steps) if first else (j>=steps)
            @pl.when(cond)
            def _():
                k=j if first else j-steps
                off=pl.multiple_of(k*tile,tile)
                act(pltpu.make_async_copy(us.at[:,pl.ds(off,tile)],upb.at[slot],in_sem.at[slot,0]))
                act(pltpu.make_async_copy(ds.at[pl.ds(off,tile),:],dnb.at[slot],in_sem.at[slot,1]))
    def flush(j,act):
        slot=lax.rem(j,2)
        for first,(us,ds) in ((True,(guph_ref,gdnh_ref)),(False,(gupo_ref,gdno_ref))):
            cond=(j<steps) if first else (j>=steps)
            @pl.when(cond)
            def _():
                k=j if first else j-steps
                off=pl.multiple_of(k*tile,tile)
                act(pltpu.make_async_copy(gub.at[slot],us.at[:,pl.ds(off,tile)],out_sem.at[slot,0]))
                act(pltpu.make_async_copy(gdb.at[slot],ds.at[pl.ds(off,tile),:],out_sem.at[slot,1]))
    start=lambda c: c.start()
    wait=lambda c: c.wait()
    fetch(jnp.int32(0),start)
    gain=gain_ref[...]; shift=shift_ref[...]
    sub=tc//2
    @pl.loop(0,2*nch)
    def _(i):
        r=pl.ds(pl.multiple_of(i*sub,16),sub)
        joined=jnp.concatenate([att_ref[p,r,:] for p in range(parts)],axis=1)
        att_s[r,:]=joined
        mid=hidden_ref[r,:]+nn(joined,outw_ref[...])
        lay_ref[r,:]=mid
        cen=mid-jnp.mean(mid,axis=1,keepdims=True)
        inv=lax.rsqrt(jnp.mean(cen*cen,axis=1,keepdims=True)+1e-5)
        xhat=cen*inv
        xhat_s[r,:]=xhat
        rstd_s[r,:]=jnp.broadcast_to(inv,(sub,128))
        n2_s[r,:]=(xhat*gain+shift).astype(BF)
        gmid_ref[r,:]=jnp.zeros((sub,d),F32)
    @pl.loop(0,2*steps)
    def _(j):
        slot=lax.rem(j,2)
        @pl.when(j+1<2*steps)
        def _(): fetch(j+1,start)
        fetch(j,wait)
        @pl.when(j>=2)
        def _(): flush(j-2,wait)
        @pl.loop(0,nch)
        def _(i):
            r=pl.ds(pl.multiple_of(i*tc,16),tc)
            for k in range(tile//fc):
                f=pl.ds(k*fc,fc)
                u=nn(n2_s[r,:],upb[slot,:,f])
                a,dg=gelu_parts(u)
                act_s[r,f]=a.astype(BF)
                ga=nt(g_ref[r,:],dnb[slot,f,:])
                gu_s[r,f]=(ga*dg).astype(BF)
        @pl.loop(0,nch)
        def _(i):
            r=pl.ds(pl.multiple_of(i*tc,16),tc)
            for k in range(3):
                cr=pl.ds(k*cc,cc)
                lay_ref[r,cr]+=nn(act_s[r,:],dnb[slot,:,cr])
                gmid_ref[r,cr]+=nt(gu_s[r,:],upb[slot,cr,:])
        for k in range(tile//fc):
            f=pl.ds(k*fc,fc)
            gdb[slot,f,:]=tn(act_s[:,f],g_ref[...]).astype(BF)
        for k in range(3):
            cr=pl.ds(k*cc,cc)
            gub[slot,cr,:]=tn(n2_s[:,cr],gu_s[...]).astype(BF)
        flush(j,start)
    small_ref[...]=jnp.zeros_like(small_ref)
    @pl.loop(0,2*nch)
    def _(i):
        r=pl.ds(pl.multiple_of(i*sub,16),sub)
        gs=gmid_ref[r,:]; xhat=xhat_s[r,:]
        small_ref[0:1,:]+=jnp.sum(gs*xhat,axis=0,keepdims=True)
        small_ref[1:2,:]+=jnp.sum(gs,axis=0,keepdims=True)
        e=gs*gain
        back=e-jnp.mean(e,axis=1,keepdims=True)-xhat*jnp.mean(e*xhat,axis=1,keepdims=True)
        gm=g_ref[r,:].astype(F32)+back*rstd_s[r,0:1]
        gmid_ref[r,:]=gm
        low=gm.astype(BF)
        n2_s[r,:]=low
        ga=nt(low,outw_ref[...]).astype(BF)
        for p in range(parts):
            gatt_ref[p,r,:]=ga[:,p*cols:(p+1)*cols]
    for k in range(3):
        cr=pl.ds(k*cc,cc)
        gow_ref[cr,:]=tn(att_s[:,cr],n2_s[...]).astype(BF)
    flush(jnp.int32(2*steps-2),wait)
    flush(jnp.int32(2*steps-1),wait)

def mlp(hidden,att,outw,gain,shift,g,upo,uph,dno,dnh):
    tokens,d=hidden.shape; half=upo.shape[1]; tile=half//3
    S=jax.ShapeDtypeStruct
    flops=2*tokens*d*(half*2*6+d*3)
    return pl.pallas_call(functools.partial(mlp_kernel,tile),
        out_shape=(S((tokens,d),F32),S((tokens,d),F32),S(att.shape,BF),S((d,d),BF),S((8,d),F32),
                   S(upo.shape,BF),S(upo.shape,BF),S(dno.shape,BF),S(dno.shape,BF)),
        in_specs=[VM]*6+[ANY]*4,
        out_specs=(VM,)*5+(ANY,)*4,
        scratch_shapes=[pltpu.VMEM((tokens,d),BF),pltpu.VMEM((tokens,d),BF),pltpu.VMEM((tokens,d),F32),pltpu.VMEM((tokens,128),F32),
            pltpu.VMEM((tokens,tile),BF),pltpu.VMEM((tokens,tile),BF),
            pltpu.VMEM((2,d,tile),BF),pltpu.VMEM((2,tile,d),BF),pltpu.VMEM((2,d,tile),BF),pltpu.VMEM((2,tile,d),BF),
            pltpu.SemaphoreType.DMA((2,2)),pltpu.SemaphoreType.DMA((2,2))],
        compiler_params=pltpu.CompilerParams(vmem_limit_bytes=62*2**20),
        cost_estimate=pl.CostEstimate(flops=flops,bytes_accessed=60*2**20,transcendentals=tokens*half*2))(
        hidden,att,outw,gain,shift,g,upo,uph,dno,dnh)


MESH=pl.DeviceIdType.MESH

def place():
    x,y,c=lax.axis_index("x"),lax.axis_index("y"),lax.axis_index("core")
    return x,y,c,2*y+x,2*y+1-x,2-2*y+x,3-2*y-x

class Links:
    def __init__(self,send,recv):
        self.send,self.recv,self.sent=send,recv,[]
        x,y,c=lax.axis_index("x"),lax.axis_index("y"),lax.axis_index("core")
        self.to={"X":{"x":1-x},"Y":{"y":1-y},"D":{"x":1-x,"y":1-y},"C":{"core":1-c}}
    def meet(self,who):
        barrier=pltpu.get_barrier_semaphore()
        for t in who:
            pl.semaphore_signal(barrier,inc=1,device_id=self.to[t],device_id_type=MESH)
        pl.semaphore_wait(barrier,len(who))
    def start(self,k,t,src,dst):
        copy=pltpu.make_async_remote_copy(src_ref=src,dst_ref=dst,send_sem=self.send.at[k],recv_sem=self.recv.at[k],
                                          device_id=self.to[t],device_id_type=MESH)
        copy.start()
        self.sent.append(copy)
    def got(self,k,t,dst):
        pltpu.make_async_remote_copy(src_ref=dst,dst_ref=dst,send_sem=self.send.at[k],recv_sem=self.recv.at[k],
                                     device_id=self.to[t],device_id_type=MESH).wait_recv()
    def finish(self):
        for copy in self.sent: copy.wait_send()

def first_kernel(block_ref,long_ref,skip_ref,qkvw_ref,vec_ref,
                 hidden_out,normed_out,qkv_out,heads_out,wskip_out,vec_out,
                 ws,ns,hs,piece,hid,qs,vs,send,recv,local):
    x,y,c,w,wx,wy,wd=place()
    tokens,d=block_ref.shape
    sr=skip_ref.shape[0]; half=sr//2; part=half//2
    kr=qkvw_ref.shape[0]; kh=kr//2; hd=qkvw_ref.shape[1]//12
    tc=tokens//4
    mul=pl.multiple_of
    net=Links(send,recv)
    net.meet("XYDC")
    def srows(b,core,p): return pl.ds(mul(b*sr+core*half+p*part,16),part)
    def mine(p): return pl.ds(mul(c*half+p*part,16),part)
    net.start(0,"X",skip_ref.at[mine(0)],ws.at[srows(w,c,0)])
    net.start(2,"Y",skip_ref.at[mine(1)],ws.at[srows(w,c,1)])
    net.start(1,"X",skip_ref.at[mine(1)],ws.at[srows(w,c,1)])
    net.start(3,"Y",skip_ref.at[mine(0)],ws.at[srows(w,c,0)])
    own=pltpu.make_async_copy(skip_ref,ws.at[pl.ds(mul(w*sr,16),sr)],local.at[0])
    own.start()
    for k,t in ((30,"X"),(31,"Y"),(32,"D")): net.start(k,t,vec_ref,vs.at[w])
    vs[w]=vec_ref[...]
    for p in range(4):
        piece[p]=jnp.concatenate([qkvw_ref[:,(s*4+p)*hd:(s*4+p+1)*hd] for s in range(3)],axis=1)
    own_heads=pltpu.make_async_copy(piece.at[w],hs.at[pl.ds(mul(w*kr,16),kr)],local.at[1])
    own_heads.start()
    def pass_on(k,t,b,p,onward):
        r=srows(b,c,p)
        net.got(k,t,ws.at[r])
        for k2,t2 in onward: net.start(k2,t2,ws.at[r],ws.at[r])
    pass_on(0,"X",wx,0,((4,"Y"),(6,"C")))
    pass_on(2,"Y",wy,1,((5,"X"),(7,"C")))
    pass_on(1,"X",wx,1,((8,"C"),))
    pass_on(3,"Y",wy,0,((9,"C"),))
    def hrows(b,core): return pl.ds(mul(b*kr+core*kh,16),kh)
    cut=pl.ds(mul(c*kh,16),kh)
    net.start(12,"X",piece.at[wx,cut],hs.at[hrows(w,c)])
    net.start(13,"Y",piece.at[wy,cut],hs.at[hrows(w,c)])
    net.start(14,"D",piece.at[wd,cut],hs.at[hrows(w,c)])
    own.wait()
    net.got(6,"C",ws.at[srows(wx,1-c,0)])
    net.got(8,"C",ws.at[srows(wx,1-c,1)])
    near=pl.ds(mul(y*d,16),d); far=pl.ds(mul((1-y)*d,16),d)
    def tok(i): return pl.ds(mul(i*tc,16),tc)
    @pl.loop(0,4)
    def _(i):
        lhs=jnp.where(y==0,block_ref[tok(i),:],long_ref[tok(i),:])
        hid[tok(i),:]=nn(lhs,ws[near,:])
    pass_on(4,"Y",wd,0,((10,"C"),))
    pass_on(5,"X",wd,1,((11,"C"),))
    net.got(7,"C",ws.at[srows(wy,1-c,1)])
    net.got(9,"C",ws.at[srows(wy,1-c,0)])
    net.got(10,"C",ws.at[srows(wd,1-c,0)])
    net.got(11,"C",ws.at[srows(wd,1-c,1)])
    for k,t,b in ((30,"X",wx),(31,"Y",wy),(32,"D",wd)): net.got(k,t,vs.at[b])
    gain=jnp.concatenate([vs[p,0:1,:] for p in range(4)],axis=1)
    shift=jnp.concatenate([vs[p,1:2,:] for p in range(4)],axis=1)
    def nrows(b,i): return pl.ds(mul(b*tokens+i*tc,16),tc)
    def spread(i,t):
        net.start((18 if t=="X" else 22)+i,t,ns.at[nrows(w,i)],ns.at[nrows(w,i)])
    for i in range(4):
        r=tok(i)
        lhs=jnp.where(y==0,long_ref[r,:],block_ref[r,:])
        h=hid[r,:]+nn(lhs,ws[far,:])
        hid[r,:]=h
        cen=h-jnp.mean(h,axis=1,keepdims=True)
        inv=lax.rsqrt(jnp.mean(cen*cen,axis=1,keepdims=True)+1e-5)
        ns[nrows(w,i),:]=(cen*inv*gain+shift).astype(BF)
        spread(i,"XYXY"[i])
    for i,t in ((1,"X"),(0,"Y"),(3,"X"),(2,"Y")): spread(i,t)
    outs=[]
    def put(k,src,dst):
        copy=pltpu.make_async_copy(src,dst,local.at[k]); copy.start(); outs.append(copy)
    put(2,ws,wskip_out); put(3,hid,hidden_out); put(7,vs,vec_out)
    for j,(t,b) in enumerate((("X",wx),("Y",wy),("D",wd))):
        net.got(12+j,t,hs.at[hrows(b,c)])
        net.start(15+j,"C",hs.at[hrows(b,c)],hs.at[hrows(b,c)])
    for j,b in enumerate((wx,wy,wd)):
        net.got(15+j,"C",hs.at[hrows(b,1-c)])
    own_heads.wait()
    put(4,hs,heads_out)
    def project(b,i): qs[nrows(b,i),:]=nn(ns[nrows(b,i),:],hs[...]).astype(BF)
    @pl.loop(0,4)
    def _(i): project(w,i)
    for i,t,b,k,k2,t2 in ((0,"X",wx,18,26,"Y"),(1,"Y",wy,22,27,"X"),(2,"X",wx,18,28,"Y"),(3,"Y",wy,22,29,"X")):
        net.got(k+i,t,ns.at[nrows(b,i)])
        net.start(k2,t2,ns.at[nrows(b,i)],ns.at[nrows(b,i)])
    @pl.loop(0,2)
    def _(i): project(wx,2*i)
    @pl.loop(0,2)
    def _(i): project(wy,2*i+1)
    for i in (1,3):
        net.got(18+i,"X",ns.at[nrows(wx,i)])
        project(wx,i)
        net.got(22+i-1,"Y",ns.at[nrows(wy,i-1)])
        project(wy,i-1)
    for i,t,k in ((0,"Y",26),(1,"X",27),(2,"Y",28),(3,"X",29)):
        net.got(k,t,ns.at[nrows(wd,i)])
        project(wd,i)
    put(5,ns,normed_out); put(6,qs,qkv_out)
    for copy in outs: copy.wait()
    net.finish()

def first(block,long,skipw,qkvw,vecs):
    tokens,d=block.shape; S=jax.ShapeDtypeStruct; hd3=qkvw.shape[1]//4
    V=pltpu.VMEM
    return pl.pallas_call(first_kernel,
        out_shape=(S((tokens,d),F32),S((4*tokens,d),BF),S((4*tokens,hd3),BF),S((d,hd3),BF),S((2*d,d),BF),S((4,)+vecs.shape,F32)),
        in_specs=[VM]*5,out_specs=(ANY,)*6,
        scratch_shapes=[V((2*d,d),BF),V((4*tokens,d),BF),V((d,hd3),BF),V((4,d//4,hd3),BF),V((tokens,d),F32),V((4*tokens,hd3),BF),V((4,)+vecs.shape,F32),
            pltpu.SemaphoreType.DMA((33,)),pltpu.SemaphoreType.DMA((33,)),pltpu.SemaphoreType.DMA((8,))],
        compiler_params=pltpu.CompilerParams(vmem_limit_bytes=56*2**20,collective_id=0,has_side_effects=True),
        cost_estimate=pl.CostEstimate(flops=2*tokens*d*d*5,bytes_accessed=40*2**20,transcendentals=0))(
        block,long,skipw,qkvw,vecs)

class Chain:
    def __init__(self,net,k,own,up_in,down_in):
        self.net,self.k,self.own=net,k,own
        self.up_in,self.down_in=up_in,down_in
        self.z,self.n=lax.axis_index("z"),lax.axis_size("z")
    def copy(self,up,src):
        k=self.k+(0 if up else 1)
        return pltpu.make_async_remote_copy(src_ref=src,dst_ref=self.up_in if up else self.down_in,
            send_sem=self.net.send.at[k],recv_sem=self.net.recv.at[k],
            device_id={"z":self.z+1 if up else self.z-1},device_id_type=MESH)
    def hop(self,h):
        for up in (True,False):
            inn,other=(self.up_in,self.down_in) if up else (self.down_in,self.up_in)
            last_one=self.n-1-h<h or (self.n-1-h==h and not up)
            @pl.when(self.z==(h if up else self.n-1-h))
            def _():
                if h==0:
                    self.copy(up,self.own).start()
                else:
                    self.copy(up,inn).wait_recv()
                    mine,came=self.own[...].astype(F32),inn[...].astype(F32)
                    inn[...]=(mine+came).astype(inn.dtype)
                    if last_one:
                        self.own[...]=(other[...].astype(F32)+came).astype(self.own.dtype)
                    self.copy(up,inn).start()
    def total(self):
        first,final=self.z==0,self.z==self.n-1
        for end,up,inn in ((first,True,self.down_in),(final,False,self.up_in)):
            @pl.when(end)
            def _():
                self.copy(not up,inn).wait_recv()
                self.copy(up,self.own).wait_send()
                self.own[...]=(self.own[...].astype(F32)+inn[...].astype(F32)).astype(self.own.dtype)
        @pl.when(jnp.logical_not(first|final))
        def _():
            self.copy(True,self.up_in).wait_send()
            self.copy(False,self.down_in).wait_send()

def meet_all(net,who):
    z,n=lax.axis_index("z"),lax.axis_size("z")
    barrier=pltpu.get_barrier_semaphore()
    for t in who:
        pl.semaphore_signal(barrier,inc=1,device_id=net.to[t],device_id_type=MESH)
    @pl.when(z>0)
    def _(): pl.semaphore_signal(barrier,inc=1,device_id={"z":z-1},device_id_type=MESH)
    @pl.when(z<n-1)
    def _(): pl.semaphore_signal(barrier,inc=1,device_id={"z":z+1},device_id_type=MESH)
    ends=(z==0)|(z==n-1)
    @pl.when(ends)
    def _(): pl.semaphore_wait(barrier,len(who)+1)
    @pl.when(jnp.logical_not(ends))
    def _(): pl.semaphore_wait(barrier,len(who)+2)

SEG=3
def last_kernel(gq_ref,heads_ref,normed_ref,hidden_ref,gmid_ref,gain_ref,block_ref,long_ref,wskip_ref,small_ref,eu_ref,ed_ref,eo_ref,
                gin_out,gsk_out,small_out,gqkv_out,gskip_out,early_out,late_out,
                big,part,rx,ry,dx,dy,gw,gwr,gsr,qz,fq,sdx,sdy,srx,sry,own,sz,fs,sm,sin,smz,es,eup,edown,hg,send,recv,local,esem,hsem):
    x,y,c,w,wx,wy,wd=place()
    tokens,d=block_ref.shape
    tc=tokens//4; kr=d//4; kh=kr//2; sr=d//2; sh=sr//2; sq=sh//2
    mul=pl.multiple_of
    net=Links(send,recv)
    load=pltpu.make_async_copy(normed_ref,big,local.at[0])
    load.start()
    eseg=[pl.ds(i*kh,kh) for i in range(9)]
    eload=[pltpu.make_async_copy(eu_ref.at[:,pl.ds(i*d,d)] if i<4 else ed_ref.at[pl.ds((i-4)*kh,kh)] if i<8 else eo_ref,es.at[eseg[i]],esem.at[i]) for i in range(9)]
    for copy in eload: copy.start()
    ford=(0,2,1,3)
    def stream(j):
        r=pl.ds(ford[j]*tc,tc)
        return [pltpu.make_async_copy(ref.at[r],hg.at[j%2,m],hsem.at[j%2,m]) for m,ref in enumerate((hidden_ref,gmid_ref))]
    for j in range(2):
        for copy in stream(j): copy.start()
    meet_all(net,"XYDC")
    def tok(i): return pl.ds(i*tc,tc)
    early=[Chain(net,56+2*i,es.at[r],eup.at[r],edown.at[r]) for i,r in enumerate(eseg)]
    for copy in eload: copy.wait()
    halves=[pl.ds(i*2*kh,2*kh) for i in range(2)]
    mids=[Chain(net,40+2*i,gwr.at[r],qz.at[0,r],qz.at[1,r]) for i,r in enumerate(halves)]
    queue=early[:3]+mids+early[3:]
    for chain in queue[:3]: chain.hop(0)
    def tick(i):
        for h in range(1,lax.axis_size("z")-1):
            if 0<=i-h+1<len(queue): queue[i-h+1].hop(h)
    def pr(s,i): return pl.ds(s*tokens+i*tc,tc)
    def partial(b,i):
        return nt(gq_ref[pl.ds(mul(b*tokens+i*tc,16),tc),:],heads_ref[...])
    for i,t,dst,k in ((0,"X",dx,0),(2,"Y",dy,2),(1,"X",dx,1),(3,"Y",dy,3)):
        part[pr(2,i),:]=partial(wd,i).astype(BF)
        net.start(k,t,part.at[pr(2,i)],dst.at[tok(i%2)])
    for i,t,b,dst,k in ((0,"X",wx,rx,4),(2,"Y",wy,ry,10),(1,"X",wx,rx,5),(3,"Y",wy,ry,11)):
        s=0 if t=="X" else 1
        part[pr(s,i),:]=partial(b,i).astype(BF)
        net.start(k,t,part.at[pr(s,i)],dst.at[tok(i)])
    @pl.loop(0,4)
    def _(i):
        r=pl.ds(mul(i*tc,16),tc)
        part[pl.ds(mul(3*tokens+i*tc,16),tc),:]=nt(gq_ref[pl.ds(mul(w*tokens+i*tc,16),tc),:],heads_ref[...]).astype(BF)
    load.wait()
    cc=d//3
    def weight_grad(k):
        cr=pl.ds(k*cc,cc)
        gw[cr,:]=tn(big[:,cr],gq_ref[...]).astype(BF)
    def relay(i,t,b,dst,k,src,k2,t2):
        s=0 if t=="X" else 1
        mine=partial(b,i)
        net.got(k2,t2,src.at[tok(i%2)])
        part[pr(s,i),:]=(mine+src[tok(i%2),:].astype(F32)).astype(BF)
        net.start(k,t,part.at[pr(s,i)],dst.at[tok(i)])
    weight_grad(0)
    relay(2,"X",wx,rx,6,dy,2,"Y")
    relay(0,"Y",wy,ry,8,dx,0,"X")
    weight_grad(1)
    tick(0)
    weight_grad(2)
    def rows(b,core): return pl.ds(mul(b*kr+core*kh,16),kh)
    for b in range(4):
        net.start(12+b,"C",gw.at[rows(b,1-c)],gwr.at[pl.ds(b*kh,kh)])
    relay(3,"X",wx,rx,7,dy,3,"Y")
    tick(1)
    relay(1,"Y",wy,ry,9,dx,1,"X")
    tick(2)
    for b in range(4):
        r=pl.ds(b*kh,kh)
        net.got(12+b,"C",gwr.at[r])
        gwr[r,:]=(gwr[r,:].astype(F32)+gw[rows(b,c),:].astype(F32)).astype(BF)
    for chain in queue[3:]: chain.hop(0)
    gain=gain_ref[...]
    sm[...]=jnp.zeros_like(sm)
    for j,i in enumerate(ford):
        r=tok(i)
        tick(3+j)
        for copy in stream(j): copy.wait()
        net.got(4+i,"X",rx.at[r])
        net.got(8+i,"Y",ry.at[r])
        gf=part[pr(3,i),:].astype(F32)+rx[r,:].astype(F32)+ry[r,:].astype(F32)
        h=hg[j%2,0]
        cen=h-jnp.mean(h,axis=1,keepdims=True)
        inv=lax.rsqrt(jnp.mean(cen*cen,axis=1,keepdims=True)+1e-5)
        xhat=cen*inv
        sm[0:1,:]+=jnp.sum(gf*xhat,axis=0,keepdims=True)
        sm[1:2,:]+=jnp.sum(gf,axis=0,keepdims=True)
        e=gf*gain
        back=e-jnp.mean(e,axis=1,keepdims=True)-xhat*jnp.mean(e*xhat,axis=1,keepdims=True)
        big[pl.ds(2*d+i*tc,tc),:]=(hg[j%2,1]+back*inv).astype(BF)
        if j<2:
            for copy in stream(j+2): copy.start()
    sm[2:4,:]=small_ref[0:2,:]
    lates=[pltpu.make_async_copy(block_ref,rx,local.at[2]),pltpu.make_async_copy(long_ref,ry,local.at[3])]
    for copy in lates: copy.start()
    tick(7)
    for chain in mids: chain.total()
    def qrows(b): return pl.ds(mul(b*kh,16),kh)
    for j,(t,b) in enumerate((("X",wx),("Y",wy),("D",wd))):
        net.start(29+j,t,gwr.at[qrows(b)],fq.at[w,c])
    fq[w,c]=gwr[qrows(w),:]
    for copy in lates: copy.wait()
    for k in range(6):
        src=rx if k<3 else ry
        big[pl.ds(k*cc,cc),:]=tn(src[:,(k%3)*cc:(k%3+1)*cc],big[2*d:2*d+tokens,:]).astype(BF)
    def srows(b,core): return pl.ds(mul(b*sr+core*sh,16),sh)
    for b in range(4):
        net.start(16+b,"C",big.at[srows(b,1-c)],gsr.at[pl.ds(b*sh,sh)])
    net.start(20,"C",sm,sin.at[0])
    tick(8)
    for copy in net.sent[:16]: copy.wait_send()
    net.sent=net.sent[16:]
    wload=pltpu.make_async_copy(wskip_ref,part.at[pl.ds(0,2*d)],local.at[1])
    wload.start()
    for b in range(4):
        r=pl.ds(b*sh,sh)
        net.got(16+b,"C",gsr.at[r])
        gsr[r,:]=(gsr[r,:].astype(F32)+big[srows(b,c),:].astype(F32)).astype(BF)
    def quarter(b,i): return pl.ds(mul(b*sh+i*sq,16),sq)
    top,low=pl.ds(0,sq),pl.ds(sq,sq)
    net.start(21,"X",gsr.at[quarter(wd,0)],sdx)
    net.start(22,"Y",gsr.at[quarter(wd,1)],sdy)
    net.start(23,"X",gsr.at[quarter(wx,0)],srx.at[top])
    net.start(24,"Y",gsr.at[quarter(wy,1)],sry.at[low])
    tick(9)
    net.got(20,"C",sin.at[0])
    smz[6]=sm[...]+sin[0]
    net.start(27,"X",smz.at[6],sin.at[1])
    wload.wait()
    @pl.loop(0,4)
    def _(i):
        r=pl.ds(mul(i*tc,16),tc)
        gh=big[pl.ds(mul(2*d+i*tc,16),tc),:]
        rx[r,:]=nt(gh,part[:d,:]).astype(BF)
        ry[r,:]=nt(gh,part[d:2*d,:]).astype(BF)
    outs=[]
    def put(k,src,dst):
        copy=pltpu.make_async_copy(src,dst,local.at[k]); copy.start(); outs.append(copy)
    put(2,rx,gin_out); put(3,ry,gsk_out)
    tick(10)
    net.got(21,"X",sdx)
    gsr[quarter(wy,0),:]=(gsr[quarter(wy,0),:].astype(F32)+sdx[...].astype(F32)).astype(BF)
    net.start(25,"Y",gsr.at[quarter(wy,0)],sry.at[top])
    net.got(22,"Y",sdy)
    gsr[quarter(wx,1),:]=(gsr[quarter(wx,1),:].astype(F32)+sdy[...].astype(F32)).astype(BF)
    net.start(26,"X",gsr.at[quarter(wx,1)],srx.at[low])
    for i in range(11,len(queue)+lax.axis_size("z")-3): tick(i)
    net.got(27,"X",sin.at[1])
    smz[0]=smz[6]+sin[1]
    net.start(28,"Y",smz.at[0],sin.at[2])
    for j,(t,b) in enumerate((("X",wx),("Y",wy),("D",wd))):
        net.got(29+j,t,fq.at[b,c])
    for b in range(4):
        net.start(32+b,"C",fq.at[b,c],fq.at[b,c])
    net.got(28,"Y",sin.at[2])
    smz[1]=smz[0]+sin[2]
    net.got(23,"X",srx.at[top]); net.got(25,"Y",sry.at[top])
    net.got(24,"Y",sry.at[low]); net.got(26,"X",srx.at[low])
    own[...]=(gsr[pl.ds(mul(w*sh,16),sh),:].astype(F32)+srx[...].astype(F32)+sry[...].astype(F32)).astype(BF)
    seg=sh//SEG
    chains=[Chain(net,44,smz.at[1],smz.at[2],smz.at[3])]
    for i in range(SEG):
        r=pl.ds(i*seg,seg)
        chains.append(Chain(net,46+2*i,own.at[r],sz.at[0,r],sz.at[1,r]))
    for h in range(lax.axis_size("z")-1):
        for chain in chains: chain.hop(h)
    for chain in chains: chain.total()
    net.start(36,"C",own,fs)
    for i,chain in enumerate(early):
        chain.total()
        net.start(74+i,"C",es.at[eseg[i]],late_out.at[eseg[i]])
    put(8,es,early_out)
    for b in range(4): net.got(32+b,"C",fq.at[b,1-c])
    put(4,fq,gqkv_out); put(5,smz.at[1],small_out); put(6,own,gskip_out.at[c])
    net.got(36,"C",fs)
    put(7,fs,gskip_out.at[1-c])
    for i,r in enumerate(eseg): net.got(74+i,"C",late_out.at[r])
    for copy in outs: copy.wait()
    net.finish()

def last(gq,heads,normed,hidden,gmid,gain,block,long,wskip,small,eu,ed,eo):
    tokens,d=block.shape; S=jax.ShapeDtypeStruct; hd3=gq.shape[1]
    V=pltpu.VMEM
    return pl.pallas_call(last_kernel,
        out_shape=(S((tokens,d),BF),S((tokens,d),BF),S((8,d),F32),S((4,2,d//8,hd3),BF),S((2,d//4,d),BF),S((9*d//8,d),BF),S((9*d//8,d),BF)),
        in_specs=[VM,VM,ANY,ANY,ANY,VM,ANY,ANY,ANY,VM,ANY,ANY,ANY],out_specs=(ANY,)*7,
        scratch_shapes=[V((4*tokens,d),BF),V((4*tokens,d),BF),V((tokens,d),BF),V((tokens,d),BF),V((tokens//2,d),BF),V((tokens//2,d),BF),
            V((d,hd3),BF),V((d//2,hd3),BF),V((d,d),BF),V((2,d//2,hd3),BF),V((4,2,d//8,hd3),BF),
            V((d//8,d),BF),V((d//8,d),BF),V((d//4,d),BF),V((d//4,d),BF),V((d//4,d),BF),V((2,d//4,d),BF),V((d//4,d),BF),
            V((8,d),F32),V((3,8,d),F32),V((7,8,d),F32),
            V((9*d//8,d),BF),V((9*d//8,d),BF),V((9*d//8,d),BF),V((2,2,tokens//4,d),F32),
            pltpu.SemaphoreType.DMA((83,)),pltpu.SemaphoreType.DMA((83,)),pltpu.SemaphoreType.DMA((9,)),pltpu.SemaphoreType.DMA((9,)),pltpu.SemaphoreType.DMA((2,2))],
        compiler_params=pltpu.CompilerParams(vmem_limit_bytes=63*2**20,collective_id=1,has_side_effects=True),
        cost_estimate=pl.CostEstimate(flops=2*tokens*d*d*10,bytes_accessed=60*2**20,transcendentals=0))(
        gq,heads,normed,hidden,gmid,gain,block,long,wskip,small,eu,ed,eo)

SPLIT=((0,640),(640,512))
def middle_kernel(hidden_ref,att_ref,g_ref,gain_ref,shift_ref,outw_ref,outx_ref,outy_ref,upw_ref,upx_ref,upy_ref,dnw_ref,
                  lay_out,gmid_ref,gh_out,gow_out,small_ref,gup_out,gdn_out,sxu_out,sxd_out,syu_out,syd_out,uland,dland,ux_out,uy_out,dx_out,dy_out,
                  att_in,att_s,outw_s,n2_s,xhat_s,rstd_s,lay_s,act_s,gu_s,upb,dnb,gub,gdb,land_u,land_d,low_s,
                  send,recv,csend,crecv,fetch_sem,flush_sem,local,usem,urecv,bring_sem):
    x,y,c,w,wx,wy,wd=place()
    tokens,d=hidden_ref.shape
    cols=att_ref.shape[1]
    kr=d//4; kh=kr//2; dh=d//2; dq=dh//2
    tc=tokens//4; th=tokens//2
    mul=pl.multiple_of
    net=Links(send,recv)
    left=[]
    def start(k,t,src,dst,view):
        pltpu.make_async_remote_copy(src_ref=src,dst_ref=dst,send_sem=send.at[k],recv_sem=recv.at[k],
                                     device_id=net.to[t],device_id_type=MESH).start()
        left.append((k,t,view))
    def blk(b): return pl.ds(mul(b*d,128),d)
    def urow(b,core): return pl.ds(mul(b*kr+core*kh,16),kh)
    def drow(b,core,p): return pl.ds(mul(b*d+core*dh+p*dq,16),dq)
    def trow(b): return pl.ds(mul(b*tokens,16),tokens)
    uview=uland.at[pl.ds(0,kh),pl.ds(0,d)]
    dview=dland.at[pl.ds(0,dq)]
    net.meet("XYDC")
    for j,(t,b) in enumerate((("X",wx),("Y",wy),("D",wd))):
        start(j,t,att_ref.at[trow(b)],att_in.at[w],att_in.at[0])
    own_att=pltpu.make_async_copy(att_ref.at[trow(w)],att_in.at[w],local.at[0])
    own_att.start()
    cut=kh//32*16+16
    def orow(b,core,lo,n): return pl.ds(mul(b*kr+core*kh+lo,16),n)
    start(3,"Y",outx_ref.at[pl.ds(0,cut)],outw_s.at[orow(wx,c,0,cut)],outw_s.at[pl.ds(0,cut)])
    start(4,"X",outy_ref.at[pl.ds(cut,kh-cut)],outw_s.at[orow(wy,c,cut,kh-cut)],outw_s.at[pl.ds(0,kh-cut)])
    start(5,"C",outx_ref,outw_s.at[urow(wx,c)],outw_s.at[pl.ds(0,kh)])
    start(6,"C",outy_ref,outw_s.at[urow(wy,c)],outw_s.at[pl.ds(0,kh)])
    start(7,"Y",upx_ref.at[:,blk(wy)],uland.at[urow(wx,c),blk(wy)],uview)
    start(8,"X",upy_ref.at[:,blk(w)],uland.at[urow(wy,c),blk(w)],uview)
    order=(w,wx,wd,wy)
    def up_core(i):
        start(11+2*i,"C",upx_ref.at[:,blk(order[i])],uland.at[urow(wx,c),blk(order[i])],uview)
        start(12+2*i,"C",upy_ref.at[:,blk(order[i])],uland.at[urow(wy,c),blk(order[i])],uview)
    up_core(0)
    outw_s[pl.ds(mul(w*kr,16),kr),:]=outw_ref[...]
    outw_s[urow(wx,c),:]=outx_ref[...]
    outw_s[urow(wy,c),:]=outy_ref[...]

    diag_id=(7,8,9,10)
    def diag_from(i): return "YX"[i%2]
    def up_relay(i):
        view=uland.at[urow(wd,c),blk(order[i])]
        net.got(diag_id[i],diag_from(i),view)
        start(19+i,"C",view,view,uview)
    def up_sources(i):
        b=order[i]
        net.got(11+2*i,"C",uland.at[urow(wx,1-c),blk(b)])
        net.got(12+2*i,"C",uland.at[urow(wy,1-c),blk(b)])
        net.got(19+i,"C",uland.at[urow(wd,1-c),blk(b)])
        return [(upw_ref.at[:,blk(b)],pl.ds(mul(w*kr,16),kr)),(upx_ref.at[:,blk(b)],urow(wx,c)),(upy_ref.at[:,blk(b)],urow(wy,c)),
                (uland.at[urow(wx,1-c),blk(b)],urow(wx,1-c)),(uland.at[urow(wy,1-c),blk(b)],urow(wy,1-c)),
                (uland.at[pl.ds(mul(wd*kr,16),kr),blk(b)],pl.ds(mul(wd*kr,16),kr))]
    def fetch(i):
        slot=i%2
        for j,(src,rows) in enumerate(up_sources(i)):
            pltpu.make_async_copy(src,upb.at[slot,rows],fetch_sem.at[slot,j]).start()
        src=dnw_ref if i==0 else dland.at[pl.ds(mul(order[i]*d,16),d)]
        pltpu.make_async_copy(src,dnb.at[slot],fetch_sem.at[slot,6]).start()
    def fetched(slot):
        for j,n in enumerate((kr,kh,kh,kh,kh,kr)):
            view=upb.at[slot,pl.ds(0,n)]
            pltpu.make_async_copy(view,view,fetch_sem.at[slot,j]).wait()
        pltpu.make_async_copy(dnb.at[slot],dnb.at[slot],fetch_sem.at[slot,6]).wait()
    def down_relay(k,t,b,p,onward):
        r=drow(b,c,p)
        net.got(k,t,dland.at[r])
        for k2,t2 in onward: start(k2,t2,dland.at[r],dland.at[r],dview)
    def down_core(k,b,p): net.got(k,"C",dland.at[drow(b,1-c,p)])

    for j,(t,b) in enumerate((("X",wx),("Y",wy),("D",wd))):
        net.got(j,t,att_in.at[b])
    start(9,"Y",upx_ref.at[:,blk(wx)],uland.at[urow(wx,c),blk(wx)],uview)
    start(10,"X",upy_ref.at[:,blk(wd)],uland.at[urow(wy,c),blk(wd)],uview)
    def dmine(p): return dnw_ref.at[pl.ds(mul(c*dh+p*dq,16),dq)]
    start(23,"X",dmine(0),dland.at[drow(w,c,0)],dview)
    start(25,"Y",dmine(1),dland.at[drow(w,c,1)],dview)
    start(24,"X",dmine(1),dland.at[drow(w,c,1)],dview)
    start(26,"Y",dmine(0),dland.at[drow(w,c,0)],dview)
    net.got(3,"Y",outw_s.at[orow(wd,c,0,cut)])
    net.got(4,"X",outw_s.at[orow(wd,c,cut,kh-cut)])
    start(35,"C",outw_s.at[urow(wd,c)],outw_s.at[urow(wd,c)],outw_s.at[pl.ds(0,kh)])
    up_relay(0)
    for i in (1,2,3): up_core(i)
    net.got(5,"C",outw_s.at[urow(wx,1-c)]); net.got(6,"C",outw_s.at[urow(wy,1-c)])
    net.got(35,"C",outw_s.at[urow(wd,1-c)])
    own_att.wait()
    fetch(0)
    gain=gain_ref[...]; shift=shift_ref[...]
    @pl.loop(0,4)
    def _(i):
        r=pl.ds(mul(i*tc,16),tc)
        joined=jnp.concatenate([att_in[p,r,:] for p in range(4)],axis=1)
        att_s[r,:]=joined
        mid=hidden_ref[r,:]+nn(joined,outw_s[...])
        lay_s[r,:]=mid
        cen=mid-jnp.mean(mid,axis=1,keepdims=True)
        inv=lax.rsqrt(jnp.mean(cen*cen,axis=1,keepdims=True)+1e-5)
        xhat=cen*inv
        xhat_s[r,:]=xhat
        rstd_s[r,:]=jnp.broadcast_to(inv,(tc,128))
        n2_s[r,:]=(xhat*gain+shift).astype(BF)
        gmid_ref[r,:]=jnp.zeros((tc,d),F32)

    def pieces(slot):
        out=[(gub,pl.ds(mul(p*kr+(1-c)*kh,16),kh),land_u.at[slot,pl.ds(p*kh,kh)]) for p in range(4)]
        return out+[(gdb,pl.ds(mul((1-c)*dh,16),dh),land_d.at[slot])]
    def exchange(slot,act):
        for j,(ref,r,dst) in enumerate(pieces(slot)):
            act(pltpu.make_async_remote_copy(src_ref=ref.at[r],dst_ref=dst,send_sem=csend.at[slot,j],recv_sem=crecv.at[slot,j],
                                             device_id=net.to["C"],device_id_type=MESH))
    def flush(b,act):
        for p in range(4):
            act(pltpu.make_async_copy(gub.at[pl.ds(mul(p*kr+c*kh,16),kh)],gup_out.at[pl.ds(p*kh,kh),blk(b)],flush_sem.at[p]))
        act(pltpu.make_async_copy(gdb.at[pl.ds(mul(c*dh,16),dh)],gdn_out.at[pl.ds(mul(b*dh,16),dh)],flush_sem.at[4]))
    go=lambda copy: copy.start()
    done=lambda copy: copy.wait()
    def finalize(i):
        slot=lax.rem(i,2)
        exchange(slot,lambda copy: copy.wait())
        for p in range(4):
            r=pl.ds(mul(p*kr+c*kh,16),kh)
            gub[r,:]=(gub[r,:].astype(F32)+land_u[slot,pl.ds(p*kh,kh),:].astype(F32)).astype(BF)
        for p in range(2):
            r=pl.ds(mul(c*dh+p*dq,16),dq)
            gdb[r,:]=(gdb[r,:].astype(F32)+land_d[slot,pl.ds(p*dq,dq),:].astype(F32)).astype(BF)
    def block_of(i):
        return 2*lax.rem(y+i//2,2)+lax.rem(x+(i+1)//2,2)

    usend=[pl.ds(0,cut),pl.ds(cut,kh-cut)]
    def ahead(i,b,act):
        for j,(t,dst) in enumerate((("X",ux_out),("Y",uy_out))):
            n=usend[j]
            src=gup_out.at[pl.ds(mul(wd*kh+n.start,16),n.size),blk(b)]
            act(pltpu.make_async_remote_copy(src_ref=src,dst_ref=dst.at[:,blk(b)],send_sem=usem.at[i,j],recv_sem=urecv.at[i,j],
                                             device_id=net.to[t],device_id_type=MESH))
    def ahead_down(act):
        for j,(t,dst) in enumerate((("X",dx_out),("Y",dy_out))):
            act(pltpu.make_async_remote_copy(src_ref=gdn_out.at[pl.ds(mul(wd*dh+j*dq,16),dq)],dst_ref=dst,
                                             send_sem=usem.at[4,j],recv_sem=urecv.at[4,j],device_id=net.to[t],device_id_type=MESH))
    def weight_grads():
        for lo,n in SPLIT:
            f=pl.ds(lo,n)
            gdb[f,:]=tn(act_s[:,f],g_ref[...]).astype(BF)
            gub[f,:]=tn(n2_s[:,f],gu_s[...]).astype(BF)
    @pl.loop(0,4)
    def _(i):
        slot=lax.rem(i,2)
        fetched(slot)
        @pl.loop(0,2)
        def _(t):
            r=pl.ds(mul(t*th,16),th)
            for lo,n in SPLIT:
                f=pl.ds(lo,n)
                u=nn(n2_s[r,:],upb[slot,:,f])
                a,dg=gelu_parts(u)
                act_s[r,f]=a.astype(BF)
                gu_s[r,f]=(nt(g_ref[r,:],dnb[slot,f,:])*dg).astype(BF)
        @pl.when(i>=1)
        def _():
            finalize(i-1)
            flush(block_of(i-1),go)
        @pl.when(i==0)
        def _():
            for j in (1,2,3): up_relay(j)
        @pl.loop(0,2)
        def _(t):
            r=pl.ds(mul(t*th,16),th)
            for lo,n in SPLIT:
                f=pl.ds(lo,n)
                lay_s[r,f]+=nn(act_s[r,:],dnb[slot,:,f])
                gmid_ref[r,f]+=nt(gu_s[r,:],upb[slot,f,:])
        @pl.when(i==0)
        def _():
            down_relay(23,"X",wx,0,((27,"Y"),(29,"C")))
            down_relay(25,"Y",wy,1,((28,"X"),(30,"C")))
            down_relay(24,"X",wx,1,((31,"C"),))
            down_core(29,wx,0); down_core(31,wx,1)
            fetch(1)
        @pl.when(i==1)
        def _():
            down_relay(27,"Y",wd,0,((33,"C"),))
            down_relay(28,"X",wd,1,((34,"C"),))
            down_relay(26,"Y",wy,0,((32,"C"),))
            down_core(33,wd,0); down_core(34,wd,1)
            fetch(2)
        @pl.when(i==2)
        def _():
            down_core(30,wy,1); down_core(32,wy,0)
            fetch(3)
        @pl.when(i>=1)
        def _():
            flush(block_of(i-1),done)
            ahead(i-1,block_of(i-1),go)
        @pl.when(i==3)
        def _(): ahead_down(go)
        @pl.when(i<3)
        def _():
            weight_grads()
            exchange(slot,go)
    small_ref[...]=jnp.zeros_like(small_ref)
    for i in range(4):
        r=pl.ds(i*tc,tc)
        gs=gmid_ref[r,:]; xhat=xhat_s[r,:]
        small_ref[0:1,:]+=jnp.sum(gs*xhat,axis=0,keepdims=True)
        small_ref[1:2,:]+=jnp.sum(gs,axis=0,keepdims=True)
        e=gs*gain
        back=e-jnp.mean(e,axis=1,keepdims=True)-xhat*jnp.mean(e*xhat,axis=1,keepdims=True)
        gm=g_ref[r,:].astype(F32)+back*rstd_s[r,0:1]
        gmid_ref[r,:]=gm
        low=gm.astype(BF)
        low_s[r,:]=low
        ga=nt(low,outw_s[...]).astype(BF)
        for p in range(4): att_in[p,r,:]=ga[:,p*cols:(p+1)*cols]
        for j,(t,b) in enumerate((("X",wx),("Y",wy),("D",wd))):
            start(36+3*i+j,t,att_in.at[b,r],gh_out.at[w,r],gh_out.at[0,pl.ds(0,tc)])
    own_grad=pltpu.make_async_copy(att_in.at[w],gh_out.at[w],local.at[2])
    own_grad.start()
    weight_grads()
    exchange(1,go)
    act_s[...]=lay_s[...].astype(BF)
    lay_copy=pltpu.make_async_copy(act_s,lay_out,local.at[1])
    lay_copy.start()
    finalize(3)
    flush(wy,go)
    flush(wy,done)
    ahead(3,wy,go)
    for lo,n in SPLIT:
        f=pl.ds(lo,n)
        gub[f,:]=tn(att_s[:,f],low_s[...]).astype(BF)
    for p in range(4):
        start(48+p,"C",gub.at[pl.ds(mul(p*kr+(1-c)*kh,16),kh)],land_u.at[0,pl.ds(p*kh,kh)],land_u.at[0,pl.ds(0,kh)])
    def bring(k,src,dst):
        copy=pltpu.make_async_copy(src,dst,bring_sem.at[k]); copy.start(); return copy
    def spot(j,b): return pl.ds((4*j+b)*kh,kh)
    copies=[]
    for j,b2 in enumerate((wx,wy)):
        for b in range(4):
            copies.append(bring(4*j+b,gup_out.at[pl.ds(mul(b2*kh,16),kh),pl.ds(b*d,d)],upb.at[0,spot(j,b)]))
        copies.append(bring(16+j,gdn_out.at[pl.ds(mul(b2*dh,16),dh)],dnb.at[0,pl.ds(j*dh,dh)]))
    for i in range(4): ahead(i,order[i],done)
    ahead_down(done)
    for j,(src,n) in enumerate(((uy_out,usend[1]),(ux_out,usend[0]))):
        for b in range(4):
            copies.append(bring(8+4*j+b,src.at[:,pl.ds(b*d,d)],upb.at[1,pl.ds((4*j+b)*kh,n.size)]))
    copies.append(bring(18,dy_out,dnb.at[1,pl.ds(0,dq)]))
    copies.append(bring(19,dx_out,dnb.at[1,pl.ds(dq,dq)]))
    for copy in copies: copy.wait()
    copies=[]
    for j,(uo,do) in enumerate(((sxu_out,sxd_out),(syu_out,syd_out))):
        n=usend[1-j]
        for b in range(4):
            lo=(4*j+b)*kh
            r=pl.ds(lo+n.start,n.size)
            upb[0,r,:]=(upb[0,r,:].astype(F32)+upb[1,pl.ds(lo,n.size),:].astype(F32)).astype(BF)
            copies.append(bring(4*j+b,upb.at[0,spot(j,b)],uo.at[:,pl.ds(b*d,d)]))
        r=pl.ds(j*dh+(1-j)*dq,dq)
        dnb[0,r,:]=(dnb[0,r,:].astype(F32)+dnb[1,pl.ds(j*dq,dq),:].astype(F32)).astype(BF)
        copies.append(bring(16+j,dnb.at[0,pl.ds(j*dh,dh)],do.at[pl.ds(0,dh)]))
    for p in range(4):
        net.got(48+p,"C",land_u.at[0,pl.ds(p*kh,kh)])
        r=pl.ds(mul(p*kr+c*kh,16),kh)
        land_u[1,pl.ds(p*kh,kh),:]=(gub[r,:].astype(F32)+land_u[0,pl.ds(p*kh,kh),:].astype(F32)).astype(BF)
    for k,(b,dst) in enumerate(((w,gow_out.at[0]),(wd,gow_out.at[1]),(wx,sxd_out.at[pl.ds(dh,kh)]),(wy,syd_out.at[pl.ds(dh,kh)]))):
        copies.append(bring(8+k,land_u.at[1,pl.ds(mul(b*kh,16),kh)],dst))
    for i in range(4):
        for j,(t,b) in enumerate((("X",wx),("Y",wy),("D",wd))):
            net.got(36+3*i+j,t,gh_out.at[b,pl.ds(i*tc,tc)])
    for copy in [lay_copy,own_grad]+copies: copy.wait()
    for k,t,view in left:
        pltpu.make_async_remote_copy(src_ref=view,dst_ref=view,send_sem=send.at[k],recv_sem=recv.at[k],
                                     device_id=net.to[t],device_id_type=MESH).wait_send()

def middle(hidden,att,g,gain,shift,outw,outx,outy,upw,upx,upy,dnw):
    tokens,d=hidden.shape; cols=att.shape[1]; ff=upw.shape[1]
    S=jax.ShapeDtypeStruct; V=pltpu.VMEM; D=pltpu.SemaphoreType.DMA
    kh=d//8; cut=kh//32*16+16
    return pl.pallas_call(middle_kernel,
        out_shape=(S((tokens,d),BF),S((tokens,d),F32),S((4,tokens,cols),BF),S((2,kh,d),BF),S((8,d),F32),S((d//2,ff),BF),S((ff//2,d),BF),
                   S((kh,ff),BF),S((ff//8+kh,d),BF),S((kh,ff),BF),S((ff//8+kh,d),BF),
                   S((d,ff),BF),S((ff,d),BF),S((cut,ff),BF),S((kh-cut,ff),BF),S((ff//16,d),BF),S((ff//16,d),BF)),
        in_specs=[VM,ANY]+[VM]*6+[ANY]*4,out_specs=(ANY,VM,ANY,ANY,VM)+(ANY,)*12,
        scratch_shapes=[V((4,tokens,cols),BF),V((tokens,d),BF),V((d,d),BF),V((tokens,d),BF),V((tokens,d),F32),V((tokens,128),F32),
            V((tokens,d),F32),V((tokens,d),BF),V((tokens,d),BF),V((2,d,d),BF),V((2,d,d),BF),V((d,d),BF),V((d,d),BF),
            V((2,d//2,d),BF),V((2,d//2,d),BF),V((tokens,d),BF),D((52,)),D((52,)),D((2,5)),D((2,5)),D((2,7)),D((5,)),D((4,)),
            D((5,2)),D((5,2)),D((20,))],
        compiler_params=pltpu.CompilerParams(vmem_limit_bytes=63*2**20,collective_id=2,has_side_effects=True),
        cost_estimate=pl.CostEstimate(flops=2*tokens*d*(ff*6+d*3),bytes_accessed=60*2**20,transcendentals=tokens*ff*2))(
        hidden,att,g,gain,shift,outw,outx,outy,upw,upx,upy,dnw)

def assemble_kernel(lay_ref,gin_ref,gsk_ref,skip_ref,gq_ref,em_ref,eo_ref,
                    lay_out,gin_out,gsk_out,skip_out,qkv_out,up_out,down_out,out_out,
                    s0,s1,s2,s3,s4,s5,s6,s7,local):
    first=lax.axis_index("core")==0
    copies=[]
    def put(src,dst):
        copy=pltpu.make_async_copy(src,dst,local.at[len(copies)]); copy.start(); copies.append(copy)
    def chunks(n,body,size=144):
        @pl.loop(0,n//size)
        def _(i): body(pl.ds(pl.multiple_of(i*size,16),size))
    def wide(dst,src):
        def body(r): dst[r,:]=src[r,:].astype(F32)
        chunks(dst.shape[0],body,208 if dst.shape[0]%208==0 else 144)
    wide(s7,lay_ref); put(s7,lay_out)
    wide(s0,gin_ref); put(s0,gin_out)
    wide(s1,gsk_ref); put(s1,gsk_out)
    kh=s6.shape[1]; d=s6.shape[2]
    def pair(dst,seg,rows,cols,size=48):
        @pl.loop(0,kh//size)
        def _(i):
            r=pl.ds(pl.multiple_of(seg*kh+i*size,16),size)
            to=pl.ds(pl.multiple_of(rows+i*size,16),size)
            m,o=em_ref[r,:].astype(F32),eo_ref[r,:].astype(F32)
            dst[0,to,cols]=jnp.where(first,m,o)
            dst[1,to,cols]=jnp.where(first,o,m)
    for b in range(4): pair(s4,b,0,pl.ds(b*d,d))
    put(s4,up_out)
    for b in range(4): pair(s5,4+b,b*kh,pl.ds(0,d))
    put(s5,down_out)
    pair(s6,8,0,pl.ds(0,d)); put(s6,out_out)
    def skip(r): s2[r,:]=skip_ref[r,:].astype(F32)
    chunks(s2.shape[0],skip); put(s2,skip_out)
    hd=gq_ref.shape[3]//3; kh=gq_ref.shape[2]
    for core in range(2):
        for i in range(kh//48):
            r=pl.ds(i*48,48)
            s3[pl.ds(core*kh+i*48,48),:]=jnp.concatenate([gq_ref[p,core,r,s*hd:(s+1)*hd].astype(F32) for s in range(3) for p in range(4)],axis=1)
    put(s3,qkv_out)
    for copy in copies: copy.wait()

def assemble(lay,gin,gsk,skip,gq,em,eo):
    S=lambda *s: jax.ShapeDtypeStruct(s,F32)
    tokens,d=gin.shape
    shapes=(S(tokens,d),S(tokens,d),S(*skip.shape),S(d//4,3*d),S(2,d//8,4*d),S(2,d//2,d),S(2,d//8,d))
    return pl.pallas_call(assemble_kernel,out_shape=(shapes[0],)+shapes,in_specs=[VM]*7,out_specs=(ANY,)*8,
        scratch_shapes=[pltpu.VMEM(s.shape,F32) for s in shapes+shapes[:1]]+[pltpu.SemaphoreType.DMA((8,))],
        compiler_params=pltpu.CompilerParams(vmem_limit_bytes=60*2**20),
        cost_estimate=pl.CostEstimate(flops=0,bytes_accessed=40*2**20,transcendentals=0))(
        lay,gin,gsk,skip,gq,em,eo)

from jax.sharding import Mesh, PartitionSpec as P
WIDE=("y","x"); ROWS=("z","core")
SWAP=[(0,1),(1,0)]

def swap_cores(values):
    return lax.ppermute(values,"core",SWAP)

def pick(values, index, axis):
    return lax.dynamic_index_in_dim(values,index,axis,keepdims=False)

def place_halves(mine, other, core, axis):
    first=jnp.where(core==0,mine,other); second=jnp.where(core==0,other,mine)
    return jnp.stack([first,second],axis=axis)

def dot(a,b): return jnp.dot(a,b,preferred_element_type=F32)

def norm(values):
    cen=values-jnp.mean(values,axis=1,keepdims=True)
    inv=lax.rsqrt(jnp.mean(cen*cen,axis=1,keepdims=True)+1e-5)
    return cen*inv,inv

def on_device(nw, block_input, long_skip, segment_ids, item_lengths, skip_weight, first_gain, first_shift, qkv_weight,
              out_weight, second_gain, second_shift, up_weight, down_weight, output_grad):
    core=lax.axis_index("core")
    _,tokens,d=block_input.shape
    heads=qkv_weight.shape[1]//(3*HEAD*nw); hd=heads*HEAD
    ff=up_weight.shape[1]; fb=ff//(2*nw)
    gather=lambda v: lax.all_gather(v,WIDE,axis=0,tiled=True)
    near=nw==4
    vecs=jnp.stack([first_gain,first_shift,second_gain,second_shift]+[first_gain]*4).astype(F32)
    if near:
        hidden,normed_all,qkv,w_heads,w_skip,vecs=first(block_input[0],long_skip[0],skip_weight,qkv_weight,vecs)
        vec=vecs.transpose(1,0,2).reshape(8,d)
        gain1,shift1,gain2,shift2=[vec[i:i+1] for i in range(4)]
        half=lambda v: lax.dynamic_slice_in_dim(v,core*(v.shape[0]//2),v.shape[0]//2)
        qkv,up_half,out_half=lax.optimization_barrier((qkv,half(up_weight),half(out_weight)))
        up_x,out_x=lax.ppermute((up_half,out_half),"x",SWAP)
        up_y,out_y=lax.ppermute((up_half,out_half),"y",SWAP)
    else:
        vec=gather(vecs.astype(BF).T).T.astype(F32)
        gain1,shift1,gain2,shift2=[vec[i:i+1] for i in range(4)]
        w_skip=gather(skip_weight)
        joined=jnp.concatenate([block_input[0],long_skip[0]],axis=1)
        w_heads=qkv_weight.reshape(d//nw,3,nw,hd).transpose(2,0,1,3)
        w_heads=lax.all_to_all(w_heads,WIDE,0,0).reshape(d,3*hd)
        hidden=dot(joined,w_skip)
        xhat1,inv1=norm(hidden)
        normed_all=gather((xhat1*gain1+shift1).astype(BF))
        qkv=dot(normed_all,w_heads).astype(BF)
    att,lse=attend(item_lengths,qkv,heads)
    if near:
        lay,gmid,gatt,gow,small,gup,gdn,sxu,sxd,syu,syd=middle(hidden,att,output_grad[0],gain2,shift2,out_weight,out_x,out_y,
            up_weight,up_x,up_y,down_weight)[:11]
    else:
        w_out=gather(out_weight)
        up_mine=gather(pick(up_weight.reshape(d//nw,nw,2,fb),core,2).reshape(d//nw,nw*fb))
        down_mine=gather(pick(down_weight.reshape(2,fb,d),core,0))
        up_other,down_other=swap_cores(up_mine),swap_cores(down_mine)
        att=lax.all_to_all(att.reshape(nw,tokens,hd),WIDE,0,0)
        lay,gmid,gatt,gow,small,gupo,guph,gdno,gdnh=mlp(hidden,att,w_out,gain2,shift2,output_grad[0],up_mine,up_other,down_mine,down_other)
        gatt=lax.all_to_all(gatt,WIDE,0,0)
    grad_heads=gatt.reshape(nw*tokens,hd)

    def scatter(mine,other):
        both=(mine.astype(F32)+swap_cores(other).astype(F32)).astype(BF)
        return lax.psum_scatter(both,WIDE,scatter_dimension=0,tiled=True)
    def both_cores(mine,axis):
        return place_halves(mine,swap_cores(mine),core,axis).astype(F32)
    def by_rows(grad):
        cut=grad.reshape(nw,2,-1,grad.shape[1])
        return scatter(pick(cut,core,1).reshape(-1,grad.shape[1]),pick(cut,1-core,1).reshape(-1,grad.shape[1]))
    if near:
        wide=2*lax.axis_index("y")+lax.axis_index("x")
        part=lambda v: lax.dynamic_index_in_dim(v.reshape(4,-1,v.shape[1]),wide,0,False)
        from_x=lax.ppermute((sxu,sxd),"x",SWAP)
        from_y=lax.ppermute((syu,syd),"y",SWAP)
        from_d=lax.ppermute(gow[1],WIDE,[(i,3-i) for i in range(4)])
    else:
        early=scatter(gupo,guph),scatter(gdno,gdnh),by_rows(gow)
    grad_qkv=attend_back(item_lengths,qkv,grad_heads,lse,heads)
    if near:
        grad_qkv,from_x,from_y,from_d=lax.optimization_barrier((grad_qkv,from_x,from_y,from_d))
        up_sum=part(gup).astype(F32)+from_x[0].astype(F32)+from_y[0].astype(F32)
        rows=gdn.shape[0]//4
        pair=from_x[1].astype(F32)+from_y[1].astype(F32)
        down_sum=part(gdn).astype(F32)+pair[:rows]
        out_sum=gow[0].astype(F32)+pair[rows:]+from_d.astype(F32)
        early=up_sum.astype(BF),down_sum.astype(BF),out_sum.astype(BF)
    grad_qkv,early=lax.optimization_barrier((grad_qkv,early))
    if not near: early=lax.psum(early,"z")
    if near:
        gin,gsk,smalls,gqkv,gskip,mine,other=last(grad_qkv,w_heads,normed_all,hidden,gmid,gain1,block_input[0],long_skip[0],w_skip,small,*early)
        lay,gin,gsk,skip_share,qkv_share,up_share,down_share,out_share=assemble(lay,gin,gsk,gskip.reshape(-1,d),gqkv,mine,other)
        up_share,down_share,out_share=up_share.reshape(-1,ff),down_share.reshape(-1,d),out_share.reshape(-1,d)
        smalls=lax.dynamic_slice_in_dim(smalls[:4],(2*lax.axis_index("y")+lax.axis_index("x"))*(d//nw),d//nw,axis=1).T
    else:
        part_first=nt(grad_qkv,w_heads).astype(BF)
        grad_first=lax.psum_scatter(part_first,WIDE,scatter_dimension=0,tiled=True).astype(F32)
        gqkv=tn(normed_all,grad_qkv).astype(BF).reshape(nw,2,d//nw//2,3*hd)
        gqkv=(pick(gqkv,core,1).astype(F32)+swap_cores(pick(gqkv,1-core,1)).astype(F32)).astype(BF)
        e1=grad_first*gain1
        across=inv1*(e1-jnp.mean(e1,axis=1,keepdims=True)-xhat1*jnp.mean(e1*xhat1,axis=1,keepdims=True))
        grad_hidden=(gmid+across).astype(BF)
        gskip=by_rows(tn(joined,grad_hidden).astype(BF))
        grad_joined=nt(grad_hidden,w_skip)
        gin,gsk=grad_joined[:,:d],grad_joined[:,d:]
        small1=jnp.stack([jnp.sum(grad_first*xhat1,axis=0),jnp.sum(grad_first,axis=0)])
        gqkv,gskip,early=lax.optimization_barrier((gqkv,gskip,early))
        gqkv,gskip=lax.psum((gqkv,gskip),"z")
        up_share=both_cores(early[0].reshape(d//nw,nw,fb),2).reshape(d//nw,ff)
        down_share=both_cores(early[1],0).reshape(ff//nw,d)
        out_share=both_cores(early[2],0).reshape(d//nw,d)
        skip_share=both_cores(gskip,0).reshape(2*d//nw,d)
        gqkv=lax.all_to_all(gqkv,WIDE,0,0).reshape(nw,-1,3,hd).transpose(1,2,0,3)
        qkv_share=both_cores(gqkv,0).reshape(d//nw,-1)
        smalls=jnp.stack([small1[0],small1[1],small[0],small[1]],axis=1)
        smalls=lax.psum(lax.psum_scatter(smalls.astype(BF),WIDE,scatter_dimension=0,tiled=True),ROWS).astype(F32)
    return (lay[None],gin[None],gsk[None],skip_share,smalls[:,0],smalls[:,1],qkv_share,out_share,
            smalls[:,2],smalls[:,3],up_share,down_share)

def solution(mesh):
    rows,wide=mesh.devices.shape
    side=2 if wide==4 else int(wide**0.5)
    grid=Mesh(mesh.devices.reshape(rows//2,2,wide//side,side),("z","core","y","x"))
    tok=P(ROWS,WIDE,None); row=P(ROWS,None); mat=P(WIDE,None); vec=P(WIDE)
    return jax.shard_map(functools.partial(on_device,wide),mesh=grid,
        in_specs=(tok,tok,row,row,mat,vec,vec,mat,mat,vec,vec,mat,mat,tok),
        out_specs=(tok,tok,tok,mat,vec,vec,mat,mat,vec,vec,mat,mat),check_vma=False)
```

```python
import functools
import jax, jax.numpy as jnp
from jax import lax
from jax.experimental import pallas as pl
from jax.experimental.pallas import tpu as pltpu
HEAD=72; SHORT=258; LONG=1026; NITEM=12
LOG2E=1.4426950408889634
SCALE=HEAD**-0.5
QT=384

def kwin(n): return (n + 29 + 31)//32*32
def qwin(n): return (n + 15 + QT-1)//QT*QT

def nt(a,b): return lax.dot_general(a,b,(((1,),(1,)),((),())),preferred_element_type=jnp.float32)
def nn(a,b): return lax.dot_general(a,b,(((1,),(0,)),((),())),preferred_element_type=jnp.float32)
def tn(a,b): return lax.dot_general(a,b,(((0,),(0,)),((),())),preferred_element_type=jnp.float32)

def windows(start, size, row_len):
    k0 = pl.multiple_of(jnp.minimum(start//16*16, row_len-kwin(size)),16)
    q0 = pl.multiple_of(jnp.minimum(start//16*16, row_len-qwin(size)),16)
    return k0,q0

def split_heads(src_ref, dst_ref, count, chunk=416):
    rows=src_ref.shape[0]
    @pl.loop(0, rows//chunk)
    def _(i):
        r=pl.ds(pl.multiple_of(i*chunk,16),chunk)
        block=src_ref[r,:]
        for j in range(count):
            dst_ref[j,r,:]=block[:,j*HEAD:(j+1)*HEAD]

def join_heads(src_ref, dst_ref, count, chunk=416):
    rows=dst_ref.shape[0]
    @pl.loop(0, rows//chunk)
    def _(i):
        r=pl.ds(pl.multiple_of(i*chunk,16),chunk)
        dst_ref[r,:]=jnp.concatenate([src_ref[j,r,:] for j in range(count)],axis=1)

def zero(ref, chunk=416):
    rows=ref.shape[1]
    @pl.loop(0, rows//chunk)
    def _(i):
        r=pl.ds(pl.multiple_of(i*chunk,16),chunk)
        for j in range(ref.shape[0]):
            ref[j,r,:]=jnp.zeros((chunk,ref.shape[2]),ref.dtype)

LANES=256
def pack_heads(src_ref, dst_ref, tail_ref, count):
    size=tail_ref.shape[0]//4
    @pl.loop(0,4)
    def _(b):
        tails=[]
        for j in range(4):
            r=pl.ds(pl.multiple_of((4*b+j)*size,16),size)
            row=jnp.concatenate([src_ref[h,r,:] for h in range(count)],axis=1)
            dst_ref[r,:]=row[:,:LANES]
            tails.append(row[:,LANES:])
        tail_ref[pl.ds(pl.multiple_of(b*size,16),size),:]=jnp.concatenate(tails,axis=1)

def unpack_heads(src_ref, tail_ref, dst_ref, count):
    size=tail_ref.shape[0]//4; width=tail_ref.shape[1]//4
    @pl.loop(0,4)
    def _(b):
        tail=tail_ref[pl.ds(pl.multiple_of(b*size,16),size),:]
        for j in range(4):
            r=pl.ds(pl.multiple_of((4*b+j)*size,16),size)
            row=jnp.concatenate([src_ref[r,:],tail[:,j*width:(j+1)*width]],axis=1)
            for h in range(count): dst_ref[h,r,:]=row[:,h*HEAD:(h+1)*HEAD]

def for_items(len_ref, one):
    def step(i, start):
        size=len_ref[0,i]
        @pl.when(size==LONG)
        def _(): one(i,start,LONG)
        @pl.when(size==SHORT)
        def _(): one(i,start,SHORT)
        return start+size
    lax.fori_loop(0,len_ref.shape[1],step,jnp.int32(0))

def mask_edges(values, start, k0, size, fill):
    n=values.shape[0]; body=size//32*32
    off=start-k0
    top=lax.broadcasted_iota(jnp.int32,(32,values.shape[1]),0)
    low=jnp.where(top>=off,values[:32],fill)
    high=jnp.where(top+body<off+size,values[body:],fill)
    return jnp.concatenate([low,values[32:body],high],axis=0)

def attend_kernel(heads, len_ref, qkv_ref, *refs):
    *outs, lse_ref, split_ref, acc_ref=refs
    row_len=qkv_ref.shape[0]
    split_heads(qkv_ref, split_ref, 3*heads)
    zero(acc_ref)
    lse_ref[...]=jnp.zeros_like(lse_ref)
    def one(item,start,size):
        k0,q0=windows(start,size,row_len)
        kr=pl.ds(k0,kwin(size))
        @pl.loop(0,qwin(size)//QT)
        def _(t):
            qr=pl.ds(pl.multiple_of(q0+t*QT,16),QT)
            col=q0+t*QT+lax.broadcasted_iota(jnp.int32,(1,QT),1)
            live=(col>=start)&(col<start+size)
            for h in range(heads):
                s=nt(split_ref[heads+h,kr,:],split_ref[h,qr,:])
                s=mask_edges(s,start,k0,size,-1e30)
                m=jnp.max(s,axis=0,keepdims=True)
                p=jnp.exp2((s-m)*(SCALE*LOG2E))
                l=jnp.sum(p,axis=0,keepdims=True)
                o=tn(split_ref[2*heads+h,kr,:],p.astype(jnp.bfloat16))
                o=jnp.where(live,o/l,0.0)
                acc_ref[h,qr,:]+=o.T.astype(jnp.bfloat16)
                lse_ref[item,pl.ds(t*heads+h,1),:]=m*(SCALE*LOG2E)+jnp.log2(l)
    for_items(len_ref,one)
    if len(outs)==2: pack_heads(acc_ref,*outs,heads)
    else: join_heads(acc_ref,outs[0],heads)

def attend_back_kernel(heads, len_ref, qkv_ref, *refs):
    *grads, lse_ref, out_ref, split_ref, gsplit_ref, acc_ref, dk_ref, dv_ref=refs
    row_len=qkv_ref.shape[0]
    split_heads(qkv_ref, split_ref, 3*heads)
    if len(grads)==2: unpack_heads(*grads,gsplit_ref,heads)
    else: split_heads(grads[0],gsplit_ref,heads)
    zero(acc_ref)
    def one(item,start,size):
        k0,q0=windows(start,size,row_len)
        kw=kwin(size)
        kr=pl.ds(k0,kw)
        for h in range(heads):
            dk_ref[h,:kw,:]=jnp.zeros((kw,HEAD),jnp.float32)
            dv_ref[h,:kw,:]=jnp.zeros((kw,HEAD),jnp.float32)
        @pl.loop(0,qwin(size)//QT)
        def _(t):
            qr=pl.ds(pl.multiple_of(q0+t*QT,16),QT)
            col=q0+t*QT+lax.broadcasted_iota(jnp.int32,(1,QT),1)
            live=(col>=start)&(col<start+size)
            for h in range(heads):
                k=split_ref[heads+h,kr,:]; q=split_ref[h,qr,:]; g=gsplit_ref[h,qr,:]
                lse=jnp.where(live,lse_ref[item,pl.ds(t*heads+h,1),:],1e30)
                s=nt(k,q)
                p=jnp.exp2(s*(SCALE*LOG2E)-lse)
                p=mask_edges(p,start,k0,size,0.0)
                dv_ref[h,:kw,:]+=nn(p.astype(jnp.bfloat16),g)
                dp=nt(split_ref[2*heads+h,kr,:],g)
                delta=jnp.sum(p*dp,axis=0,keepdims=True)
                ds=(p*(dp-delta)).astype(jnp.bfloat16)
                dk_ref[h,:kw,:]+=nn(ds,q)
                dq=tn(k,ds)*SCALE
                acc_ref[h,qr,:]+=dq.T.astype(jnp.bfloat16)
        for h in range(heads):
            acc_ref[heads+h,kr,:]+=(dk_ref[h,:kw,:]*SCALE).astype(jnp.bfloat16)
            acc_ref[2*heads+h,kr,:]+=dv_ref[h,:kw,:].astype(jnp.bfloat16)
    for_items(len_ref,one)
    join_heads(acc_ref,out_ref,3*heads)

VM=pl.BlockSpec(memory_space=pltpu.VMEM); SM=pl.BlockSpec(memory_space=pltpu.SMEM)
def attend(lens,qkv,heads,packed=False):
    n=qkv.shape[0]
    nt_=heads*(qwin(LONG)//QT)
    shapes=((n,LANES),(n//4,4*(heads*HEAD-LANES))) if packed else ((n,heads*HEAD),)
    return pl.pallas_call(functools.partial(attend_kernel,heads),
      out_shape=tuple(jax.ShapeDtypeStruct(s,jnp.bfloat16) for s in shapes)+(jax.ShapeDtypeStruct((NITEM,nt_,QT),jnp.float32),),
      in_specs=[SM,VM],out_specs=(VM,)*(len(shapes)+1),
      scratch_shapes=[pltpu.VMEM((3*heads,n,HEAD),jnp.bfloat16),pltpu.VMEM((heads,n,HEAD),jnp.bfloat16)],
      compiler_params=pltpu.CompilerParams(vmem_limit_bytes=56*2**20),
      cost_estimate=pl.CostEstimate(flops=heads*n*n*HEAD*4,bytes_accessed=12*2**20,transcendentals=heads*n*n//3))(lens,qkv)
def attend_back(lens,qkv,grads,lse,heads):
    n=qkv.shape[0]
    return pl.pallas_call(functools.partial(attend_back_kernel,heads),
      out_shape=jax.ShapeDtypeStruct((n,3*heads*HEAD),jnp.bfloat16),
      in_specs=[SM,VM]+[VM]*len(grads)+[VM],out_specs=VM,
      scratch_shapes=[pltpu.VMEM((3*heads,n,HEAD),jnp.bfloat16),pltpu.VMEM((heads,n,HEAD),jnp.bfloat16),pltpu.VMEM((3*heads,n,HEAD),jnp.bfloat16),
        pltpu.VMEM((heads,kwin(LONG),HEAD),jnp.float32),pltpu.VMEM((heads,kwin(LONG),HEAD),jnp.float32)],
      compiler_params=pltpu.CompilerParams(vmem_limit_bytes=60*2**20),
      cost_estimate=pl.CostEstimate(flops=heads*n*n*HEAD*10,bytes_accessed=20*2**20,transcendentals=heads*n*n//3))(lens,qkv,*grads,lse)


F32=jnp.float32; BF=jnp.bfloat16
ANY=pl.BlockSpec(memory_space=pl.ANY)

def gelu_parts(u):
    z=jnp.exp2(u*u*(-0.5*1.4426950408889634))
    t=1.0/(1.0+(0.3275911*0.7071067811865476)*jnp.abs(u))
    poly=((((1.061405429*t-1.453152027)*t+1.421413741)*t-0.284496736)*t+0.254829592)*t
    tail=0.5*poly*z
    cdf=jnp.where(u>=0,1.0-tail,tail)
    return u*cdf, cdf+u*(z*0.3989422804014327)

def mlp_kernel(tile, hidden_ref, att_ref, outw_ref, gain_ref, shift_ref, g_ref, upo_ref, uph_ref, dno_ref, dnh_ref,
               lay_ref, gmid_ref, gatt_ref, gow_ref, small_ref, gupo_ref, guph_ref, gdno_ref, gdnh_ref,
               att_s, n2_s, xhat_s, rstd_s, act_s, gu_s, upb, dnb, gub, gdb, in_sem, out_sem):
    parts,tokens,cols=att_ref.shape
    d=hidden_ref.shape[1]
    tc=tokens//2 if tokens>416 else tokens
    nch=tokens//tc
    half=upo_ref.shape[1]; steps=half//tile
    cc=d//3; fc=256

    def fetch(j,act):
        slot=lax.rem(j,2)
        for first,(us,ds) in ((True,(uph_ref,dnh_ref)),(False,(upo_ref,dno_ref))):
            cond=(j<steps) if first else (j>=steps)
            @pl.when(cond)
            def _():
                k=j if first else j-steps
                off=pl.multiple_of(k*tile,tile)
                act(pltpu.make_async_copy(us.at[:,pl.ds(off,tile)],upb.at[slot],in_sem.at[slot,0]))
                act(pltpu.make_async_copy(ds.at[pl.ds(off,tile),:],dnb.at[slot],in_sem.at[slot,1]))
    def flush(j,act):
        slot=lax.rem(j,2)
        for first,(us,ds) in ((True,(guph_ref,gdnh_ref)),(False,(gupo_ref,gdno_ref))):
            cond=(j<steps) if first else (j>=steps)
            @pl.when(cond)
            def _():
                k=j if first else j-steps
                off=pl.multiple_of(k*tile,tile)
                act(pltpu.make_async_copy(gub.at[slot],us.at[:,pl.ds(off,tile)],out_sem.at[slot,0]))
                act(pltpu.make_async_copy(gdb.at[slot],ds.at[pl.ds(off,tile),:],out_sem.at[slot,1]))
    start=lambda c: c.start()
    wait=lambda c: c.wait()
    fetch(jnp.int32(0),start)
    gain=gain_ref[...]; shift=shift_ref[...]
    sub=tc//2
    @pl.loop(0,2*nch)
    def _(i):
        r=pl.ds(pl.multiple_of(i*sub,16),sub)
        joined=jnp.concatenate([att_ref[p,r,:] for p in range(parts)],axis=1)
        att_s[r,:]=joined
        mid=hidden_ref[r,:]+nn(joined,outw_ref[...])
        lay_ref[r,:]=mid
        cen=mid-jnp.mean(mid,axis=1,keepdims=True)
        inv=lax.rsqrt(jnp.mean(cen*cen,axis=1,keepdims=True)+1e-5)
        xhat=cen*inv
        xhat_s[r,:]=xhat
        rstd_s[r,:]=jnp.broadcast_to(inv,(sub,128))
        n2_s[r,:]=(xhat*gain+shift).astype(BF)
        gmid_ref[r,:]=jnp.zeros((sub,d),F32)
    @pl.loop(0,2*steps)
    def _(j):
        slot=lax.rem(j,2)
        @pl.when(j+1<2*steps)
        def _(): fetch(j+1,start)
        fetch(j,wait)
        @pl.when(j>=2)
        def _(): flush(j-2,wait)
        @pl.loop(0,nch)
        def _(i):
            r=pl.ds(pl.multiple_of(i*tc,16),tc)
            for k in range(tile//fc):
                f=pl.ds(k*fc,fc)
                u=nn(n2_s[r,:],upb[slot,:,f])
                a,dg=gelu_parts(u)
                act_s[r,f]=a.astype(BF)
                ga=nt(g_ref[r,:],dnb[slot,f,:])
                gu_s[r,f]=(ga*dg).astype(BF)
        @pl.loop(0,nch)
        def _(i):
            r=pl.ds(pl.multiple_of(i*tc,16),tc)
            for k in range(3):
                cr=pl.ds(k*cc,cc)
                lay_ref[r,cr]+=nn(act_s[r,:],dnb[slot,:,cr])
                gmid_ref[r,cr]+=nt(gu_s[r,:],upb[slot,cr,:])
        for k in range(tile//fc):
            f=pl.ds(k*fc,fc)
            gdb[slot,f,:]=tn(act_s[:,f],g_ref[...]).astype(BF)
        for k in range(3):
            cr=pl.ds(k*cc,cc)
            gub[slot,cr,:]=tn(n2_s[:,cr],gu_s[...]).astype(BF)
        flush(j,start)
    small_ref[...]=jnp.zeros_like(small_ref)
    @pl.loop(0,2*nch)
    def _(i):
        r=pl.ds(pl.multiple_of(i*sub,16),sub)
        gs=gmid_ref[r,:]; xhat=xhat_s[r,:]
        small_ref[0:1,:]+=jnp.sum(gs*xhat,axis=0,keepdims=True)
        small_ref[1:2,:]+=jnp.sum(gs,axis=0,keepdims=True)
        e=gs*gain
        back=e-jnp.mean(e,axis=1,keepdims=True)-xhat*jnp.mean(e*xhat,axis=1,keepdims=True)
        gm=g_ref[r,:].astype(F32)+back*rstd_s[r,0:1]
        gmid_ref[r,:]=gm
        low=gm.astype(BF)
        n2_s[r,:]=low
        ga=nt(low,outw_ref[...]).astype(BF)
        for p in range(parts):
            gatt_ref[p,r,:]=ga[:,p*cols:(p+1)*cols]
    for k in range(3):
        cr=pl.ds(k*cc,cc)
        gow_ref[cr,:]=tn(att_s[:,cr],n2_s[...]).astype(BF)
    flush(jnp.int32(2*steps-2),wait)
    flush(jnp.int32(2*steps-1),wait)

def mlp(hidden,att,outw,gain,shift,g,upo,uph,dno,dnh):
    tokens,d=hidden.shape; half=upo.shape[1]; tile=half//3
    S=jax.ShapeDtypeStruct
    flops=2*tokens*d*(half*2*6+d*3)
    return pl.pallas_call(functools.partial(mlp_kernel,tile),
        out_shape=(S((tokens,d),F32),S((tokens,d),F32),S(att.shape,BF),S((d,d),BF),S((8,d),F32),
                   S(upo.shape,BF),S(upo.shape,BF),S(dno.shape,BF),S(dno.shape,BF)),
        in_specs=[VM]*6+[ANY]*4,
        out_specs=(VM,)*5+(ANY,)*4,
        scratch_shapes=[pltpu.VMEM((tokens,d),BF),pltpu.VMEM((tokens,d),BF),pltpu.VMEM((tokens,d),F32),pltpu.VMEM((tokens,128),F32),
            pltpu.VMEM((tokens,tile),BF),pltpu.VMEM((tokens,tile),BF),
            pltpu.VMEM((2,d,tile),BF),pltpu.VMEM((2,tile,d),BF),pltpu.VMEM((2,d,tile),BF),pltpu.VMEM((2,tile,d),BF),
            pltpu.SemaphoreType.DMA((2,2)),pltpu.SemaphoreType.DMA((2,2))],
        compiler_params=pltpu.CompilerParams(vmem_limit_bytes=62*2**20),
        cost_estimate=pl.CostEstimate(flops=flops,bytes_accessed=60*2**20,transcendentals=tokens*half*2))(
        hidden,att,outw,gain,shift,g,upo,uph,dno,dnh)


MESH=pl.DeviceIdType.MESH

def place():
    x,y,c=lax.axis_index("x"),lax.axis_index("y"),lax.axis_index("core")
    return x,y,c,2*y+x,2*y+1-x,2-2*y+x,3-2*y-x

class Links:
    def __init__(self,send,recv):
        self.send,self.recv,self.sent=send,recv,[]
        x,y,c=lax.axis_index("x"),lax.axis_index("y"),lax.axis_index("core")
        self.to={"X":{"x":1-x},"Y":{"y":1-y},"D":{"x":1-x,"y":1-y},"C":{"core":1-c}}
    def meet(self,who):
        barrier=pltpu.get_barrier_semaphore()
        for t in who:
            pl.semaphore_signal(barrier,inc=1,device_id=self.to[t],device_id_type=MESH)
        pl.semaphore_wait(barrier,len(who))
    def start(self,k,t,src,dst):
        copy=pltpu.make_async_remote_copy(src_ref=src,dst_ref=dst,send_sem=self.send.at[k],recv_sem=self.recv.at[k],
                                          device_id=self.to[t],device_id_type=MESH)
        copy.start()
        self.sent.append(copy)
    def got(self,k,t,dst):
        pltpu.make_async_remote_copy(src_ref=dst,dst_ref=dst,send_sem=self.send.at[k],recv_sem=self.recv.at[k],
                                     device_id=self.to[t],device_id_type=MESH).wait_recv()
    def finish(self):
        for copy in self.sent: copy.wait_send()

def first_kernel(block_ref,long_ref,skip_ref,qkvw_ref,vec_ref,
                 hidden_out,normed_out,qkv_out,heads_out,wskip_out,vec_out,
                 ws,ns,hs,piece,hid,qs,vs,send,recv,local):
    x,y,c,w,wx,wy,wd=place()
    tokens,d=block_ref.shape
    sr=skip_ref.shape[0]; half=sr//2; part=half//2
    kr=qkvw_ref.shape[0]; kh=kr//2; hd=qkvw_ref.shape[1]//12
    tc=tokens//4
    mul=pl.multiple_of
    net=Links(send,recv)
    net.meet("XYDC")
    def srows(b,core,p): return pl.ds(mul(b*sr+core*half+p*part,16),part)
    def mine(p): return pl.ds(mul(c*half+p*part,16),part)
    net.start(0,"X",skip_ref.at[mine(0)],ws.at[srows(w,c,0)])
    net.start(2,"Y",skip_ref.at[mine(1)],ws.at[srows(w,c,1)])
    net.start(1,"X",skip_ref.at[mine(1)],ws.at[srows(w,c,1)])
    net.start(3,"Y",skip_ref.at[mine(0)],ws.at[srows(w,c,0)])
    own=pltpu.make_async_copy(skip_ref,ws.at[pl.ds(mul(w*sr,16),sr)],local.at[0])
    own.start()
    for k,t in ((30,"X"),(31,"Y"),(32,"D")): net.start(k,t,vec_ref,vs.at[w])
    vs[w]=vec_ref[...]
    for p in range(4):
        piece[p]=jnp.concatenate([qkvw_ref[:,(s*4+p)*hd:(s*4+p+1)*hd] for s in range(3)],axis=1)
    own_heads=pltpu.make_async_copy(piece.at[w],hs.at[pl.ds(mul(w*kr,16),kr)],local.at[1])
    own_heads.start()
    def pass_on(k,t,b,p,onward):
        r=srows(b,c,p)
        net.got(k,t,ws.at[r])
        for k2,t2 in onward: net.start(k2,t2,ws.at[r],ws.at[r])
    pass_on(0,"X",wx,0,((4,"Y"),(6,"C")))
    pass_on(2,"Y",wy,1,((5,"X"),(7,"C")))
    pass_on(1,"X",wx,1,((8,"C"),))
    pass_on(3,"Y",wy,0,((9,"C"),))
    def hrows(b,core): return pl.ds(mul(b*kr+core*kh,16),kh)
    cut=pl.ds(mul(c*kh,16),kh)
    net.start(12,"X",piece.at[wx,cut],hs.at[hrows(w,c)])
    net.start(13,"Y",piece.at[wy,cut],hs.at[hrows(w,c)])
    net.start(14,"D",piece.at[wd,cut],hs.at[hrows(w,c)])
    own.wait()
    net.got(6,"C",ws.at[srows(wx,1-c,0)])
    net.got(8,"C",ws.at[srows(wx,1-c,1)])
    near=pl.ds(mul(y*d,16),d); far=pl.ds(mul((1-y)*d,16),d)
    def tok(i): return pl.ds(mul(i*tc,16),tc)
    @pl.loop(0,4)
    def _(i):
        lhs=jnp.where(y==0,block_ref[tok(i),:],long_ref[tok(i),:])
        hid[tok(i),:]=nn(lhs,ws[near,:])
    pass_on(4,"Y",wd,0,((10,"C"),))
    pass_on(5,"X",wd,1,((11,"C"),))
    net.got(7,"C",ws.at[srows(wy,1-c,1)])
    net.got(9,"C",ws.at[srows(wy,1-c,0)])
    net.got(10,"C",ws.at[srows(wd,1-c,0)])
    net.got(11,"C",ws.at[srows(wd,1-c,1)])
    for k,t,b in ((30,"X",wx),(31,"Y",wy),(32,"D",wd)): net.got(k,t,vs.at[b])
    gain=jnp.concatenate([vs[p,0:1,:] for p in range(4)],axis=1)
    shift=jnp.concatenate([vs[p,1:2,:] for p in range(4)],axis=1)
    def nrows(b,i): return pl.ds(mul(b*tokens+i*tc,16),tc)
    def spread(i,t):
        net.start((18 if t=="X" else 22)+i,t,ns.at[nrows(w,i)],ns.at[nrows(w,i)])
    for i in range(4):
        r=tok(i)
        lhs=jnp.where(y==0,long_ref[r,:],block_ref[r,:])
        h=hid[r,:]+nn(lhs,ws[far,:])
        hid[r,:]=h
        cen=h-jnp.mean(h,axis=1,keepdims=True)
        inv=lax.rsqrt(jnp.mean(cen*cen,axis=1,keepdims=True)+1e-5)
        ns[nrows(w,i),:]=(cen*inv*gain+shift).astype(BF)
        spread(i,"XYXY"[i])
    for i,t in ((1,"X"),(0,"Y"),(3,"X"),(2,"Y")): spread(i,t)
    outs=[]
    def put(k,src,dst):
        copy=pltpu.make_async_copy(src,dst,local.at[k]); copy.start(); outs.append(copy)
    put(2,ws,wskip_out); put(3,hid,hidden_out); put(7,vs,vec_out)
    for j,(t,b) in enumerate((("X",wx),("Y",wy),("D",wd))):
        net.got(12+j,t,hs.at[hrows(b,c)])
        net.start(15+j,"C",hs.at[hrows(b,c)],hs.at[hrows(b,c)])
    for j,b in enumerate((wx,wy,wd)):
        net.got(15+j,"C",hs.at[hrows(b,1-c)])
    own_heads.wait()
    put(4,hs,heads_out)
    def project(b,i): qs[nrows(b,i),:]=nn(ns[nrows(b,i),:],hs[...]).astype(BF)
    @pl.loop(0,4)
    def _(i): project(w,i)
    for i,t,b,k,k2,t2 in ((0,"X",wx,18,26,"Y"),(1,"Y",wy,22,27,"X"),(2,"X",wx,18,28,"Y"),(3,"Y",wy,22,29,"X")):
        net.got(k+i,t,ns.at[nrows(b,i)])
        net.start(k2,t2,ns.at[nrows(b,i)],ns.at[nrows(b,i)])
    @pl.loop(0,2)
    def _(i): project(wx,2*i)
    @pl.loop(0,2)
    def _(i): project(wy,2*i+1)
    for i in (1,3):
        net.got(18+i,"X",ns.at[nrows(wx,i)])
        project(wx,i)
        net.got(22+i-1,"Y",ns.at[nrows(wy,i-1)])
        project(wy,i-1)
    for i,t,k in ((0,"Y",26),(1,"X",27),(2,"Y",28),(3,"X",29)):
        net.got(k,t,ns.at[nrows(wd,i)])
        project(wd,i)
    put(5,ns,normed_out); put(6,qs,qkv_out)
    for copy in outs: copy.wait()
    net.finish()

def first(block,long,skipw,qkvw,vecs):
    tokens,d=block.shape; S=jax.ShapeDtypeStruct; hd3=qkvw.shape[1]//4
    V=pltpu.VMEM
    return pl.pallas_call(first_kernel,
        out_shape=(S((tokens,d),F32),S((4*tokens,d),BF),S((4*tokens,hd3),BF),S((d,hd3),BF),S((2*d,d),BF),S((4,)+vecs.shape,F32)),
        in_specs=[VM]*5,out_specs=(ANY,)*6,
        scratch_shapes=[V((2*d,d),BF),V((4*tokens,d),BF),V((d,hd3),BF),V((4,d//4,hd3),BF),V((tokens,d),F32),V((4*tokens,hd3),BF),V((4,)+vecs.shape,F32),
            pltpu.SemaphoreType.DMA((33,)),pltpu.SemaphoreType.DMA((33,)),pltpu.SemaphoreType.DMA((8,))],
        compiler_params=pltpu.CompilerParams(vmem_limit_bytes=56*2**20,collective_id=0,has_side_effects=True),
        cost_estimate=pl.CostEstimate(flops=2*tokens*d*d*5,bytes_accessed=40*2**20,transcendentals=0))(
        block,long,skipw,qkvw,vecs)

class Chain:
    def __init__(self,net,k,own,up_in,down_in):
        self.net,self.k,self.own=net,k,own
        self.up_in,self.down_in=up_in,down_in
        self.z,self.n=lax.axis_index("z"),lax.axis_size("z")
    def copy(self,up,src):
        k=self.k+(0 if up else 1)
        return pltpu.make_async_remote_copy(src_ref=src,dst_ref=self.up_in if up else self.down_in,
            send_sem=self.net.send.at[k],recv_sem=self.net.recv.at[k],
            device_id={"z":self.z+1 if up else self.z-1},device_id_type=MESH)
    def hop(self,h):
        for up in (True,False):
            inn,other=(self.up_in,self.down_in) if up else (self.down_in,self.up_in)
            last_one=self.n-1-h<h or (self.n-1-h==h and not up)
            @pl.when(self.z==(h if up else self.n-1-h))
            def _():
                if h==0:
                    self.copy(up,self.own).start()
                else:
                    self.copy(up,inn).wait_recv()
                    mine,came=self.own[...].astype(F32),inn[...].astype(F32)
                    inn[...]=(mine+came).astype(inn.dtype)
                    if last_one:
                        self.own[...]=(other[...].astype(F32)+came).astype(self.own.dtype)
                    self.copy(up,inn).start()
    def total(self):
        first,final=self.z==0,self.z==self.n-1
        for end,up,inn in ((first,True,self.down_in),(final,False,self.up_in)):
            @pl.when(end)
            def _():
                self.copy(not up,inn).wait_recv()
                self.copy(up,self.own).wait_send()
                self.own[...]=(self.own[...].astype(F32)+inn[...].astype(F32)).astype(self.own.dtype)
        @pl.when(jnp.logical_not(first|final))
        def _():
            self.copy(True,self.up_in).wait_send()
            self.copy(False,self.down_in).wait_send()

def meet_all(net,who):
    z,n=lax.axis_index("z"),lax.axis_size("z")
    barrier=pltpu.get_barrier_semaphore()
    for t in who:
        pl.semaphore_signal(barrier,inc=1,device_id=net.to[t],device_id_type=MESH)
    @pl.when(z>0)
    def _(): pl.semaphore_signal(barrier,inc=1,device_id={"z":z-1},device_id_type=MESH)
    @pl.when(z<n-1)
    def _(): pl.semaphore_signal(barrier,inc=1,device_id={"z":z+1},device_id_type=MESH)
    ends=(z==0)|(z==n-1)
    @pl.when(ends)
    def _(): pl.semaphore_wait(barrier,len(who)+1)
    @pl.when(jnp.logical_not(ends))
    def _(): pl.semaphore_wait(barrier,len(who)+2)

SEG=3
def last_kernel(gq_ref,heads_ref,normed_ref,hidden_ref,gmid_ref,gain_ref,block_ref,long_ref,wskip_ref,small_ref,eu_ref,ed_ref,eo_ref,
                gin_out,gsk_out,small_out,gqkv_out,gskip_out,early_out,late_out,
                big,part,rx,ry,dx,dy,gw,gwr,gsr,qz,fq,sdx,sdy,srx,sry,own,sz,fs,sm,sin,smz,es,eup,edown,hg,send,recv,local,esem,hsem):
    x,y,c,w,wx,wy,wd=place()
    tokens,d=block_ref.shape
    tc=tokens//4; kr=d//4; kh=kr//2; sr=d//2; sh=sr//2; sq=sh//2
    mul=pl.multiple_of
    net=Links(send,recv)
    load=pltpu.make_async_copy(normed_ref,big,local.at[0])
    load.start()
    eseg=[pl.ds(i*kh,kh) for i in range(9)]
    eload=[pltpu.make_async_copy(eu_ref.at[:,pl.ds(i*d,d)] if i<4 else ed_ref.at[pl.ds((i-4)*kh,kh)] if i<8 else eo_ref,es.at[eseg[i]],esem.at[i]) for i in range(9)]
    for copy in eload: copy.start()
    ford=(0,2,1,3)
    def stream(j):
        r=pl.ds(ford[j]*tc,tc)
        return [pltpu.make_async_copy(ref.at[r],hg.at[j%2,m],hsem.at[j%2,m]) for m,ref in enumerate((hidden_ref,gmid_ref))]
    for j in range(2):
        for copy in stream(j): copy.start()
    meet_all(net,"XYDC")
    def tok(i): return pl.ds(i*tc,tc)
    early=[Chain(net,56+2*i,es.at[r],eup.at[r],edown.at[r]) for i,r in enumerate(eseg)]
    for copy in eload: copy.wait()
    halves=[pl.ds(i*2*kh,2*kh) for i in range(2)]
    mids=[Chain(net,40+2*i,gwr.at[r],qz.at[0,r],qz.at[1,r]) for i,r in enumerate(halves)]
    queue=early[:3]+mids+early[3:]
    for chain in queue[:3]: chain.hop(0)
    def tick(i):
        for h in range(1,lax.axis_size("z")-1):
            if 0<=i-h+1<len(queue): queue[i-h+1].hop(h)
    def pr(s,i): return pl.ds(s*tokens+i*tc,tc)
    def partial(b,i):
        return nt(gq_ref[pl.ds(mul(b*tokens+i*tc,16),tc),:],heads_ref[...])
    for i,t,dst,k in ((0,"X",dx,0),(2,"Y",dy,2),(1,"X",dx,1),(3,"Y",dy,3)):
        part[pr(2,i),:]=partial(wd,i).astype(BF)
        net.start(k,t,part.at[pr(2,i)],dst.at[tok(i%2)])
    for i,t,b,dst,k in ((0,"X",wx,rx,4),(2,"Y",wy,ry,10),(1,"X",wx,rx,5),(3,"Y",wy,ry,11)):
        s=0 if t=="X" else 1
        part[pr(s,i),:]=partial(b,i).astype(BF)
        net.start(k,t,part.at[pr(s,i)],dst.at[tok(i)])
    @pl.loop(0,4)
    def _(i):
        r=pl.ds(mul(i*tc,16),tc)
        part[pl.ds(mul(3*tokens+i*tc,16),tc),:]=nt(gq_ref[pl.ds(mul(w*tokens+i*tc,16),tc),:],heads_ref[...]).astype(BF)
    load.wait()
    cc=d//3
    def weight_grad(k):
        cr=pl.ds(k*cc,cc)
        gw[cr,:]=tn(big[:,cr],gq_ref[...]).astype(BF)
    def relay(i,t,b,dst,k,src,k2,t2):
        s=0 if t=="X" else 1
        mine=partial(b,i)
        net.got(k2,t2,src.at[tok(i%2)])
        part[pr(s,i),:]=(mine+src[tok(i%2),:].astype(F32)).astype(BF)
        net.start(k,t,part.at[pr(s,i)],dst.at[tok(i)])
    weight_grad(0)
    relay(2,"X",wx,rx,6,dy,2,"Y")
    relay(0,"Y",wy,ry,8,dx,0,"X")
    weight_grad(1)
    tick(0)
    weight_grad(2)
    def rows(b,core): return pl.ds(mul(b*kr+core*kh,16),kh)
    for b in range(4):
        net.start(12+b,"C",gw.at[rows(b,1-c)],gwr.at[pl.ds(b*kh,kh)])
    relay(3,"X",wx,rx,7,dy,3,"Y")
    tick(1)
    relay(1,"Y",wy,ry,9,dx,1,"X")
    tick(2)
    for b in range(4):
        r=pl.ds(b*kh,kh)
        net.got(12+b,"C",gwr.at[r])
        gwr[r,:]=(gwr[r,:].astype(F32)+gw[rows(b,c),:].astype(F32)).astype(BF)
    for chain in queue[3:]: chain.hop(0)
    gain=gain_ref[...]
    sm[...]=jnp.zeros_like(sm)
    for j,i in enumerate(ford):
        r=tok(i)
        tick(3+j)
        for copy in stream(j): copy.wait()
        net.got(4+i,"X",rx.at[r])
        net.got(8+i,"Y",ry.at[r])
        gf=part[pr(3,i),:].astype(F32)+rx[r,:].astype(F32)+ry[r,:].astype(F32)
        h=hg[j%2,0]
        cen=h-jnp.mean(h,axis=1,keepdims=True)
        inv=lax.rsqrt(jnp.mean(cen*cen,axis=1,keepdims=True)+1e-5)
        xhat=cen*inv
        sm[0:1,:]+=jnp.sum(gf*xhat,axis=0,keepdims=True)
        sm[1:2,:]+=jnp.sum(gf,axis=0,keepdims=True)
        e=gf*gain
        back=e-jnp.mean(e,axis=1,keepdims=True)-xhat*jnp.mean(e*xhat,axis=1,keepdims=True)
        big[pl.ds(2*d+i*tc,tc),:]=(hg[j%2,1]+back*inv).astype(BF)
        if j<2:
            for copy in stream(j+2): copy.start()
    sm[2:4,:]=small_ref[0:2,:]
    lates=[pltpu.make_async_copy(block_ref,rx,local.at[2]),pltpu.make_async_copy(long_ref,ry,local.at[3])]
    for copy in lates: copy.start()
    tick(7)
    for chain in mids: chain.total()
    def qrows(b): return pl.ds(mul(b*kh,16),kh)
    for j,(t,b) in enumerate((("X",wx),("Y",wy),("D",wd))):
        net.start(29+j,t,gwr.at[qrows(b)],fq.at[w,c])
    fq[w,c]=gwr[qrows(w),:]
    for copy in lates: copy.wait()
    for k in range(6):
        src=rx if k<3 else ry
        big[pl.ds(k*cc,cc),:]=tn(src[:,(k%3)*cc:(k%3+1)*cc],big[2*d:2*d+tokens,:]).astype(BF)
    def srows(b,core): return pl.ds(mul(b*sr+core*sh,16),sh)
    for b in range(4):
        net.start(16+b,"C",big.at[srows(b,1-c)],gsr.at[pl.ds(b*sh,sh)])
    net.start(20,"C",sm,sin.at[0])
    tick(8)
    for copy in net.sent[:16]: copy.wait_send()
    net.sent=net.sent[16:]
    wload=pltpu.make_async_copy(wskip_ref,part.at[pl.ds(0,2*d)],local.at[1])
    wload.start()
    for b in range(4):
        r=pl.ds(b*sh,sh)
        net.got(16+b,"C",gsr.at[r])
        gsr[r,:]=(gsr[r,:].astype(F32)+big[srows(b,c),:].astype(F32)).astype(BF)
    def quarter(b,i): return pl.ds(mul(b*sh+i*sq,16),sq)
    top,low=pl.ds(0,sq),pl.ds(sq,sq)
    net.start(21,"X",gsr.at[quarter(wd,0)],sdx)
    net.start(22,"Y",gsr.at[quarter(wd,1)],sdy)
    net.start(23,"X",gsr.at[quarter(wx,0)],srx.at[top])
    net.start(24,"Y",gsr.at[quarter(wy,1)],sry.at[low])
    tick(9)
    net.got(20,"C",sin.at[0])
    smz[6]=sm[...]+sin[0]
    net.start(27,"X",smz.at[6],sin.at[1])
    wload.wait()
    @pl.loop(0,4)
    def _(i):
        r=pl.ds(mul(i*tc,16),tc)
        gh=big[pl.ds(mul(2*d+i*tc,16),tc),:]
        rx[r,:]=nt(gh,part[:d,:]).astype(BF)
        ry[r,:]=nt(gh,part[d:2*d,:]).astype(BF)
    outs=[]
    def put(k,src,dst):
        copy=pltpu.make_async_copy(src,dst,local.at[k]); copy.start(); outs.append(copy)
    put(2,rx,gin_out); put(3,ry,gsk_out)
    tick(10)
    net.got(21,"X",sdx)
    gsr[quarter(wy,0),:]=(gsr[quarter(wy,0),:].astype(F32)+sdx[...].astype(F32)).astype(BF)
    net.start(25,"Y",gsr.at[quarter(wy,0)],sry.at[top])
    net.got(22,"Y",sdy)
    gsr[quarter(wx,1),:]=(gsr[quarter(wx,1),:].astype(F32)+sdy[...].astype(F32)).astype(BF)
    net.start(26,"X",gsr.at[quarter(wx,1)],srx.at[low])
    for i in range(11,len(queue)+lax.axis_size("z")-3): tick(i)
    net.got(27,"X",sin.at[1])
    smz[0]=smz[6]+sin[1]
    net.start(28,"Y",smz.at[0],sin.at[2])
    for j,(t,b) in enumerate((("X",wx),("Y",wy),("D",wd))):
        net.got(29+j,t,fq.at[b,c])
    for b in range(4):
        net.start(32+b,"C",fq.at[b,c],fq.at[b,c])
    net.got(28,"Y",sin.at[2])
    smz[1]=smz[0]+sin[2]
    net.got(23,"X",srx.at[top]); net.got(25,"Y",sry.at[top])
    net.got(24,"Y",sry.at[low]); net.got(26,"X",srx.at[low])
    own[...]=(gsr[pl.ds(mul(w*sh,16),sh),:].astype(F32)+srx[...].astype(F32)+sry[...].astype(F32)).astype(BF)
    seg=sh//SEG
    chains=[Chain(net,44,smz.at[1],smz.at[2],smz.at[3])]
    for i in range(SEG):
        r=pl.ds(i*seg,seg)
        chains.append(Chain(net,46+2*i,own.at[r],sz.at[0,r],sz.at[1,r]))
    for h in range(lax.axis_size("z")-1):
        for chain in chains: chain.hop(h)
    for chain in chains: chain.total()
    net.start(36,"C",own,fs)
    for i,chain in enumerate(early):
        chain.total()
        net.start(74+i,"C",es.at[eseg[i]],late_out.at[eseg[i]])
    put(8,es,early_out)
    for b in range(4): net.got(32+b,"C",fq.at[b,1-c])
    put(4,fq,gqkv_out); put(5,smz.at[1],small_out); put(6,own,gskip_out.at[c])
    net.got(36,"C",fs)
    put(7,fs,gskip_out.at[1-c])
    for i,r in enumerate(eseg): net.got(74+i,"C",late_out.at[r])
    for copy in outs: copy.wait()
    net.finish()

def last(gq,heads,normed,hidden,gmid,gain,block,long,wskip,small,eu,ed,eo):
    tokens,d=block.shape; S=jax.ShapeDtypeStruct; hd3=gq.shape[1]
    V=pltpu.VMEM
    return pl.pallas_call(last_kernel,
        out_shape=(S((tokens,d),BF),S((tokens,d),BF),S((8,d),F32),S((4,2,d//8,hd3),BF),S((2,d//4,d),BF),S((9*d//8,d),BF),S((9*d//8,d),BF)),
        in_specs=[VM,VM,ANY,ANY,ANY,VM,ANY,ANY,ANY,VM,ANY,ANY,ANY],out_specs=(ANY,)*7,
        scratch_shapes=[V((4*tokens,d),BF),V((4*tokens,d),BF),V((tokens,d),BF),V((tokens,d),BF),V((tokens//2,d),BF),V((tokens//2,d),BF),
            V((d,hd3),BF),V((d//2,hd3),BF),V((d,d),BF),V((2,d//2,hd3),BF),V((4,2,d//8,hd3),BF),
            V((d//8,d),BF),V((d//8,d),BF),V((d//4,d),BF),V((d//4,d),BF),V((d//4,d),BF),V((2,d//4,d),BF),V((d//4,d),BF),
            V((8,d),F32),V((3,8,d),F32),V((7,8,d),F32),
            V((9*d//8,d),BF),V((9*d//8,d),BF),V((9*d//8,d),BF),V((2,2,tokens//4,d),F32),
            pltpu.SemaphoreType.DMA((83,)),pltpu.SemaphoreType.DMA((83,)),pltpu.SemaphoreType.DMA((9,)),pltpu.SemaphoreType.DMA((9,)),pltpu.SemaphoreType.DMA((2,2))],
        compiler_params=pltpu.CompilerParams(vmem_limit_bytes=63*2**20,collective_id=1,has_side_effects=True),
        cost_estimate=pl.CostEstimate(flops=2*tokens*d*d*10,bytes_accessed=60*2**20,transcendentals=0))(
        gq,heads,normed,hidden,gmid,gain,block,long,wskip,small,eu,ed,eo)

SPLIT=((0,640),(640,512))
def middle_kernel(hidden_ref,att_ref,tail_ref,g_ref,gain_ref,shift_ref,outw_ref,outx_ref,outy_ref,upw_ref,upx_ref,upy_ref,dnw_ref,
                  lay_out,gmid_ref,gh_out,ght_out,gow_out,small_ref,gup_out,gdn_out,sxu_out,sxd_out,syu_out,syd_out,uland,dland,ux_out,uy_out,dx_out,dy_out,
                  att_in,tail_in,att_s,outw_s,n2_s,xhat_s,rstd_s,lay_s,act_s,gu_s,upb,dnb,gub,gdb,land_u,land_d,low_s,
                  send,recv,csend,crecv,fetch_sem,flush_sem,local,usem,urecv,bring_sem):
    x,y,c,w,wx,wy,wd=place()
    tokens,d=hidden_ref.shape
    wide_cols=att_ref.shape[1]; quarter=tail_ref.shape[1]//4; cols=wide_cols+quarter
    kr=d//4; kh=kr//2; dh=d//2; dq=dh//2
    tc=tokens//4; th=tokens//2
    mul=pl.multiple_of
    net=Links(send,recv)
    left=[]
    def start(k,t,src,dst,view):
        pltpu.make_async_remote_copy(src_ref=src,dst_ref=dst,send_sem=send.at[k],recv_sem=recv.at[k],
                                     device_id=net.to[t],device_id_type=MESH).start()
        left.append((k,t,view))
    def blk(b): return pl.ds(mul(b*d,128),d)
    def urow(b,core): return pl.ds(mul(b*kr+core*kh,16),kh)
    def drow(b,core,p): return pl.ds(mul(b*d+core*dh+p*dq,16),dq)
    def trow(b): return pl.ds(mul(b*tokens,16),tokens)
    def tails(b): return pl.ds(mul(b*tc,16),tc)
    uview=uland.at[pl.ds(0,kh),pl.ds(0,d)]
    dview=dland.at[pl.ds(0,dq)]
    net.meet("XYDC")
    for j,(t,b) in enumerate((("X",wx),("Y",wy),("D",wd))):
        start(j,t,att_ref.at[trow(b)],att_in.at[w],att_in.at[0])
        start(52+j,t,tail_ref.at[tails(b)],tail_in.at[w],tail_in.at[0])
    own_att=[pltpu.make_async_copy(att_ref.at[trow(w)],att_in.at[w],local.at[0]),pltpu.make_async_copy(tail_ref.at[tails(w)],tail_in.at[w],local.at[3])]
    for copy in own_att: copy.start()
    cut=kh//32*16+16
    def orow(b,core,lo,n): return pl.ds(mul(b*kr+core*kh+lo,16),n)
    start(3,"Y",outx_ref.at[pl.ds(0,cut)],outw_s.at[orow(wx,c,0,cut)],outw_s.at[pl.ds(0,cut)])
    start(4,"X",outy_ref.at[pl.ds(cut,kh-cut)],outw_s.at[orow(wy,c,cut,kh-cut)],outw_s.at[pl.ds(0,kh-cut)])
    start(5,"C",outx_ref,outw_s.at[urow(wx,c)],outw_s.at[pl.ds(0,kh)])
    start(6,"C",outy_ref,outw_s.at[urow(wy,c)],outw_s.at[pl.ds(0,kh)])
    start(7,"Y",upx_ref.at[:,blk(wy)],uland.at[urow(wx,c),blk(wy)],uview)
    start(8,"X",upy_ref.at[:,blk(w)],uland.at[urow(wy,c),blk(w)],uview)
    order=(w,wx,wd,wy)
    def up_core(i):
        start(11+2*i,"C",upx_ref.at[:,blk(order[i])],uland.at[urow(wx,c),blk(order[i])],uview)
        start(12+2*i,"C",upy_ref.at[:,blk(order[i])],uland.at[urow(wy,c),blk(order[i])],uview)
    up_core(0)
    outw_s[pl.ds(mul(w*kr,16),kr),:]=outw_ref[...]
    outw_s[urow(wx,c),:]=outx_ref[...]
    outw_s[urow(wy,c),:]=outy_ref[...]

    diag_id=(7,8,9,10)
    def diag_from(i): return "YX"[i%2]
    def up_relay(i):
        view=uland.at[urow(wd,c),blk(order[i])]
        net.got(diag_id[i],diag_from(i),view)
        start(19+i,"C",view,view,uview)
    def up_sources(i):
        b=order[i]
        net.got(11+2*i,"C",uland.at[urow(wx,1-c),blk(b)])
        net.got(12+2*i,"C",uland.at[urow(wy,1-c),blk(b)])
        net.got(19+i,"C",uland.at[urow(wd,1-c),blk(b)])
        return [(upw_ref.at[:,blk(b)],pl.ds(mul(w*kr,16),kr)),(upx_ref.at[:,blk(b)],urow(wx,c)),(upy_ref.at[:,blk(b)],urow(wy,c)),
                (uland.at[urow(wx,1-c),blk(b)],urow(wx,1-c)),(uland.at[urow(wy,1-c),blk(b)],urow(wy,1-c)),
                (uland.at[pl.ds(mul(wd*kr,16),kr),blk(b)],pl.ds(mul(wd*kr,16),kr))]
    def fetch(i):
        slot=i%2
        for j,(src,rows) in enumerate(up_sources(i)):
            pltpu.make_async_copy(src,upb.at[slot,rows],fetch_sem.at[slot,j]).start()
        src=dnw_ref if i==0 else dland.at[pl.ds(mul(order[i]*d,16),d)]
        pltpu.make_async_copy(src,dnb.at[slot],fetch_sem.at[slot,6]).start()
    def fetched(slot):
        for j,n in enumerate((kr,kh,kh,kh,kh,kr)):
            view=upb.at[slot,pl.ds(0,n)]
            pltpu.make_async_copy(view,view,fetch_sem.at[slot,j]).wait()
        pltpu.make_async_copy(dnb.at[slot],dnb.at[slot],fetch_sem.at[slot,6]).wait()
    def down_relay(k,t,b,p,onward):
        r=drow(b,c,p)
        net.got(k,t,dland.at[r])
        for k2,t2 in onward: start(k2,t2,dland.at[r],dland.at[r],dview)
    def down_core(k,b,p): net.got(k,"C",dland.at[drow(b,1-c,p)])

    for j,(t,b) in enumerate((("X",wx),("Y",wy),("D",wd))):
        net.got(j,t,att_in.at[b])
        net.got(52+j,t,tail_in.at[b])
    start(9,"Y",upx_ref.at[:,blk(wx)],uland.at[urow(wx,c),blk(wx)],uview)
    start(10,"X",upy_ref.at[:,blk(wd)],uland.at[urow(wy,c),blk(wd)],uview)
    def dmine(p): return dnw_ref.at[pl.ds(mul(c*dh+p*dq,16),dq)]
    start(23,"X",dmine(0),dland.at[drow(w,c,0)],dview)
    start(25,"Y",dmine(1),dland.at[drow(w,c,1)],dview)
    start(24,"X",dmine(1),dland.at[drow(w,c,1)],dview)
    start(26,"Y",dmine(0),dland.at[drow(w,c,0)],dview)
    net.got(3,"Y",outw_s.at[orow(wd,c,0,cut)])
    net.got(4,"X",outw_s.at[orow(wd,c,cut,kh-cut)])
    start(35,"C",outw_s.at[urow(wd,c)],outw_s.at[urow(wd,c)],outw_s.at[pl.ds(0,kh)])
    up_relay(0)
    for i in (1,2,3): up_core(i)
    net.got(5,"C",outw_s.at[urow(wx,1-c)]); net.got(6,"C",outw_s.at[urow(wy,1-c)])
    net.got(35,"C",outw_s.at[urow(wd,1-c)])
    for copy in own_att: copy.wait()
    fetch(0)
    gain=gain_ref[...]; shift=shift_ref[...]
    for i in range(4):
        r=pl.ds(i*tc,tc)
        joined=jnp.concatenate([v for p in range(4) for v in (att_in[p,r,:],tail_in[p,:,i*quarter:(i+1)*quarter])],axis=1)
        att_s[r,:]=joined
        mid=hidden_ref[r,:]+nn(joined,outw_s[...])
        lay_s[r,:]=mid
        cen=mid-jnp.mean(mid,axis=1,keepdims=True)
        inv=lax.rsqrt(jnp.mean(cen*cen,axis=1,keepdims=True)+1e-5)
        xhat=cen*inv
        xhat_s[r,:]=xhat
        rstd_s[r,:]=jnp.broadcast_to(inv,(tc,128))
        n2_s[r,:]=(xhat*gain+shift).astype(BF)
        gmid_ref[r,:]=jnp.zeros((tc,d),F32)

    def pieces(slot):
        out=[(gub,pl.ds(mul(p*kr+(1-c)*kh,16),kh),land_u.at[slot,pl.ds(p*kh,kh)]) for p in range(4)]
        return out+[(gdb,pl.ds(mul((1-c)*dh,16),dh),land_d.at[slot])]
    def exchange(slot,act):
        for j,(ref,r,dst) in enumerate(pieces(slot)):
            act(pltpu.make_async_remote_copy(src_ref=ref.at[r],dst_ref=dst,send_sem=csend.at[slot,j],recv_sem=crecv.at[slot,j],
                                             device_id=net.to["C"],device_id_type=MESH))
    def flush(b,act):
        for p in range(4):
            act(pltpu.make_async_copy(gub.at[pl.ds(mul(p*kr+c*kh,16),kh)],gup_out.at[pl.ds(p*kh,kh),blk(b)],flush_sem.at[p]))
        act(pltpu.make_async_copy(gdb.at[pl.ds(mul(c*dh,16),dh)],gdn_out.at[pl.ds(mul(b*dh,16),dh)],flush_sem.at[4]))
    go=lambda copy: copy.start()
    done=lambda copy: copy.wait()
    def finalize(i):
        slot=lax.rem(i,2)
        exchange(slot,lambda copy: copy.wait())
        for p in range(4):
            r=pl.ds(mul(p*kr+c*kh,16),kh)
            gub[r,:]=(gub[r,:].astype(F32)+land_u[slot,pl.ds(p*kh,kh),:].astype(F32)).astype(BF)
        for p in range(2):
            r=pl.ds(mul(c*dh+p*dq,16),dq)
            gdb[r,:]=(gdb[r,:].astype(F32)+land_d[slot,pl.ds(p*dq,dq),:].astype(F32)).astype(BF)
    def block_of(i):
        return 2*lax.rem(y+i//2,2)+lax.rem(x+(i+1)//2,2)

    usend=[pl.ds(0,cut),pl.ds(cut,kh-cut)]
    def ahead(i,b,act):
        for j,(t,dst) in enumerate((("X",ux_out),("Y",uy_out))):
            n=usend[j]
            src=gup_out.at[pl.ds(mul(wd*kh+n.start,16),n.size),blk(b)]
            act(pltpu.make_async_remote_copy(src_ref=src,dst_ref=dst.at[:,blk(b)],send_sem=usem.at[i,j],recv_sem=urecv.at[i,j],
                                             device_id=net.to[t],device_id_type=MESH))
    def ahead_down(act):
        for j,(t,dst) in enumerate((("X",dx_out),("Y",dy_out))):
            act(pltpu.make_async_remote_copy(src_ref=gdn_out.at[pl.ds(mul(wd*dh+j*dq,16),dq)],dst_ref=dst,
                                             send_sem=usem.at[4,j],recv_sem=urecv.at[4,j],device_id=net.to[t],device_id_type=MESH))
    def weight_grads():
        for lo,n in SPLIT:
            f=pl.ds(lo,n)
            gdb[f,:]=tn(act_s[:,f],g_ref[...]).astype(BF)
            gub[f,:]=tn(n2_s[:,f],gu_s[...]).astype(BF)
    @pl.loop(0,4)
    def _(i):
        slot=lax.rem(i,2)
        fetched(slot)
        @pl.loop(0,2)
        def _(t):
            r=pl.ds(mul(t*th,16),th)
            for lo,n in SPLIT:
                f=pl.ds(lo,n)
                u=nn(n2_s[r,:],upb[slot,:,f])
                a,dg=gelu_parts(u)
                act_s[r,f]=a.astype(BF)
                gu_s[r,f]=(nt(g_ref[r,:],dnb[slot,f,:])*dg).astype(BF)
        @pl.when(i>=1)
        def _():
            finalize(i-1)
            flush(block_of(i-1),go)
        @pl.when(i==0)
        def _():
            for j in (1,2,3): up_relay(j)
        @pl.loop(0,2)
        def _(t):
            r=pl.ds(mul(t*th,16),th)
            for lo,n in SPLIT:
                f=pl.ds(lo,n)
                lay_s[r,f]+=nn(act_s[r,:],dnb[slot,:,f])
                gmid_ref[r,f]+=nt(gu_s[r,:],upb[slot,f,:])
        @pl.when(i==0)
        def _():
            down_relay(23,"X",wx,0,((27,"Y"),(29,"C")))
            down_relay(25,"Y",wy,1,((28,"X"),(30,"C")))
            down_relay(24,"X",wx,1,((31,"C"),))
            down_core(29,wx,0); down_core(31,wx,1)
            fetch(1)
        @pl.when(i==1)
        def _():
            down_relay(27,"Y",wd,0,((33,"C"),))
            down_relay(28,"X",wd,1,((34,"C"),))
            down_relay(26,"Y",wy,0,((32,"C"),))
            down_core(33,wd,0); down_core(34,wd,1)
            fetch(2)
        @pl.when(i==2)
        def _():
            down_core(30,wy,1); down_core(32,wy,0)
            fetch(3)
        @pl.when(i>=1)
        def _():
            flush(block_of(i-1),done)
            ahead(i-1,block_of(i-1),go)
        @pl.when(i==3)
        def _(): ahead_down(go)
        @pl.when(i<3)
        def _():
            weight_grads()
            exchange(slot,go)
    small_ref[...]=jnp.zeros_like(small_ref)
    for i in range(4):
        r=pl.ds(i*tc,tc)
        gs=gmid_ref[r,:]; xhat=xhat_s[r,:]
        small_ref[0:1,:]+=jnp.sum(gs*xhat,axis=0,keepdims=True)
        small_ref[1:2,:]+=jnp.sum(gs,axis=0,keepdims=True)
        e=gs*gain
        back=e-jnp.mean(e,axis=1,keepdims=True)-xhat*jnp.mean(e*xhat,axis=1,keepdims=True)
        gm=g_ref[r,:].astype(F32)+back*rstd_s[r,0:1]
        gmid_ref[r,:]=gm
        low=gm.astype(BF)
        low_s[r,:]=low
        ga=nt(low,outw_s[...]).astype(BF)
        for p in range(4):
            att_in[p,r,:]=ga[:,p*cols:p*cols+wide_cols]
            tail_in[p,:,i*quarter:(i+1)*quarter]=ga[:,p*cols+wide_cols:(p+1)*cols]
        for j,(t,b) in enumerate((("X",wx),("Y",wy),("D",wd))):
            start(36+3*i+j,t,att_in.at[b,r],gh_out.at[w,r],gh_out.at[0,pl.ds(0,tc)])
    for j,(t,b) in enumerate((("X",wx),("Y",wy),("D",wd))):
        start(55+j,t,tail_in.at[b],ght_out.at[w],tail_in.at[0])
    own_grad=[pltpu.make_async_copy(att_in.at[w],gh_out.at[w],local.at[2]),pltpu.make_async_copy(tail_in.at[w],ght_out.at[w],local.at[0])]
    for copy in own_grad: copy.start()
    weight_grads()
    exchange(1,go)
    act_s[...]=lay_s[...].astype(BF)
    lay_copy=pltpu.make_async_copy(act_s,lay_out,local.at[1])
    lay_copy.start()
    finalize(3)
    flush(wy,go)
    flush(wy,done)
    ahead(3,wy,go)
    for lo,n in SPLIT:
        f=pl.ds(lo,n)
        gub[f,:]=tn(att_s[:,f],low_s[...]).astype(BF)
    for p in range(4):
        start(48+p,"C",gub.at[pl.ds(mul(p*kr+(1-c)*kh,16),kh)],land_u.at[0,pl.ds(p*kh,kh)],land_u.at[0,pl.ds(0,kh)])
    def bring(k,src,dst):
        copy=pltpu.make_async_copy(src,dst,bring_sem.at[k]); copy.start(); return copy
    def spot(j,b): return pl.ds((4*j+b)*kh,kh)
    copies=[]
    for j,b2 in enumerate((wx,wy)):
        for b in range(4):
            copies.append(bring(4*j+b,gup_out.at[pl.ds(mul(b2*kh,16),kh),pl.ds(b*d,d)],upb.at[0,spot(j,b)]))
        copies.append(bring(16+j,gdn_out.at[pl.ds(mul(b2*dh,16),dh)],dnb.at[0,pl.ds(j*dh,dh)]))
    for i in range(4): ahead(i,order[i],done)
    ahead_down(done)
    for j,(src,n) in enumerate(((uy_out,usend[1]),(ux_out,usend[0]))):
        for b in range(4):
            copies.append(bring(8+4*j+b,src.at[:,pl.ds(b*d,d)],upb.at[1,pl.ds((4*j+b)*kh,n.size)]))
    copies.append(bring(18,dy_out,dnb.at[1,pl.ds(0,dq)]))
    copies.append(bring(19,dx_out,dnb.at[1,pl.ds(dq,dq)]))
    for copy in copies: copy.wait()
    copies=[]
    for j,(uo,do) in enumerate(((sxu_out,sxd_out),(syu_out,syd_out))):
        n=usend[1-j]
        for b in range(4):
            lo=(4*j+b)*kh
            r=pl.ds(lo+n.start,n.size)
            upb[0,r,:]=(upb[0,r,:].astype(F32)+upb[1,pl.ds(lo,n.size),:].astype(F32)).astype(BF)
            copies.append(bring(4*j+b,upb.at[0,spot(j,b)],uo.at[:,pl.ds(b*d,d)]))
        r=pl.ds(j*dh+(1-j)*dq,dq)
        dnb[0,r,:]=(dnb[0,r,:].astype(F32)+dnb[1,pl.ds(j*dq,dq),:].astype(F32)).astype(BF)
        copies.append(bring(16+j,dnb.at[0,pl.ds(j*dh,dh)],do.at[pl.ds(0,dh)]))
    for p in range(4):
        net.got(48+p,"C",land_u.at[0,pl.ds(p*kh,kh)])
        r=pl.ds(mul(p*kr+c*kh,16),kh)
        land_u[1,pl.ds(p*kh,kh),:]=(gub[r,:].astype(F32)+land_u[0,pl.ds(p*kh,kh),:].astype(F32)).astype(BF)
    for k,(b,dst) in enumerate(((w,gow_out.at[0]),(wd,gow_out.at[1]),(wx,sxd_out.at[pl.ds(dh,kh)]),(wy,syd_out.at[pl.ds(dh,kh)]))):
        copies.append(bring(8+k,land_u.at[1,pl.ds(mul(b*kh,16),kh)],dst))
    for i in range(4):
        for j,(t,b) in enumerate((("X",wx),("Y",wy),("D",wd))):
            net.got(36+3*i+j,t,gh_out.at[b,pl.ds(i*tc,tc)])
    for j,(t,b) in enumerate((('X',wx),('Y',wy),('D',wd))): net.got(55+j,t,ght_out.at[b])
    for copy in [lay_copy]+own_grad+copies: copy.wait()
    for k,t,view in left:
        pltpu.make_async_remote_copy(src_ref=view,dst_ref=view,send_sem=send.at[k],recv_sem=recv.at[k],
                                     device_id=net.to[t],device_id_type=MESH).wait_send()

def middle(hidden,att,tail,g,gain,shift,outw,outx,outy,upw,upx,upy,dnw):
    tokens,d=hidden.shape; cols=att.shape[1]; ff=upw.shape[1]
    S=jax.ShapeDtypeStruct; V=pltpu.VMEM; D=pltpu.SemaphoreType.DMA
    kh=d//8; cut=kh//32*16+16
    return pl.pallas_call(middle_kernel,
        out_shape=(S((tokens,d),BF),S((tokens,d),F32),S((4,tokens,cols),BF),S((4,tokens//4,tail.shape[1]),BF),S((2,kh,d),BF),S((8,d),F32),S((d//2,ff),BF),S((ff//2,d),BF),
                   S((kh,ff),BF),S((ff//8+kh,d),BF),S((kh,ff),BF),S((ff//8+kh,d),BF),
                   S((d,ff),BF),S((ff,d),BF),S((cut,ff),BF),S((kh-cut,ff),BF),S((ff//16,d),BF),S((ff//16,d),BF)),
        in_specs=[VM,ANY,ANY]+[VM]*6+[ANY]*4,out_specs=(ANY,VM,ANY,ANY,ANY,VM)+(ANY,)*12,
        scratch_shapes=[V((4,tokens,cols),BF),V((4,tokens//4,tail.shape[1]),BF),V((tokens,d),BF),V((d,d),BF),V((tokens,d),BF),V((tokens,d),F32),V((tokens,128),F32),
            V((tokens,d),F32),V((tokens,d),BF),V((tokens,d),BF),V((2,d,d),BF),V((2,d,d),BF),V((d,d),BF),V((d,d),BF),
            V((2,d//2,d),BF),V((2,d//2,d),BF),V((tokens,d),BF),D((58,)),D((58,)),D((2,5)),D((2,5)),D((2,7)),D((5,)),D((4,)),
            D((5,2)),D((5,2)),D((20,))],
        compiler_params=pltpu.CompilerParams(vmem_limit_bytes=63*2**20,collective_id=2,has_side_effects=True),
        cost_estimate=pl.CostEstimate(flops=2*tokens*d*(ff*6+d*3),bytes_accessed=60*2**20,transcendentals=tokens*ff*2))(
        hidden,att,tail,g,gain,shift,outw,outx,outy,upw,upx,upy,dnw)

def assemble_kernel(lay_ref,gin_ref,gsk_ref,skip_ref,gq_ref,em_ref,eo_ref,
                    lay_out,gin_out,gsk_out,skip_out,qkv_out,up_out,down_out,out_out,
                    s0,s1,s2,s3,s4,s5,s6,s7,local):
    first=lax.axis_index("core")==0
    copies=[]
    def put(src,dst):
        copy=pltpu.make_async_copy(src,dst,local.at[len(copies)]); copy.start(); copies.append(copy)
    def chunks(n,body,size=144):
        @pl.loop(0,n//size)
        def _(i): body(pl.ds(pl.multiple_of(i*size,16),size))
    def wide(dst,src):
        def body(r): dst[r,:]=src[r,:].astype(F32)
        chunks(dst.shape[0],body,208 if dst.shape[0]%208==0 else 144)
    wide(s7,lay_ref); put(s7,lay_out)
    wide(s0,gin_ref); put(s0,gin_out)
    wide(s1,gsk_ref); put(s1,gsk_out)
    kh=s6.shape[1]; d=s6.shape[2]
    def pair(dst,seg,rows,cols,size=48):
        @pl.loop(0,kh//size)
        def _(i):
            r=pl.ds(pl.multiple_of(seg*kh+i*size,16),size)
            to=pl.ds(pl.multiple_of(rows+i*size,16),size)
            m,o=em_ref[r,:].astype(F32),eo_ref[r,:].astype(F32)
            dst[0,to,cols]=jnp.where(first,m,o)
            dst[1,to,cols]=jnp.where(first,o,m)
    for b in range(4): pair(s4,b,0,pl.ds(b*d,d))
    put(s4,up_out)
    for b in range(4): pair(s5,4+b,b*kh,pl.ds(0,d))
    put(s5,down_out)
    pair(s6,8,0,pl.ds(0,d)); put(s6,out_out)
    def skip(r): s2[r,:]=skip_ref[r,:].astype(F32)
    chunks(s2.shape[0],skip); put(s2,skip_out)
    hd=gq_ref.shape[3]//3; kh=gq_ref.shape[2]
    for core in range(2):
        for i in range(kh//48):
            r=pl.ds(i*48,48)
            s3[pl.ds(core*kh+i*48,48),:]=jnp.concatenate([gq_ref[p,core,r,s*hd:(s+1)*hd].astype(F32) for s in range(3) for p in range(4)],axis=1)
    put(s3,qkv_out)
    for copy in copies: copy.wait()

def assemble(lay,gin,gsk,skip,gq,em,eo):
    S=lambda *s: jax.ShapeDtypeStruct(s,F32)
    tokens,d=gin.shape
    shapes=(S(tokens,d),S(tokens,d),S(*skip.shape),S(d//4,3*d),S(2,d//8,4*d),S(2,d//2,d),S(2,d//8,d))
    return pl.pallas_call(assemble_kernel,out_shape=(shapes[0],)+shapes,in_specs=[VM]*7,out_specs=(ANY,)*8,
        scratch_shapes=[pltpu.VMEM(s.shape,F32) for s in shapes+shapes[:1]]+[pltpu.SemaphoreType.DMA((8,))],
        compiler_params=pltpu.CompilerParams(vmem_limit_bytes=60*2**20),
        cost_estimate=pl.CostEstimate(flops=0,bytes_accessed=40*2**20,transcendentals=0))(
        lay,gin,gsk,skip,gq,em,eo)

from jax.sharding import Mesh, PartitionSpec as P
WIDE=("y","x"); ROWS=("z","core")
SWAP=[(0,1),(1,0)]

def swap_cores(values):
    return lax.ppermute(values,"core",SWAP)

def pick(values, index, axis):
    return lax.dynamic_index_in_dim(values,index,axis,keepdims=False)

def place_halves(mine, other, core, axis):
    first=jnp.where(core==0,mine,other); second=jnp.where(core==0,other,mine)
    return jnp.stack([first,second],axis=axis)

def dot(a,b): return jnp.dot(a,b,preferred_element_type=F32)

def norm(values):
    cen=values-jnp.mean(values,axis=1,keepdims=True)
    inv=lax.rsqrt(jnp.mean(cen*cen,axis=1,keepdims=True)+1e-5)
    return cen*inv,inv

def on_device(nw, block_input, long_skip, segment_ids, item_lengths, skip_weight, first_gain, first_shift, qkv_weight,
              out_weight, second_gain, second_shift, up_weight, down_weight, output_grad):
    core=lax.axis_index("core")
    _,tokens,d=block_input.shape
    heads=qkv_weight.shape[1]//(3*HEAD*nw); hd=heads*HEAD
    ff=up_weight.shape[1]; fb=ff//(2*nw)
    gather=lambda v: lax.all_gather(v,WIDE,axis=0,tiled=True)
    near=nw==4
    vecs=jnp.stack([first_gain,first_shift,second_gain,second_shift]+[first_gain]*4).astype(F32)
    if near:
        hidden,normed_all,qkv,w_heads,w_skip,vecs=first(block_input[0],long_skip[0],skip_weight,qkv_weight,vecs)
        vec=vecs.transpose(1,0,2).reshape(8,d)
        gain1,shift1,gain2,shift2=[vec[i:i+1] for i in range(4)]
        half=lambda v: lax.dynamic_slice_in_dim(v,core*(v.shape[0]//2),v.shape[0]//2)
        qkv,up_half,out_half=lax.optimization_barrier((qkv,half(up_weight),half(out_weight)))
        up_x,out_x=lax.ppermute((up_half,out_half),"x",SWAP)
        up_y,out_y=lax.ppermute((up_half,out_half),"y",SWAP)
    else:
        vec=gather(vecs.astype(BF).T).T.astype(F32)
        gain1,shift1,gain2,shift2=[vec[i:i+1] for i in range(4)]
        w_skip=gather(skip_weight)
        joined=jnp.concatenate([block_input[0],long_skip[0]],axis=1)
        w_heads=qkv_weight.reshape(d//nw,3,nw,hd).transpose(2,0,1,3)
        w_heads=lax.all_to_all(w_heads,WIDE,0,0).reshape(d,3*hd)
        hidden=dot(joined,w_skip)
        xhat1,inv1=norm(hidden)
        normed_all=gather((xhat1*gain1+shift1).astype(BF))
        qkv=dot(normed_all,w_heads).astype(BF)
    *att,lse=attend(item_lengths,qkv,heads,near)
    if near:
        lay,gmid,gatt,gtail,gow,small,gup,gdn,sxu,sxd,syu,syd=middle(hidden,*att,output_grad[0],gain2,shift2,out_weight,out_x,out_y,
            up_weight,up_x,up_y,down_weight)[:12]
        grad_heads=gatt.reshape(nw*tokens,-1),gtail.reshape(tokens,-1)
    else:
        w_out=gather(out_weight)
        up_mine=gather(pick(up_weight.reshape(d//nw,nw,2,fb),core,2).reshape(d//nw,nw*fb))
        down_mine=gather(pick(down_weight.reshape(2,fb,d),core,0))
        up_other,down_other=swap_cores(up_mine),swap_cores(down_mine)
        att=lax.all_to_all(att[0].reshape(nw,tokens,hd),WIDE,0,0)
        lay,gmid,gatt,gow,small,gupo,guph,gdno,gdnh=mlp(hidden,att,w_out,gain2,shift2,output_grad[0],up_mine,up_other,down_mine,down_other)
        grad_heads=(lax.all_to_all(gatt,WIDE,0,0).reshape(nw*tokens,hd),)

    def scatter(mine,other):
        both=(mine.astype(F32)+swap_cores(other).astype(F32)).astype(BF)
        return lax.psum_scatter(both,WIDE,scatter_dimension=0,tiled=True)
    def both_cores(mine,axis):
        return place_halves(mine,swap_cores(mine),core,axis).astype(F32)
    def by_rows(grad):
        cut=grad.reshape(nw,2,-1,grad.shape[1])
        return scatter(pick(cut,core,1).reshape(-1,grad.shape[1]),pick(cut,1-core,1).reshape(-1,grad.shape[1]))
    if near:
        wide=2*lax.axis_index("y")+lax.axis_index("x")
        part=lambda v: lax.dynamic_index_in_dim(v.reshape(4,-1,v.shape[1]),wide,0,False)
        from_x=lax.ppermute((sxu,sxd),"x",SWAP)
        from_y=lax.ppermute((syu,syd),"y",SWAP)
        from_d=lax.ppermute(gow[1],WIDE,[(i,3-i) for i in range(4)])
    else:
        early=scatter(gupo,guph),scatter(gdno,gdnh),by_rows(gow)
    grad_qkv=attend_back(item_lengths,qkv,grad_heads,lse,heads)
    if near:
        grad_qkv,from_x,from_y,from_d=lax.optimization_barrier((grad_qkv,from_x,from_y,from_d))
        up_sum=part(gup).astype(F32)+from_x[0].astype(F32)+from_y[0].astype(F32)
        rows=gdn.shape[0]//4
        pair=from_x[1].astype(F32)+from_y[1].astype(F32)
        down_sum=part(gdn).astype(F32)+pair[:rows]
        out_sum=gow[0].astype(F32)+pair[rows:]+from_d.astype(F32)
        early=up_sum.astype(BF),down_sum.astype(BF),out_sum.astype(BF)
    grad_qkv,early=lax.optimization_barrier((grad_qkv,early))
    if not near: early=lax.psum(early,"z")
    if near:
        gin,gsk,smalls,gqkv,gskip,mine,other=last(grad_qkv,w_heads,normed_all,hidden,gmid,gain1,block_input[0],long_skip[0],w_skip,small,*early)
        lay,gin,gsk,skip_share,qkv_share,up_share,down_share,out_share=assemble(lay,gin,gsk,gskip.reshape(-1,d),gqkv,mine,other)
        up_share,down_share,out_share=up_share.reshape(-1,ff),down_share.reshape(-1,d),out_share.reshape(-1,d)
        smalls=lax.dynamic_slice_in_dim(smalls[:4],(2*lax.axis_index("y")+lax.axis_index("x"))*(d//nw),d//nw,axis=1).T
    else:
        part_first=nt(grad_qkv,w_heads).astype(BF)
        grad_first=lax.psum_scatter(part_first,WIDE,scatter_dimension=0,tiled=True).astype(F32)
        gqkv=tn(normed_all,grad_qkv).astype(BF).reshape(nw,2,d//nw//2,3*hd)
        gqkv=(pick(gqkv,core,1).astype(F32)+swap_cores(pick(gqkv,1-core,1)).astype(F32)).astype(BF)
        e1=grad_first*gain1
        across=inv1*(e1-jnp.mean(e1,axis=1,keepdims=True)-xhat1*jnp.mean(e1*xhat1,axis=1,keepdims=True))
        grad_hidden=(gmid+across).astype(BF)
        gskip=by_rows(tn(joined,grad_hidden).astype(BF))
        grad_joined=nt(grad_hidden,w_skip)
        gin,gsk=grad_joined[:,:d],grad_joined[:,d:]
        small1=jnp.stack([jnp.sum(grad_first*xhat1,axis=0),jnp.sum(grad_first,axis=0)])
        gqkv,gskip,early=lax.optimization_barrier((gqkv,gskip,early))
        gqkv,gskip=lax.psum((gqkv,gskip),"z")
        up_share=both_cores(early[0].reshape(d//nw,nw,fb),2).reshape(d//nw,ff)
        down_share=both_cores(early[1],0).reshape(ff//nw,d)
        out_share=both_cores(early[2],0).reshape(d//nw,d)
        skip_share=both_cores(gskip,0).reshape(2*d//nw,d)
        gqkv=lax.all_to_all(gqkv,WIDE,0,0).reshape(nw,-1,3,hd).transpose(1,2,0,3)
        qkv_share=both_cores(gqkv,0).reshape(d//nw,-1)
        smalls=jnp.stack([small1[0],small1[1],small[0],small[1]],axis=1)
        smalls=lax.psum(lax.psum_scatter(smalls.astype(BF),WIDE,scatter_dimension=0,tiled=True),ROWS).astype(F32)
    return (lay[None],gin[None],gsk[None],skip_share,smalls[:,0],smalls[:,1],qkv_share,out_share,
            smalls[:,2],smalls[:,3],up_share,down_share)

def solution(mesh):
    rows,wide=mesh.devices.shape
    side=2 if wide==4 else int(wide**0.5)
    grid=Mesh(mesh.devices.reshape(rows//2,2,wide//side,side),("z","core","y","x"))
    tok=P(ROWS,WIDE,None); row=P(ROWS,None); mat=P(WIDE,None); vec=P(WIDE)
    return jax.shard_map(functools.partial(on_device,wide),mesh=grid,
        in_specs=(tok,tok,row,row,mat,vec,vec,mat,mat,vec,vec,mat,mat,tok),
        out_specs=(tok,tok,tok,mat,vec,vec,mat,mat,vec,vec,mat,mat),check_vma=False)
```

```python
import functools
import jax, jax.numpy as jnp
from jax import lax
from jax.experimental import pallas as pl
from jax.experimental.pallas import tpu as pltpu
HEAD=72; SHORT=258; LONG=1026; NITEM=12
LOG2E=1.4426950408889634
SCALE=HEAD**-0.5
QT=384

def kwin(n): return (n + 29 + 31)//32*32
def qwin(n): return (n + 15 + QT-1)//QT*QT
def qtile(n): return qwin(n) if n==LONG else QT

def nt(a,b): return lax.dot_general(a,b,(((1,),(1,)),((),())),preferred_element_type=jnp.float32)
def nn(a,b): return lax.dot_general(a,b,(((1,),(0,)),((),())),preferred_element_type=jnp.float32)
def tn(a,b): return lax.dot_general(a,b,(((0,),(0,)),((),())),preferred_element_type=jnp.float32)

def windows(start, size, row_len):
    k0 = pl.multiple_of(jnp.minimum(start//16*16, row_len-kwin(size)),16)
    q0 = pl.multiple_of(jnp.minimum(start//16*16, row_len-qwin(size)),16)
    return k0,q0

def split_heads(src_ref, dst_ref, count, chunk=416):
    rows=src_ref.shape[0]
    @pl.loop(0, rows//chunk)
    def _(i):
        r=pl.ds(pl.multiple_of(i*chunk,16),chunk)
        block=src_ref[r,:]
        for j in range(count):
            dst_ref[j,r,:]=block[:,j*HEAD:(j+1)*HEAD]

def join_heads(src_ref, dst_ref, count, chunk=416):
    rows=dst_ref.shape[0]
    @pl.loop(0, rows//chunk)
    def _(i):
        r=pl.ds(pl.multiple_of(i*chunk,16),chunk)
        dst_ref[r,:]=jnp.concatenate([src_ref[j,r,:] for j in range(count)],axis=1)

def zero(ref, chunk=416):
    rows=ref.shape[1]
    @pl.loop(0, rows//chunk)
    def _(i):
        r=pl.ds(pl.multiple_of(i*chunk,16),chunk)
        for j in range(ref.shape[0]):
            ref[j,r,:]=jnp.zeros((chunk,ref.shape[2]),ref.dtype)

LANES=256
def pack_heads(src_ref, dst_ref, tail_ref, count):
    size=tail_ref.shape[0]//4
    @pl.loop(0,4)
    def _(b):
        tails=[]
        for j in range(4):
            r=pl.ds(pl.multiple_of((4*b+j)*size,16),size)
            row=jnp.concatenate([src_ref[h,r,:] for h in range(count)],axis=1)
            dst_ref[r,:]=row[:,:LANES]
            tails.append(row[:,LANES:])
        tail_ref[pl.ds(pl.multiple_of(b*size,16),size),:]=jnp.concatenate(tails,axis=1)

def unpack_heads(src_ref, tail_ref, dst_ref, count):
    size=tail_ref.shape[0]//4; width=tail_ref.shape[1]//4
    @pl.loop(0,4)
    def _(b):
        tail=tail_ref[pl.ds(pl.multiple_of(b*size,16),size),:]
        for j in range(4):
            r=pl.ds(pl.multiple_of((4*b+j)*size,16),size)
            row=jnp.concatenate([src_ref[r,:],tail[:,j*width:(j+1)*width]],axis=1)
            for h in range(count): dst_ref[h,r,:]=row[:,h*HEAD:(h+1)*HEAD]

def for_items(len_ref, one):
    def step(i, start):
        size=len_ref[0,i]
        @pl.when(size==LONG)
        def _(): one(i,start,LONG)
        @pl.when(size==SHORT)
        def _(): one(i,start,SHORT)
        return start+size
    lax.fori_loop(0,len_ref.shape[1],step,jnp.int32(0))

def mask_edges(values, start, k0, size, fill):
    n=values.shape[0]; body=size//32*32
    off=start-k0
    top=lax.broadcasted_iota(jnp.int32,(32,values.shape[1]),0)
    low=jnp.where(top>=off,values[:32],fill)
    high=jnp.where(top+body<off+size,values[body:],fill)
    return jnp.concatenate([low,values[32:body],high],axis=0)

def attend_kernel(heads, len_ref, qkv_ref, *refs):
    *outs, lse_ref, split_ref, acc_ref=refs
    row_len=qkv_ref.shape[0]
    split_heads(qkv_ref, split_ref, 3*heads)
    zero(acc_ref)
    lse_ref[...]=jnp.zeros_like(lse_ref)
    def one(item,start,size):
        k0,q0=windows(start,size,row_len)
        kr=pl.ds(k0,kwin(size))
        qt=qtile(size)
        @pl.loop(0,qwin(size)//qt)
        def _(t):
            qr=pl.ds(pl.multiple_of(q0+t*qt,16),qt)
            col=q0+t*qt+lax.broadcasted_iota(jnp.int32,(1,qt),1)
            live=(col>=start)&(col<start+size)
            for h in range(heads):
                s=nt(split_ref[heads+h,kr,:],split_ref[h,qr,:])
                s=mask_edges(s,start,k0,size,-1e30)
                m=jnp.max(s,axis=0,keepdims=True)
                p=jnp.exp2((s-m)*(SCALE*LOG2E))
                l=jnp.sum(p,axis=0,keepdims=True)
                o=tn(split_ref[2*heads+h,kr,:],p.astype(jnp.bfloat16))
                o=jnp.where(live,o/l,0.0)
                acc_ref[h,qr,:]+=o.T.astype(jnp.bfloat16)
                lse_ref[item,pl.ds(t*heads+h,1),:qt]=m*(SCALE*LOG2E)+jnp.log2(l)
    for_items(len_ref,one)
    if len(outs)==2: pack_heads(acc_ref,*outs,heads)
    else: join_heads(acc_ref,outs[0],heads)

def attend_back_kernel(heads, len_ref, qkv_ref, *refs):
    *grads, lse_ref, out_ref, split_ref, gsplit_ref, acc_ref, dk_ref, dv_ref=refs
    row_len=qkv_ref.shape[0]
    split_heads(qkv_ref, split_ref, 3*heads)
    if len(grads)==2: unpack_heads(*grads,gsplit_ref,heads)
    else: split_heads(grads[0],gsplit_ref,heads)
    zero(acc_ref)
    def one(item,start,size):
        k0,q0=windows(start,size,row_len)
        kw=kwin(size)
        kr=pl.ds(k0,kw)
        for h in range(heads):
            dk_ref[h,:kw,:]=jnp.zeros((kw,HEAD),jnp.float32)
            dv_ref[h,:kw,:]=jnp.zeros((kw,HEAD),jnp.float32)
        qt=qtile(size)
        @pl.loop(0,qwin(size)//qt)
        def _(t):
            qr=pl.ds(pl.multiple_of(q0+t*qt,16),qt)
            col=q0+t*qt+lax.broadcasted_iota(jnp.int32,(1,qt),1)
            live=(col>=start)&(col<start+size)
            for h in range(heads):
                k=split_ref[heads+h,kr,:]; q=split_ref[h,qr,:]; g=gsplit_ref[h,qr,:]
                lse=jnp.where(live,lse_ref[item,pl.ds(t*heads+h,1),:qt],1e30)
                s=nt(k,q)
                p=jnp.exp2(s*(SCALE*LOG2E)-lse)
                p=mask_edges(p,start,k0,size,0.0)
                dv_ref[h,:kw,:]+=nn(p.astype(jnp.bfloat16),g)
                dp=nt(split_ref[2*heads+h,kr,:],g)
                delta=jnp.sum(p*dp,axis=0,keepdims=True)
                ds=(p*(dp-delta)).astype(jnp.bfloat16)
                dk_ref[h,:kw,:]+=nn(ds,q)
                dq=tn(k,ds)*SCALE
                acc_ref[h,qr,:]+=dq.T.astype(jnp.bfloat16)
        for h in range(heads):
            acc_ref[heads+h,kr,:]+=(dk_ref[h,:kw,:]*SCALE).astype(jnp.bfloat16)
            acc_ref[2*heads+h,kr,:]+=dv_ref[h,:kw,:].astype(jnp.bfloat16)
    for_items(len_ref,one)
    join_heads(acc_ref,out_ref,3*heads)

VM=pl.BlockSpec(memory_space=pltpu.VMEM); SM=pl.BlockSpec(memory_space=pltpu.SMEM)
def attend(lens,qkv,heads,packed=False):
    n=qkv.shape[0]
    nt_=max(8,heads*(qwin(LONG)//qtile(LONG)))
    shapes=((n,LANES),(n//4,4*(heads*HEAD-LANES))) if packed else ((n,heads*HEAD),)
    return pl.pallas_call(functools.partial(attend_kernel,heads),
      out_shape=tuple(jax.ShapeDtypeStruct(s,jnp.bfloat16) for s in shapes)+(jax.ShapeDtypeStruct((NITEM,nt_,qtile(LONG)),jnp.float32),),
      in_specs=[SM,VM],out_specs=(VM,)*(len(shapes)+1),
      scratch_shapes=[pltpu.VMEM((3*heads,n,HEAD),jnp.bfloat16),pltpu.VMEM((heads,n,HEAD),jnp.bfloat16)],
      compiler_params=pltpu.CompilerParams(vmem_limit_bytes=56*2**20),
      cost_estimate=pl.CostEstimate(flops=heads*n*n*HEAD*4,bytes_accessed=12*2**20,transcendentals=heads*n*n//3))(lens,qkv)
def attend_back(lens,qkv,grads,lse,heads):
    n=qkv.shape[0]
    return pl.pallas_call(functools.partial(attend_back_kernel,heads),
      out_shape=jax.ShapeDtypeStruct((n,3*heads*HEAD),jnp.bfloat16),
      in_specs=[SM,VM]+[VM]*len(grads)+[VM],out_specs=VM,
      scratch_shapes=[pltpu.VMEM((3*heads,n,HEAD),jnp.bfloat16),pltpu.VMEM((heads,n,HEAD),jnp.bfloat16),pltpu.VMEM((3*heads,n,HEAD),jnp.bfloat16),
        pltpu.VMEM((heads,kwin(LONG),HEAD),jnp.float32),pltpu.VMEM((heads,kwin(LONG),HEAD),jnp.float32)],
      compiler_params=pltpu.CompilerParams(vmem_limit_bytes=60*2**20),
      cost_estimate=pl.CostEstimate(flops=heads*n*n*HEAD*10,bytes_accessed=20*2**20,transcendentals=heads*n*n//3))(lens,qkv,*grads,lse)


F32=jnp.float32; BF=jnp.bfloat16
ANY=pl.BlockSpec(memory_space=pl.ANY)

def gelu_parts(u):
    z=jnp.exp2(u*u*(-0.5*1.4426950408889634))
    t=1.0/(1.0+(0.3275911*0.7071067811865476)*jnp.abs(u))
    poly=((((1.061405429*t-1.453152027)*t+1.421413741)*t-0.284496736)*t+0.254829592)*t
    tail=0.5*poly*z
    cdf=jnp.where(u>=0,1.0-tail,tail)
    return u*cdf, cdf+u*(z*0.3989422804014327)

def mlp_kernel(tile, hidden_ref, att_ref, outw_ref, gain_ref, shift_ref, g_ref, upo_ref, uph_ref, dno_ref, dnh_ref,
               lay_ref, gmid_ref, gatt_ref, gow_ref, small_ref, gupo_ref, guph_ref, gdno_ref, gdnh_ref,
               att_s, n2_s, xhat_s, rstd_s, act_s, gu_s, upb, dnb, gub, gdb, in_sem, out_sem):
    parts,tokens,cols=att_ref.shape
    d=hidden_ref.shape[1]
    tc=tokens//2 if tokens>416 else tokens
    nch=tokens//tc
    half=upo_ref.shape[1]; steps=half//tile
    cc=d//3; fc=256

    def fetch(j,act):
        slot=lax.rem(j,2)
        for first,(us,ds) in ((True,(uph_ref,dnh_ref)),(False,(upo_ref,dno_ref))):
            cond=(j<steps) if first else (j>=steps)
            @pl.when(cond)
            def _():
                k=j if first else j-steps
                off=pl.multiple_of(k*tile,tile)
                act(pltpu.make_async_copy(us.at[:,pl.ds(off,tile)],upb.at[slot],in_sem.at[slot,0]))
                act(pltpu.make_async_copy(ds.at[pl.ds(off,tile),:],dnb.at[slot],in_sem.at[slot,1]))
    def flush(j,act):
        slot=lax.rem(j,2)
        for first,(us,ds) in ((True,(guph_ref,gdnh_ref)),(False,(gupo_ref,gdno_ref))):
            cond=(j<steps) if first else (j>=steps)
            @pl.when(cond)
            def _():
                k=j if first else j-steps
                off=pl.multiple_of(k*tile,tile)
                act(pltpu.make_async_copy(gub.at[slot],us.at[:,pl.ds(off,tile)],out_sem.at[slot,0]))
                act(pltpu.make_async_copy(gdb.at[slot],ds.at[pl.ds(off,tile),:],out_sem.at[slot,1]))
    start=lambda c: c.start()
    wait=lambda c: c.wait()
    fetch(jnp.int32(0),start)
    gain=gain_ref[...]; shift=shift_ref[...]
    sub=tc//2
    @pl.loop(0,2*nch)
    def _(i):
        r=pl.ds(pl.multiple_of(i*sub,16),sub)
        joined=jnp.concatenate([att_ref[p,r,:] for p in range(parts)],axis=1)
        att_s[r,:]=joined
        mid=hidden_ref[r,:]+nn(joined,outw_ref[...])
        lay_ref[r,:]=mid
        cen=mid-jnp.mean(mid,axis=1,keepdims=True)
        inv=lax.rsqrt(jnp.mean(cen*cen,axis=1,keepdims=True)+1e-5)
        xhat=cen*inv
        xhat_s[r,:]=xhat
        rstd_s[r,:]=jnp.broadcast_to(inv,(sub,128))
        n2_s[r,:]=(xhat*gain+shift).astype(BF)
        gmid_ref[r,:]=jnp.zeros((sub,d),F32)
    @pl.loop(0,2*steps)
    def _(j):
        slot=lax.rem(j,2)
        @pl.when(j+1<2*steps)
        def _(): fetch(j+1,start)
        fetch(j,wait)
        @pl.when(j>=2)
        def _(): flush(j-2,wait)
        @pl.loop(0,nch)
        def _(i):
            r=pl.ds(pl.multiple_of(i*tc,16),tc)
            for k in range(tile//fc):
                f=pl.ds(k*fc,fc)
                u=nn(n2_s[r,:],upb[slot,:,f])
                a,dg=gelu_parts(u)
                act_s[r,f]=a.astype(BF)
                ga=nt(g_ref[r,:],dnb[slot,f,:])
                gu_s[r,f]=(ga*dg).astype(BF)
        @pl.loop(0,nch)
        def _(i):
            r=pl.ds(pl.multiple_of(i*tc,16),tc)
            for k in range(3):
                cr=pl.ds(k*cc,cc)
                lay_ref[r,cr]+=nn(act_s[r,:],dnb[slot,:,cr])
                gmid_ref[r,cr]+=nt(gu_s[r,:],upb[slot,cr,:])
        for k in range(tile//fc):
            f=pl.ds(k*fc,fc)
            gdb[slot,f,:]=tn(act_s[:,f],g_ref[...]).astype(BF)
        for k in range(3):
            cr=pl.ds(k*cc,cc)
            gub[slot,cr,:]=tn(n2_s[:,cr],gu_s[...]).astype(BF)
        flush(j,start)
    small_ref[...]=jnp.zeros_like(small_ref)
    @pl.loop(0,2*nch)
    def _(i):
        r=pl.ds(pl.multiple_of(i*sub,16),sub)
        gs=gmid_ref[r,:]; xhat=xhat_s[r,:]
        small_ref[0:1,:]+=jnp.sum(gs*xhat,axis=0,keepdims=True)
        small_ref[1:2,:]+=jnp.sum(gs,axis=0,keepdims=True)
        e=gs*gain
        back=e-jnp.mean(e,axis=1,keepdims=True)-xhat*jnp.mean(e*xhat,axis=1,keepdims=True)
        gm=g_ref[r,:].astype(F32)+back*rstd_s[r,0:1]
        gmid_ref[r,:]=gm
        low=gm.astype(BF)
        n2_s[r,:]=low
        ga=nt(low,outw_ref[...]).astype(BF)
        for p in range(parts):
            gatt_ref[p,r,:]=ga[:,p*cols:(p+1)*cols]
    for k in range(3):
        cr=pl.ds(k*cc,cc)
        gow_ref[cr,:]=tn(att_s[:,cr],n2_s[...]).astype(BF)
    flush(jnp.int32(2*steps-2),wait)
    flush(jnp.int32(2*steps-1),wait)

def mlp(hidden,att,outw,gain,shift,g,upo,uph,dno,dnh):
    tokens,d=hidden.shape; half=upo.shape[1]; tile=half//3
    S=jax.ShapeDtypeStruct
    flops=2*tokens*d*(half*2*6+d*3)
    return pl.pallas_call(functools.partial(mlp_kernel,tile),
        out_shape=(S((tokens,d),F32),S((tokens,d),F32),S(att.shape,BF),S((d,d),BF),S((8,d),F32),
                   S(upo.shape,BF),S(upo.shape,BF),S(dno.shape,BF),S(dno.shape,BF)),
        in_specs=[VM]*6+[ANY]*4,
        out_specs=(VM,)*5+(ANY,)*4,
        scratch_shapes=[pltpu.VMEM((tokens,d),BF),pltpu.VMEM((tokens,d),BF),pltpu.VMEM((tokens,d),F32),pltpu.VMEM((tokens,128),F32),
            pltpu.VMEM((tokens,tile),BF),pltpu.VMEM((tokens,tile),BF),
            pltpu.VMEM((2,d,tile),BF),pltpu.VMEM((2,tile,d),BF),pltpu.VMEM((2,d,tile),BF),pltpu.VMEM((2,tile,d),BF),
            pltpu.SemaphoreType.DMA((2,2)),pltpu.SemaphoreType.DMA((2,2))],
        compiler_params=pltpu.CompilerParams(vmem_limit_bytes=62*2**20),
        cost_estimate=pl.CostEstimate(flops=flops,bytes_accessed=60*2**20,transcendentals=tokens*half*2))(
        hidden,att,outw,gain,shift,g,upo,uph,dno,dnh)


MESH=pl.DeviceIdType.MESH

def place():
    x,y,c=lax.axis_index("x"),lax.axis_index("y"),lax.axis_index("core")
    return x,y,c,2*y+x,2*y+1-x,2-2*y+x,3-2*y-x

class Links:
    def __init__(self,send,recv):
        self.send,self.recv,self.sent=send,recv,[]
        x,y,c=lax.axis_index("x"),lax.axis_index("y"),lax.axis_index("core")
        self.to={"X":{"x":1-x},"Y":{"y":1-y},"D":{"x":1-x,"y":1-y},"C":{"core":1-c}}
    def meet(self,who):
        barrier=pltpu.get_barrier_semaphore()
        for t in who:
            pl.semaphore_signal(barrier,inc=1,device_id=self.to[t],device_id_type=MESH)
        pl.semaphore_wait(barrier,len(who))
    def start(self,k,t,src,dst):
        copy=pltpu.make_async_remote_copy(src_ref=src,dst_ref=dst,send_sem=self.send.at[k],recv_sem=self.recv.at[k],
                                          device_id=self.to[t],device_id_type=MESH)
        copy.start()
        self.sent.append(copy)
    def got(self,k,t,dst):
        pltpu.make_async_remote_copy(src_ref=dst,dst_ref=dst,send_sem=self.send.at[k],recv_sem=self.recv.at[k],
                                     device_id=self.to[t],device_id_type=MESH).wait_recv()
    def finish(self):
        for copy in self.sent: copy.wait_send()

def first_kernel(block_ref,long_ref,skip_ref,qkvw_ref,vec_ref,
                 hidden_out,normed_out,qkv_out,heads_out,wskip_out,vec_out,
                 ws,ns,hs,piece,hid,qs,vs,send,recv,local):
    x,y,c,w,wx,wy,wd=place()
    tokens,d=block_ref.shape
    sr=skip_ref.shape[0]; half=sr//2; part=half//2
    kr=qkvw_ref.shape[0]; kh=kr//2; hd=qkvw_ref.shape[1]//12
    tc=tokens//4
    mul=pl.multiple_of
    net=Links(send,recv)
    net.meet("XYDC")
    def srows(b,core,p): return pl.ds(mul(b*sr+core*half+p*part,16),part)
    def mine(p): return pl.ds(mul(c*half+p*part,16),part)
    net.start(0,"X",skip_ref.at[mine(0)],ws.at[srows(w,c,0)])
    net.start(2,"Y",skip_ref.at[mine(1)],ws.at[srows(w,c,1)])
    net.start(1,"X",skip_ref.at[mine(1)],ws.at[srows(w,c,1)])
    net.start(3,"Y",skip_ref.at[mine(0)],ws.at[srows(w,c,0)])
    own=pltpu.make_async_copy(skip_ref,ws.at[pl.ds(mul(w*sr,16),sr)],local.at[0])
    own.start()
    for k,t in ((30,"X"),(31,"Y"),(32,"D")): net.start(k,t,vec_ref,vs.at[w])
    vs[w]=vec_ref[...]
    for p in range(4):
        piece[p]=jnp.concatenate([qkvw_ref[:,(s*4+p)*hd:(s*4+p+1)*hd] for s in range(3)],axis=1)
    own_heads=pltpu.make_async_copy(piece.at[w],hs.at[pl.ds(mul(w*kr,16),kr)],local.at[1])
    own_heads.start()
    def pass_on(k,t,b,p,onward):
        r=srows(b,c,p)
        net.got(k,t,ws.at[r])
        for k2,t2 in onward: net.start(k2,t2,ws.at[r],ws.at[r])
    pass_on(0,"X",wx,0,((4,"Y"),(6,"C")))
    pass_on(2,"Y",wy,1,((5,"X"),(7,"C")))
    pass_on(1,"X",wx,1,((8,"C"),))
    pass_on(3,"Y",wy,0,((9,"C"),))
    def hrows(b,core): return pl.ds(mul(b*kr+core*kh,16),kh)
    cut=pl.ds(mul(c*kh,16),kh)
    net.start(12,"X",piece.at[wx,cut],hs.at[hrows(w,c)])
    net.start(13,"Y",piece.at[wy,cut],hs.at[hrows(w,c)])
    net.start(14,"D",piece.at[wd,cut],hs.at[hrows(w,c)])
    own.wait()
    net.got(6,"C",ws.at[srows(wx,1-c,0)])
    net.got(8,"C",ws.at[srows(wx,1-c,1)])
    near=pl.ds(mul(y*d,16),d); far=pl.ds(mul((1-y)*d,16),d)
    def tok(i): return pl.ds(mul(i*tc,16),tc)
    @pl.loop(0,4)
    def _(i):
        lhs=jnp.where(y==0,block_ref[tok(i),:],long_ref[tok(i),:])
        hid[tok(i),:]=nn(lhs,ws[near,:])
    pass_on(4,"Y",wd,0,((10,"C"),))
    pass_on(5,"X",wd,1,((11,"C"),))
    net.got(7,"C",ws.at[srows(wy,1-c,1)])
    net.got(9,"C",ws.at[srows(wy,1-c,0)])
    net.got(10,"C",ws.at[srows(wd,1-c,0)])
    net.got(11,"C",ws.at[srows(wd,1-c,1)])
    for k,t,b in ((30,"X",wx),(31,"Y",wy),(32,"D",wd)): net.got(k,t,vs.at[b])
    gain=jnp.concatenate([vs[p,0:1,:] for p in range(4)],axis=1)
    shift=jnp.concatenate([vs[p,1:2,:] for p in range(4)],axis=1)
    def nrows(b,i): return pl.ds(mul(b*tokens+i*tc,16),tc)
    def spread(i,t):
        net.start((18 if t=="X" else 22)+i,t,ns.at[nrows(w,i)],ns.at[nrows(w,i)])
    for i in range(4):
        r=tok(i)
        lhs=jnp.where(y==0,long_ref[r,:],block_ref[r,:])
        h=hid[r,:]+nn(lhs,ws[far,:])
        hid[r,:]=h
        cen=h-jnp.mean(h,axis=1,keepdims=True)
        inv=lax.rsqrt(jnp.mean(cen*cen,axis=1,keepdims=True)+1e-5)
        ns[nrows(w,i),:]=(cen*inv*gain+shift).astype(BF)
        spread(i,"XYXY"[i])
    for i,t in ((1,"X"),(0,"Y"),(3,"X"),(2,"Y")): spread(i,t)
    outs=[]
    def put(k,src,dst):
        copy=pltpu.make_async_copy(src,dst,local.at[k]); copy.start(); outs.append(copy)
    put(2,ws,wskip_out); put(3,hid,hidden_out); put(7,vs,vec_out)
    for j,(t,b) in enumerate((("X",wx),("Y",wy),("D",wd))):
        net.got(12+j,t,hs.at[hrows(b,c)])
        net.start(15+j,"C",hs.at[hrows(b,c)],hs.at[hrows(b,c)])
    for j,b in enumerate((wx,wy,wd)):
        net.got(15+j,"C",hs.at[hrows(b,1-c)])
    own_heads.wait()
    put(4,hs,heads_out)
    def project(b,i): qs[nrows(b,i),:]=nn(ns[nrows(b,i),:],hs[...]).astype(BF)
    @pl.loop(0,4)
    def _(i): project(w,i)
    for i,t,b,k,k2,t2 in ((0,"X",wx,18,26,"Y"),(1,"Y",wy,22,27,"X"),(2,"X",wx,18,28,"Y"),(3,"Y",wy,22,29,"X")):
        net.got(k+i,t,ns.at[nrows(b,i)])
        net.start(k2,t2,ns.at[nrows(b,i)],ns.at[nrows(b,i)])
    @pl.loop(0,2)
    def _(i): project(wx,2*i)
    @pl.loop(0,2)
    def _(i): project(wy,2*i+1)
    for i in (1,3):
        net.got(18+i,"X",ns.at[nrows(wx,i)])
        project(wx,i)
        net.got(22+i-1,"Y",ns.at[nrows(wy,i-1)])
        project(wy,i-1)
    for i,t,k in ((0,"Y",26),(1,"X",27),(2,"Y",28),(3,"X",29)):
        net.got(k,t,ns.at[nrows(wd,i)])
        project(wd,i)
    put(5,ns,normed_out); put(6,qs,qkv_out)
    for copy in outs: copy.wait()
    net.finish()

def first(block,long,skipw,qkvw,vecs):
    tokens,d=block.shape; S=jax.ShapeDtypeStruct; hd3=qkvw.shape[1]//4
    V=pltpu.VMEM
    return pl.pallas_call(first_kernel,
        out_shape=(S((tokens,d),F32),S((4*tokens,d),BF),S((4*tokens,hd3),BF),S((d,hd3),BF),S((2*d,d),BF),S((4,)+vecs.shape,F32)),
        in_specs=[VM]*5,out_specs=(ANY,)*6,
        scratch_shapes=[V((2*d,d),BF),V((4*tokens,d),BF),V((d,hd3),BF),V((4,d//4,hd3),BF),V((tokens,d),F32),V((4*tokens,hd3),BF),V((4,)+vecs.shape,F32),
            pltpu.SemaphoreType.DMA((33,)),pltpu.SemaphoreType.DMA((33,)),pltpu.SemaphoreType.DMA((8,))],
        compiler_params=pltpu.CompilerParams(vmem_limit_bytes=56*2**20,collective_id=0,has_side_effects=True),
        cost_estimate=pl.CostEstimate(flops=2*tokens*d*d*5,bytes_accessed=40*2**20,transcendentals=0))(
        block,long,skipw,qkvw,vecs)

class Chain:
    def __init__(self,net,k,own,up_in,down_in):
        self.net,self.k,self.own=net,k,own
        self.up_in,self.down_in=up_in,down_in
        self.z,self.n=lax.axis_index("z"),lax.axis_size("z")
    def copy(self,up,src):
        k=self.k+(0 if up else 1)
        return pltpu.make_async_remote_copy(src_ref=src,dst_ref=self.up_in if up else self.down_in,
            send_sem=self.net.send.at[k],recv_sem=self.net.recv.at[k],
            device_id={"z":self.z+1 if up else self.z-1},device_id_type=MESH)
    def hop(self,h):
        for up in (True,False):
            inn,other=(self.up_in,self.down_in) if up else (self.down_in,self.up_in)
            last_one=self.n-1-h<h or (self.n-1-h==h and not up)
            @pl.when(self.z==(h if up else self.n-1-h))
            def _():
                if h==0:
                    self.copy(up,self.own).start()
                else:
                    self.copy(up,inn).wait_recv()
                    mine,came=self.own[...].astype(F32),inn[...].astype(F32)
                    inn[...]=(mine+came).astype(inn.dtype)
                    if last_one:
                        self.own[...]=(other[...].astype(F32)+came).astype(self.own.dtype)
                    self.copy(up,inn).start()
    def total(self):
        first,final=self.z==0,self.z==self.n-1
        for end,up,inn in ((first,True,self.down_in),(final,False,self.up_in)):
            @pl.when(end)
            def _():
                self.copy(not up,inn).wait_recv()
                self.copy(up,self.own).wait_send()
                self.own[...]=(self.own[...].astype(F32)+inn[...].astype(F32)).astype(self.own.dtype)
        @pl.when(jnp.logical_not(first|final))
        def _():
            self.copy(True,self.up_in).wait_send()
            self.copy(False,self.down_in).wait_send()

def meet_all(net,who):
    z,n=lax.axis_index("z"),lax.axis_size("z")
    barrier=pltpu.get_barrier_semaphore()
    for t in who:
        pl.semaphore_signal(barrier,inc=1,device_id=net.to[t],device_id_type=MESH)
    @pl.when(z>0)
    def _(): pl.semaphore_signal(barrier,inc=1,device_id={"z":z-1},device_id_type=MESH)
    @pl.when(z<n-1)
    def _(): pl.semaphore_signal(barrier,inc=1,device_id={"z":z+1},device_id_type=MESH)
    ends=(z==0)|(z==n-1)
    @pl.when(ends)
    def _(): pl.semaphore_wait(barrier,len(who)+1)
    @pl.when(jnp.logical_not(ends))
    def _(): pl.semaphore_wait(barrier,len(who)+2)

SEG=3
def last_kernel(gq_ref,heads_ref,normed_ref,hidden_ref,gmid_ref,gain_ref,block_ref,long_ref,wskip_ref,small_ref,eu_ref,ed_ref,eo_ref,
                gin_out,gsk_out,small_out,gqkv_out,gskip_out,early_out,late_out,
                big,part,rx,ry,dx,dy,gw,gwr,gsr,qz,fq,sdx,sdy,srx,sry,own,sz,fs,sm,sin,smz,es,eup,edown,hg,send,recv,local,esem,hsem):
    x,y,c,w,wx,wy,wd=place()
    tokens,d=block_ref.shape
    tc=tokens//4; kr=d//4; kh=kr//2; sr=d//2; sh=sr//2; sq=sh//2
    mul=pl.multiple_of
    net=Links(send,recv)
    load=pltpu.make_async_copy(normed_ref,big,local.at[0])
    load.start()
    eseg=[pl.ds(i*kh,kh) for i in range(9)]
    eload=[pltpu.make_async_copy(eu_ref.at[:,pl.ds(i*d,d)] if i<4 else ed_ref.at[pl.ds((i-4)*kh,kh)] if i<8 else eo_ref,es.at[eseg[i]],esem.at[i]) for i in range(9)]
    for copy in eload: copy.start()
    ford=(0,2,1,3)
    def stream(j):
        r=pl.ds(ford[j]*tc,tc)
        return [pltpu.make_async_copy(ref.at[r],hg.at[j%2,m],hsem.at[j%2,m]) for m,ref in enumerate((hidden_ref,gmid_ref))]
    for j in range(2):
        for copy in stream(j): copy.start()
    meet_all(net,"XYDC")
    def tok(i): return pl.ds(i*tc,tc)
    early=[Chain(net,56+2*i,es.at[r],eup.at[r],edown.at[r]) for i,r in enumerate(eseg)]
    for copy in eload: copy.wait()
    halves=[pl.ds(i*2*kh,2*kh) for i in range(2)]
    mids=[Chain(net,40+2*i,gwr.at[r],qz.at[0,r],qz.at[1,r]) for i,r in enumerate(halves)]
    queue=early[:3]+mids+early[3:]
    for chain in queue[:3]: chain.hop(0)
    def tick(i):
        for h in range(1,lax.axis_size("z")-1):
            if 0<=i-h+1<len(queue): queue[i-h+1].hop(h)
    def pr(s,i): return pl.ds(s*tokens+i*tc,tc)
    def partial(b,i):
        return nt(gq_ref[pl.ds(mul(b*tokens+i*tc,16),tc),:],heads_ref[...])
    for i,t,dst,k in ((0,"X",dx,0),(2,"Y",dy,2),(1,"X",dx,1),(3,"Y",dy,3)):
        part[pr(2,i),:]=partial(wd,i).astype(BF)
        net.start(k,t,part.at[pr(2,i)],dst.at[tok(i%2)])
    for i,t,b,dst,k in ((0,"X",wx,rx,4),(2,"Y",wy,ry,10),(1,"X",wx,rx,5),(3,"Y",wy,ry,11)):
        s=0 if t=="X" else 1
        part[pr(s,i),:]=partial(b,i).astype(BF)
        net.start(k,t,part.at[pr(s,i)],dst.at[tok(i)])
    @pl.loop(0,4)
    def _(i):
        r=pl.ds(mul(i*tc,16),tc)
        part[pl.ds(mul(3*tokens+i*tc,16),tc),:]=nt(gq_ref[pl.ds(mul(w*tokens+i*tc,16),tc),:],heads_ref[...]).astype(BF)
    load.wait()
    cc=d//3
    def weight_grad(k):
        cr=pl.ds(k*cc,cc)
        gw[cr,:]=tn(big[:,cr],gq_ref[...]).astype(BF)
    def relay(i,t,b,dst,k,src,k2,t2):
        s=0 if t=="X" else 1
        mine=partial(b,i)
        net.got(k2,t2,src.at[tok(i%2)])
        part[pr(s,i),:]=(mine+src[tok(i%2),:].astype(F32)).astype(BF)
        net.start(k,t,part.at[pr(s,i)],dst.at[tok(i)])
    weight_grad(0)
    relay(2,"X",wx,rx,6,dy,2,"Y")
    relay(0,"Y",wy,ry,8,dx,0,"X")
    weight_grad(1)
    tick(0)
    weight_grad(2)
    def rows(b,core): return pl.ds(mul(b*kr+core*kh,16),kh)
    for b in range(4):
        net.start(12+b,"C",gw.at[rows(b,1-c)],gwr.at[pl.ds(b*kh,kh)])
    relay(3,"X",wx,rx,7,dy,3,"Y")
    tick(1)
    relay(1,"Y",wy,ry,9,dx,1,"X")
    tick(2)
    for b in range(4):
        r=pl.ds(b*kh,kh)
        net.got(12+b,"C",gwr.at[r])
        gwr[r,:]=(gwr[r,:].astype(F32)+gw[rows(b,c),:].astype(F32)).astype(BF)
    for chain in queue[3:]: chain.hop(0)
    gain=gain_ref[...]
    sm[...]=jnp.zeros_like(sm)
    for j,i in enumerate(ford):
        r=tok(i)
        tick(3+j)
        for copy in stream(j): copy.wait()
        net.got(4+i,"X",rx.at[r])
        net.got(8+i,"Y",ry.at[r])
        gf=part[pr(3,i),:].astype(F32)+rx[r,:].astype(F32)+ry[r,:].astype(F32)
        h=hg[j%2,0]
        cen=h-jnp.mean(h,axis=1,keepdims=True)
        inv=lax.rsqrt(jnp.mean(cen*cen,axis=1,keepdims=True)+1e-5)
        xhat=cen*inv
        sm[0:1,:]+=jnp.sum(gf*xhat,axis=0,keepdims=True)
        sm[1:2,:]+=jnp.sum(gf,axis=0,keepdims=True)
        e=gf*gain
        back=e-jnp.mean(e,axis=1,keepdims=True)-xhat*jnp.mean(e*xhat,axis=1,keepdims=True)
        big[pl.ds(2*d+i*tc,tc),:]=(hg[j%2,1]+back*inv).astype(BF)
        if j<2:
            for copy in stream(j+2): copy.start()
    sm[2:4,:]=small_ref[0:2,:]
    lates=[pltpu.make_async_copy(block_ref,rx,local.at[2]),pltpu.make_async_copy(long_ref,ry,local.at[3])]
    for copy in lates: copy.start()
    tick(7)
    for chain in mids: chain.total()
    def qrows(b): return pl.ds(mul(b*kh,16),kh)
    for j,(t,b) in enumerate((("X",wx),("Y",wy),("D",wd))):
        net.start(29+j,t,gwr.at[qrows(b)],fq.at[w,c])
    fq[w,c]=gwr[qrows(w),:]
    for copy in lates: copy.wait()
    for k in range(6):
        src=rx if k<3 else ry
        big[pl.ds(k*cc,cc),:]=tn(src[:,(k%3)*cc:(k%3+1)*cc],big[2*d:2*d+tokens,:]).astype(BF)
    def srows(b,core): return pl.ds(mul(b*sr+core*sh,16),sh)
    for b in range(4):
        net.start(16+b,"C",big.at[srows(b,1-c)],gsr.at[pl.ds(b*sh,sh)])
    net.start(20,"C",sm,sin.at[0])
    tick(8)
    for copy in net.sent[:16]: copy.wait_send()
    net.sent=net.sent[16:]
    wload=pltpu.make_async_copy(wskip_ref,part.at[pl.ds(0,2*d)],local.at[1])
    wload.start()
    for b in range(4):
        r=pl.ds(b*sh,sh)
        net.got(16+b,"C",gsr.at[r])
        gsr[r,:]=(gsr[r,:].astype(F32)+big[srows(b,c),:].astype(F32)).astype(BF)
    def quarter(b,i): return pl.ds(mul(b*sh+i*sq,16),sq)
    top,low=pl.ds(0,sq),pl.ds(sq,sq)
    net.start(21,"X",gsr.at[quarter(wd,0)],sdx)
    net.start(22,"Y",gsr.at[quarter(wd,1)],sdy)
    net.start(23,"X",gsr.at[quarter(wx,0)],srx.at[top])
    net.start(24,"Y",gsr.at[quarter(wy,1)],sry.at[low])
    tick(9)
    net.got(20,"C",sin.at[0])
    smz[6]=sm[...]+sin[0]
    net.start(27,"X",smz.at[6],sin.at[1])
    wload.wait()
    @pl.loop(0,4)
    def _(i):
        r=pl.ds(mul(i*tc,16),tc)
        gh=big[pl.ds(mul(2*d+i*tc,16),tc),:]
        rx[r,:]=nt(gh,part[:d,:]).astype(BF)
        ry[r,:]=nt(gh,part[d:2*d,:]).astype(BF)
    outs=[]
    def put(k,src,dst):
        copy=pltpu.make_async_copy(src,dst,local.at[k]); copy.start(); outs.append(copy)
    put(2,rx,gin_out); put(3,ry,gsk_out)
    tick(10)
    net.got(21,"X",sdx)
    gsr[quarter(wy,0),:]=(gsr[quarter(wy,0),:].astype(F32)+sdx[...].astype(F32)).astype(BF)
    net.start(25,"Y",gsr.at[quarter(wy,0)],sry.at[top])
    net.got(22,"Y",sdy)
    gsr[quarter(wx,1),:]=(gsr[quarter(wx,1),:].astype(F32)+sdy[...].astype(F32)).astype(BF)
    net.start(26,"X",gsr.at[quarter(wx,1)],srx.at[low])
    for i in range(11,len(queue)+lax.axis_size("z")-3): tick(i)
    net.got(27,"X",sin.at[1])
    smz[0]=smz[6]+sin[1]
    net.start(28,"Y",smz.at[0],sin.at[2])
    for j,(t,b) in enumerate((("X",wx),("Y",wy),("D",wd))):
        net.got(29+j,t,fq.at[b,c])
    for b in range(4):
        net.start(32+b,"C",fq.at[b,c],fq.at[b,c])
    net.got(28,"Y",sin.at[2])
    smz[1]=smz[0]+sin[2]
    net.got(23,"X",srx.at[top]); net.got(25,"Y",sry.at[top])
    net.got(24,"Y",sry.at[low]); net.got(26,"X",srx.at[low])
    own[...]=(gsr[pl.ds(mul(w*sh,16),sh),:].astype(F32)+srx[...].astype(F32)+sry[...].astype(F32)).astype(BF)
    seg=sh//SEG
    chains=[Chain(net,44,smz.at[1],smz.at[2],smz.at[3])]
    for i in range(SEG):
        r=pl.ds(i*seg,seg)
        chains.append(Chain(net,46+2*i,own.at[r],sz.at[0,r],sz.at[1,r]))
    for h in range(lax.axis_size("z")-1):
        for chain in chains: chain.hop(h)
    for chain in chains: chain.total()
    net.start(36,"C",own,fs)
    for i,chain in enumerate(early):
        chain.total()
        net.start(74+i,"C",es.at[eseg[i]],late_out.at[eseg[i]])
    put(8,es,early_out)
    for b in range(4): net.got(32+b,"C",fq.at[b,1-c])
    put(4,fq,gqkv_out); put(5,smz.at[1],small_out); put(6,own,gskip_out.at[c])
    net.got(36,"C",fs)
    put(7,fs,gskip_out.at[1-c])
    for i,r in enumerate(eseg): net.got(74+i,"C",late_out.at[r])
    for copy in outs: copy.wait()
    net.finish()

def last(gq,heads,normed,hidden,gmid,gain,block,long,wskip,small,eu,ed,eo):
    tokens,d=block.shape; S=jax.ShapeDtypeStruct; hd3=gq.shape[1]
    V=pltpu.VMEM
    return pl.pallas_call(last_kernel,
        out_shape=(S((tokens,d),BF),S((tokens,d),BF),S((8,d),F32),S((4,2,d//8,hd3),BF),S((2,d//4,d),BF),S((9*d//8,d),BF),S((9*d//8,d),BF)),
        in_specs=[VM,VM,ANY,ANY,ANY,VM,ANY,ANY,ANY,VM,ANY,ANY,ANY],out_specs=(ANY,)*7,
        scratch_shapes=[V((4*tokens,d),BF),V((4*tokens,d),BF),V((tokens,d),BF),V((tokens,d),BF),V((tokens//2,d),BF),V((tokens//2,d),BF),
            V((d,hd3),BF),V((d//2,hd3),BF),V((d,d),BF),V((2,d//2,hd3),BF),V((4,2,d//8,hd3),BF),
            V((d//8,d),BF),V((d//8,d),BF),V((d//4,d),BF),V((d//4,d),BF),V((d//4,d),BF),V((2,d//4,d),BF),V((d//4,d),BF),
            V((8,d),F32),V((3,8,d),F32),V((7,8,d),F32),
            V((9*d//8,d),BF),V((9*d//8,d),BF),V((9*d//8,d),BF),V((2,2,tokens//4,d),F32),
            pltpu.SemaphoreType.DMA((83,)),pltpu.SemaphoreType.DMA((83,)),pltpu.SemaphoreType.DMA((9,)),pltpu.SemaphoreType.DMA((9,)),pltpu.SemaphoreType.DMA((2,2))],
        compiler_params=pltpu.CompilerParams(vmem_limit_bytes=63*2**20,collective_id=1,has_side_effects=True),
        cost_estimate=pl.CostEstimate(flops=2*tokens*d*d*10,bytes_accessed=60*2**20,transcendentals=0))(
        gq,heads,normed,hidden,gmid,gain,block,long,wskip,small,eu,ed,eo)

SPLIT=((0,1152),)
def middle_kernel(hidden_ref,att_ref,tail_ref,g_ref,gain_ref,shift_ref,outw_ref,outx_ref,outy_ref,upw_ref,upx_ref,upy_ref,dnw_ref,
                  lay_out,gmid_ref,gh_out,ght_out,gow_out,small_ref,gup_out,gdn_out,sxu_out,sxd_out,syu_out,syd_out,uland,dland,ux_out,uy_out,dx_out,dy_out,
                  att_in,tail_in,att_s,outw_s,n2_s,xhat_s,rstd_s,lay_s,act_s,gu_s,upb,dnb,gub,gdb,land_u,land_d,low_s,
                  send,recv,csend,crecv,fetch_sem,flush_sem,local,usem,urecv,bring_sem):
    x,y,c,w,wx,wy,wd=place()
    tokens,d=hidden_ref.shape
    wide_cols=att_ref.shape[1]; quarter=tail_ref.shape[1]//4; cols=wide_cols+quarter
    kr=d//4; kh=kr//2; dh=d//2; dq=dh//2
    tc=tokens//4; th=tokens//2
    mul=pl.multiple_of
    net=Links(send,recv)
    left=[]
    def start(k,t,src,dst,view):
        pltpu.make_async_remote_copy(src_ref=src,dst_ref=dst,send_sem=send.at[k],recv_sem=recv.at[k],
                                     device_id=net.to[t],device_id_type=MESH).start()
        left.append((k,t,view))
    def blk(b): return pl.ds(mul(b*d,128),d)
    def urow(b,core): return pl.ds(mul(b*kr+core*kh,16),kh)
    def drow(b,core,p): return pl.ds(mul(b*d+core*dh+p*dq,16),dq)
    def trow(b): return pl.ds(mul(b*tokens,16),tokens)
    def tails(b): return pl.ds(mul(b*tc,16),tc)
    uview=uland.at[pl.ds(0,kh),pl.ds(0,d)]
    dview=dland.at[pl.ds(0,dq)]
    net.meet("XYDC")
    for j,(t,b) in enumerate((("X",wx),("Y",wy),("D",wd))):
        start(j,t,att_ref.at[trow(b)],att_in.at[w],att_in.at[0])
        start(52+j,t,tail_ref.at[tails(b)],tail_in.at[w],tail_in.at[0])
    own_att=[pltpu.make_async_copy(att_ref.at[trow(w)],att_in.at[w],local.at[0]),pltpu.make_async_copy(tail_ref.at[tails(w)],tail_in.at[w],local.at[3])]
    for copy in own_att: copy.start()
    cut=kh//32*16+16
    def orow(b,core,lo,n): return pl.ds(mul(b*kr+core*kh+lo,16),n)
    start(3,"Y",outx_ref.at[pl.ds(0,cut)],outw_s.at[orow(wx,c,0,cut)],outw_s.at[pl.ds(0,cut)])
    start(4,"X",outy_ref.at[pl.ds(cut,kh-cut)],outw_s.at[orow(wy,c,cut,kh-cut)],outw_s.at[pl.ds(0,kh-cut)])
    start(5,"C",outx_ref,outw_s.at[urow(wx,c)],outw_s.at[pl.ds(0,kh)])
    start(6,"C",outy_ref,outw_s.at[urow(wy,c)],outw_s.at[pl.ds(0,kh)])
    start(7,"Y",upx_ref.at[:,blk(wy)],uland.at[urow(wx,c),blk(wy)],uview)
    start(8,"X",upy_ref.at[:,blk(w)],uland.at[urow(wy,c),blk(w)],uview)
    order=(w,wx,wd,wy)
    def up_core(i):
        start(11+2*i,"C",upx_ref.at[:,blk(order[i])],uland.at[urow(wx,c),blk(order[i])],uview)
        start(12+2*i,"C",upy_ref.at[:,blk(order[i])],uland.at[urow(wy,c),blk(order[i])],uview)
    up_core(0)
    outw_s[pl.ds(mul(w*kr,16),kr),:]=outw_ref[...]
    outw_s[urow(wx,c),:]=outx_ref[...]
    outw_s[urow(wy,c),:]=outy_ref[...]

    diag_id=(7,8,9,10)
    def diag_from(i): return "YX"[i%2]
    def up_relay(i):
        view=uland.at[urow(wd,c),blk(order[i])]
        net.got(diag_id[i],diag_from(i),view)
        start(19+i,"C",view,view,uview)
    def up_sources(i):
        b=order[i]
        net.got(11+2*i,"C",uland.at[urow(wx,1-c),blk(b)])
        net.got(12+2*i,"C",uland.at[urow(wy,1-c),blk(b)])
        net.got(19+i,"C",uland.at[urow(wd,1-c),blk(b)])
        return [(upw_ref.at[:,blk(b)],pl.ds(mul(w*kr,16),kr)),(upx_ref.at[:,blk(b)],urow(wx,c)),(upy_ref.at[:,blk(b)],urow(wy,c)),
                (uland.at[urow(wx,1-c),blk(b)],urow(wx,1-c)),(uland.at[urow(wy,1-c),blk(b)],urow(wy,1-c)),
                (uland.at[pl.ds(mul(wd*kr,16),kr),blk(b)],pl.ds(mul(wd*kr,16),kr))]
    def fetch(i):
        slot=i%2
        for j,(src,rows) in enumerate(up_sources(i)):
            pltpu.make_async_copy(src,upb.at[slot,rows],fetch_sem.at[slot,j]).start()
        src=dnw_ref if i==0 else dland.at[pl.ds(mul(order[i]*d,16),d)]
        pltpu.make_async_copy(src,dnb.at[slot],fetch_sem.at[slot,6]).start()
    def fetched(slot):
        for j,n in enumerate((kr,kh,kh,kh,kh,kr)):
            view=upb.at[slot,pl.ds(0,n)]
            pltpu.make_async_copy(view,view,fetch_sem.at[slot,j]).wait()
        pltpu.make_async_copy(dnb.at[slot],dnb.at[slot],fetch_sem.at[slot,6]).wait()
    def down_relay(k,t,b,p,onward):
        r=drow(b,c,p)
        net.got(k,t,dland.at[r])
        for k2,t2 in onward: start(k2,t2,dland.at[r],dland.at[r],dview)
    def down_core(k,b,p): net.got(k,"C",dland.at[drow(b,1-c,p)])

    for j,(t,b) in enumerate((("X",wx),("Y",wy),("D",wd))):
        net.got(j,t,att_in.at[b])
        net.got(52+j,t,tail_in.at[b])
    start(9,"Y",upx_ref.at[:,blk(wx)],uland.at[urow(wx,c),blk(wx)],uview)
    start(10,"X",upy_ref.at[:,blk(wd)],uland.at[urow(wy,c),blk(wd)],uview)
    def dmine(p): return dnw_ref.at[pl.ds(mul(c*dh+p*dq,16),dq)]
    start(23,"X",dmine(0),dland.at[drow(w,c,0)],dview)
    start(25,"Y",dmine(1),dland.at[drow(w,c,1)],dview)
    start(24,"X",dmine(1),dland.at[drow(w,c,1)],dview)
    start(26,"Y",dmine(0),dland.at[drow(w,c,0)],dview)
    net.got(3,"Y",outw_s.at[orow(wd,c,0,cut)])
    net.got(4,"X",outw_s.at[orow(wd,c,cut,kh-cut)])
    start(35,"C",outw_s.at[urow(wd,c)],outw_s.at[urow(wd,c)],outw_s.at[pl.ds(0,kh)])
    up_relay(0)
    for i in (1,2,3): up_core(i)
    net.got(5,"C",outw_s.at[urow(wx,1-c)]); net.got(6,"C",outw_s.at[urow(wy,1-c)])
    net.got(35,"C",outw_s.at[urow(wd,1-c)])
    for copy in own_att: copy.wait()
    fetch(0)
    gain=gain_ref[...]; shift=shift_ref[...]
    for i in range(4):
        r=pl.ds(i*tc,tc)
        joined=jnp.concatenate([v for p in range(4) for v in (att_in[p,r,:],tail_in[p,:,i*quarter:(i+1)*quarter])],axis=1)
        att_s[r,:]=joined
        mid=hidden_ref[r,:]+nn(joined,outw_s[...])
        lay_s[r,:]=mid
        cen=mid-jnp.mean(mid,axis=1,keepdims=True)
        inv=lax.rsqrt(jnp.mean(cen*cen,axis=1,keepdims=True)+1e-5)
        xhat=cen*inv
        xhat_s[r,:]=xhat
        rstd_s[r,:]=jnp.broadcast_to(inv,(tc,128))
        n2_s[r,:]=(xhat*gain+shift).astype(BF)
        gmid_ref[r,:]=jnp.zeros((tc,d),F32)

    def pieces(slot):
        out=[(gub,pl.ds(mul(p*kr+(1-c)*kh,16),kh),land_u.at[slot,pl.ds(p*kh,kh)]) for p in range(4)]
        return out+[(gdb,pl.ds(mul((1-c)*dh,16),dh),land_d.at[slot])]
    def exchange(slot,act):
        for j,(ref,r,dst) in enumerate(pieces(slot)):
            act(pltpu.make_async_remote_copy(src_ref=ref.at[r],dst_ref=dst,send_sem=csend.at[slot,j],recv_sem=crecv.at[slot,j],
                                             device_id=net.to["C"],device_id_type=MESH))
    def flush(b,act):
        for p in range(4):
            act(pltpu.make_async_copy(gub.at[pl.ds(mul(p*kr+c*kh,16),kh)],gup_out.at[pl.ds(p*kh,kh),blk(b)],flush_sem.at[p]))
        act(pltpu.make_async_copy(gdb.at[pl.ds(mul(c*dh,16),dh)],gdn_out.at[pl.ds(mul(b*dh,16),dh)],flush_sem.at[4]))
    go=lambda copy: copy.start()
    done=lambda copy: copy.wait()
    def finalize(i):
        slot=lax.rem(i,2)
        exchange(slot,lambda copy: copy.wait())
        for p in range(4):
            r=pl.ds(mul(p*kr+c*kh,16),kh)
            gub[r,:]=(gub[r,:].astype(F32)+land_u[slot,pl.ds(p*kh,kh),:].astype(F32)).astype(BF)
        for p in range(2):
            r=pl.ds(mul(c*dh+p*dq,16),dq)
            gdb[r,:]=(gdb[r,:].astype(F32)+land_d[slot,pl.ds(p*dq,dq),:].astype(F32)).astype(BF)
    def block_of(i):
        return 2*lax.rem(y+i//2,2)+lax.rem(x+(i+1)//2,2)

    usend=[pl.ds(0,cut),pl.ds(cut,kh-cut)]
    def ahead(i,b,act):
        for j,(t,dst) in enumerate((("X",ux_out),("Y",uy_out))):
            n=usend[j]
            src=gup_out.at[pl.ds(mul(wd*kh+n.start,16),n.size),blk(b)]
            act(pltpu.make_async_remote_copy(src_ref=src,dst_ref=dst.at[:,blk(b)],send_sem=usem.at[i,j],recv_sem=urecv.at[i,j],
                                             device_id=net.to[t],device_id_type=MESH))
    def ahead_down(act):
        for j,(t,dst) in enumerate((("X",dx_out),("Y",dy_out))):
            act(pltpu.make_async_remote_copy(src_ref=gdn_out.at[pl.ds(mul(wd*dh+j*dq,16),dq)],dst_ref=dst,
                                             send_sem=usem.at[4,j],recv_sem=urecv.at[4,j],device_id=net.to[t],device_id_type=MESH))
    def weight_grads():
        for lo,n in SPLIT:
            f=pl.ds(lo,n)
            gdb[f,:]=tn(act_s[:,f],g_ref[...]).astype(BF)
            gub[f,:]=tn(n2_s[:,f],gu_s[...]).astype(BF)
    @pl.loop(0,4)
    def _(i):
        slot=lax.rem(i,2)
        fetched(slot)
        @pl.loop(0,2)
        def _(t):
            r=pl.ds(mul(t*th,16),th)
            for lo,n in SPLIT:
                f=pl.ds(lo,n)
                u=nn(n2_s[r,:],upb[slot,:,f])
                a,dg=gelu_parts(u)
                act_s[r,f]=a.astype(BF)
                gu_s[r,f]=(nt(g_ref[r,:],dnb[slot,f,:])*dg).astype(BF)
        @pl.when(i>=1)
        def _():
            finalize(i-1)
            flush(block_of(i-1),go)
        @pl.when(i==0)
        def _():
            for j in (1,2,3): up_relay(j)
        @pl.loop(0,2)
        def _(t):
            r=pl.ds(mul(t*th,16),th)
            for lo,n in SPLIT:
                f=pl.ds(lo,n)
                lay_s[r,f]+=nn(act_s[r,:],dnb[slot,:,f])
                gmid_ref[r,f]+=nt(gu_s[r,:],upb[slot,f,:])
        @pl.when(i==0)
        def _():
            down_relay(23,"X",wx,0,((27,"Y"),(29,"C")))
            down_relay(25,"Y",wy,1,((28,"X"),(30,"C")))
            down_relay(24,"X",wx,1,((31,"C"),))
            down_core(29,wx,0); down_core(31,wx,1)
            fetch(1)
        @pl.when(i==1)
        def _():
            down_relay(27,"Y",wd,0,((33,"C"),))
            down_relay(28,"X",wd,1,((34,"C"),))
            down_relay(26,"Y",wy,0,((32,"C"),))
            down_core(33,wd,0); down_core(34,wd,1)
            fetch(2)
        @pl.when(i==2)
        def _():
            down_core(30,wy,1); down_core(32,wy,0)
            fetch(3)
        @pl.when(i>=1)
        def _():
            flush(block_of(i-1),done)
            ahead(i-1,block_of(i-1),go)
        @pl.when(i==3)
        def _(): ahead_down(go)
        @pl.when(i<3)
        def _():
            weight_grads()
            exchange(slot,go)
    small_ref[...]=jnp.zeros_like(small_ref)
    for i in range(4):
        r=pl.ds(i*tc,tc)
        gs=gmid_ref[r,:]; xhat=xhat_s[r,:]
        small_ref[0:1,:]+=jnp.sum(gs*xhat,axis=0,keepdims=True)
        small_ref[1:2,:]+=jnp.sum(gs,axis=0,keepdims=True)
        e=gs*gain
        back=e-jnp.mean(e,axis=1,keepdims=True)-xhat*jnp.mean(e*xhat,axis=1,keepdims=True)
        gm=g_ref[r,:].astype(F32)+back*rstd_s[r,0:1]
        gmid_ref[r,:]=gm
        low=gm.astype(BF)
        low_s[r,:]=low
        ga=nt(low,outw_s[...]).astype(BF)
        for p in range(4):
            att_in[p,r,:]=ga[:,p*cols:p*cols+wide_cols]
            tail_in[p,:,i*quarter:(i+1)*quarter]=ga[:,p*cols+wide_cols:(p+1)*cols]
        for j,(t,b) in enumerate((("X",wx),("Y",wy),("D",wd))):
            start(36+3*i+j,t,att_in.at[b,r],gh_out.at[w,r],gh_out.at[0,pl.ds(0,tc)])
    for j,(t,b) in enumerate((("X",wx),("Y",wy),("D",wd))):
        start(55+j,t,tail_in.at[b],ght_out.at[w],tail_in.at[0])
    own_grad=[pltpu.make_async_copy(att_in.at[w],gh_out.at[w],local.at[2]),pltpu.make_async_copy(tail_in.at[w],ght_out.at[w],local.at[0])]
    for copy in own_grad: copy.start()
    weight_grads()
    exchange(1,go)
    act_s[...]=lay_s[...].astype(BF)
    lay_copy=pltpu.make_async_copy(act_s,lay_out,local.at[1])
    lay_copy.start()
    finalize(3)
    flush(wy,go)
    flush(wy,done)
    ahead(3,wy,go)
    for lo,n in SPLIT:
        f=pl.ds(lo,n)
        gub[f,:]=tn(att_s[:,f],low_s[...]).astype(BF)
    for p in range(4):
        start(48+p,"C",gub.at[pl.ds(mul(p*kr+(1-c)*kh,16),kh)],land_u.at[0,pl.ds(p*kh,kh)],land_u.at[0,pl.ds(0,kh)])
    def bring(k,src,dst):
        copy=pltpu.make_async_copy(src,dst,bring_sem.at[k]); copy.start(); return copy
    def spot(j,b): return pl.ds((4*j+b)*kh,kh)
    copies=[]
    for j,b2 in enumerate((wx,wy)):
        for b in range(4):
            copies.append(bring(4*j+b,gup_out.at[pl.ds(mul(b2*kh,16),kh),pl.ds(b*d,d)],upb.at[0,spot(j,b)]))
        copies.append(bring(16+j,gdn_out.at[pl.ds(mul(b2*dh,16),dh)],dnb.at[0,pl.ds(j*dh,dh)]))
    for i in range(4): ahead(i,order[i],done)
    ahead_down(done)
    for j,(src,n) in enumerate(((uy_out,usend[1]),(ux_out,usend[0]))):
        for b in range(4):
            copies.append(bring(8+4*j+b,src.at[:,pl.ds(b*d,d)],upb.at[1,pl.ds((4*j+b)*kh,n.size)]))
    copies.append(bring(18,dy_out,dnb.at[1,pl.ds(0,dq)]))
    copies.append(bring(19,dx_out,dnb.at[1,pl.ds(dq,dq)]))
    for copy in copies: copy.wait()
    copies=[]
    for j,(uo,do) in enumerate(((sxu_out,sxd_out),(syu_out,syd_out))):
        n=usend[1-j]
        for b in range(4):
            lo=(4*j+b)*kh
            r=pl.ds(lo+n.start,n.size)
            upb[0,r,:]=(upb[0,r,:].astype(F32)+upb[1,pl.ds(lo,n.size),:].astype(F32)).astype(BF)
            copies.append(bring(4*j+b,upb.at[0,spot(j,b)],uo.at[:,pl.ds(b*d,d)]))
        r=pl.ds(j*dh+(1-j)*dq,dq)
        dnb[0,r,:]=(dnb[0,r,:].astype(F32)+dnb[1,pl.ds(j*dq,dq),:].astype(F32)).astype(BF)
        copies.append(bring(16+j,dnb.at[0,pl.ds(j*dh,dh)],do.at[pl.ds(0,dh)]))
    for p in range(4):
        net.got(48+p,"C",land_u.at[0,pl.ds(p*kh,kh)])
        r=pl.ds(mul(p*kr+c*kh,16),kh)
        land_u[1,pl.ds(p*kh,kh),:]=(gub[r,:].astype(F32)+land_u[0,pl.ds(p*kh,kh),:].astype(F32)).astype(BF)
    for k,(b,dst) in enumerate(((w,gow_out.at[0]),(wd,gow_out.at[1]),(wx,sxd_out.at[pl.ds(dh,kh)]),(wy,syd_out.at[pl.ds(dh,kh)]))):
        copies.append(bring(8+k,land_u.at[1,pl.ds(mul(b*kh,16),kh)],dst))
    for i in range(4):
        for j,(t,b) in enumerate((("X",wx),("Y",wy),("D",wd))):
            net.got(36+3*i+j,t,gh_out.at[b,pl.ds(i*tc,tc)])
    for j,(t,b) in enumerate((('X',wx),('Y',wy),('D',wd))): net.got(55+j,t,ght_out.at[b])
    for copy in [lay_copy]+own_grad+copies: copy.wait()
    for k,t,view in left:
        pltpu.make_async_remote_copy(src_ref=view,dst_ref=view,send_sem=send.at[k],recv_sem=recv.at[k],
                                     device_id=net.to[t],device_id_type=MESH).wait_send()

def middle(hidden,att,tail,g,gain,shift,outw,outx,outy,upw,upx,upy,dnw):
    tokens,d=hidden.shape; cols=att.shape[1]; ff=upw.shape[1]
    S=jax.ShapeDtypeStruct; V=pltpu.VMEM; D=pltpu.SemaphoreType.DMA
    kh=d//8; cut=kh//32*16+16
    return pl.pallas_call(middle_kernel,
        out_shape=(S((tokens,d),BF),S((tokens,d),F32),S((4,tokens,cols),BF),S((4,tokens//4,tail.shape[1]),BF),S((2,kh,d),BF),S((8,d),F32),S((d//2,ff),BF),S((ff//2,d),BF),
                   S((kh,ff),BF),S((ff//8+kh,d),BF),S((kh,ff),BF),S((ff//8+kh,d),BF),
                   S((d,ff),BF),S((ff,d),BF),S((cut,ff),BF),S((kh-cut,ff),BF),S((ff//16,d),BF),S((ff//16,d),BF)),
        in_specs=[VM,ANY,ANY]+[VM]*6+[ANY]*4,out_specs=(ANY,VM,ANY,ANY,ANY,VM)+(ANY,)*12,
        scratch_shapes=[V((4,tokens,cols),BF),V((4,tokens//4,tail.shape[1]),BF),V((tokens,d),BF),V((d,d),BF),V((tokens,d),BF),V((tokens,d),F32),V((tokens,128),F32),
            V((tokens,d),F32),V((tokens,d),BF),V((tokens,d),BF),V((2,d,d),BF),V((2,d,d),BF),V((d,d),BF),V((d,d),BF),
            V((2,d//2,d),BF),V((2,d//2,d),BF),V((tokens,d),BF),D((58,)),D((58,)),D((2,5)),D((2,5)),D((2,7)),D((5,)),D((4,)),
            D((5,2)),D((5,2)),D((20,))],
        compiler_params=pltpu.CompilerParams(vmem_limit_bytes=63*2**20,collective_id=2,has_side_effects=True),
        cost_estimate=pl.CostEstimate(flops=2*tokens*d*(ff*6+d*3),bytes_accessed=60*2**20,transcendentals=tokens*ff*2))(
        hidden,att,tail,g,gain,shift,outw,outx,outy,upw,upx,upy,dnw)

def assemble_kernel(lay_ref,gin_ref,gsk_ref,skip_ref,gq_ref,em_ref,eo_ref,
                    lay_out,gin_out,gsk_out,skip_out,qkv_out,up_out,down_out,out_out,
                    s0,s1,s2,s3,s4,s5,s6,s7,local):
    first=lax.axis_index("core")==0
    copies=[]
    def put(src,dst):
        copy=pltpu.make_async_copy(src,dst,local.at[len(copies)]); copy.start(); copies.append(copy)
    def chunks(n,body,size=144):
        @pl.loop(0,n//size)
        def _(i): body(pl.ds(pl.multiple_of(i*size,16),size))
    def wide(dst,src):
        def body(r): dst[r,:]=src[r,:].astype(F32)
        chunks(dst.shape[0],body,208 if dst.shape[0]%208==0 else 144)
    wide(s7,lay_ref); put(s7,lay_out)
    wide(s0,gin_ref); put(s0,gin_out)
    wide(s1,gsk_ref); put(s1,gsk_out)
    kh=s6.shape[1]; d=s6.shape[2]
    def pair(dst,seg,rows,cols,size=48):
        @pl.loop(0,kh//size)
        def _(i):
            r=pl.ds(pl.multiple_of(seg*kh+i*size,16),size)
            to=pl.ds(pl.multiple_of(rows+i*size,16),size)
            m,o=em_ref[r,:].astype(F32),eo_ref[r,:].astype(F32)
            dst[0,to,cols]=jnp.where(first,m,o)
            dst[1,to,cols]=jnp.where(first,o,m)
    for b in range(4): pair(s4,b,0,pl.ds(b*d,d))
    put(s4,up_out)
    for b in range(4): pair(s5,4+b,b*kh,pl.ds(0,d))
    put(s5,down_out)
    pair(s6,8,0,pl.ds(0,d)); put(s6,out_out)
    def skip(r): s2[r,:]=skip_ref[r,:].astype(F32)
    chunks(s2.shape[0],skip); put(s2,skip_out)
    hd=gq_ref.shape[3]//3; kh=gq_ref.shape[2]
    for core in range(2):
        for i in range(kh//48):
            r=pl.ds(i*48,48)
            s3[pl.ds(core*kh+i*48,48),:]=jnp.concatenate([gq_ref[p,core,r,s*hd:(s+1)*hd].astype(F32) for s in range(3) for p in range(4)],axis=1)
    put(s3,qkv_out)
    for copy in copies: copy.wait()

def assemble(lay,gin,gsk,skip,gq,em,eo):
    S=lambda *s: jax.ShapeDtypeStruct(s,F32)
    tokens,d=gin.shape
    shapes=(S(tokens,d),S(tokens,d),S(*skip.shape),S(d//4,3*d),S(2,d//8,4*d),S(2,d//2,d),S(2,d//8,d))
    return pl.pallas_call(assemble_kernel,out_shape=(shapes[0],)+shapes,in_specs=[VM]*7,out_specs=(ANY,)*8,
        scratch_shapes=[pltpu.VMEM(s.shape,F32) for s in shapes+shapes[:1]]+[pltpu.SemaphoreType.DMA((8,))],
        compiler_params=pltpu.CompilerParams(vmem_limit_bytes=60*2**20),
        cost_estimate=pl.CostEstimate(flops=0,bytes_accessed=40*2**20,transcendentals=0))(
        lay,gin,gsk,skip,gq,em,eo)

from jax.sharding import Mesh, PartitionSpec as P
WIDE=("y","x"); ROWS=("z","core")
SWAP=[(0,1),(1,0)]

def swap_cores(values):
    return lax.ppermute(values,"core",SWAP)

def pick(values, index, axis):
    return lax.dynamic_index_in_dim(values,index,axis,keepdims=False)

def place_halves(mine, other, core, axis):
    first=jnp.where(core==0,mine,other); second=jnp.where(core==0,other,mine)
    return jnp.stack([first,second],axis=axis)

def dot(a,b): return jnp.dot(a,b,preferred_element_type=F32)

def norm(values):
    cen=values-jnp.mean(values,axis=1,keepdims=True)
    inv=lax.rsqrt(jnp.mean(cen*cen,axis=1,keepdims=True)+1e-5)
    return cen*inv,inv

def on_device(nw, block_input, long_skip, segment_ids, item_lengths, skip_weight, first_gain, first_shift, qkv_weight,
              out_weight, second_gain, second_shift, up_weight, down_weight, output_grad):
    core=lax.axis_index("core")
    _,tokens,d=block_input.shape
    heads=qkv_weight.shape[1]//(3*HEAD*nw); hd=heads*HEAD
    ff=up_weight.shape[1]; fb=ff//(2*nw)
    gather=lambda v: lax.all_gather(v,WIDE,axis=0,tiled=True)
    near=nw==4
    vecs=jnp.stack([first_gain,first_shift,second_gain,second_shift]+[first_gain]*4).astype(F32)
    if near:
        hidden,normed_all,qkv,w_heads,w_skip,vecs=first(block_input[0],long_skip[0],skip_weight,qkv_weight,vecs)
        vec=vecs.transpose(1,0,2).reshape(8,d)
        gain1,shift1,gain2,shift2=[vec[i:i+1] for i in range(4)]
        half=lambda v: lax.dynamic_slice_in_dim(v,core*(v.shape[0]//2),v.shape[0]//2)
        qkv,up_half,out_half=lax.optimization_barrier((qkv,half(up_weight),half(out_weight)))
        up_x,out_x=lax.ppermute((up_half,out_half),"x",SWAP)
        up_y,out_y=lax.ppermute((up_half,out_half),"y",SWAP)
    else:
        vec=gather(vecs.astype(BF).T).T.astype(F32)
        gain1,shift1,gain2,shift2=[vec[i:i+1] for i in range(4)]
        w_skip=gather(skip_weight)
        joined=jnp.concatenate([block_input[0],long_skip[0]],axis=1)
        w_heads=qkv_weight.reshape(d//nw,3,nw,hd).transpose(2,0,1,3)
        w_heads=lax.all_to_all(w_heads,WIDE,0,0).reshape(d,3*hd)
        hidden=dot(joined,w_skip)
        xhat1,inv1=norm(hidden)
        normed_all=gather((xhat1*gain1+shift1).astype(BF))
        qkv=dot(normed_all,w_heads).astype(BF)
    *att,lse=attend(item_lengths,qkv,heads,near)
    if near:
        lay,gmid,gatt,gtail,gow,small,gup,gdn,sxu,sxd,syu,syd=middle(hidden,*att,output_grad[0],gain2,shift2,out_weight,out_x,out_y,
            up_weight,up_x,up_y,down_weight)[:12]
        grad_heads=gatt.reshape(nw*tokens,-1),gtail.reshape(tokens,-1)
    else:
        w_out=gather(out_weight)
        up_mine=gather(pick(up_weight.reshape(d//nw,nw,2,fb),core,2).reshape(d//nw,nw*fb))
        down_mine=gather(pick(down_weight.reshape(2,fb,d),core,0))
        up_other,down_other=swap_cores(up_mine),swap_cores(down_mine)
        att=lax.all_to_all(att[0].reshape(nw,tokens,hd),WIDE,0,0)
        lay,gmid,gatt,gow,small,gupo,guph,gdno,gdnh=mlp(hidden,att,w_out,gain2,shift2,output_grad[0],up_mine,up_other,down_mine,down_other)
        grad_heads=(lax.all_to_all(gatt,WIDE,0,0).reshape(nw*tokens,hd),)

    def scatter(mine,other):
        both=(mine.astype(F32)+swap_cores(other).astype(F32)).astype(BF)
        return lax.psum_scatter(both,WIDE,scatter_dimension=0,tiled=True)
    def both_cores(mine,axis):
        return place_halves(mine,swap_cores(mine),core,axis).astype(F32)
    def by_rows(grad):
        cut=grad.reshape(nw,2,-1,grad.shape[1])
        return scatter(pick(cut,core,1).reshape(-1,grad.shape[1]),pick(cut,1-core,1).reshape(-1,grad.shape[1]))
    if near:
        wide=2*lax.axis_index("y")+lax.axis_index("x")
        part=lambda v: lax.dynamic_index_in_dim(v.reshape(4,-1,v.shape[1]),wide,0,False)
        from_x=lax.ppermute((sxu,sxd),"x",SWAP)
        from_y=lax.ppermute((syu,syd),"y",SWAP)
        from_d=lax.ppermute(gow[1],WIDE,[(i,3-i) for i in range(4)])
    else:
        early=scatter(gupo,guph),scatter(gdno,gdnh),by_rows(gow)
    grad_qkv=attend_back(item_lengths,qkv,grad_heads,lse,heads)
    if near:
        grad_qkv,from_x,from_y,from_d=lax.optimization_barrier((grad_qkv,from_x,from_y,from_d))
        up_sum=part(gup).astype(F32)+from_x[0].astype(F32)+from_y[0].astype(F32)
        rows=gdn.shape[0]//4
        pair=from_x[1].astype(F32)+from_y[1].astype(F32)
        down_sum=part(gdn).astype(F32)+pair[:rows]
        out_sum=gow[0].astype(F32)+pair[rows:]+from_d.astype(F32)
        early=up_sum.astype(BF),down_sum.astype(BF),out_sum.astype(BF)
    grad_qkv,early=lax.optimization_barrier((grad_qkv,early))
    if not near: early=lax.psum(early,"z")
    if near:
        gin,gsk,smalls,gqkv,gskip,mine,other=last(grad_qkv,w_heads,normed_all,hidden,gmid,gain1,block_input[0],long_skip[0],w_skip,small,*early)
        lay,gin,gsk,skip_share,qkv_share,up_share,down_share,out_share=assemble(lay,gin,gsk,gskip.reshape(-1,d),gqkv,mine,other)
        up_share,down_share,out_share=up_share.reshape(-1,ff),down_share.reshape(-1,d),out_share.reshape(-1,d)
        smalls=lax.dynamic_slice_in_dim(smalls[:4],(2*lax.axis_index("y")+lax.axis_index("x"))*(d//nw),d//nw,axis=1).T
    else:
        part_first=nt(grad_qkv,w_heads).astype(BF)
        grad_first=lax.psum_scatter(part_first,WIDE,scatter_dimension=0,tiled=True).astype(F32)
        gqkv=tn(normed_all,grad_qkv).astype(BF).reshape(nw,2,d//nw//2,3*hd)
        gqkv=(pick(gqkv,core,1).astype(F32)+swap_cores(pick(gqkv,1-core,1)).astype(F32)).astype(BF)
        e1=grad_first*gain1
        across=inv1*(e1-jnp.mean(e1,axis=1,keepdims=True)-xhat1*jnp.mean(e1*xhat1,axis=1,keepdims=True))
        grad_hidden=(gmid+across).astype(BF)
        gskip=by_rows(tn(joined,grad_hidden).astype(BF))
        grad_joined=nt(grad_hidden,w_skip)
        gin,gsk=grad_joined[:,:d],grad_joined[:,d:]
        small1=jnp.stack([jnp.sum(grad_first*xhat1,axis=0),jnp.sum(grad_first,axis=0)])
        gqkv,gskip,early=lax.optimization_barrier((gqkv,gskip,early))
        gqkv,gskip=lax.psum((gqkv,gskip),"z")
        up_share=both_cores(early[0].reshape(d//nw,nw,fb),2).reshape(d//nw,ff)
        down_share=both_cores(early[1],0).reshape(ff//nw,d)
        out_share=both_cores(early[2],0).reshape(d//nw,d)
        skip_share=both_cores(gskip,0).reshape(2*d//nw,d)
        gqkv=lax.all_to_all(gqkv,WIDE,0,0).reshape(nw,-1,3,hd).transpose(1,2,0,3)
        qkv_share=both_cores(gqkv,0).reshape(d//nw,-1)
        smalls=jnp.stack([small1[0],small1[1],small[0],small[1]],axis=1)
        smalls=lax.psum(lax.psum_scatter(smalls.astype(BF),WIDE,scatter_dimension=0,tiled=True),ROWS).astype(F32)
    return (lay[None],gin[None],gsk[None],skip_share,smalls[:,0],smalls[:,1],qkv_share,out_share,
            smalls[:,2],smalls[:,3],up_share,down_share)

def solution(mesh):
    rows,wide=mesh.devices.shape
    side=2 if wide==4 else int(wide**0.5)
    grid=Mesh(mesh.devices.reshape(rows//2,2,wide//side,side),("z","core","y","x"))
    tok=P(ROWS,WIDE,None); row=P(ROWS,None); mat=P(WIDE,None); vec=P(WIDE)
    return jax.shard_map(functools.partial(on_device,wide),mesh=grid,
        in_specs=(tok,tok,row,row,mat,vec,vec,mat,mat,vec,vec,mat,mat,tok),
        out_specs=(tok,tok,tok,mat,vec,vec,mat,mat,vec,vec,mat,mat),check_vma=False)
```

```python
import functools
import jax, jax.numpy as jnp
from jax import lax
from jax.experimental import pallas as pl
from jax.experimental.pallas import tpu as pltpu
HEAD=72; SHORT=258; LONG=1026; NITEM=12
LOG2E=1.4426950408889634
SCALE=HEAD**-0.5
QT=384

def kwin(n): return (n + 29 + 31)//32*32
def qwin(n): return (n + 15 + QT-1)//QT*QT
def qtile(n): return qwin(n) if n==LONG else QT

def nt(a,b): return lax.dot_general(a,b,(((1,),(1,)),((),())),preferred_element_type=jnp.float32)
def nn(a,b): return lax.dot_general(a,b,(((1,),(0,)),((),())),preferred_element_type=jnp.float32)
def tn(a,b): return lax.dot_general(a,b,(((0,),(0,)),((),())),preferred_element_type=jnp.float32)

def windows(start, size, row_len):
    k0 = pl.multiple_of(jnp.minimum(start//16*16, row_len-kwin(size)),16)
    q0 = pl.multiple_of(jnp.minimum(start//16*16, row_len-qwin(size)),16)
    return k0,q0

def split_heads(src_ref, dst_ref, count, chunk=416):
    rows=src_ref.shape[0]
    @pl.loop(0, rows//chunk)
    def _(i):
        r=pl.ds(pl.multiple_of(i*chunk,16),chunk)
        block=src_ref[r,:]
        for j in range(count):
            dst_ref[j,r,:]=block[:,j*HEAD:(j+1)*HEAD]

def join_heads(src_ref, dst_ref, count, chunk=416):
    rows=dst_ref.shape[0]
    @pl.loop(0, rows//chunk)
    def _(i):
        r=pl.ds(pl.multiple_of(i*chunk,16),chunk)
        dst_ref[r,:]=jnp.concatenate([src_ref[j,r,:] for j in range(count)],axis=1)

def zero(ref, chunk=416):
    rows=ref.shape[1]
    @pl.loop(0, rows//chunk)
    def _(i):
        r=pl.ds(pl.multiple_of(i*chunk,16),chunk)
        for j in range(ref.shape[0]):
            ref[j,r,:]=jnp.zeros((chunk,ref.shape[2]),ref.dtype)

LANES=256
def pack_heads(src_ref, dst_ref, tail_ref, count):
    size=tail_ref.shape[0]//4
    @pl.loop(0,4)
    def _(b):
        tails=[]
        for j in range(4):
            r=pl.ds(pl.multiple_of((4*b+j)*size,16),size)
            row=jnp.concatenate([src_ref[h,r,:] for h in range(count)],axis=1)
            dst_ref[r,:]=row[:,:LANES]
            tails.append(row[:,LANES:])
        tail_ref[pl.ds(pl.multiple_of(b*size,16),size),:]=jnp.concatenate(tails,axis=1)

def unpack_heads(src_ref, tail_ref, dst_ref, count):
    size=tail_ref.shape[0]//4; width=tail_ref.shape[1]//4
    @pl.loop(0,4)
    def _(b):
        tail=tail_ref[pl.ds(pl.multiple_of(b*size,16),size),:]
        for j in range(4):
            r=pl.ds(pl.multiple_of((4*b+j)*size,16),size)
            row=jnp.concatenate([src_ref[r,:],tail[:,j*width:(j+1)*width]],axis=1)
            for h in range(count): dst_ref[h,r,:]=row[:,h*HEAD:(h+1)*HEAD]

def for_items(len_ref, one):
    def step(i, start):
        size=len_ref[0,i]
        @pl.when(size==LONG)
        def _(): one(i,start,LONG)
        @pl.when(size==SHORT)
        def _(): one(i,start,SHORT)
        return start+size
    lax.fori_loop(0,len_ref.shape[1],step,jnp.int32(0))

def mask_edges(values, start, k0, size, fill):
    n=values.shape[0]; body=size//32*32
    off=start-k0
    top=lax.broadcasted_iota(jnp.int32,(32,values.shape[1]),0)
    low=jnp.where(top>=off,values[:32],fill)
    high=jnp.where(top+body<off+size,values[body:],fill)
    return jnp.concatenate([low,values[32:body],high],axis=0)

def attend_kernel(heads, len_ref, qkv_ref, *refs):
    *outs, lse_ref, split_ref, acc_ref=refs
    row_len=qkv_ref.shape[0]
    split_heads(qkv_ref, split_ref, 3*heads)
    zero(acc_ref)
    lse_ref[...]=jnp.zeros_like(lse_ref)
    def one(item,start,size):
        k0,q0=windows(start,size,row_len)
        kr=pl.ds(k0,kwin(size))
        qt=qtile(size)
        @pl.loop(0,qwin(size)//qt)
        def _(t):
            qr=pl.ds(pl.multiple_of(q0+t*qt,16),qt)
            col=q0+t*qt+lax.broadcasted_iota(jnp.int32,(1,qt),1)
            live=(col>=start)&(col<start+size)
            for h in range(heads):
                s=nt(split_ref[heads+h,kr,:],split_ref[h,qr,:])
                s=mask_edges(s,start,k0,size,-1e30)
                m=jnp.max(s,axis=0,keepdims=True)
                p=jnp.exp2((s-m)*(SCALE*LOG2E))
                l=jnp.sum(p,axis=0,keepdims=True)
                o=tn(split_ref[2*heads+h,kr,:],p.astype(jnp.bfloat16))
                o=jnp.where(live,o/l,0.0)
                acc_ref[h,qr,:]+=o.T.astype(jnp.bfloat16)
                lse_ref[item,pl.ds(t*heads+h,1),:qt]=m*(SCALE*LOG2E)+jnp.log2(l)
    for_items(len_ref,one)
    if len(outs)==2: pack_heads(acc_ref,*outs,heads)
    else: join_heads(acc_ref,outs[0],heads)

def attend_back_kernel(heads, len_ref, qkv_ref, *refs):
    *grads, lse_ref, out_ref, split_ref, gsplit_ref, acc_ref, dk_ref, dv_ref=refs
    row_len=qkv_ref.shape[0]
    split_heads(qkv_ref, split_ref, 3*heads)
    if len(grads)==2: unpack_heads(*grads,gsplit_ref,heads)
    else: split_heads(grads[0],gsplit_ref,heads)
    zero(acc_ref)
    def one(item,start,size):
        k0,q0=windows(start,size,row_len)
        kw=kwin(size)
        kr=pl.ds(k0,kw)
        for h in range(heads):
            dk_ref[h,:kw,:]=jnp.zeros((kw,HEAD),jnp.float32)
            dv_ref[h,:kw,:]=jnp.zeros((kw,HEAD),jnp.float32)
        qt=qtile(size)
        @pl.loop(0,qwin(size)//qt)
        def _(t):
            qr=pl.ds(pl.multiple_of(q0+t*qt,16),qt)
            col=q0+t*qt+lax.broadcasted_iota(jnp.int32,(1,qt),1)
            live=(col>=start)&(col<start+size)
            for h in range(heads):
                k=split_ref[heads+h,kr,:]; q=split_ref[h,qr,:]; g=gsplit_ref[h,qr,:]
                lse=jnp.where(live,lse_ref[item,pl.ds(t*heads+h,1),:qt],1e30)
                s=nt(k,q)
                p=jnp.exp2(s*(SCALE*LOG2E)-lse)
                p=mask_edges(p,start,k0,size,0.0)
                dv_ref[h,:kw,:]+=nn(p.astype(jnp.bfloat16),g)
                dp=nt(split_ref[2*heads+h,kr,:],g)
                delta=jnp.sum(p*dp,axis=0,keepdims=True)
                ds=(p*(dp-delta)).astype(jnp.bfloat16)
                dk_ref[h,:kw,:]+=nn(ds,q)
                dq=tn(k,ds)*SCALE
                acc_ref[h,qr,:]+=dq.T.astype(jnp.bfloat16)
        for h in range(heads):
            acc_ref[heads+h,kr,:]+=(dk_ref[h,:kw,:]*SCALE).astype(jnp.bfloat16)
            acc_ref[2*heads+h,kr,:]+=dv_ref[h,:kw,:].astype(jnp.bfloat16)
    for_items(len_ref,one)
    join_heads(acc_ref,out_ref,3*heads)

VM=pl.BlockSpec(memory_space=pltpu.VMEM); SM=pl.BlockSpec(memory_space=pltpu.SMEM)
def attend(lens,qkv,heads,packed=False):
    n=qkv.shape[0]
    nt_=max(8,heads*(qwin(LONG)//qtile(LONG)))
    shapes=((n,LANES),(n//4,4*(heads*HEAD-LANES))) if packed else ((n,heads*HEAD),)
    return pl.pallas_call(functools.partial(attend_kernel,heads),
      out_shape=tuple(jax.ShapeDtypeStruct(s,jnp.bfloat16) for s in shapes)+(jax.ShapeDtypeStruct((NITEM,nt_,qtile(LONG)),jnp.float32),),
      in_specs=[SM,VM],out_specs=(VM,)*(len(shapes)+1),
      scratch_shapes=[pltpu.VMEM((3*heads,n,HEAD),jnp.bfloat16),pltpu.VMEM((heads,n,HEAD),jnp.bfloat16)],
      compiler_params=pltpu.CompilerParams(vmem_limit_bytes=56*2**20),
      cost_estimate=pl.CostEstimate(flops=heads*n*n*HEAD*4,bytes_accessed=12*2**20,transcendentals=heads*n*n//3))(lens,qkv)
def attend_back(lens,qkv,grads,lse,heads):
    n=qkv.shape[0]
    return pl.pallas_call(functools.partial(attend_back_kernel,heads),
      out_shape=jax.ShapeDtypeStruct((n,3*heads*HEAD),jnp.bfloat16),
      in_specs=[SM,VM]+[VM]*len(grads)+[VM],out_specs=VM,
      scratch_shapes=[pltpu.VMEM((3*heads,n,HEAD),jnp.bfloat16),pltpu.VMEM((heads,n,HEAD),jnp.bfloat16),pltpu.VMEM((3*heads,n,HEAD),jnp.bfloat16),
        pltpu.VMEM((heads,kwin(LONG),HEAD),jnp.float32),pltpu.VMEM((heads,kwin(LONG),HEAD),jnp.float32)],
      compiler_params=pltpu.CompilerParams(vmem_limit_bytes=60*2**20),
      cost_estimate=pl.CostEstimate(flops=heads*n*n*HEAD*10,bytes_accessed=20*2**20,transcendentals=heads*n*n//3))(lens,qkv,*grads,lse)


F32=jnp.float32; BF=jnp.bfloat16
ANY=pl.BlockSpec(memory_space=pl.ANY)

def gelu_parts(u):
    z=jnp.exp2(u*u*(-0.5*1.4426950408889634))
    t=1.0/(1.0+(0.3275911*0.7071067811865476)*jnp.abs(u))
    poly=((((1.061405429*t-1.453152027)*t+1.421413741)*t-0.284496736)*t+0.254829592)*t
    tail=0.5*poly*z
    cdf=jnp.where(u>=0,1.0-tail,tail)
    return u*cdf, cdf+u*(z*0.3989422804014327)

def mlp_kernel(tile, hidden_ref, att_ref, outw_ref, gain_ref, shift_ref, g_ref, upo_ref, uph_ref, dno_ref, dnh_ref,
               lay_ref, gmid_ref, gatt_ref, gow_ref, small_ref, gupo_ref, guph_ref, gdno_ref, gdnh_ref,
               att_s, n2_s, xhat_s, rstd_s, act_s, gu_s, upb, dnb, gub, gdb, in_sem, out_sem):
    parts,tokens,cols=att_ref.shape
    d=hidden_ref.shape[1]
    tc=tokens//2 if tokens>416 else tokens
    nch=tokens//tc
    half=upo_ref.shape[1]; steps=half//tile
    cc=d//3; fc=256

    def fetch(j,act):
        slot=lax.rem(j,2)
        for first,(us,ds) in ((True,(uph_ref,dnh_ref)),(False,(upo_ref,dno_ref))):
            cond=(j<steps) if first else (j>=steps)
            @pl.when(cond)
            def _():
                k=j if first else j-steps
                off=pl.multiple_of(k*tile,tile)
                act(pltpu.make_async_copy(us.at[:,pl.ds(off,tile)],upb.at[slot],in_sem.at[slot,0]))
                act(pltpu.make_async_copy(ds.at[pl.ds(off,tile),:],dnb.at[slot],in_sem.at[slot,1]))
    def flush(j,act):
        slot=lax.rem(j,2)
        for first,(us,ds) in ((True,(guph_ref,gdnh_ref)),(False,(gupo_ref,gdno_ref))):
            cond=(j<steps) if first else (j>=steps)
            @pl.when(cond)
            def _():
                k=j if first else j-steps
                off=pl.multiple_of(k*tile,tile)
                act(pltpu.make_async_copy(gub.at[slot],us.at[:,pl.ds(off,tile)],out_sem.at[slot,0]))
                act(pltpu.make_async_copy(gdb.at[slot],ds.at[pl.ds(off,tile),:],out_sem.at[slot,1]))
    start=lambda c: c.start()
    wait=lambda c: c.wait()
    fetch(jnp.int32(0),start)
    gain=gain_ref[...]; shift=shift_ref[...]
    sub=tc//2
    @pl.loop(0,2*nch)
    def _(i):
        r=pl.ds(pl.multiple_of(i*sub,16),sub)
        joined=jnp.concatenate([att_ref[p,r,:] for p in range(parts)],axis=1)
        att_s[r,:]=joined
        mid=hidden_ref[r,:]+nn(joined,outw_ref[...])
        lay_ref[r,:]=mid
        cen=mid-jnp.mean(mid,axis=1,keepdims=True)
        inv=lax.rsqrt(jnp.mean(cen*cen,axis=1,keepdims=True)+1e-5)
        xhat=cen*inv
        xhat_s[r,:]=xhat
        rstd_s[r,:]=jnp.broadcast_to(inv,(sub,128))
        n2_s[r,:]=(xhat*gain+shift).astype(BF)
        gmid_ref[r,:]=jnp.zeros((sub,d),F32)
    @pl.loop(0,2*steps)
    def _(j):
        slot=lax.rem(j,2)
        @pl.when(j+1<2*steps)
        def _(): fetch(j+1,start)
        fetch(j,wait)
        @pl.when(j>=2)
        def _(): flush(j-2,wait)
        @pl.loop(0,nch)
        def _(i):
            r=pl.ds(pl.multiple_of(i*tc,16),tc)
            for k in range(tile//fc):
                f=pl.ds(k*fc,fc)
                u=nn(n2_s[r,:],upb[slot,:,f])
                a,dg=gelu_parts(u)
                act_s[r,f]=a.astype(BF)
                ga=nt(g_ref[r,:],dnb[slot,f,:])
                gu_s[r,f]=(ga*dg).astype(BF)
        @pl.loop(0,nch)
        def _(i):
            r=pl.ds(pl.multiple_of(i*tc,16),tc)
            for k in range(3):
                cr=pl.ds(k*cc,cc)
                lay_ref[r,cr]+=nn(act_s[r,:],dnb[slot,:,cr])
                gmid_ref[r,cr]+=nt(gu_s[r,:],upb[slot,cr,:])
        for k in range(tile//fc):
            f=pl.ds(k*fc,fc)
            gdb[slot,f,:]=tn(act_s[:,f],g_ref[...]).astype(BF)
        for k in range(3):
            cr=pl.ds(k*cc,cc)
            gub[slot,cr,:]=tn(n2_s[:,cr],gu_s[...]).astype(BF)
        flush(j,start)
    small_ref[...]=jnp.zeros_like(small_ref)
    @pl.loop(0,2*nch)
    def _(i):
        r=pl.ds(pl.multiple_of(i*sub,16),sub)
        gs=gmid_ref[r,:]; xhat=xhat_s[r,:]
        small_ref[0:1,:]+=jnp.sum(gs*xhat,axis=0,keepdims=True)
        small_ref[1:2,:]+=jnp.sum(gs,axis=0,keepdims=True)
        e=gs*gain
        back=e-jnp.mean(e,axis=1,keepdims=True)-xhat*jnp.mean(e*xhat,axis=1,keepdims=True)
        gm=g_ref[r,:].astype(F32)+back*rstd_s[r,0:1]
        gmid_ref[r,:]=gm
        low=gm.astype(BF)
        n2_s[r,:]=low
        ga=nt(low,outw_ref[...]).astype(BF)
        for p in range(parts):
            gatt_ref[p,r,:]=ga[:,p*cols:(p+1)*cols]
    for k in range(3):
        cr=pl.ds(k*cc,cc)
        gow_ref[cr,:]=tn(att_s[:,cr],n2_s[...]).astype(BF)
    flush(jnp.int32(2*steps-2),wait)
    flush(jnp.int32(2*steps-1),wait)

def mlp(hidden,att,outw,gain,shift,g,upo,uph,dno,dnh):
    tokens,d=hidden.shape; half=upo.shape[1]; tile=half//3
    S=jax.ShapeDtypeStruct
    flops=2*tokens*d*(half*2*6+d*3)
    return pl.pallas_call(functools.partial(mlp_kernel,tile),
        out_shape=(S((tokens,d),F32),S((tokens,d),F32),S(att.shape,BF),S((d,d),BF),S((8,d),F32),
                   S(upo.shape,BF),S(upo.shape,BF),S(dno.shape,BF),S(dno.shape,BF)),
        in_specs=[VM]*6+[ANY]*4,
        out_specs=(VM,)*5+(ANY,)*4,
        scratch_shapes=[pltpu.VMEM((tokens,d),BF),pltpu.VMEM((tokens,d),BF),pltpu.VMEM((tokens,d),F32),pltpu.VMEM((tokens,128),F32),
            pltpu.VMEM((tokens,tile),BF),pltpu.VMEM((tokens,tile),BF),
            pltpu.VMEM((2,d,tile),BF),pltpu.VMEM((2,tile,d),BF),pltpu.VMEM((2,d,tile),BF),pltpu.VMEM((2,tile,d),BF),
            pltpu.SemaphoreType.DMA((2,2)),pltpu.SemaphoreType.DMA((2,2))],
        compiler_params=pltpu.CompilerParams(vmem_limit_bytes=62*2**20),
        cost_estimate=pl.CostEstimate(flops=flops,bytes_accessed=60*2**20,transcendentals=tokens*half*2))(
        hidden,att,outw,gain,shift,g,upo,uph,dno,dnh)


MESH=pl.DeviceIdType.MESH

def place():
    x,y,c=lax.axis_index("x"),lax.axis_index("y"),lax.axis_index("core")
    return x,y,c,2*y+x,2*y+1-x,2-2*y+x,3-2*y-x

class Links:
    def __init__(self,send,recv):
        self.send,self.recv,self.sent=send,recv,[]
        x,y,c=lax.axis_index("x"),lax.axis_index("y"),lax.axis_index("core")
        self.to={"X":{"x":1-x},"Y":{"y":1-y},"D":{"x":1-x,"y":1-y},"C":{"core":1-c}}
    def meet(self,who):
        barrier=pltpu.get_barrier_semaphore()
        for t in who:
            pl.semaphore_signal(barrier,inc=1,device_id=self.to[t],device_id_type=MESH)
        pl.semaphore_wait(barrier,len(who))
    def start(self,k,t,src,dst):
        copy=pltpu.make_async_remote_copy(src_ref=src,dst_ref=dst,send_sem=self.send.at[k],recv_sem=self.recv.at[k],
                                          device_id=self.to[t],device_id_type=MESH)
        copy.start()
        self.sent.append(copy)
    def got(self,k,t,dst):
        pltpu.make_async_remote_copy(src_ref=dst,dst_ref=dst,send_sem=self.send.at[k],recv_sem=self.recv.at[k],
                                     device_id=self.to[t],device_id_type=MESH).wait_recv()
    def finish(self):
        for copy in self.sent: copy.wait_send()

def first_kernel(block_ref,long_ref,skip_ref,qkvw_ref,vec_ref,
                 hidden_out,normed_out,qkv_out,heads_out,wskip_out,vec_out,
                 ws,ns,hs,piece,hid,qs,vs,send,recv,local):
    x,y,c,w,wx,wy,wd=place()
    tokens,d=block_ref.shape
    sr=skip_ref.shape[0]; half=sr//2; part=half//2
    kr=qkvw_ref.shape[0]; kh=kr//2; hd=qkvw_ref.shape[1]//12
    tc=tokens//4
    mul=pl.multiple_of
    net=Links(send,recv)
    net.meet("XYDC")
    def srows(b,core,p): return pl.ds(mul(b*sr+core*half+p*part,16),part)
    def mine(p): return pl.ds(mul(c*half+p*part,16),part)
    net.start(0,"X",skip_ref.at[mine(0)],ws.at[srows(w,c,0)])
    net.start(2,"Y",skip_ref.at[mine(1)],ws.at[srows(w,c,1)])
    net.start(1,"X",skip_ref.at[mine(1)],ws.at[srows(w,c,1)])
    net.start(3,"Y",skip_ref.at[mine(0)],ws.at[srows(w,c,0)])
    own=pltpu.make_async_copy(skip_ref,ws.at[pl.ds(mul(w*sr,16),sr)],local.at[0])
    own.start()
    for k,t in ((30,"X"),(31,"Y"),(32,"D")): net.start(k,t,vec_ref,vs.at[w])
    vs[w]=vec_ref[...]
    for p in range(4):
        piece[p]=jnp.concatenate([qkvw_ref[:,(s*4+p)*hd:(s*4+p+1)*hd] for s in range(3)],axis=1)
    own_heads=pltpu.make_async_copy(piece.at[w],hs.at[pl.ds(mul(w*kr,16),kr)],local.at[1])
    own_heads.start()
    def pass_on(k,t,b,p,onward):
        r=srows(b,c,p)
        net.got(k,t,ws.at[r])
        for k2,t2 in onward: net.start(k2,t2,ws.at[r],ws.at[r])
    pass_on(0,"X",wx,0,((4,"Y"),(6,"C")))
    pass_on(2,"Y",wy,1,((5,"X"),(7,"C")))
    pass_on(1,"X",wx,1,((8,"C"),))
    pass_on(3,"Y",wy,0,((9,"C"),))
    def hrows(b,core): return pl.ds(mul(b*kr+core*kh,16),kh)
    cut=pl.ds(mul(c*kh,16),kh)
    net.start(12,"X",piece.at[wx,cut],hs.at[hrows(w,c)])
    net.start(13,"Y",piece.at[wy,cut],hs.at[hrows(w,c)])
    net.start(14,"D",piece.at[wd,cut],hs.at[hrows(w,c)])
    own.wait()
    net.got(6,"C",ws.at[srows(wx,1-c,0)])
    net.got(8,"C",ws.at[srows(wx,1-c,1)])
    near=pl.ds(mul(y*d,16),d); far=pl.ds(mul((1-y)*d,16),d)
    def tok(i): return pl.ds(mul(i*tc,16),tc)
    @pl.loop(0,4)
    def _(i):
        lhs=jnp.where(y==0,block_ref[tok(i),:],long_ref[tok(i),:])
        hid[tok(i),:]=nn(lhs,ws[near,:])
    pass_on(4,"Y",wd,0,((10,"C"),))
    pass_on(5,"X",wd,1,((11,"C"),))
    net.got(7,"C",ws.at[srows(wy,1-c,1)])
    net.got(9,"C",ws.at[srows(wy,1-c,0)])
    net.got(10,"C",ws.at[srows(wd,1-c,0)])
    net.got(11,"C",ws.at[srows(wd,1-c,1)])
    for k,t,b in ((30,"X",wx),(31,"Y",wy),(32,"D",wd)): net.got(k,t,vs.at[b])
    gain=jnp.concatenate([vs[p,0:1,:] for p in range(4)],axis=1)
    shift=jnp.concatenate([vs[p,1:2,:] for p in range(4)],axis=1)
    def nrows(b,i): return pl.ds(mul(b*tokens+i*tc,16),tc)
    def spread(i,t):
        net.start((18 if t=="X" else 22)+i,t,ns.at[nrows(w,i)],ns.at[nrows(w,i)])
    for i in range(4):
        r=tok(i)
        lhs=jnp.where(y==0,long_ref[r,:],block_ref[r,:])
        h=hid[r,:]+nn(lhs,ws[far,:])
        hid[r,:]=h
        cen=h-jnp.mean(h,axis=1,keepdims=True)
        inv=lax.rsqrt(jnp.mean(cen*cen,axis=1,keepdims=True)+1e-5)
        ns[nrows(w,i),:]=(cen*inv*gain+shift).astype(BF)
        spread(i,"XYXY"[i])
    for i,t in ((1,"X"),(0,"Y"),(3,"X"),(2,"Y")): spread(i,t)
    outs=[]
    def put(k,src,dst):
        copy=pltpu.make_async_copy(src,dst,local.at[k]); copy.start(); outs.append(copy)
    put(2,ws,wskip_out); put(3,hid,hidden_out); put(7,vs,vec_out)
    for j,(t,b) in enumerate((("X",wx),("Y",wy),("D",wd))):
        net.got(12+j,t,hs.at[hrows(b,c)])
        net.start(15+j,"C",hs.at[hrows(b,c)],hs.at[hrows(b,c)])
    for j,b in enumerate((wx,wy,wd)):
        net.got(15+j,"C",hs.at[hrows(b,1-c)])
    own_heads.wait()
    put(4,hs,heads_out)
    def project(b,i): qs[nrows(b,i),:]=nn(ns[nrows(b,i),:],hs[...]).astype(BF)
    @pl.loop(0,4)
    def _(i): project(w,i)
    def put_block(k,b):
        r=pl.ds(mul(b*tokens,16),tokens)
        put(k,ns.at[r],normed_out.at[r]); put(k+4,qs.at[r],qkv_out.at[r])
    put_block(8,w)
    for i,t,b,k,k2,t2 in ((0,"X",wx,18,26,"Y"),(1,"Y",wy,22,27,"X"),(2,"X",wx,18,28,"Y"),(3,"Y",wy,22,29,"X")):
        net.got(k+i,t,ns.at[nrows(b,i)])
        net.start(k2,t2,ns.at[nrows(b,i)],ns.at[nrows(b,i)])
    @pl.loop(0,2)
    def _(i): project(wx,2*i)
    @pl.loop(0,2)
    def _(i): project(wy,2*i+1)
    for i in (1,3):
        net.got(18+i,"X",ns.at[nrows(wx,i)])
        project(wx,i)
        net.got(22+i-1,"Y",ns.at[nrows(wy,i-1)])
        project(wy,i-1)
    put_block(9,wx); put_block(10,wy)
    for i,t,k in ((0,"Y",26),(1,"X",27),(2,"Y",28),(3,"X",29)):
        net.got(k,t,ns.at[nrows(wd,i)])
        project(wd,i)
    put_block(11,wd)
    for copy in outs: copy.wait()
    net.finish()

def first(block,long,skipw,qkvw,vecs):
    tokens,d=block.shape; S=jax.ShapeDtypeStruct; hd3=qkvw.shape[1]//4
    V=pltpu.VMEM
    return pl.pallas_call(first_kernel,
        out_shape=(S((tokens,d),F32),S((4*tokens,d),BF),S((4*tokens,hd3),BF),S((d,hd3),BF),S((2*d,d),BF),S((4,)+vecs.shape,F32)),
        in_specs=[VM]*5,out_specs=(ANY,)*6,
        scratch_shapes=[V((2*d,d),BF),V((4*tokens,d),BF),V((d,hd3),BF),V((4,d//4,hd3),BF),V((tokens,d),F32),V((4*tokens,hd3),BF),V((4,)+vecs.shape,F32),
            pltpu.SemaphoreType.DMA((33,)),pltpu.SemaphoreType.DMA((33,)),pltpu.SemaphoreType.DMA((16,))],
        compiler_params=pltpu.CompilerParams(vmem_limit_bytes=56*2**20,collective_id=0,has_side_effects=True),
        cost_estimate=pl.CostEstimate(flops=2*tokens*d*d*5,bytes_accessed=40*2**20,transcendentals=0))(
        block,long,skipw,qkvw,vecs)

class Chain:
    def __init__(self,net,k,own,up_in,down_in):
        self.net,self.k,self.own=net,k,own
        self.up_in,self.down_in=up_in,down_in
        self.z,self.n=lax.axis_index("z"),lax.axis_size("z")
    def copy(self,up,src):
        k=self.k+(0 if up else 1)
        return pltpu.make_async_remote_copy(src_ref=src,dst_ref=self.up_in if up else self.down_in,
            send_sem=self.net.send.at[k],recv_sem=self.net.recv.at[k],
            device_id={"z":self.z+1 if up else self.z-1},device_id_type=MESH)
    def hop(self,h):
        for up in (True,False):
            inn,other=(self.up_in,self.down_in) if up else (self.down_in,self.up_in)
            last_one=self.n-1-h<h or (self.n-1-h==h and not up)
            @pl.when(self.z==(h if up else self.n-1-h))
            def _():
                if h==0:
                    self.copy(up,self.own).start()
                else:
                    self.copy(up,inn).wait_recv()
                    mine,came=self.own[...].astype(F32),inn[...].astype(F32)
                    inn[...]=(mine+came).astype(inn.dtype)
                    if last_one:
                        self.own[...]=(other[...].astype(F32)+came).astype(self.own.dtype)
                    self.copy(up,inn).start()
    def total(self):
        first,final=self.z==0,self.z==self.n-1
        for end,up,inn in ((first,True,self.down_in),(final,False,self.up_in)):
            @pl.when(end)
            def _():
                self.copy(not up,inn).wait_recv()
                self.copy(up,self.own).wait_send()
                self.own[...]=(self.own[...].astype(F32)+inn[...].astype(F32)).astype(self.own.dtype)
        @pl.when(jnp.logical_not(first|final))
        def _():
            self.copy(True,self.up_in).wait_send()
            self.copy(False,self.down_in).wait_send()

def meet_all(net,who):
    z,n=lax.axis_index("z"),lax.axis_size("z")
    barrier=pltpu.get_barrier_semaphore()
    for t in who:
        pl.semaphore_signal(barrier,inc=1,device_id=net.to[t],device_id_type=MESH)
    @pl.when(z>0)
    def _(): pl.semaphore_signal(barrier,inc=1,device_id={"z":z-1},device_id_type=MESH)
    @pl.when(z<n-1)
    def _(): pl.semaphore_signal(barrier,inc=1,device_id={"z":z+1},device_id_type=MESH)
    ends=(z==0)|(z==n-1)
    @pl.when(ends)
    def _(): pl.semaphore_wait(barrier,len(who)+1)
    @pl.when(jnp.logical_not(ends))
    def _(): pl.semaphore_wait(barrier,len(who)+2)

SEG=3
def last_kernel(gq_ref,heads_ref,normed_ref,hidden_ref,gmid_ref,gain_ref,block_ref,long_ref,wskip_ref,small_ref,eu_ref,ed_ref,eo_ref,
                gin_out,gsk_out,small_out,gqkv_out,gskip_out,early_out,late_out,
                big,part,rx,ry,dx,dy,gw,gwr,gsr,qz,fq,sdx,sdy,srx,sry,own,sz,fs,sm,sin,smz,es,eup,edown,hg,send,recv,local,esem,hsem):
    x,y,c,w,wx,wy,wd=place()
    tokens,d=block_ref.shape
    tc=tokens//4; kr=d//4; kh=kr//2; sr=d//2; sh=sr//2; sq=sh//2
    mul=pl.multiple_of
    net=Links(send,recv)
    load=pltpu.make_async_copy(normed_ref,big,local.at[0])
    load.start()
    eseg=[pl.ds(i*kh,kh) for i in range(9)]
    eload=[pltpu.make_async_copy(eu_ref.at[:,pl.ds(i*d,d)] if i<4 else ed_ref.at[pl.ds((i-4)*kh,kh)] if i<8 else eo_ref,es.at[eseg[i]],esem.at[i]) for i in range(9)]
    for copy in eload: copy.start()
    ford=(0,2,1,3)
    def stream(j):
        r=pl.ds(ford[j]*tc,tc)
        return [pltpu.make_async_copy(ref.at[r],hg.at[j%2,m],hsem.at[j%2,m]) for m,ref in enumerate((hidden_ref,gmid_ref))]
    for j in range(2):
        for copy in stream(j): copy.start()
    meet_all(net,"XYDC")
    def tok(i): return pl.ds(i*tc,tc)
    early=[Chain(net,56+2*i,es.at[r],eup.at[r],edown.at[r]) for i,r in enumerate(eseg)]
    for copy in eload: copy.wait()
    halves=[pl.ds(i*2*kh,2*kh) for i in range(2)]
    mids=[Chain(net,40+2*i,gwr.at[r],qz.at[0,r],qz.at[1,r]) for i,r in enumerate(halves)]
    queue=early[:3]+mids+early[3:]
    for chain in queue[:3]: chain.hop(0)
    def tick(i):
        for h in range(1,lax.axis_size("z")-1):
            if 0<=i-h+1<len(queue): queue[i-h+1].hop(h)
    def pr(s,i): return pl.ds(s*tokens+i*tc,tc)
    def partial(b,i):
        return nt(gq_ref[pl.ds(mul(b*tokens+i*tc,16),tc),:],heads_ref[...])
    for i,t,dst,k in ((0,"X",dx,0),(2,"Y",dy,2),(1,"X",dx,1),(3,"Y",dy,3)):
        part[pr(2,i),:]=partial(wd,i).astype(BF)
        net.start(k,t,part.at[pr(2,i)],dst.at[tok(i%2)])
    for i,t,b,dst,k in ((0,"X",wx,rx,4),(2,"Y",wy,ry,10),(1,"X",wx,rx,5),(3,"Y",wy,ry,11)):
        s=0 if t=="X" else 1
        part[pr(s,i),:]=partial(b,i).astype(BF)
        net.start(k,t,part.at[pr(s,i)],dst.at[tok(i)])
    @pl.loop(0,4)
    def _(i):
        r=pl.ds(mul(i*tc,16),tc)
        part[pl.ds(mul(3*tokens+i*tc,16),tc),:]=nt(gq_ref[pl.ds(mul(w*tokens+i*tc,16),tc),:],heads_ref[...]).astype(BF)
    load.wait()
    cc=d//3
    def weight_grad(k):
        cr=pl.ds(k*cc,cc)
        gw[cr,:]=tn(big[:,cr],gq_ref[...]).astype(BF)
    def relay(i,t,b,dst,k,src,k2,t2):
        s=0 if t=="X" else 1
        mine=partial(b,i)
        net.got(k2,t2,src.at[tok(i%2)])
        part[pr(s,i),:]=(mine+src[tok(i%2),:].astype(F32)).astype(BF)
        net.start(k,t,part.at[pr(s,i)],dst.at[tok(i)])
    weight_grad(0)
    relay(2,"X",wx,rx,6,dy,2,"Y")
    relay(0,"Y",wy,ry,8,dx,0,"X")
    weight_grad(1)
    tick(0)
    weight_grad(2)
    def rows(b,core): return pl.ds(mul(b*kr+core*kh,16),kh)
    for b in range(4):
        net.start(12+b,"C",gw.at[rows(b,1-c)],gwr.at[pl.ds(b*kh,kh)])
    relay(3,"X",wx,rx,7,dy,3,"Y")
    tick(1)
    relay(1,"Y",wy,ry,9,dx,1,"X")
    tick(2)
    for b in range(4):
        r=pl.ds(b*kh,kh)
        net.got(12+b,"C",gwr.at[r])
        gwr[r,:]=(gwr[r,:].astype(F32)+gw[rows(b,c),:].astype(F32)).astype(BF)
    for chain in queue[3:]: chain.hop(0)
    gain=gain_ref[...]
    sm[...]=jnp.zeros_like(sm)
    for j,i in enumerate(ford):
        r=tok(i)
        tick(3+j)
        for copy in stream(j): copy.wait()
        net.got(4+i,"X",rx.at[r])
        net.got(8+i,"Y",ry.at[r])
        gf=part[pr(3,i),:].astype(F32)+rx[r,:].astype(F32)+ry[r,:].astype(F32)
        h=hg[j%2,0]
        cen=h-jnp.mean(h,axis=1,keepdims=True)
        inv=lax.rsqrt(jnp.mean(cen*cen,axis=1,keepdims=True)+1e-5)
        xhat=cen*inv
        sm[0:1,:]+=jnp.sum(gf*xhat,axis=0,keepdims=True)
        sm[1:2,:]+=jnp.sum(gf,axis=0,keepdims=True)
        e=gf*gain
        back=e-jnp.mean(e,axis=1,keepdims=True)-xhat*jnp.mean(e*xhat,axis=1,keepdims=True)
        big[pl.ds(2*d+i*tc,tc),:]=(hg[j%2,1]+back*inv).astype(BF)
        if j<2:
            for copy in stream(j+2): copy.start()
    sm[2:4,:]=small_ref[0:2,:]
    lates=[pltpu.make_async_copy(block_ref,rx,local.at[2]),pltpu.make_async_copy(long_ref,ry,local.at[3])]
    for copy in lates: copy.start()
    tick(7)
    for chain in mids: chain.total()
    def qrows(b): return pl.ds(mul(b*kh,16),kh)
    for j,(t,b) in enumerate((("X",wx),("Y",wy),("D",wd))):
        net.start(29+j,t,gwr.at[qrows(b)],fq.at[w,c])
    fq[w,c]=gwr[qrows(w),:]
    for copy in lates: copy.wait()
    for k in range(6):
        src=rx if k<3 else ry
        big[pl.ds(k*cc,cc),:]=tn(src[:,(k%3)*cc:(k%3+1)*cc],big[2*d:2*d+tokens,:]).astype(BF)
    def srows(b,core): return pl.ds(mul(b*sr+core*sh,16),sh)
    for b in range(4):
        net.start(16+b,"C",big.at[srows(b,1-c)],gsr.at[pl.ds(b*sh,sh)])
    net.start(20,"C",sm,sin.at[0])
    tick(8)
    for copy in net.sent[:16]: copy.wait_send()
    net.sent=net.sent[16:]
    wload=pltpu.make_async_copy(wskip_ref,part.at[pl.ds(0,2*d)],local.at[1])
    wload.start()
    for b in range(4):
        r=pl.ds(b*sh,sh)
        net.got(16+b,"C",gsr.at[r])
        gsr[r,:]=(gsr[r,:].astype(F32)+big[srows(b,c),:].astype(F32)).astype(BF)
    def quarter(b,i): return pl.ds(mul(b*sh+i*sq,16),sq)
    top,low=pl.ds(0,sq),pl.ds(sq,sq)
    net.start(21,"X",gsr.at[quarter(wd,0)],sdx)
    net.start(22,"Y",gsr.at[quarter(wd,1)],sdy)
    net.start(23,"X",gsr.at[quarter(wx,0)],srx.at[top])
    net.start(24,"Y",gsr.at[quarter(wy,1)],sry.at[low])
    tick(9)
    net.got(20,"C",sin.at[0])
    smz[6]=sm[...]+sin[0]
    net.start(27,"X",smz.at[6],sin.at[1])
    wload.wait()
    @pl.loop(0,4)
    def _(i):
        r=pl.ds(mul(i*tc,16),tc)
        gh=big[pl.ds(mul(2*d+i*tc,16),tc),:]
        rx[r,:]=nt(gh,part[:d,:]).astype(BF)
        ry[r,:]=nt(gh,part[d:2*d,:]).astype(BF)
    outs=[]
    def put(k,src,dst):
        copy=pltpu.make_async_copy(src,dst,local.at[k]); copy.start(); outs.append(copy)
    put(2,rx,gin_out); put(3,ry,gsk_out)
    tick(10)
    net.got(21,"X",sdx)
    gsr[quarter(wy,0),:]=(gsr[quarter(wy,0),:].astype(F32)+sdx[...].astype(F32)).astype(BF)
    net.start(25,"Y",gsr.at[quarter(wy,0)],sry.at[top])
    net.got(22,"Y",sdy)
    gsr[quarter(wx,1),:]=(gsr[quarter(wx,1),:].astype(F32)+sdy[...].astype(F32)).astype(BF)
    net.start(26,"X",gsr.at[quarter(wx,1)],srx.at[low])
    for i in range(11,len(queue)+lax.axis_size("z")-3): tick(i)
    net.got(27,"X",sin.at[1])
    smz[0]=smz[6]+sin[1]
    net.start(28,"Y",smz.at[0],sin.at[2])
    for j,(t,b) in enumerate((("X",wx),("Y",wy),("D",wd))):
        net.got(29+j,t,fq.at[b,c])
    for b in range(4):
        net.start(32+b,"C",fq.at[b,c],fq.at[b,c])
    net.got(28,"Y",sin.at[2])
    smz[1]=smz[0]+sin[2]
    net.got(23,"X",srx.at[top]); net.got(25,"Y",sry.at[top])
    net.got(24,"Y",sry.at[low]); net.got(26,"X",srx.at[low])
    own[...]=(gsr[pl.ds(mul(w*sh,16),sh),:].astype(F32)+srx[...].astype(F32)+sry[...].astype(F32)).astype(BF)
    seg=sh//SEG
    chains=[Chain(net,44,smz.at[1],smz.at[2],smz.at[3])]
    for i in range(SEG):
        r=pl.ds(i*seg,seg)
        chains.append(Chain(net,46+2*i,own.at[r],sz.at[0,r],sz.at[1,r]))
    for h in range(lax.axis_size("z")-1):
        for chain in chains: chain.hop(h)
    for chain in chains: chain.total()
    net.start(36,"C",own,fs)
    for i,chain in enumerate(early):
        chain.total()
        net.start(74+i,"C",es.at[eseg[i]],late_out.at[eseg[i]])
    put(8,es,early_out)
    for b in range(4): net.got(32+b,"C",fq.at[b,1-c])
    put(4,fq,gqkv_out); put(5,smz.at[1],small_out); put(6,own,gskip_out.at[c])
    net.got(36,"C",fs)
    put(7,fs,gskip_out.at[1-c])
    for i,r in enumerate(eseg): net.got(74+i,"C",late_out.at[r])
    for copy in outs: copy.wait()
    net.finish()

def last(gq,heads,normed,hidden,gmid,gain,block,long,wskip,small,eu,ed,eo):
    tokens,d=block.shape; S=jax.ShapeDtypeStruct; hd3=gq.shape[1]
    V=pltpu.VMEM
    return pl.pallas_call(last_kernel,
        out_shape=(S((tokens,d),BF),S((tokens,d),BF),S((8,d),F32),S((4,2,d//8,hd3),BF),S((2,d//4,d),BF),S((9*d//8,d),BF),S((9*d//8,d),BF)),
        in_specs=[VM,VM,ANY,ANY,ANY,VM,ANY,ANY,ANY,VM,ANY,ANY,ANY],out_specs=(ANY,)*7,
        scratch_shapes=[V((4*tokens,d),BF),V((4*tokens,d),BF),V((tokens,d),BF),V((tokens,d),BF),V((tokens//2,d),BF),V((tokens//2,d),BF),
            V((d,hd3),BF),V((d//2,hd3),BF),V((d,d),BF),V((2,d//2,hd3),BF),V((4,2,d//8,hd3),BF),
            V((d//8,d),BF),V((d//8,d),BF),V((d//4,d),BF),V((d//4,d),BF),V((d//4,d),BF),V((2,d//4,d),BF),V((d//4,d),BF),
            V((8,d),F32),V((3,8,d),F32),V((7,8,d),F32),
            V((9*d//8,d),BF),V((9*d//8,d),BF),V((9*d//8,d),BF),V((2,2,tokens//4,d),F32),
            pltpu.SemaphoreType.DMA((83,)),pltpu.SemaphoreType.DMA((83,)),pltpu.SemaphoreType.DMA((9,)),pltpu.SemaphoreType.DMA((9,)),pltpu.SemaphoreType.DMA((2,2))],
        compiler_params=pltpu.CompilerParams(vmem_limit_bytes=63*2**20,collective_id=1,has_side_effects=True),
        cost_estimate=pl.CostEstimate(flops=2*tokens*d*d*10,bytes_accessed=60*2**20,transcendentals=0))(
        gq,heads,normed,hidden,gmid,gain,block,long,wskip,small,eu,ed,eo)

SPLIT=((0,1152),)
def middle_kernel(hidden_ref,att_ref,tail_ref,g_ref,gain_ref,shift_ref,outw_ref,outx_ref,outy_ref,upw_ref,upx_ref,upy_ref,dnw_ref,
                  lay_out,gmid_ref,gh_out,ght_out,gow_out,small_ref,gup_out,gdn_out,sxu_out,sxd_out,syu_out,syd_out,uland,dland,ux_out,uy_out,dx_out,dy_out,
                  att_in,tail_in,att_s,outw_s,n2_s,xhat_s,rstd_s,lay_s,act_s,gu_s,upb,dnb,gub,gdb,land_u,land_d,low_s,
                  send,recv,csend,crecv,fetch_sem,flush_sem,local,usem,urecv,bring_sem):
    x,y,c,w,wx,wy,wd=place()
    tokens,d=hidden_ref.shape
    wide_cols=att_ref.shape[1]; quarter=tail_ref.shape[1]//4; cols=wide_cols+quarter
    kr=d//4; kh=kr//2; dh=d//2; dq=dh//2
    tc=tokens//4; th=tokens//2
    mul=pl.multiple_of
    net=Links(send,recv)
    left=[]
    def start(k,t,src,dst,view):
        pltpu.make_async_remote_copy(src_ref=src,dst_ref=dst,send_sem=send.at[k],recv_sem=recv.at[k],
                                     device_id=net.to[t],device_id_type=MESH).start()
        left.append((k,t,view))
    def blk(b): return pl.ds(mul(b*d,128),d)
    def urow(b,core): return pl.ds(mul(b*kr+core*kh,16),kh)
    def drow(b,core,p): return pl.ds(mul(b*d+core*dh+p*dq,16),dq)
    def trow(b): return pl.ds(mul(b*tokens,16),tokens)
    def tails(b): return pl.ds(mul(b*tc,16),tc)
    uview=uland.at[pl.ds(0,kh),pl.ds(0,d)]
    dview=dland.at[pl.ds(0,dq)]
    net.meet("XYDC")
    for j,(t,b) in enumerate((("X",wx),("Y",wy),("D",wd))):
        start(j,t,att_ref.at[trow(b)],att_in.at[w],att_in.at[0])
        start(52+j,t,tail_ref.at[tails(b)],tail_in.at[w],tail_in.at[0])
    own_att=[pltpu.make_async_copy(att_ref.at[trow(w)],att_in.at[w],local.at[0]),pltpu.make_async_copy(tail_ref.at[tails(w)],tail_in.at[w],local.at[3])]
    for copy in own_att: copy.start()
    cut=kh//32*16+16
    def orow(b,core,lo,n): return pl.ds(mul(b*kr+core*kh+lo,16),n)
    start(3,"Y",outx_ref.at[pl.ds(0,cut)],outw_s.at[orow(wx,c,0,cut)],outw_s.at[pl.ds(0,cut)])
    start(4,"X",outy_ref.at[pl.ds(cut,kh-cut)],outw_s.at[orow(wy,c,cut,kh-cut)],outw_s.at[pl.ds(0,kh-cut)])
    start(5,"C",outx_ref,outw_s.at[urow(wx,c)],outw_s.at[pl.ds(0,kh)])
    start(6,"C",outy_ref,outw_s.at[urow(wy,c)],outw_s.at[pl.ds(0,kh)])
    start(7,"Y",upx_ref.at[:,blk(wy)],uland.at[urow(wx,c),blk(wy)],uview)
    start(8,"X",upy_ref.at[:,blk(w)],uland.at[urow(wy,c),blk(w)],uview)
    order=(w,wx,wd,wy)
    def up_core(i):
        start(11+2*i,"C",upx_ref.at[:,blk(order[i])],uland.at[urow(wx,c),blk(order[i])],uview)
        start(12+2*i,"C",upy_ref.at[:,blk(order[i])],uland.at[urow(wy,c),blk(order[i])],uview)
    up_core(0)
    outw_s[pl.ds(mul(w*kr,16),kr),:]=outw_ref[...]
    outw_s[urow(wx,c),:]=outx_ref[...]
    outw_s[urow(wy,c),:]=outy_ref[...]

    diag_id=(7,8,9,10)
    def diag_from(i): return "YX"[i%2]
    def up_relay(i):
        view=uland.at[urow(wd,c),blk(order[i])]
        net.got(diag_id[i],diag_from(i),view)
        start(19+i,"C",view,view,uview)
    def up_sources(i):
        b=order[i]
        net.got(11+2*i,"C",uland.at[urow(wx,1-c),blk(b)])
        net.got(12+2*i,"C",uland.at[urow(wy,1-c),blk(b)])
        net.got(19+i,"C",uland.at[urow(wd,1-c),blk(b)])
        return [(upw_ref.at[:,blk(b)],pl.ds(mul(w*kr,16),kr)),(upx_ref.at[:,blk(b)],urow(wx,c)),(upy_ref.at[:,blk(b)],urow(wy,c)),
                (uland.at[urow(wx,1-c),blk(b)],urow(wx,1-c)),(uland.at[urow(wy,1-c),blk(b)],urow(wy,1-c)),
                (uland.at[pl.ds(mul(wd*kr,16),kr),blk(b)],pl.ds(mul(wd*kr,16),kr))]
    def fetch(i):
        slot=i%2
        for j,(src,rows) in enumerate(up_sources(i)):
            pltpu.make_async_copy(src,upb.at[slot,rows],fetch_sem.at[slot,j]).start()
        src=dnw_ref if i==0 else dland.at[pl.ds(mul(order[i]*d,16),d)]
        pltpu.make_async_copy(src,dnb.at[slot],fetch_sem.at[slot,6]).start()
    def fetched(slot):
        for j,n in enumerate((kr,kh,kh,kh,kh,kr)):
            view=upb.at[slot,pl.ds(0,n)]
            pltpu.make_async_copy(view,view,fetch_sem.at[slot,j]).wait()
        pltpu.make_async_copy(dnb.at[slot],dnb.at[slot],fetch_sem.at[slot,6]).wait()
    def down_relay(k,t,b,p,onward):
        r=drow(b,c,p)
        net.got(k,t,dland.at[r])
        for k2,t2 in onward: start(k2,t2,dland.at[r],dland.at[r],dview)
    def down_core(k,b,p): net.got(k,"C",dland.at[drow(b,1-c,p)])

    for j,(t,b) in enumerate((("X",wx),("Y",wy),("D",wd))):
        net.got(j,t,att_in.at[b])
        net.got(52+j,t,tail_in.at[b])
    start(9,"Y",upx_ref.at[:,blk(wx)],uland.at[urow(wx,c),blk(wx)],uview)
    start(10,"X",upy_ref.at[:,blk(wd)],uland.at[urow(wy,c),blk(wd)],uview)
    def dmine(p): return dnw_ref.at[pl.ds(mul(c*dh+p*dq,16),dq)]
    start(23,"X",dmine(0),dland.at[drow(w,c,0)],dview)
    start(25,"Y",dmine(1),dland.at[drow(w,c,1)],dview)
    start(24,"X",dmine(1),dland.at[drow(w,c,1)],dview)
    start(26,"Y",dmine(0),dland.at[drow(w,c,0)],dview)
    net.got(3,"Y",outw_s.at[orow(wd,c,0,cut)])
    net.got(4,"X",outw_s.at[orow(wd,c,cut,kh-cut)])
    start(35,"C",outw_s.at[urow(wd,c)],outw_s.at[urow(wd,c)],outw_s.at[pl.ds(0,kh)])
    up_relay(0)
    for i in (1,2,3): up_core(i)
    net.got(5,"C",outw_s.at[urow(wx,1-c)]); net.got(6,"C",outw_s.at[urow(wy,1-c)])
    net.got(35,"C",outw_s.at[urow(wd,1-c)])
    for copy in own_att: copy.wait()
    fetch(0)
    gain=gain_ref[...]; shift=shift_ref[...]
    for i in range(4):
        r=pl.ds(i*tc,tc)
        joined=jnp.concatenate([v for p in range(4) for v in (att_in[p,r,:],tail_in[p,:,i*quarter:(i+1)*quarter])],axis=1)
        att_s[r,:]=joined
        mid=hidden_ref[r,:]+nn(joined,outw_s[...])
        lay_s[r,:]=mid
        cen=mid-jnp.mean(mid,axis=1,keepdims=True)
        inv=lax.rsqrt(jnp.mean(cen*cen,axis=1,keepdims=True)+1e-5)
        xhat=cen*inv
        xhat_s[r,:]=xhat
        rstd_s[r,:]=jnp.broadcast_to(inv,(tc,128))
        n2_s[r,:]=(xhat*gain+shift).astype(BF)
        gmid_ref[r,:]=jnp.zeros((tc,d),F32)

    def pieces(slot):
        out=[(gub,pl.ds(mul(p*kr+(1-c)*kh,16),kh),land_u.at[slot,pl.ds(p*kh,kh)]) for p in range(4)]
        return out+[(gdb,pl.ds(mul((1-c)*dh,16),dh),land_d.at[slot])]
    def exchange(slot,act):
        for j,(ref,r,dst) in enumerate(pieces(slot)):
            act(pltpu.make_async_remote_copy(src_ref=ref.at[r],dst_ref=dst,send_sem=csend.at[slot,j],recv_sem=crecv.at[slot,j],
                                             device_id=net.to["C"],device_id_type=MESH))
    def flush(b,act):
        for p in range(4):
            act(pltpu.make_async_copy(gub.at[pl.ds(mul(p*kr+c*kh,16),kh)],gup_out.at[pl.ds(p*kh,kh),blk(b)],flush_sem.at[p]))
        act(pltpu.make_async_copy(gdb.at[pl.ds(mul(c*dh,16),dh)],gdn_out.at[pl.ds(mul(b*dh,16),dh)],flush_sem.at[4]))
    go=lambda copy: copy.start()
    done=lambda copy: copy.wait()
    def finalize(i):
        slot=lax.rem(i,2)
        exchange(slot,lambda copy: copy.wait())
        for p in range(4):
            r=pl.ds(mul(p*kr+c*kh,16),kh)
            gub[r,:]=(gub[r,:].astype(F32)+land_u[slot,pl.ds(p*kh,kh),:].astype(F32)).astype(BF)
        for p in range(2):
            r=pl.ds(mul(c*dh+p*dq,16),dq)
            gdb[r,:]=(gdb[r,:].astype(F32)+land_d[slot,pl.ds(p*dq,dq),:].astype(F32)).astype(BF)
    def block_of(i):
        return 2*lax.rem(y+i//2,2)+lax.rem(x+(i+1)//2,2)

    usend=[pl.ds(0,cut),pl.ds(cut,kh-cut)]
    def ahead(i,b,act):
        for j,(t,dst) in enumerate((("X",ux_out),("Y",uy_out))):
            n=usend[j]
            src=gup_out.at[pl.ds(mul(wd*kh+n.start,16),n.size),blk(b)]
            act(pltpu.make_async_remote_copy(src_ref=src,dst_ref=dst.at[:,blk(b)],send_sem=usem.at[i,j],recv_sem=urecv.at[i,j],
                                             device_id=net.to[t],device_id_type=MESH))
    def ahead_down(act):
        for j,(t,dst) in enumerate((("X",dx_out),("Y",dy_out))):
            act(pltpu.make_async_remote_copy(src_ref=gdn_out.at[pl.ds(mul(wd*dh+j*dq,16),dq)],dst_ref=dst,
                                             send_sem=usem.at[4,j],recv_sem=urecv.at[4,j],device_id=net.to[t],device_id_type=MESH))
    def weight_grads():
        for lo,n in SPLIT:
            f=pl.ds(lo,n)
            gdb[f,:]=tn(act_s[:,f],g_ref[...]).astype(BF)
            gub[f,:]=tn(n2_s[:,f],gu_s[...]).astype(BF)
    @pl.loop(0,4)
    def _(i):
        slot=lax.rem(i,2)
        fetched(slot)
        @pl.loop(0,2)
        def _(t):
            r=pl.ds(mul(t*th,16),th)
            for lo,n in SPLIT:
                f=pl.ds(lo,n)
                u=nn(n2_s[r,:],upb[slot,:,f])
                a,dg=gelu_parts(u)
                act_s[r,f]=a.astype(BF)
                gu_s[r,f]=(nt(g_ref[r,:],dnb[slot,f,:])*dg).astype(BF)
        @pl.when(i>=1)
        def _():
            finalize(i-1)
            flush(block_of(i-1),go)
        @pl.when(i==0)
        def _():
            for j in (1,2,3): up_relay(j)
        @pl.loop(0,2)
        def _(t):
            r=pl.ds(mul(t*th,16),th)
            for lo,n in SPLIT:
                f=pl.ds(lo,n)
                lay_s[r,f]+=nn(act_s[r,:],dnb[slot,:,f])
                gmid_ref[r,f]+=nt(gu_s[r,:],upb[slot,f,:])
        @pl.when(i==0)
        def _():
            down_relay(23,"X",wx,0,((27,"Y"),(29,"C")))
            down_relay(25,"Y",wy,1,((28,"X"),(30,"C")))
            down_relay(24,"X",wx,1,((31,"C"),))
            down_core(29,wx,0); down_core(31,wx,1)
            fetch(1)
        @pl.when(i==1)
        def _():
            down_relay(27,"Y",wd,0,((33,"C"),))
            down_relay(28,"X",wd,1,((34,"C"),))
            down_relay(26,"Y",wy,0,((32,"C"),))
            down_core(33,wd,0); down_core(34,wd,1)
            fetch(2)
        @pl.when(i==2)
        def _():
            down_core(30,wy,1); down_core(32,wy,0)
            fetch(3)
        @pl.when(i>=1)
        def _():
            flush(block_of(i-1),done)
            ahead(i-1,block_of(i-1),go)
        @pl.when(i==3)
        def _(): ahead_down(go)
        @pl.when(i<3)
        def _():
            weight_grads()
            exchange(slot,go)
    small_ref[...]=jnp.zeros_like(small_ref)
    for i in range(4):
        r=pl.ds(i*tc,tc)
        gs=gmid_ref[r,:]; xhat=xhat_s[r,:]
        small_ref[0:1,:]+=jnp.sum(gs*xhat,axis=0,keepdims=True)
        small_ref[1:2,:]+=jnp.sum(gs,axis=0,keepdims=True)
        e=gs*gain
        back=e-jnp.mean(e,axis=1,keepdims=True)-xhat*jnp.mean(e*xhat,axis=1,keepdims=True)
        gm=g_ref[r,:].astype(F32)+back*rstd_s[r,0:1]
        gmid_ref[r,:]=gm
        low=gm.astype(BF)
        low_s[r,:]=low
        ga=nt(low,outw_s[...]).astype(BF)
        for p in range(4):
            att_in[p,r,:]=ga[:,p*cols:p*cols+wide_cols]
            tail_in[p,:,i*quarter:(i+1)*quarter]=ga[:,p*cols+wide_cols:(p+1)*cols]
        for j,(t,b) in enumerate((("X",wx),("Y",wy),("D",wd))):
            start(36+3*i+j,t,att_in.at[b,r],gh_out.at[w,r],gh_out.at[0,pl.ds(0,tc)])
    for j,(t,b) in enumerate((("X",wx),("Y",wy),("D",wd))):
        start(55+j,t,tail_in.at[b],ght_out.at[w],tail_in.at[0])
    own_grad=[pltpu.make_async_copy(att_in.at[w],gh_out.at[w],local.at[2]),pltpu.make_async_copy(tail_in.at[w],ght_out.at[w],local.at[0])]
    for copy in own_grad: copy.start()
    weight_grads()
    exchange(1,go)
    act_s[...]=lay_s[...].astype(BF)
    lay_copy=pltpu.make_async_copy(act_s,lay_out,local.at[1])
    lay_copy.start()
    finalize(3)
    flush(wy,go)
    flush(wy,done)
    ahead(3,wy,go)
    for lo,n in SPLIT:
        f=pl.ds(lo,n)
        gub[f,:]=tn(att_s[:,f],low_s[...]).astype(BF)
    for p in range(4):
        start(48+p,"C",gub.at[pl.ds(mul(p*kr+(1-c)*kh,16),kh)],land_u.at[0,pl.ds(p*kh,kh)],land_u.at[0,pl.ds(0,kh)])
    def bring(k,src,dst):
        copy=pltpu.make_async_copy(src,dst,bring_sem.at[k]); copy.start(); return copy
    def spot(j,b): return pl.ds((4*j+b)*kh,kh)
    copies=[]
    for j,b2 in enumerate((wx,wy)):
        for b in range(4):
            copies.append(bring(4*j+b,gup_out.at[pl.ds(mul(b2*kh,16),kh),pl.ds(b*d,d)],upb.at[0,spot(j,b)]))
        copies.append(bring(16+j,gdn_out.at[pl.ds(mul(b2*dh,16),dh)],dnb.at[0,pl.ds(j*dh,dh)]))
    for i in range(4): ahead(i,order[i],done)
    ahead_down(done)
    for j,(src,n) in enumerate(((uy_out,usend[1]),(ux_out,usend[0]))):
        for b in range(4):
            copies.append(bring(8+4*j+b,src.at[:,pl.ds(b*d,d)],upb.at[1,pl.ds((4*j+b)*kh,n.size)]))
    copies.append(bring(18,dy_out,dnb.at[1,pl.ds(0,dq)]))
    copies.append(bring(19,dx_out,dnb.at[1,pl.ds(dq,dq)]))
    for copy in copies: copy.wait()
    copies=[]
    for j,(uo,do) in enumerate(((sxu_out,sxd_out),(syu_out,syd_out))):
        n=usend[1-j]
        for b in range(4):
            lo=(4*j+b)*kh
            r=pl.ds(lo+n.start,n.size)
            upb[0,r,:]=(upb[0,r,:].astype(F32)+upb[1,pl.ds(lo,n.size),:].astype(F32)).astype(BF)
            copies.append(bring(4*j+b,upb.at[0,spot(j,b)],uo.at[:,pl.ds(b*d,d)]))
        r=pl.ds(j*dh+(1-j)*dq,dq)
        dnb[0,r,:]=(dnb[0,r,:].astype(F32)+dnb[1,pl.ds(j*dq,dq),:].astype(F32)).astype(BF)
        copies.append(bring(16+j,dnb.at[0,pl.ds(j*dh,dh)],do.at[pl.ds(0,dh)]))
    for p in range(4):
        net.got(48+p,"C",land_u.at[0,pl.ds(p*kh,kh)])
        r=pl.ds(mul(p*kr+c*kh,16),kh)
        land_u[1,pl.ds(p*kh,kh),:]=(gub[r,:].astype(F32)+land_u[0,pl.ds(p*kh,kh),:].astype(F32)).astype(BF)
    for k,(b,dst) in enumerate(((w,gow_out.at[0]),(wd,gow_out.at[1]),(wx,sxd_out.at[pl.ds(dh,kh)]),(wy,syd_out.at[pl.ds(dh,kh)]))):
        copies.append(bring(8+k,land_u.at[1,pl.ds(mul(b*kh,16),kh)],dst))
    for i in range(4):
        for j,(t,b) in enumerate((("X",wx),("Y",wy),("D",wd))):
            net.got(36+3*i+j,t,gh_out.at[b,pl.ds(i*tc,tc)])
    for j,(t,b) in enumerate((('X',wx),('Y',wy),('D',wd))): net.got(55+j,t,ght_out.at[b])
    for copy in [lay_copy]+own_grad+copies: copy.wait()
    for k,t,view in left:
        pltpu.make_async_remote_copy(src_ref=view,dst_ref=view,send_sem=send.at[k],recv_sem=recv.at[k],
                                     device_id=net.to[t],device_id_type=MESH).wait_send()

def middle(hidden,att,tail,g,gain,shift,outw,outx,outy,upw,upx,upy,dnw):
    tokens,d=hidden.shape; cols=att.shape[1]; ff=upw.shape[1]
    S=jax.ShapeDtypeStruct; V=pltpu.VMEM; D=pltpu.SemaphoreType.DMA
    kh=d//8; cut=kh//32*16+16
    return pl.pallas_call(middle_kernel,
        out_shape=(S((tokens,d),BF),S((tokens,d),F32),S((4,tokens,cols),BF),S((4,tokens//4,tail.shape[1]),BF),S((2,kh,d),BF),S((8,d),F32),S((d//2,ff),BF),S((ff//2,d),BF),
                   S((kh,ff),BF),S((ff//8+kh,d),BF),S((kh,ff),BF),S((ff//8+kh,d),BF),
                   S((d,ff),BF),S((ff,d),BF),S((cut,ff),BF),S((kh-cut,ff),BF),S((ff//16,d),BF),S((ff//16,d),BF)),
        in_specs=[VM,ANY,ANY]+[VM]*6+[ANY]*4,out_specs=(ANY,VM,ANY,ANY,ANY,VM)+(ANY,)*12,
        scratch_shapes=[V((4,tokens,cols),BF),V((4,tokens//4,tail.shape[1]),BF),V((tokens,d),BF),V((d,d),BF),V((tokens,d),BF),V((tokens,d),F32),V((tokens,128),F32),
            V((tokens,d),F32),V((tokens,d),BF),V((tokens,d),BF),V((2,d,d),BF),V((2,d,d),BF),V((d,d),BF),V((d,d),BF),
            V((2,d//2,d),BF),V((2,d//2,d),BF),V((tokens,d),BF),D((58,)),D((58,)),D((2,5)),D((2,5)),D((2,7)),D((5,)),D((4,)),
            D((5,2)),D((5,2)),D((20,))],
        compiler_params=pltpu.CompilerParams(vmem_limit_bytes=63*2**20,collective_id=2,has_side_effects=True),
        cost_estimate=pl.CostEstimate(flops=2*tokens*d*(ff*6+d*3),bytes_accessed=60*2**20,transcendentals=tokens*ff*2))(
        hidden,att,tail,g,gain,shift,outw,outx,outy,upw,upx,upy,dnw)

def assemble_kernel(lay_ref,gin_ref,gsk_ref,skip_ref,gq_ref,em_ref,eo_ref,
                    lay_out,gin_out,gsk_out,skip_out,qkv_out,up_out,down_out,out_out,
                    s0,s1,s2,s3,s4,s5,s6,s7,local):
    first=lax.axis_index("core")==0
    copies=[]
    def put(src,dst):
        copy=pltpu.make_async_copy(src,dst,local.at[len(copies)]); copy.start(); copies.append(copy)
    def chunks(n,body,size=144):
        @pl.loop(0,n//size)
        def _(i): body(pl.ds(pl.multiple_of(i*size,16),size))
    def wide(dst,src):
        def body(r): dst[r,:]=src[r,:].astype(F32)
        chunks(dst.shape[0],body,208 if dst.shape[0]%208==0 else 144)
    wide(s7,lay_ref); put(s7,lay_out)
    wide(s0,gin_ref); put(s0,gin_out)
    wide(s1,gsk_ref); put(s1,gsk_out)
    kh=s6.shape[1]; d=s6.shape[2]
    def pair(dst,seg,rows,cols,size=48):
        @pl.loop(0,kh//size)
        def _(i):
            r=pl.ds(pl.multiple_of(seg*kh+i*size,16),size)
            to=pl.ds(pl.multiple_of(rows+i*size,16),size)
            m,o=em_ref[r,:].astype(F32),eo_ref[r,:].astype(F32)
            dst[0,to,cols]=jnp.where(first,m,o)
            dst[1,to,cols]=jnp.where(first,o,m)
    for b in range(4): pair(s4,b,0,pl.ds(b*d,d))
    put(s4,up_out)
    for b in range(4): pair(s5,4+b,b*kh,pl.ds(0,d))
    put(s5,down_out)
    pair(s6,8,0,pl.ds(0,d)); put(s6,out_out)
    def skip(r): s2[r,:]=skip_ref[r,:].astype(F32)
    chunks(s2.shape[0],skip); put(s2,skip_out)
    hd=gq_ref.shape[3]//3; kh=gq_ref.shape[2]
    for core in range(2):
        for i in range(kh//48):
            r=pl.ds(i*48,48)
            s3[pl.ds(core*kh+i*48,48),:]=jnp.concatenate([gq_ref[p,core,r,s*hd:(s+1)*hd].astype(F32) for s in range(3) for p in range(4)],axis=1)
    put(s3,qkv_out)
    for copy in copies: copy.wait()

def assemble(lay,gin,gsk,skip,gq,em,eo):
    S=lambda *s: jax.ShapeDtypeStruct(s,F32)
    tokens,d=gin.shape
    shapes=(S(tokens,d),S(tokens,d),S(*skip.shape),S(d//4,3*d),S(2,d//8,4*d),S(2,d//2,d),S(2,d//8,d))
    return pl.pallas_call(assemble_kernel,out_shape=(shapes[0],)+shapes,in_specs=[VM]*7,out_specs=(ANY,)*8,
        scratch_shapes=[pltpu.VMEM(s.shape,F32) for s in shapes+shapes[:1]]+[pltpu.SemaphoreType.DMA((8,))],
        compiler_params=pltpu.CompilerParams(vmem_limit_bytes=60*2**20),
        cost_estimate=pl.CostEstimate(flops=0,bytes_accessed=40*2**20,transcendentals=0))(
        lay,gin,gsk,skip,gq,em,eo)

from jax.sharding import Mesh, PartitionSpec as P
WIDE=("y","x"); ROWS=("z","core")
SWAP=[(0,1),(1,0)]

def swap_cores(values):
    return lax.ppermute(values,"core",SWAP)

def pick(values, index, axis):
    return lax.dynamic_index_in_dim(values,index,axis,keepdims=False)

def place_halves(mine, other, core, axis):
    first=jnp.where(core==0,mine,other); second=jnp.where(core==0,other,mine)
    return jnp.stack([first,second],axis=axis)

def dot(a,b): return jnp.dot(a,b,preferred_element_type=F32)

def norm(values):
    cen=values-jnp.mean(values,axis=1,keepdims=True)
    inv=lax.rsqrt(jnp.mean(cen*cen,axis=1,keepdims=True)+1e-5)
    return cen*inv,inv

def on_device(nw, block_input, long_skip, segment_ids, item_lengths, skip_weight, first_gain, first_shift, qkv_weight,
              out_weight, second_gain, second_shift, up_weight, down_weight, output_grad):
    core=lax.axis_index("core")
    _,tokens,d=block_input.shape
    heads=qkv_weight.shape[1]//(3*HEAD*nw); hd=heads*HEAD
    ff=up_weight.shape[1]; fb=ff//(2*nw)
    gather=lambda v: lax.all_gather(v,WIDE,axis=0,tiled=True)
    near=nw==4
    vecs=jnp.stack([first_gain,first_shift,second_gain,second_shift]+[first_gain]*4).astype(F32)
    if near:
        hidden,normed_all,qkv,w_heads,w_skip,vecs=first(block_input[0],long_skip[0],skip_weight,qkv_weight,vecs)
        vec=vecs.transpose(1,0,2).reshape(8,d)
        gain1,shift1,gain2,shift2=[vec[i:i+1] for i in range(4)]
        half=lambda v: lax.dynamic_slice_in_dim(v,core*(v.shape[0]//2),v.shape[0]//2)
        qkv,up_half,out_half=lax.optimization_barrier((qkv,half(up_weight),half(out_weight)))
        up_x,out_x=lax.ppermute((up_half,out_half),"x",SWAP)
        up_y,out_y=lax.ppermute((up_half,out_half),"y",SWAP)
    else:
        vec=gather(vecs.astype(BF).T).T.astype(F32)
        gain1,shift1,gain2,shift2=[vec[i:i+1] for i in range(4)]
        w_skip=gather(skip_weight)
        joined=jnp.concatenate([block_input[0],long_skip[0]],axis=1)
        w_heads=qkv_weight.reshape(d//nw,3,nw,hd).transpose(2,0,1,3)
        w_heads=lax.all_to_all(w_heads,WIDE,0,0).reshape(d,3*hd)
        hidden=dot(joined,w_skip)
        xhat1,inv1=norm(hidden)
        normed_all=gather((xhat1*gain1+shift1).astype(BF))
        qkv=dot(normed_all,w_heads).astype(BF)
    *att,lse=attend(item_lengths,qkv,heads,near)
    if near:
        lay,gmid,gatt,gtail,gow,small,gup,gdn,sxu,sxd,syu,syd=middle(hidden,*att,output_grad[0],gain2,shift2,out_weight,out_x,out_y,
            up_weight,up_x,up_y,down_weight)[:12]
        grad_heads=gatt.reshape(nw*tokens,-1),gtail.reshape(tokens,-1)
    else:
        w_out=gather(out_weight)
        up_mine=gather(pick(up_weight.reshape(d//nw,nw,2,fb),core,2).reshape(d//nw,nw*fb))
        down_mine=gather(pick(down_weight.reshape(2,fb,d),core,0))
        up_other,down_other=swap_cores(up_mine),swap_cores(down_mine)
        att=lax.all_to_all(att[0].reshape(nw,tokens,hd),WIDE,0,0)
        lay,gmid,gatt,gow,small,gupo,guph,gdno,gdnh=mlp(hidden,att,w_out,gain2,shift2,output_grad[0],up_mine,up_other,down_mine,down_other)
        grad_heads=(lax.all_to_all(gatt,WIDE,0,0).reshape(nw*tokens,hd),)

    def scatter(mine,other):
        both=(mine.astype(F32)+swap_cores(other).astype(F32)).astype(BF)
        return lax.psum_scatter(both,WIDE,scatter_dimension=0,tiled=True)
    def both_cores(mine,axis):
        return place_halves(mine,swap_cores(mine),core,axis).astype(F32)
    def by_rows(grad):
        cut=grad.reshape(nw,2,-1,grad.shape[1])
        return scatter(pick(cut,core,1).reshape(-1,grad.shape[1]),pick(cut,1-core,1).reshape(-1,grad.shape[1]))
    if near:
        wide=2*lax.axis_index("y")+lax.axis_index("x")
        part=lambda v: lax.dynamic_index_in_dim(v.reshape(4,-1,v.shape[1]),wide,0,False)
        from_x=lax.ppermute((sxu,sxd),"x",SWAP)
        from_y=lax.ppermute((syu,syd),"y",SWAP)
        from_d=lax.ppermute(gow[1],WIDE,[(i,3-i) for i in range(4)])
    else:
        early=scatter(gupo,guph),scatter(gdno,gdnh),by_rows(gow)
    grad_qkv=attend_back(item_lengths,qkv,grad_heads,lse,heads)
    if near:
        grad_qkv,from_x,from_y,from_d=lax.optimization_barrier((grad_qkv,from_x,from_y,from_d))
        up_sum=part(gup).astype(F32)+from_x[0].astype(F32)+from_y[0].astype(F32)
        rows=gdn.shape[0]//4
        pair=from_x[1].astype(F32)+from_y[1].astype(F32)
        down_sum=part(gdn).astype(F32)+pair[:rows]
        out_sum=gow[0].astype(F32)+pair[rows:]+from_d.astype(F32)
        early=up_sum.astype(BF),down_sum.astype(BF),out_sum.astype(BF)
    grad_qkv,early=lax.optimization_barrier((grad_qkv,early))
    if not near: early=lax.psum(early,"z")
    if near:
        gin,gsk,smalls,gqkv,gskip,mine,other=last(grad_qkv,w_heads,normed_all,hidden,gmid,gain1,block_input[0],long_skip[0],w_skip,small,*early)
        lay,gin,gsk,skip_share,qkv_share,up_share,down_share,out_share=assemble(lay,gin,gsk,gskip.reshape(-1,d),gqkv,mine,other)
        up_share,down_share,out_share=up_share.reshape(-1,ff),down_share.reshape(-1,d),out_share.reshape(-1,d)
        smalls=lax.dynamic_slice_in_dim(smalls[:4],(2*lax.axis_index("y")+lax.axis_index("x"))*(d//nw),d//nw,axis=1).T
    else:
        part_first=nt(grad_qkv,w_heads).astype(BF)
        grad_first=lax.psum_scatter(part_first,WIDE,scatter_dimension=0,tiled=True).astype(F32)
        gqkv=tn(normed_all,grad_qkv).astype(BF).reshape(nw,2,d//nw//2,3*hd)
        gqkv=(pick(gqkv,core,1).astype(F32)+swap_cores(pick(gqkv,1-core,1)).astype(F32)).astype(BF)
        e1=grad_first*gain1
        across=inv1*(e1-jnp.mean(e1,axis=1,keepdims=True)-xhat1*jnp.mean(e1*xhat1,axis=1,keepdims=True))
        grad_hidden=(gmid+across).astype(BF)
        gskip=by_rows(tn(joined,grad_hidden).astype(BF))
        grad_joined=nt(grad_hidden,w_skip)
        gin,gsk=grad_joined[:,:d],grad_joined[:,d:]
        small1=jnp.stack([jnp.sum(grad_first*xhat1,axis=0),jnp.sum(grad_first,axis=0)])
        gqkv,gskip,early=lax.optimization_barrier((gqkv,gskip,early))
        gqkv,gskip=lax.psum((gqkv,gskip),"z")
        up_share=both_cores(early[0].reshape(d//nw,nw,fb),2).reshape(d//nw,ff)
        down_share=both_cores(early[1],0).reshape(ff//nw,d)
        out_share=both_cores(early[2],0).reshape(d//nw,d)
        skip_share=both_cores(gskip,0).reshape(2*d//nw,d)
        gqkv=lax.all_to_all(gqkv,WIDE,0,0).reshape(nw,-1,3,hd).transpose(1,2,0,3)
        qkv_share=both_cores(gqkv,0).reshape(d//nw,-1)
        smalls=jnp.stack([small1[0],small1[1],small[0],small[1]],axis=1)
        smalls=lax.psum(lax.psum_scatter(smalls.astype(BF),WIDE,scatter_dimension=0,tiled=True),ROWS).astype(F32)
    return (lay[None],gin[None],gsk[None],skip_share,smalls[:,0],smalls[:,1],qkv_share,out_share,
            smalls[:,2],smalls[:,3],up_share,down_share)

def solution(mesh):
    rows,wide=mesh.devices.shape
    side=2 if wide==4 else int(wide**0.5)
    grid=Mesh(mesh.devices.reshape(rows//2,2,wide//side,side),("z","core","y","x"))
    tok=P(ROWS,WIDE,None); row=P(ROWS,None); mat=P(WIDE,None); vec=P(WIDE)
    return jax.shard_map(functools.partial(on_device,wide),mesh=grid,
        in_specs=(tok,tok,row,row,mat,vec,vec,mat,mat,vec,vec,mat,mat,tok),
        out_specs=(tok,tok,tok,mat,vec,vec,mat,mat,vec,vec,mat,mat),check_vma=False)
```
